32 devices in a mesh: grp: 2 (over y), lon: 4 (over z), lat: 4 (over x, core).
Axes of the slice: x: 2, y: 2, z: 4, core: 2. Of those that a mesh axis runs over, the one named last changes fastest.
Arguments:
- grid_in: bfloat16 [64, 1024, 474], P(('grp', 'lat'), 'lon'), parts along dimension 0, may hold values from -6 to 6
- mesh_lat: bfloat16 [8192, 512], P(('grp', 'lon', 'lat')), parts along dimension 0, may hold values from -6 to 6
- edge_w: bfloat16 [1024, 128, 128], P(('grp', 'lon', 'lat')), parts along dimension 0, may hold values from -0.23925781 to 0.23925781
- edge_src: int32 [1024], P(('grp', 'lon', 'lat')), parts along dimension 0, may hold values from 0 to 39
- edge_dst: int32 [1024], P(('grp', 'lon', 'lat')), parts along dimension 0, may hold values from 0 to 1
- block_count: int32 [32], P(('grp', 'lon', 'lat')), parts along dimension 0, may hold values from 16 to 32, as said below
- embed_w: bfloat16 [474, 512], replicated, may hold values from -0.25 to 0.25
- message_w: bfloat16 [512, 512], replicated, may hold values from -0.25 to 0.25
- up_w: bfloat16 [512, 512], replicated, may hold values from -0.25 to 0.25
- out_w: bfloat16 [512, 512], replicated, may hold values from -0.25 to 0.25
- gain: float32 [512], replicated, may hold values from 0.1 to 1.9
- cot: bfloat16 [8192, 512], P(('grp', 'lon', 'lat')), parts along dimension 0, may hold values from -6 to 6
Outputs:
- mesh_new: bfloat16 [8192, 512], P(('grp', 'lon', 'lat')), parts along dimension 0
- mesh_latent_gradient: float32 [8192, 512], P(('grp', 'lon', 'lat')), parts along dimension 0
- grad_embed: float32 [948, 512], P('grp'), parts along dimension 0
- grad_message: float32 [1024, 512], P('grp'), parts along dimension 0
- grad_up: float32 [1024, 512], P('grp'), parts along dimension 0
- grad_out: float32 [1024, 512], P('grp'), parts along dimension 0
- grad_gain: float32 [1024], P('grp'), parts along dimension 0
The draws below stay inside these ranges and needn't reach their ends.
There are 2 independent parts, one for each index of `grp`. The reference program is written for one: setup_inputs(seed, part) draws one part's arguments, and reference() takes and returns one part's arrays. A program takes and returns all parts, laid end to end along the dimension named above; an argument that names none is the same for every part. Nothing has to cross between parts.
Inputs may be any that keep to these rules, and one draw needn't show every extreme that they name: `block_count`: each tile uses between 16 and 32 slots; some tile uses all 32.
All inputs are finite; a program needn't handle non-finite values.
Results may differ from the reference program's by a relative error of at most 0.013.
Values may be sent and summed in bfloat16 or wider, within the bound.
No kernel may reach another device: no remote copies, remote signals or barrier semaphores. Data moves between devices by JAX's collectives and lax.ppermute only.
A program may use at most 128 MiB of HBM per device.

```python
import jax
import jax.numpy as jnp
from jax import lax

D = 512
F = 474
BLK = 128
GR = 8
GC = 256
NB = 32
MB = 2
GRID_R = 32
GRID_C = 1024
MESH = 4096
NBLK = 512
N_LON = 4
N_LAT = 4


def draw_block_count(key, part):
    key = jax.random.fold_in(key, 11)
    key_loads, key_chosen = jax.random.split(key)
    tile_total = N_LON * N_LAT
    loads = jax.random.randint(key_loads, (tile_total,), NB // 2, NB + 1)
    chosen = jax.random.randint(key_chosen, (), 0, tile_total)
    return jnp.where(jnp.arange(tile_total) == chosen, NB, loads).astype(jnp.int32)


def touch_ends(array, key, smallest, largest):
    longest = array.shape.index(max(array.shape))
    spots = []
    for shift in (0, 1):
        where = [jax.random.randint(jax.random.fold_in(key, axis), (), 0, length) for axis, length in enumerate(array.shape)]
        where[longest] = (where[longest] + shift) % array.shape[longest]
        spots.append(tuple(where))
    return array.at[spots[0]].set(smallest).at[spots[1]].set(largest)


def block_scale(stream_key, extent, cuts, low, high):
    def one(dim, shards_of):
        draws = jax.random.uniform(jax.random.fold_in(jax.random.fold_in(stream_key, 6), dim), (shards_of,), jnp.float32, low / len(cuts), high / len(cuts))
        return jnp.repeat(jnp.exp(draws), extent[dim] // shards_of).reshape((-1,) + (1,) * (len(extent) - dim - 1))

    factor_of = one(*cuts[0])
    for cut in cuts[1:]:
        factor_of = factor_of * one(*cut)
    return factor_of


def centred(own_key, extent, scale, limit, shards=(), kind=jnp.bfloat16):
    loudness = block_scale(own_key, extent, shards, -0.22, 0.18) if shards else 1.0
    drawn = jax.random.normal(own_key, extent, jnp.float32) * scale * loudness
    return jnp.minimum(jnp.maximum(drawn, -limit), limit).astype(kind)


def setup_inputs(seed: int = 0, part: int = 0) -> dict:
    splits = jax.random.split(jax.random.key(seed), 13)
    part_splits = jax.random.split(jax.random.fold_in(splits[12], part), 13)
    grid_in = centred(part_splits[0], (GRID_R, GRID_C, F), 1.0, 6.0, ((0, 4), (1, 4)))
    mesh_lat = centred(part_splits[1], (MESH, D), 1.0, 6.0, ((0, 16),))
    edge_w = centred(part_splits[2], (NBLK, BLK, BLK), 0.04, 0.23925781, ((0, 16),))
    edge_src = touch_ends(jax.random.randint(part_splits[3], (NBLK,), 0, GR * 5), jax.random.fold_in(part_splits[3], 1), 0, (GR * 5) - 1).astype(jnp.int32)
    edge_dst = touch_ends(jax.random.randint(part_splits[4], (NBLK,), 0, MB), jax.random.fold_in(part_splits[4], 1), 0, MB - 1).astype(jnp.int32)
    block_count = draw_block_count(jax.random.fold_in(jax.random.fold_in(splits[12], part), 71), part)
    embed_w = centred(splits[6], (F, D), F ** -0.5, 0.25)
    message_w = centred(splits[7], (D, D), D ** -0.5, 0.25)
    up_w = centred(splits[8], (D, D), D ** -0.5, 0.25)
    out_w = centred(splits[9], (D, D), D ** -0.5, 0.25)
    gain = jnp.clip(1.0 + 0.18 * jax.random.normal(splits[10], (D,), jnp.float32), 0.1, 1.9)
    cot = centred(part_splits[11], (MESH, D), 1.0, 6.0, ((0, 16),))
    return {"grid_in": grid_in, "mesh_lat": mesh_lat, "edge_w": edge_w, "edge_src": edge_src, "edge_dst": edge_dst, "block_count": block_count, "embed_w": embed_w, "message_w": message_w, "up_w": up_w, "out_w": out_w, "gain": gain, "cot": cot}


epsilon = 1e-05

def silu_slope(value_entries):
    sigma = jax.nn.sigmoid(value_entries)
    return sigma * (1.0 + value_entries * (1.0 - sigma))

def reference(grid_in, mesh_lat, edge_w, edge_src, edge_dst, block_count, embed_w, message_w, up_w, out_w, gain, cot):
    lat_tiles = N_LAT
    lon_tiles = N_LON
    half_block = BLK // 2
    pieces = (GC + BLK) // half_block
    windows = pieces - 1
    devices_part = lat_tiles * lon_tiles
    floating_dtype = jnp.float32
    grid_tiles = grid_in.reshape(lat_tiles, GR * GRID_C, F)

    def embed_tile(inputs):
        pre = jnp.dot(inputs, embed_w, preferred_element_type=floating_dtype)
        hidden = jax.nn.silu(pre).astype(jnp.bfloat16)
        message = jnp.dot(hidden, message_w, preferred_element_type=floating_dtype).astype(jnp.bfloat16)
        return (hidden, message)
    hidden_all, message_all = lax.map(embed_tile, grid_tiles)
    message_rows = message_all.reshape(lat_tiles, GR, GRID_C, D)
    weights_dev = edge_w.reshape(devices_part, NB, BLK, BLK)
    source_dev = edge_src.reshape(devices_part, NB)
    target_dev = edge_dst.reshape(devices_part, NB)
    mesh_dev = mesh_lat.reshape(devices_part, MB * BLK, D)
    cot_dev = cot.reshape(devices_part, MB * BLK, D)
    gain_float = gain.astype(floating_dtype)

    def device(index):
        lon_index = index // lat_tiles
        lat_index = index % lat_tiles
        columns = (lon_index * GC - half_block + jnp.arange(GC + BLK, dtype=jnp.int32)) % GRID_C
        tile_rows = lax.dynamic_index_in_dim(message_rows, lat_index, 0, keepdims=False)
        extended = jnp.take(tile_rows, columns, axis=1)
        halves = extended.reshape(GR * pieces, half_block, D)
        source = source_dev[index]
        first = (source // windows * pieces + source % windows).astype(jnp.int32)
        block_groups = jnp.concatenate((halves[first], halves[first + 1]), axis=1)
        active = (jnp.arange(NB, dtype=jnp.int32) < block_count[index]).astype(jnp.bfloat16)
        weight_entries = weights_dev[index] * active[:, None, None]
        target = target_dev[index]
        product_terms = jnp.einsum('yjc,ycz->yjz', weight_entries.astype(floating_dtype), block_groups.astype(floating_dtype))
        aggregate = jax.ops.segment_sum(product_terms, target, num_segments=MB).reshape(MB * BLK, D)
        mesh_rows = mesh_dev[index].astype(floating_dtype)
        cot_rows = cot_dev[index]
        summed = mesh_rows + aggregate
        rinv = lax.rsqrt(lax.optimization_barrier(jnp.mean(summed * summed, axis=1, keepdims=True)) + epsilon)
        qhat = summed * rinv
        normed = (qhat * gain_float).astype(jnp.bfloat16)
        pre_up = jnp.dot(normed, up_w, preferred_element_type=floating_dtype)
        update = jax.nn.silu(pre_up).astype(jnp.bfloat16)
        mesh_new = (mesh_rows + jnp.dot(update, out_w, preferred_element_type=floating_dtype)).astype(jnp.bfloat16)
        grad_out = jnp.dot(update.T, cot_rows, preferred_element_type=floating_dtype)
        grad_update = jnp.dot(cot_rows, out_w.T, preferred_element_type=floating_dtype)
        grad_pre_up = (grad_update * silu_slope(pre_up)).astype(jnp.bfloat16)
        grad_up = jnp.dot(normed.T, grad_pre_up, preferred_element_type=floating_dtype)
        grad_normed = jnp.dot(grad_pre_up, up_w.T, preferred_element_type=floating_dtype)
        grad_gain = lax.optimization_barrier(jnp.sum(grad_normed * qhat, axis=0))
        grad_qhat = grad_normed * gain_float
        grad_q = rinv * (grad_qhat - qhat * lax.optimization_barrier(jnp.mean(grad_qhat * qhat, axis=1, keepdims=True)))
        mesh_latent_gradient = cot_rows.astype(floating_dtype) + grad_q
        grad_aggregate = grad_q.astype(jnp.bfloat16).reshape(MB, BLK, D)
        selected_entries = grad_aggregate[target]
        backward_result = jnp.einsum('woi,won->win', weight_entries.astype(floating_dtype), selected_entries.astype(floating_dtype))
        spread = jnp.zeros((GR * pieces, half_block, D), floating_dtype)
        spread = spread.at[first].add(backward_result[:, :half_block]).at[first + 1].add(backward_result[:, half_block:])
        return (mesh_new, mesh_latent_gradient, spread.reshape(GR, GC + BLK, D), grad_out, grad_up, grad_gain)
    outputs = lax.map(device, jnp.arange(devices_part, dtype=jnp.int32))
    new_all, grad_mesh_all, back_all, out_terms, up_terms, gain_terms = outputs
    back_grid = back_all.reshape(lon_tiles, lat_tiles, GR, GC + BLK, D)
    middle = back_grid[:, :, :, half_block:half_block + GC]
    west_rim = back_grid[:, :, :, :half_block]
    east_rim = back_grid[:, :, :, half_block + GC:]
    middle = middle.at[:, :, :, GC - half_block:].add(jnp.roll(west_rim, -1, axis=0))
    middle = middle.at[:, :, :, :half_block].add(jnp.roll(east_rim, 1, axis=0))
    message_grad = jnp.transpose(middle, (1, 2, 0, 3, 4)).reshape(lat_tiles, GR * GRID_C, D)

    def grid_back(pack):
        inputs, hidden, field = pack
        grad_message_b = field.astype(jnp.bfloat16)
        grad_msg = jnp.dot(hidden.T, grad_message_b, preferred_element_type=floating_dtype)
        grad_hidden = jnp.dot(grad_message_b, message_w.T, preferred_element_type=floating_dtype)
        pre = jnp.dot(inputs, embed_w, preferred_element_type=floating_dtype)
        grad_pre = (grad_hidden * silu_slope(pre)).astype(jnp.bfloat16)
        grad_emb = jnp.dot(inputs.T, grad_pre, preferred_element_type=floating_dtype)
        return (grad_msg, grad_emb)
    message_terms, embed_terms = lax.map(grid_back, (grid_tiles, hidden_all, message_grad))
    return (new_all.reshape(MESH, D), grad_mesh_all.reshape(MESH, D), lax.optimization_barrier(jnp.sum(embed_terms, axis=0)), lax.optimization_barrier(jnp.sum(message_terms, axis=0)), lax.optimization_barrier(jnp.sum(up_terms, axis=0)), lax.optimization_barrier(jnp.sum(out_terms, axis=0)), lax.optimization_barrier(jnp.sum(gain_terms, axis=0)))
```

```python
import jax
import jax.numpy as jnp
from jax import lax
from jax.experimental import pallas as pl
from jax.experimental.pallas import tpu as pltpu
from jax.sharding import PartitionSpec as P

epsilon = 1e-05
BF = jnp.bfloat16
F32 = jnp.float32
VMEM_BYTES = 48 * 1024 * 1024


def contract(a, b, dim_a, dim_b):
    return lax.dot_general(a, b, (((dim_a,), (dim_b,)), ((), ())), preferred_element_type=F32)


def silu_pair(pre):
    sigma = jax.nn.sigmoid(pre)
    return pre * sigma, sigma * (1.0 + pre * (1.0 - sigma))


def own_kernel(src, dst, count, grid, embed_w, edge_w, cot, out_w, a_halo, a_t, h_own, slope, x_t, grad_update, acc):
    rows, cols, features = grid.shape
    block = edge_w.shape[1]
    half = block // 2
    own_blocks = cols // block
    windows = 2 * own_blocks + 1
    nodes = acc.shape[1]
    acc[...] = jnp.zeros(acc.shape, F32)
    lane = lax.broadcasted_iota(jnp.int32, (block, block), 1)

    def slot(b, carry):
        source = src[b]
        row = source // windows
        window = source - row * windows
        at = window // 2
        target = pl.ds(pl.multiple_of(dst[b] * block, block), block)
        weights = edge_w[b].astype(F32)

        @pl.when(window % 2 == 1)
        def _():
            acc[row * own_blocks + at, target, :] += weights

        @pl.when(window % 2 == 0)
        def _():
            halo_block = rows * own_blocks + row
            turned = pltpu.roll(weights, half, 1)
            first = jnp.where(at == 0, halo_block, row * own_blocks + at - 1)
            second = jnp.where(at == own_blocks, halo_block, row * own_blocks + at)
            acc[first, target, :] += jnp.where(lane >= half, turned, 0.0)
            acc[second, target, :] += jnp.where(lane < half, turned, 0.0)

        return carry

    lax.fori_loop(0, count[0], slot, 0)
    total = jnp.zeros(h_own.shape, F32)
    for r in range(rows):
        part = jnp.concatenate([acc[r * own_blocks + k] for k in range(own_blocks)], axis=1)
        a_t[r * cols : (r + 1) * cols, :] = part.T.astype(BF)
        inputs = grid[r]
        pre = contract(inputs, embed_w[...], 1, 0)
        hidden, hidden_slope = silu_pair(pre)
        slope[r * cols : (r + 1) * cols, :] = hidden_slope.astype(BF)
        total += contract(part.astype(BF), hidden.astype(BF), 1, 0)
        x_t[:, r * cols : (r + 1) * cols] = inputs.T
    h_own[...] = total
    base = rows * own_blocks
    for r in range(rows):
        part = acc[base + r]
        a_halo[:, r * block : (r + 1) * block] = part.astype(BF)
        a_t[(base + r) * block : (base + r + 1) * block, :] = part.T.astype(BF)
    grad_update[...] = contract(cot[...], out_w[...], 1, 1)


def mesh_kernel(
    me, east, west, a_halo, h_own, embed_w, message_w, up_w, out_w, gain, mesh_lat, cot, grad_update,
    mesh_new, mesh_grad, grads, grad_gain, back, slope, x_t, stack,
):
    rows, half, features = east.shape
    latent = message_w.shape[0]
    total = h_own[...]
    for r in range(rows):
        at = slice(r * 2 * half, (r + 1) * 2 * half)
        inputs = jnp.concatenate([east[r], west[r]], axis=0)
        x_t[:, at] = inputs.T
        hidden, hidden_slope = silu_pair(contract(inputs, embed_w[...], 1, 0))
        slope[at, :] = hidden_slope.astype(BF)
        total += contract(a_halo[:, at], hidden.astype(BF), 1, 0)
    gathered = total.astype(BF)
    mesh_rows = mesh_lat[...].astype(F32)
    summed = mesh_rows + contract(gathered, message_w[...], 1, 0)
    rinv = lax.rsqrt(jnp.mean(summed * summed, axis=1, keepdims=True) + epsilon)
    qhat = summed * rinv
    gains = gain[...]
    normed = (qhat * gains).astype(BF)
    pre_up = contract(normed, up_w[...], 1, 0)
    silu_up, up_slope = silu_pair(pre_up)
    update = silu_up.astype(BF)
    grad_pre_up = (grad_update[...] * up_slope).astype(BF)
    grad_normed = contract(grad_pre_up, up_w[...], 1, 1)
    grad_gain[...] = jnp.sum(grad_normed * qhat, axis=0, keepdims=True)
    grad_qhat = grad_normed * gains
    grad_q = rinv * (grad_qhat - qhat * jnp.mean(grad_qhat * qhat, axis=1, keepdims=True))
    grad_aggregate = grad_q.astype(BF)
    back[...] = contract(grad_aggregate, message_w[...], 1, 1).astype(BF)
    mesh_grad[...] = cot[...].astype(F32) + grad_q
    mesh_new[...] = (mesh_rows + contract(update, out_w[...], 1, 0)).astype(BF)
    stack[:latent, :] = contract(gathered, grad_aggregate, 0, 0).astype(BF)
    stack[latent : 2 * latent, :] = contract(normed, grad_pre_up, 0, 0).astype(BF)
    stack[2 * latent :, :] = contract(update, cot[...], 0, 0).astype(BF)
    parts, count, size, _ = grads.shape
    for p in range(parts):
        for j in range(count):
            at = pl.multiple_of((p * count + (me[p] ^ j)) * size, 16)
            grads[p, j] = stack[pl.ds(at, size), :]


def grid_kernel(me, back, a_t, slope_own, slope_halo, x_t_own, x_t_halo, grad_gain, grads, total):
    step = pl.program_id(0)
    steps = pl.num_programs(0)
    features = x_t_own.shape[0]

    def term(slope, x_t):
        hidden = contract(a_t[...], back[...], 1, 0)
        grad_pre = (hidden * slope[...].astype(F32)).astype(BF)
        return contract(x_t[...], grad_pre, 1, 0)

    @pl.when(step == 0)
    def _():
        total[...] = jnp.zeros(total.shape, F32)
        total[features : features + 1, :] = grad_gain[...]

    @pl.when(step < steps - 2)
    def _():
        total[:features, :] += term(slope_own, x_t_own)

    @pl.when(step >= steps - 2)
    def _():
        total[:features, :] += term(slope_halo, x_t_halo)

    @pl.when(step == steps - 1)
    def _():
        parts, count, size, _ = grads.shape
        for p in range(parts):
            for j in range(count):
                at = pl.multiple_of((p * count + (me[p] ^ j)) * size, 8)
                grads[p, j] = total[pl.ds(at, size), :].astype(BF)


def order_kernel(me, kept, got, *outs):
    parts, half, size, latent = kept.shape
    count = 2 * half
    rows = outs[0].shape[0]
    pieces = []
    for p in range(parts):
        top = (me[p] >= half).astype(jnp.int32)
        low = me[p] & (half - 1)
        for a in range(count):
            mine = kept[p, (a & (half - 1)) ^ low]
            theirs = got[p, (a & (half - 1)) ^ low]
            chunk = jnp.where(top == a // half, mine, theirs).astype(F32)
            first = (p * count + a) * size
            pieces.append((first, chunk))
    for first, chunk in pieces:
        start = 0
        for out in outs:
            low = max(first, start)
            high = min(first + size, start + out.shape[0])
            if low < high:
                out[low - start : high - start, :] = chunk[low - first : high - first]
            start += out.shape[0]


SMEM = pl.BlockSpec(memory_space=pltpu.SMEM)
VMEM = pl.BlockSpec(memory_space=pltpu.VMEM)


def bits(axis):
    return [(axis, 1 << k) for k in range(lax.axis_size(axis).bit_length() - 1)]


def swapped(value, axis, bit):
    return lax.ppermute(value, axis, [(i, i ^ bit) for i in range(lax.axis_size(axis))])


def chunk_count(steps, rows):
    count = 1
    while count < 2 ** len(steps) and rows % (32 * count) == 0:
        count *= 2
    return count


def place(steps, count):
    used = steps[: count.bit_length() - 1]
    me = jnp.int32(0)
    for axis, bit in used:
        me = 2 * me + ((lax.axis_index(axis) & bit) != 0).astype(jnp.int32)
    return me


def summed_over(chunks, steps):
    acc = chunks
    halved = []
    for axis, bit in steps:
        if acc.shape[0] > 1:
            half = acc.shape[0] // 2
            got = swapped(acc[half:], axis, bit)
            acc = (acc[:half].astype(F32) + got.astype(F32)).astype(BF)
            halved.append((axis, bit))
        else:
            acc = (acc.astype(F32) + swapped(acc, axis, bit).astype(F32)).astype(BF)
    for axis, bit in halved[:0:-1]:
        acc = jnp.concatenate([acc, swapped(acc, axis, bit)], axis=0)
    return acc, swapped(acc, *halved[0])


def on_device(grid_in, mesh_lat, edge_w, edge_src, edge_dst, block_count, embed_w, message_w, up_w, out_w, gain, cot):
    rows, cols, features = grid_in.shape
    latent = message_w.shape[0]
    slots, block, _ = edge_w.shape
    half = block // 2
    nodes = mesh_lat.shape[0]
    own = rows * cols
    halo = rows * block
    blocks = (own + halo) // block
    params = pltpu.CompilerParams(vmem_limit_bytes=VMEM_BYTES)

    count = lax.axis_size("lon")
    east = lax.ppermute(grid_in[:, :half], "lon", [((i + 1) % count, i) for i in range(count)])
    west = lax.ppermute(grid_in[:, cols - half :], "lon", [(i, (i + 1) % count) for i in range(count)])

    shape = jax.ShapeDtypeStruct
    a_halo, a_t, h_own, slope_own, x_t_own, grad_update = pl.pallas_call(
        own_kernel,
        name="own_points",
        in_specs=[SMEM] * 3 + [VMEM] * 5,
        out_specs=[VMEM] * 6,
        out_shape=[
            shape((nodes, halo), BF),
            shape((own + halo, nodes), BF),
            shape((nodes, latent), F32),
            shape((own, latent), BF),
            shape((features, own), BF),
            shape((nodes, latent), F32),
        ],
        scratch_shapes=[pltpu.VMEM((blocks, nodes, block), F32)],
        compiler_params=params,
        cost_estimate=pl.CostEstimate(flops=4_000_000_000, bytes_accessed=14_000_000, transcendentals=2_000_000),
    )(edge_src, edge_dst, block_count, grid_in, embed_w, edge_w, cot, out_w)

    lat_bits, lon_bits = bits("lat"), bits("lon")
    x_first = lat_bits + lon_bits
    z_first = lat_bits[:1] + lon_bits + lat_bits[1:]
    orders = (x_first, z_first)
    mesh_count = chunk_count(x_first, 3 * latent // 2)
    mesh_me = jnp.stack([place(order, mesh_count) for order in orders])
    mesh_new, mesh_grad, mesh_terms, gain_term, back, slope_halo, x_t_halo = pl.pallas_call(
        mesh_kernel,
        name="mesh_nodes",
        in_specs=[SMEM] + [VMEM] * 12,
        out_specs=[VMEM] * 7,
        out_shape=[
            shape((nodes, latent), BF),
            shape((nodes, latent), F32),
            shape((2, mesh_count, 3 * latent // 2 // mesh_count, latent), BF),
            shape((1, latent), F32),
            shape((nodes, latent), BF),
            shape((halo, latent), BF),
            shape((features, halo), BF),
        ],
        scratch_shapes=[pltpu.VMEM((3 * latent, latent), BF)],
        compiler_params=params,
        cost_estimate=pl.CostEstimate(flops=2_500_000_000, bytes_accessed=10_000_000, transcendentals=1_000_000),
    )(
        mesh_me, east, west, a_halo, h_own, embed_w, message_w, up_w, out_w, gain.reshape(1, latent),
        mesh_lat, cot, grad_update,
    )

    padded = -(-(features + 1) // 128) * 128
    embed_count = chunk_count(x_first, padded)
    embed_me = jnp.stack([place(x_first, embed_count)])
    tile = halo // 2
    own_steps = own // tile
    steps = own_steps + 2
    embed_terms = pl.pallas_call(
        grid_kernel,
        name="grid_points",
        grid_spec=pltpu.PrefetchScalarGridSpec(
            num_scalar_prefetch=1,
            grid=(steps,),
            in_specs=[
                pl.BlockSpec((nodes, latent), lambda i, me: (0, 0)),
                pl.BlockSpec((tile, nodes), lambda i, me: (i, 0)),
                pl.BlockSpec((tile, latent), lambda i, me: (jnp.minimum(i, own_steps - 1), 0)),
                pl.BlockSpec((tile, latent), lambda i, me: (jnp.maximum(i - own_steps, 0), 0)),
                pl.BlockSpec((features, tile), lambda i, me: (0, jnp.minimum(i, own_steps - 1))),
                pl.BlockSpec((features, tile), lambda i, me: (0, jnp.maximum(i - own_steps, 0))),
                pl.BlockSpec((1, latent), lambda i, me: (0, 0)),
            ],
            out_specs=pl.BlockSpec((1, embed_count, padded // embed_count, latent), lambda i, me: (0, 0, 0, 0)),
            scratch_shapes=[pltpu.VMEM((padded, latent), F32)],
        ),
        out_shape=shape((1, embed_count, padded // embed_count, latent), BF),
        compiler_params=params,
        cost_estimate=pl.CostEstimate(flops=2_400_000_000, bytes_accessed=9_000_000, transcendentals=0),
    )(embed_me, back, a_t, slope_own, slope_halo, x_t_own, x_t_halo, gain_term)

    pairs = [summed_over(mesh_terms[k], order) for k, order in enumerate(orders)]
    embed_pair = summed_over(embed_terms[0], x_first)

    def ordered(me, pairs, row_counts):
        kept = jnp.stack([pair[0] for pair in pairs])
        got = jnp.stack([pair[1] for pair in pairs])
        return pl.pallas_call(
            order_kernel,
            name="ordered",
            in_specs=[SMEM, VMEM, VMEM],
            out_specs=[VMEM] * len(row_counts),
            out_shape=[shape((n, latent), F32) for n in row_counts],
            compiler_params=params,
            cost_estimate=pl.CostEstimate(flops=0, bytes_accessed=4_000_000, transcendentals=0),
        )(me, kept, got)

    grad_message, grad_up, grad_out = ordered(mesh_me, pairs, [latent] * 3)
    grad_embed, rest = ordered(embed_me, [embed_pair], [features, padded - features])
    return (mesh_new, mesh_grad, grad_embed, grad_message, grad_up, grad_out, rest[0])


def solution(mesh):
    tiles = ("grp", "lon", "lat")
    return jax.shard_map(
        on_device,
        mesh=mesh,
        in_specs=(
            P(("grp", "lat"), "lon", None),
            P(tiles, None),
            P(tiles, None, None),
            P(tiles),
            P(tiles),
            P(tiles),
            P(),
            P(),
            P(),
            P(),
            P(),
            P(tiles, None),
        ),
        out_specs=(
            P(tiles, None),
            P(tiles, None),
            P("grp", None),
            P("grp", None),
            P("grp", None),
            P("grp", None),
            P("grp"),
        ),
        check_vma=False,
    )
```

```python
import jax
import jax.numpy as jnp
from jax import lax
from jax.experimental import pallas as pl
from jax.experimental.pallas import tpu as pltpu
from jax.sharding import PartitionSpec as P

epsilon = 1e-05
BF = jnp.bfloat16
F32 = jnp.float32
MIB = 1024 * 1024
SMEM = pl.BlockSpec(memory_space=pltpu.SMEM)
VMEM = pl.BlockSpec(memory_space=pltpu.VMEM)
shape = jax.ShapeDtypeStruct


def contract(a, b, dim_a, dim_b):
    return lax.dot_general(a, b, (((dim_a,), (dim_b,)), ((), ())), preferred_element_type=F32)


def silu_pair(pre):
    sigma = jax.nn.sigmoid(pre)
    return pre * sigma, sigma * (1.0 + pre * (1.0 - sigma))


def pack_kernel(grid, to_west, to_east, wide):
    features, rows, cols = grid.shape
    half = to_west.shape[1] // rows
    block = 2 * half
    last = cols // block - 1
    for k in (0, last):
        wide[k] = grid[:, :, k * block : (k + 1) * block].astype(F32).reshape(features * rows, block)
    lane = lax.broadcasted_iota(jnp.int32, (features, block), 1)
    for pair in range(rows // 2):
        even = pl.ds(2 * pair, features, stride=rows)
        odd = pl.ds(2 * pair + 1, features, stride=rows)
        at = slice(pair * block, (pair + 1) * block)
        head = jnp.where(lane < half, wide[0, even, :], pltpu.roll(wide[0, odd, :], half, 1))
        tail = jnp.where(lane < half, pltpu.roll(wide[last, even, :], half, 1), wide[last, odd, :])
        to_west[:, at] = head.astype(BF)
        to_east[:, at] = tail.astype(BF)


def own_kernel(
    src, dst, count, grid, embed_w, edge_w, cot, out_w,
    weights_all, x_t, embed_t, h_own, slope, grad_update, acc, wide,
):
    features, rows, cols = grid.shape
    block = edge_w.shape[1]
    half = block // 2
    own_blocks = cols // block
    windows = 2 * own_blocks + 1
    west_base = rows * own_blocks
    east_base = west_base + rows // 2
    acc[...] = jnp.zeros(acc.shape, F32)
    lane = lax.broadcasted_iota(jnp.int32, (block, block), 1)

    def slot(b, carry):
        source = src[b]
        row = source // windows
        window = source - row * windows
        at = window // 2
        target = pl.ds(pl.multiple_of(dst[b] * block, block), block)
        weights = edge_w[b].astype(F32)

        @pl.when(window % 2 == 1)
        def _():
            acc[row * own_blocks + at, target, :] += weights

        @pl.when(window % 2 == 0)
        def _():
            turned = pltpu.roll(weights, half, 1)
            odd_row = row % 2 == 1
            first = jnp.where(at == 0, west_base + row // 2, row * own_blocks + at - 1)
            first_high = (at > 0) | odd_row
            second = jnp.where(at == own_blocks, east_base + row // 2, row * own_blocks + at)
            second_high = (at == own_blocks) & odd_row
            acc[first, target, :] += jnp.where(
                first_high, jnp.where(lane >= half, turned, 0.0), jnp.where(lane < half, weights, 0.0)
            )
            acc[second, target, :] += jnp.where(
                second_high, jnp.where(lane >= half, weights, 0.0), jnp.where(lane < half, turned, 0.0)
            )

        return carry

    lax.fori_loop(0, count[0], slot, 0)
    for k in range(acc.shape[0]):
        weights_all[:, k * block : (k + 1) * block] = acc[k].astype(BF)
    for k in range(own_blocks):
        wide[k] = grid[:, :, k * block : (k + 1) * block].astype(F32).reshape(features * rows, block)
    embed_t[...] = embed_w[...].T
    total = jnp.zeros(h_own.shape, F32)
    for r in range(rows):
        at = slice(r * cols, (r + 1) * cols)
        for k in range(own_blocks):
            x_t[:, r * cols + k * block : r * cols + (k + 1) * block] = wide[
                k, pl.ds(r, features, stride=rows), :
            ].astype(BF)
        hidden, hidden_slope = silu_pair(contract(embed_t[...], x_t[:, at], 1, 0))
        slope[:, at] = hidden_slope.astype(BF)
        total += contract(weights_all[:, at], hidden.astype(BF), 1, 1)
    h_own[...] = total
    grad_update[...] = contract(cot[...], out_w[...], 1, 1)


def halo_part(x, embed_t, weights, slope):
    hidden, hidden_slope = silu_pair(contract(embed_t[...], x[...], 1, 0))
    slope[...] = hidden_slope.astype(BF)
    return contract(weights, hidden.astype(BF), 1, 1)


def west_kernel(first, x, embed_t, weights_all, h_own, h_sum, slope):
    points = x.shape[1]
    h_sum[...] = h_own[...] + halo_part(x, embed_t, weights_all[:, first : first + points], slope)


def mesh_kernel(
    perm, x, embed_t, weights_all, h_sum, message_w, up_w, out_w, gain, mesh_lat, cot, grad_update,
    mesh_new, mesh_grad, grads_0, grads_1, grad_gain, back, slope, stack,
):
    points = x.shape[1]
    first = weights_all.shape[1] - points
    total = h_sum[...] + halo_part(x, embed_t, weights_all[:, first:], slope)
    gathered = total.astype(BF)
    mesh_rows = mesh_lat[...].astype(F32)
    summed = mesh_rows + contract(gathered, message_w[...], 1, 0)
    rinv = lax.rsqrt(jnp.mean(summed * summed, axis=1, keepdims=True) + epsilon)
    qhat = summed * rinv
    gains = gain[...]
    normed = (qhat * gains).astype(BF)
    pre_up = contract(normed, up_w[...], 1, 0)
    silu_up, up_slope = silu_pair(pre_up)
    update = silu_up.astype(BF)
    grad_pre_up = (grad_update[...] * up_slope).astype(BF)
    grad_normed = contract(grad_pre_up, up_w[...], 1, 1)
    grad_gain[...] = jnp.sum(grad_normed * qhat, axis=0, keepdims=True)
    grad_qhat = grad_normed * gains
    grad_q = rinv * (grad_qhat - qhat * jnp.mean(grad_qhat * qhat, axis=1, keepdims=True))
    grad_aggregate = grad_q.astype(BF)
    back[...] = contract(message_w[...], grad_aggregate, 1, 1).astype(BF)
    mesh_grad[...] = cot[...].astype(F32) + grad_q
    mesh_new[...] = (mesh_rows + contract(update, out_w[...], 1, 0)).astype(BF)
    stack[0] = contract(gathered, grad_aggregate, 0, 0).astype(BF)
    stack[1] = contract(normed, grad_pre_up, 0, 0).astype(BF)
    stack[2] = contract(update, cot[...], 0, 0).astype(BF)
    _, matrices, size, _ = grads_0.shape
    for j in range(4):
        at = pl.multiple_of(perm[j] * (2 * size), 2 * size)
        for k in range(matrices):
            grads_0[j, k] = stack[k, pl.ds(at, size), :]
            grads_1[j, k] = stack[k, pl.ds(at + size, size), :]


def grid_kernel(perm, back, weights_all, slope_own, slope_west, slope_east, x_own, x_west, x_east, grad_gain, grads, total):
    features = x_own.shape[0]
    tile = x_west.shape[1]
    pieces = []
    for x, slope in ((x_own, slope_own), (x_west, slope_west), (x_east, slope_east)):
        pieces += [(x, slope, k) for k in range(x.shape[1] // tile)]
    sums = jnp.zeros((features, total.shape[1]), F32)
    for n, (x, slope, k) in enumerate(pieces):
        at = slice(k * tile, (k + 1) * tile)
        hidden = contract(back[...], weights_all[:, n * tile : (n + 1) * tile], 1, 0)
        grad_pre = (hidden * slope[:, at].astype(F32)).astype(BF)
        sums += contract(x[:, at], grad_pre, 1, 1)
    total[...] = jnp.zeros(total.shape, F32)
    total[:features, :] = sums
    total[features : features + 1, :] = grad_gain[...]
    size = grads.shape[2]
    for j in range(4):
        grads[j, 0] = total[pl.ds(pl.multiple_of(perm[j] * size, size), size), :].astype(BF)


def order_mesh_kernel(perm, *refs):
    chunks, outs = refs[:-3], refs[-3:]
    for part in range(2):
        for j, chunk in enumerate(chunks[4 * part : 4 * part + 4]):
            size = chunk.shape[1]
            at = pl.multiple_of(perm[j] * (2 * size), 2 * size) + part * size
            for k, out in enumerate(outs):
                out[pl.ds(at, size), :] = chunk[k].astype(F32)


def order_grid_kernel(perm, *refs):
    chunks, (grad_embed, grad_gain, total) = refs[:4], refs[4:]
    for j, chunk in enumerate(chunks):
        size = chunk.shape[1]
        total[pl.ds(pl.multiple_of(perm[j] * size, size), size), :] = chunk[0].astype(F32)
    features = grad_embed.shape[0]
    grad_embed[...] = total[:features, :]
    grad_gain[...] = total[features : features + 1, :]


def role_steps():
    lat = [("lat", 2 << k) for k in range(lax.axis_size("lat").bit_length() - 2)]
    lon = [("lon", 1 << k) for k in range(lax.axis_size("lon").bit_length() - 1)]
    return (lat + lon, lon + lat)


def core_swapped(value):
    return lax.ppermute(value, "lat", [(i, i ^ 1) for i in range(lax.axis_size("lat"))])


def swapped(value, step):
    lats = lax.axis_size("lat")
    pairs = []
    for lon in range(lax.axis_size("lon")):
        for lat in range(lats):
            axis, bit = role_steps()[lat & 1][step]
            other = (lon ^ bit) * lats + lat if axis == "lon" else lon * lats + (lat ^ bit)
            pairs.append((lon * lats + lat, other))
    return lax.ppermute(value, ("lon", "lat"), pairs)


def chunk_order():
    core = lax.axis_index("lat") & 1
    side = [((lax.axis_index(axis) & bit) != 0).astype(jnp.int32) for axis, bit in (s[0] for s in role_steps())]
    mine = jnp.where(core == 0, side[0], side[1])
    theirs = jnp.where(core == 0, side[1], side[0])
    return jnp.stack([2 * core + mine, 2 * core + 1 - mine, 2 - 2 * core + theirs, 3 - 2 * core - theirs])


def added(a, b):
    return (a.astype(F32) + b.astype(F32)).astype(BF)


def all_summed(grads):
    kept = added(grads[:2], core_swapped(grads[2:]))
    mine = added(kept[0], swapped(kept[1], 0))
    for step in range(1, len(role_steps()[0])):
        mine = added(mine, swapped(mine, step))
    partners = swapped(mine, 0)
    return mine, partners, core_swapped(mine), core_swapped(partners)


def on_device(grid_in, mesh_lat, edge_w, edge_src, edge_dst, block_count, embed_w, message_w, up_w, out_w, gain, cot):
    rows, cols, features = grid_in.shape
    latent = message_w.shape[0]
    block = edge_w.shape[1]
    half = block // 2
    nodes = mesh_lat.shape[0]
    own = rows * cols
    side = rows * half
    points = own + 2 * side
    grid = jnp.transpose(grid_in, (2, 0, 1))

    def call(kernel, name, in_specs, out_shape, flops, bytes_accessed, limit, scratch_shapes=()):
        return pl.pallas_call(
            kernel,
            name=name,
            in_specs=in_specs,
            out_specs=[VMEM] * len(out_shape),
            out_shape=out_shape,
            scratch_shapes=list(scratch_shapes),
            compiler_params=pltpu.CompilerParams(vmem_limit_bytes=limit * MIB),
            cost_estimate=pl.CostEstimate(flops=flops, bytes_accessed=bytes_accessed, transcendentals=0),
        )

    to_west, to_east = call(
        pack_kernel, "pack", [VMEM], [shape((features, side), BF)] * 2, 0, 3 * MIB, 20,
        [pltpu.VMEM((cols // block, features * rows, block), F32)],
    )(grid)
    count = lax.axis_size("lon")
    x_west = lax.ppermute(to_east, "lon", [(i, (i + 1) % count) for i in range(count)])
    x_east = lax.ppermute(to_west, "lon", [((i + 1) % count, i) for i in range(count)])

    weights_all, x_own, embed_t, h_own, slope_own, grad_update = call(
        own_kernel, "own_points", [SMEM] * 3 + [VMEM] * 5,
        [
            shape((nodes, points), BF),
            shape((features, own), BF),
            shape((latent, features), BF),
            shape((nodes, latent), F32),
            shape((latent, own), BF),
            shape((nodes, latent), F32),
        ],
        4_000_000_000, 12 * MIB, 32,
        [pltpu.VMEM((points // block, nodes, block), F32), pltpu.VMEM((cols // block, features * rows, block), F32)],
    )(edge_src, edge_dst, block_count, grid, embed_w, edge_w, cot, out_w)

    h_sum, slope_west = call(
        lambda *refs: west_kernel(own, *refs), "west_points", [VMEM] * 4,
        [shape((nodes, latent), F32), shape((latent, side), BF)],
        600_000_000, 3 * MIB, 16,
    )(x_west, embed_t, weights_all, h_own)

    perm = chunk_order()
    mesh_new, mesh_grad, grads_0, grads_1, gain_term, back, slope_east = call(
        mesh_kernel, "mesh_nodes", [SMEM] + [VMEM] * 11,
        [
            shape((nodes, latent), BF),
            shape((nodes, latent), F32),
            shape((4, 3, latent // 8, latent), BF),
            shape((4, 3, latent // 8, latent), BF),
            shape((1, latent), F32),
            shape((latent, nodes), BF),
            shape((latent, side), BF),
        ],
        2_000_000_000, 8 * MIB, 16, [pltpu.VMEM((3, latent, latent), BF)],
    )(
        perm, x_east, embed_t, weights_all, h_sum, message_w, up_w, out_w, gain.reshape(1, latent),
        mesh_lat, cot, grad_update,
    )

    padded = -(-(features + 1) // 128) * 128
    (grads_2,) = call(
        grid_kernel, "grid_points", [SMEM] + [VMEM] * 9, [shape((4, 1, padded // 4, latent), BF)],
        2_400_000_000, 9 * MIB, 16, [pltpu.VMEM((padded, latent), F32)],
    )(perm, back, weights_all, slope_own, slope_west, slope_east, x_own, x_west, x_east, gain_term)

    summed = [all_summed(grads) for grads in (grads_0, grads_1, grads_2)]
    grad_message, grad_up, grad_out = call(
        order_mesh_kernel, "order_mesh", [SMEM] + [VMEM] * 8, [shape((latent, latent), F32)] * 3, 0, 5 * MIB, 16
    )(perm, *summed[0], *summed[1])
    grad_embed, grad_gain = call(
        order_grid_kernel, "order_grid", [SMEM] + [VMEM] * 4,
        [shape((features, latent), F32), shape((1, latent), F32)], 0, 2 * MIB, 16,
        [pltpu.VMEM((padded, latent), F32)],
    )(perm, *summed[2])
    return (mesh_new, mesh_grad, grad_embed, grad_message, grad_up, grad_out, grad_gain[0])


def solution(mesh):
    tiles = ("grp", "lon", "lat")
    return jax.shard_map(
        on_device,
        mesh=mesh,
        in_specs=(
            P(("grp", "lat"), "lon", None),
            P(tiles, None),
            P(tiles, None, None),
            P(tiles),
            P(tiles),
            P(tiles),
            P(),
            P(),
            P(),
            P(),
            P(),
            P(tiles, None),
        ),
        out_specs=(
            P(tiles, None),
            P(tiles, None),
            P("grp", None),
            P("grp", None),
            P("grp", None),
            P("grp", None),
            P("grp"),
        ),
        check_vma=False,
    )
```

```python
import jax
import jax.numpy as jnp
from jax import lax
from jax.experimental import pallas as pl
from jax.experimental.pallas import tpu as pltpu
from jax.sharding import PartitionSpec as P

epsilon = 1e-05
BF = jnp.bfloat16
F32 = jnp.float32
MIB = 1024 * 1024
PIECE = 128
SMEM = pl.BlockSpec(memory_space=pltpu.SMEM)
VMEM = pl.BlockSpec(memory_space=pltpu.VMEM)
HBM = pl.BlockSpec(memory_space=pltpu.HBM)
shape = jax.ShapeDtypeStruct


def contract(a, b, dim_a, dim_b):
    return lax.dot_general(a, b, (((dim_a,), (dim_b,)), ((), ())), preferred_element_type=F32)


def silu_pair(pre):
    sigma = jax.nn.sigmoid(pre)
    return pre * sigma, sigma * (1.0 + pre * (1.0 - sigma))


def pack_kernel(grid, to_west, to_east, held, wide, sems):
    features, rows, cols = grid.shape
    half = to_west.shape[1] // rows
    block = 2 * half
    last = cols // block - 1
    pieces = []
    for n, first in enumerate(range(0, features, PIECE)):
        at = pl.ds(first, min(PIECE, features - first))
        pieces.append((at, pltpu.make_async_copy(grid.at[at], held.at[at], sems.at[n])))
    for _, copy in pieces:
        copy.start()
    for at, copy in pieces:
        copy.wait()
        size = at.size
        for k in (0, last):
            wide[k, pl.ds(at.start * rows, size * rows), :] = (
                held[at, :, k * block : (k + 1) * block].astype(F32).reshape(size * rows, block)
            )
        lane = lax.broadcasted_iota(jnp.int32, (size, block), 1)
        for pair in range(rows // 2):
            even = pl.ds(at.start * rows + 2 * pair, size, stride=rows)
            odd = pl.ds(at.start * rows + 2 * pair + 1, size, stride=rows)
            to = slice(pair * block, (pair + 1) * block)
            head = jnp.where(lane < half, wide[0, even, :], pltpu.roll(wide[0, odd, :], half, 1))
            tail = jnp.where(lane < half, pltpu.roll(wide[last, even, :], half, 1), wide[last, odd, :])
            to_west[at, to] = head.astype(BF)
            to_east[at, to] = tail.astype(BF)


def own_kernel(
    src, dst, count, grid, embed_w, edge_w, cot, out_w,
    weights_all, x_t, embed_t, h_own, slope, grad_update, acc, wide,
):
    features, rows, cols = grid.shape
    block = edge_w.shape[1]
    half = block // 2
    own_blocks = cols // block
    windows = 2 * own_blocks + 1
    west_base = rows * own_blocks
    east_base = west_base + rows // 2
    acc[...] = jnp.zeros(acc.shape, F32)
    lane = lax.broadcasted_iota(jnp.int32, (block, block), 1)

    def slot(b, carry):
        source = src[b]
        row = source // windows
        window = source - row * windows
        at = window // 2
        target = pl.ds(pl.multiple_of(dst[b] * block, block), block)
        weights = edge_w[b].astype(F32)

        @pl.when(window % 2 == 1)
        def _():
            acc[row * own_blocks + at, target, :] += weights

        @pl.when(window % 2 == 0)
        def _():
            turned = pltpu.roll(weights, half, 1)
            odd_row = row % 2 == 1
            first = jnp.where(at == 0, west_base + row // 2, row * own_blocks + at - 1)
            first_high = (at > 0) | odd_row
            second = jnp.where(at == own_blocks, east_base + row // 2, row * own_blocks + at)
            second_high = (at == own_blocks) & odd_row
            acc[first, target, :] += jnp.where(
                first_high, jnp.where(lane >= half, turned, 0.0), jnp.where(lane < half, weights, 0.0)
            )
            acc[second, target, :] += jnp.where(
                second_high, jnp.where(lane >= half, weights, 0.0), jnp.where(lane < half, turned, 0.0)
            )

        return carry

    lax.fori_loop(0, count[0], slot, 0)
    for k in range(acc.shape[0]):
        weights_all[:, k * block : (k + 1) * block] = acc[k].astype(BF)
    for k in range(own_blocks):
        wide[k] = grid[:, :, k * block : (k + 1) * block].astype(F32).reshape(features * rows, block)
    embed_t[...] = embed_w[...].T
    total = jnp.zeros(h_own.shape, F32)
    for r in range(rows):
        at = slice(r * cols, (r + 1) * cols)
        for k in range(own_blocks):
            x_t[:, r * cols + k * block : r * cols + (k + 1) * block] = wide[
                k, pl.ds(r, features, stride=rows), :
            ].astype(BF)
        hidden, hidden_slope = silu_pair(contract(embed_t[...], x_t[:, at], 1, 0))
        slope[:, at] = hidden_slope.astype(BF)
        total += contract(weights_all[:, at], hidden.astype(BF), 1, 1)
    h_own[...] = total
    grad_update[...] = contract(cot[...], out_w[...], 1, 1)


def halo_part(x, embed_t, weights, slope):
    hidden, hidden_slope = silu_pair(contract(embed_t[...], x[...], 1, 0))
    slope[...] = hidden_slope.astype(BF)
    return contract(weights, hidden.astype(BF), 1, 1)


def west_kernel(first, x, embed_t, weights_all, h_own, h_sum, slope):
    points = x.shape[1]
    h_sum[...] = h_own[...] + halo_part(x, embed_t, weights_all[:, first : first + points], slope)


def to_chunks(grads, stack, perm):
    count, matrices, size, _ = grads.shape
    for j in range(count):
        at = pl.ds(pl.multiple_of(perm[j] * size, size), size)
        for k in range(matrices):
            grads[j, k] = stack[k, at, :]


def from_chunks(outs, chunks, perm):
    j = 0
    for chunk in chunks:
        for n in range(chunk.shape[0]):
            size = chunk.shape[2]
            at = pl.ds(pl.multiple_of(perm[j] * size, size), size)
            for k, out in enumerate(outs):
                out[at, :] = chunk[n, k].astype(F32)
            j += 1


def mesh_kernel(
    perm, x, embed_t, weights_all, h_sum, message_w, up_w, gain, mesh_lat, cot, grad_update,
    grads, mesh_grad, grad_gain, grad_aggregate, update, slope, stack,
):
    points = x.shape[1]
    first = weights_all.shape[1] - points
    total = h_sum[...] + halo_part(x, embed_t, weights_all[:, first:], slope)
    gathered = total.astype(BF)
    summed = mesh_lat[...].astype(F32) + contract(gathered, message_w[...], 1, 0)
    rinv = lax.rsqrt(jnp.mean(summed * summed, axis=1, keepdims=True) + epsilon)
    qhat = summed * rinv
    gains = gain[...]
    normed = (qhat * gains).astype(BF)
    pre_up = contract(normed, up_w[...], 1, 0)
    silu_up, up_slope = silu_pair(pre_up)
    update[...] = silu_up.astype(BF)
    grad_pre_up = (grad_update[...] * up_slope).astype(BF)
    grad_normed = contract(grad_pre_up, up_w[...], 1, 1)
    grad_gain[...] = jnp.sum(grad_normed * qhat, axis=0, keepdims=True)
    grad_qhat = grad_normed * gains
    grad_q = rinv * (grad_qhat - qhat * jnp.mean(grad_qhat * qhat, axis=1, keepdims=True))
    grad_aggregate[...] = grad_q.astype(BF)
    mesh_grad[...] = cot[...].astype(F32) + grad_q
    stack[0] = contract(gathered, grad_q.astype(BF), 0, 0).astype(BF)
    stack[1] = contract(normed, grad_pre_up, 0, 0).astype(BF)
    to_chunks(grads, stack, perm)


def tail_kernel(grad_aggregate, update, message_w, out_w, mesh_lat, cot, back, mesh_new, grad_out):
    back[...] = contract(message_w[...], grad_aggregate[...], 1, 1).astype(BF)
    mesh_new[...] = (mesh_lat[...].astype(F32) + contract(update[...], out_w[...], 1, 0)).astype(BF)
    grad_out[...] = contract(update[...], cot[...], 0, 0).astype(BF)


def grid_kernel(
    perm, back, weights_all, slope_own, slope_west, slope_east, x_own, x_west, x_east, grad_gain, grad_out, grads, stack
):
    features = x_own.shape[0]
    tile = x_west.shape[1]
    pieces = []
    for x, slope in ((x_own, slope_own), (x_west, slope_west), (x_east, slope_east)):
        pieces += [(x, slope, k) for k in range(x.shape[1] // tile)]
    sums = jnp.zeros((features, stack.shape[2]), F32)
    for n, (x, slope, k) in enumerate(pieces):
        at = slice(k * tile, (k + 1) * tile)
        hidden = contract(back[...], weights_all[:, n * tile : (n + 1) * tile], 1, 0)
        grad_pre = (hidden * slope[:, at].astype(F32)).astype(BF)
        sums += contract(x[:, at], grad_pre, 1, 1)
    stack[0] = grad_out[...].astype(F32)
    stack[1] = jnp.zeros(stack.shape[1:], F32)
    stack[1, :features, :] = sums
    stack[1, features : features + 1, :] = grad_gain[...]
    count, matrices, size, _ = grads.shape
    for j in range(count):
        at = pl.ds(pl.multiple_of(perm[j] * size, size), size)
        for k in range(matrices):
            grads[j, k] = stack[k, at, :].astype(BF)


def order_mesh_kernel(perm, *refs):
    from_chunks(refs[-2:], refs[:-2], perm)


def order_grid_kernel(perm, *refs):
    grad_out, grad_embed, grad_gain, total = refs[-4:]
    from_chunks((grad_out, total), refs[:-4], perm)
    features = grad_embed.shape[0]
    grad_embed[...] = total[:features, :]
    grad_gain[...] = total[features : features + 1, :]


def role_steps():
    lat = [("lat", 2 << k) for k in range(lax.axis_size("lat").bit_length() - 2)]
    lon = [("lon", 1 << k) for k in range(lax.axis_size("lon").bit_length() - 1)]
    return (lat + lon, lon + lat)


def core_swapped(value):
    return lax.ppermute(value, "lat", [(i, i ^ 1) for i in range(lax.axis_size("lat"))])


def swapped(value, step):
    lats = lax.axis_size("lat")
    pairs = []
    for lon in range(lax.axis_size("lon")):
        for lat in range(lats):
            axis, bit = role_steps()[lat & 1][step]
            other = (lon ^ bit) * lats + lat if axis == "lon" else lon * lats + (lat ^ bit)
            pairs.append((lon * lats + lat, other))
    return lax.ppermute(value, ("lon", "lat"), pairs)


def chunk_order():
    core = lax.axis_index("lat") & 1
    sides = []
    for steps in role_steps():
        low = [((lax.axis_index(axis) & bit) != 0).astype(jnp.int32) for axis, bit in steps[:2]]
        sides.append(2 * low[0] + low[1])
    mine = jnp.where(core == 0, sides[0], sides[1])
    theirs = jnp.where(core == 0, sides[1], sides[0])
    return jnp.stack([4 * core + (mine ^ j) for j in range(4)] + [4 - 4 * core + (theirs ^ j) for j in range(4)])


def added(a, b):
    return (a.astype(F32) + b.astype(F32)).astype(BF)


def core_summed(grads):
    return added(grads[:4], core_swapped(grads[4:]))


def all_summed(kept):
    kept = added(kept[:2], swapped(kept[2:], 0))
    mine = added(kept[:1], swapped(kept[1:], 1))
    for step in range(2, len(role_steps()[0])):
        mine = added(mine, swapped(mine, step))
    second = swapped(mine, 1)
    first = swapped(jnp.concatenate([mine, second]), 0)
    return mine, second, first, core_swapped(mine), core_swapped(second), core_swapped(first)


def on_device(grid_in, mesh_lat, edge_w, edge_src, edge_dst, block_count, embed_w, message_w, up_w, out_w, gain, cot):
    rows, cols, features = grid_in.shape
    latent = message_w.shape[0]
    block = edge_w.shape[1]
    half = block // 2
    nodes = mesh_lat.shape[0]
    own = rows * cols
    side = rows * half
    points = own + 2 * side
    grid = jnp.transpose(grid_in, (2, 0, 1))

    def call(kernel, name, in_specs, out_shape, flops, bytes_accessed, limit, scratch_shapes=()):
        return pl.pallas_call(
            kernel,
            name=name,
            in_specs=in_specs,
            out_specs=[VMEM] * len(out_shape),
            out_shape=out_shape,
            scratch_shapes=list(scratch_shapes),
            compiler_params=pltpu.CompilerParams(vmem_limit_bytes=limit * MIB),
            cost_estimate=pl.CostEstimate(flops=flops, bytes_accessed=bytes_accessed, transcendentals=0),
        )

    to_west, to_east = call(
        pack_kernel, "pack", [HBM], [shape((features, side), BF)] * 2, 0, 3 * MIB, 20,
        [
            pltpu.VMEM((features, rows, cols), BF),
            pltpu.VMEM((cols // block, features * rows, block), F32),
            pltpu.SemaphoreType.DMA((-(-features // PIECE),)),
        ],
    )(grid)
    count = lax.axis_size("lon")
    x_west = lax.ppermute(to_east, "lon", [(i, (i + 1) % count) for i in range(count)])
    x_east = lax.ppermute(to_west, "lon", [((i + 1) % count, i) for i in range(count)])

    weights_all, x_own, embed_t, h_own, slope_own, grad_update = call(
        own_kernel, "own_points", [SMEM] * 3 + [VMEM] * 5,
        [
            shape((nodes, points), BF),
            shape((features, own), BF),
            shape((latent, features), BF),
            shape((nodes, latent), F32),
            shape((latent, own), BF),
            shape((nodes, latent), F32),
        ],
        4_000_000_000, 12 * MIB, 32,
        [pltpu.VMEM((points // block, nodes, block), F32), pltpu.VMEM((cols // block, features * rows, block), F32)],
    )(edge_src, edge_dst, block_count, grid, embed_w, edge_w, cot, out_w)

    h_sum, slope_west = call(
        lambda *refs: west_kernel(own, *refs), "west_points", [VMEM] * 4,
        [shape((nodes, latent), F32), shape((latent, side), BF)],
        600_000_000, 3 * MIB, 16,
    )(x_west, embed_t, weights_all, h_own)

    perm = chunk_order()
    grads_a, mesh_grad, gain_term, grad_aggregate, update, slope_east = call(
        mesh_kernel, "mesh_nodes", [SMEM] + [VMEM] * 10,
        [
            shape((8, 2, latent // 8, latent), BF),
            shape((nodes, latent), F32),
            shape((1, latent), F32),
            shape((nodes, latent), BF),
            shape((nodes, latent), BF),
            shape((latent, side), BF),
        ],
        2_000_000_000, 8 * MIB, 16, [pltpu.VMEM((2, latent, latent), BF)],
    )(perm, x_east, embed_t, weights_all, h_sum, message_w, up_w, gain.reshape(1, latent), mesh_lat, cot, grad_update)
    back, mesh_new, grad_out_term = call(
        tail_kernel, "mesh_tail", [VMEM] * 6,
        [shape((latent, nodes), BF), shape((nodes, latent), BF), shape((latent, latent), BF)],
        400_000_000, 3 * MIB, 16,
    )(grad_aggregate, update, message_w, out_w, mesh_lat, cot)

    kept_a, back = lax.optimization_barrier((core_summed(grads_a), back))
    padded = -(-(features + 1) // 128) * 128
    assert padded == latent
    (grads_b,) = call(
        grid_kernel, "grid_points", [SMEM] + [VMEM] * 10, [shape((8, 2, latent // 8, latent), BF)],
        2_400_000_000, 9 * MIB, 16, [pltpu.VMEM((2, latent, latent), F32)],
    )(perm, back, weights_all, slope_own, slope_west, slope_east, x_own, x_west, x_east, gain_term, grad_out_term)

    summed_a = all_summed(kept_a)
    summed_b = all_summed(core_summed(grads_b))
    square = shape((latent, latent), F32)
    grad_message, grad_up = call(
        order_mesh_kernel, "order_a", [SMEM] + [VMEM] * 6, [square, square], 0, 3 * MIB, 16
    )(perm, *summed_a)
    grad_out, grad_embed, grad_gain = call(
        order_grid_kernel, "order_b", [SMEM] + [VMEM] * 6,
        [square, shape((features, latent), F32), shape((1, latent), F32)], 0, 3 * MIB, 16,
        [pltpu.VMEM((latent, latent), F32)],
    )(perm, *summed_b)
    return (mesh_new, mesh_grad, grad_embed, grad_message, grad_up, grad_out, grad_gain[0])


def solution(mesh):
    tiles = ("grp", "lon", "lat")
    return jax.shard_map(
        on_device,
        mesh=mesh,
        in_specs=(
            P(("grp", "lat"), "lon", None),
            P(tiles, None),
            P(tiles, None, None),
            P(tiles),
            P(tiles),
            P(tiles),
            P(),
            P(),
            P(),
            P(),
            P(),
            P(tiles, None),
        ),
        out_specs=(
            P(tiles, None),
            P(tiles, None),
            P("grp", None),
            P("grp", None),
            P("grp", None),
            P("grp", None),
            P("grp"),
        ),
        check_vma=False,
    )
```

```python
import jax
import jax.numpy as jnp
from jax import lax
from jax.experimental import pallas as pl
from jax.experimental.pallas import tpu as pltpu
from jax.sharding import PartitionSpec as P

epsilon = 1e-05
BF = jnp.bfloat16
F32 = jnp.float32
MIB = 1024 * 1024
PIECE = 128
SMEM = pl.BlockSpec(memory_space=pltpu.SMEM)
VMEM = pl.BlockSpec(memory_space=pltpu.VMEM)
HBM = pl.BlockSpec(memory_space=pltpu.HBM)
shape = jax.ShapeDtypeStruct


def contract(a, b, dim_a, dim_b):
    return lax.dot_general(a, b, (((dim_a,), (dim_b,)), ((), ())), preferred_element_type=F32)


def silu_pair(pre):
    sigma = jax.nn.sigmoid(pre)
    return pre * sigma, sigma * (1.0 + pre * (1.0 - sigma))


def pack_kernel(grid, to_west, to_east, held, wide, sems):
    features, rows, cols = grid.shape
    half = to_west.shape[1] // rows
    block = 2 * half
    last = cols // block - 1
    pieces = []
    for n, first in enumerate(range(0, features, PIECE)):
        at = pl.ds(first, min(PIECE, features - first))
        pieces.append((at, pltpu.make_async_copy(grid.at[at], held.at[at], sems.at[n])))
    for _, copy in pieces:
        copy.start()
    for at, copy in pieces:
        copy.wait()
        size = at.size
        for k in (0, last):
            wide[k, pl.ds(at.start * rows, size * rows), :] = (
                held[at, :, k * block : (k + 1) * block].astype(F32).reshape(size * rows, block)
            )
        lane = lax.broadcasted_iota(jnp.int32, (size, block), 1)
        for pair in range(rows // 2):
            even = pl.ds(at.start * rows + 2 * pair, size, stride=rows)
            odd = pl.ds(at.start * rows + 2 * pair + 1, size, stride=rows)
            to = slice(pair * block, (pair + 1) * block)
            head = jnp.where(lane < half, wide[0, even, :], pltpu.roll(wide[0, odd, :], half, 1))
            tail = jnp.where(lane < half, pltpu.roll(wide[last, even, :], half, 1), wide[last, odd, :])
            to_west[at, to] = head.astype(BF)
            to_east[at, to] = tail.astype(BF)


def own_kernel(
    src, dst, count, grid, embed_w, edge_w, cot, out_w,
    weights_all, x_t, embed_t, h_own, slope, grad_update, acc, wide,
):
    features, rows, cols = grid.shape
    block = edge_w.shape[1]
    half = block // 2
    own_blocks = cols // block
    windows = 2 * own_blocks + 1
    west_base = rows * own_blocks
    east_base = west_base + rows // 2
    acc[...] = jnp.zeros(acc.shape, F32)
    lane = lax.broadcasted_iota(jnp.int32, (block, block), 1)

    def slot(b, carry):
        source = src[b]
        row = source // windows
        window = source - row * windows
        at = window // 2
        target = pl.ds(pl.multiple_of(dst[b] * block, block), block)
        weights = edge_w[b].astype(F32)

        @pl.when(window % 2 == 1)
        def _():
            acc[row * own_blocks + at, target, :] += weights

        @pl.when(window % 2 == 0)
        def _():
            turned = pltpu.roll(weights, half, 1)
            odd_row = row % 2 == 1
            first = jnp.where(at == 0, west_base + row // 2, row * own_blocks + at - 1)
            first_high = (at > 0) | odd_row
            second = jnp.where(at == own_blocks, east_base + row // 2, row * own_blocks + at)
            second_high = (at == own_blocks) & odd_row
            acc[first, target, :] += jnp.where(
                first_high, jnp.where(lane >= half, turned, 0.0), jnp.where(lane < half, weights, 0.0)
            )
            acc[second, target, :] += jnp.where(
                second_high, jnp.where(lane >= half, weights, 0.0), jnp.where(lane < half, turned, 0.0)
            )

        return carry

    lax.fori_loop(0, count[0], slot, 0)
    for k in range(acc.shape[0]):
        weights_all[:, k * block : (k + 1) * block] = acc[k].astype(BF)
    for k in range(own_blocks):
        wide[k] = grid[:, :, k * block : (k + 1) * block].astype(F32).reshape(features * rows, block)
    embed_t[...] = embed_w[...].T
    total = jnp.zeros(h_own.shape, F32)
    for r in range(rows):
        at = slice(r * cols, (r + 1) * cols)
        for k in range(own_blocks):
            x_t[:, r * cols + k * block : r * cols + (k + 1) * block] = wide[
                k, pl.ds(r, features, stride=rows), :
            ].astype(BF)
        hidden, hidden_slope = silu_pair(contract(embed_t[...], x_t[:, at], 1, 0))
        slope[:, at] = hidden_slope.astype(BF)
        total += contract(weights_all[:, at], hidden.astype(BF), 1, 1)
    h_own[...] = total
    grad_update[...] = contract(cot[...], out_w[...], 1, 1)


def halo_part(x, embed_t, weights, slope):
    hidden, hidden_slope = silu_pair(contract(embed_t[...], x[...], 1, 0))
    slope[...] = hidden_slope.astype(BF)
    return contract(weights, hidden.astype(BF), 1, 1)


def west_kernel(first, x, embed_t, weights_all, h_own, h_sum, slope):
    points = x.shape[1]
    h_sum[...] = h_own[...] + halo_part(x, embed_t, weights_all[:, first : first + points], slope)


def to_chunks(grads, stack, perm):
    count, matrices, size, _ = grads.shape
    for j in range(count):
        at = pl.ds(pl.multiple_of(perm[j] * size, size), size)
        for k in range(matrices):
            grads[j, k] = stack[k, at, :]


def from_chunks(outs, chunks, perm):
    j = 0
    for chunk in chunks:
        for n in range(chunk.shape[0]):
            size = chunk.shape[2]
            at = pl.ds(pl.multiple_of(perm[j] * size, size), size)
            for k, out in enumerate(outs):
                out[at, :] = chunk[n, k].astype(F32)
            j += 1


def mesh_kernel(
    perm, x, embed_t, weights_all, h_sum, message_w, up_w, gain, mesh_lat, cot, grad_update,
    grads, mesh_grad, grad_gain, grad_aggregate, update, slope, stack,
):
    points = x.shape[1]
    first = weights_all.shape[1] - points
    total = h_sum[...] + halo_part(x, embed_t, weights_all[:, first:], slope)
    gathered = total.astype(BF)
    summed = mesh_lat[...].astype(F32) + contract(gathered, message_w[...], 1, 0)
    rinv = lax.rsqrt(jnp.mean(summed * summed, axis=1, keepdims=True) + epsilon)
    qhat = summed * rinv
    gains = gain[...]
    normed = (qhat * gains).astype(BF)
    pre_up = contract(normed, up_w[...], 1, 0)
    silu_up, up_slope = silu_pair(pre_up)
    update[...] = silu_up.astype(BF)
    grad_pre_up = (grad_update[...] * up_slope).astype(BF)
    grad_normed = contract(grad_pre_up, up_w[...], 1, 1)
    grad_gain[...] = jnp.sum(grad_normed * qhat, axis=0, keepdims=True)
    grad_qhat = grad_normed * gains
    grad_q = rinv * (grad_qhat - qhat * jnp.mean(grad_qhat * qhat, axis=1, keepdims=True))
    grad_aggregate[...] = grad_q.astype(BF)
    mesh_grad[...] = cot[...].astype(F32) + grad_q
    stack[0] = contract(gathered, grad_q.astype(BF), 0, 0).astype(BF)
    stack[1] = contract(normed, grad_pre_up, 0, 0).astype(BF)
    to_chunks(grads, stack, perm)


def tail_kernel(grad_aggregate, update, message_w, out_w, mesh_lat, cot, back, mesh_new, grad_out):
    back[...] = contract(message_w[...], grad_aggregate[...], 1, 1).astype(BF)
    mesh_new[...] = (mesh_lat[...].astype(F32) + contract(update[...], out_w[...], 1, 0)).astype(BF)
    grad_out[...] = contract(update[...], cot[...], 0, 0).astype(BF)


def grid_kernel(
    perm, back, weights_all, slope_own, slope_west, slope_east, x_own, x_west, x_east, grad_gain, grad_out, grads, stack
):
    features = x_own.shape[0]
    tile = x_west.shape[1]
    pieces = []
    for x, slope in ((x_own, slope_own), (x_west, slope_west), (x_east, slope_east)):
        pieces += [(x, slope, k) for k in range(x.shape[1] // tile)]
    sums = jnp.zeros((features, stack.shape[2]), F32)
    for n, (x, slope, k) in enumerate(pieces):
        at = slice(k * tile, (k + 1) * tile)
        hidden = contract(back[...], weights_all[:, n * tile : (n + 1) * tile], 1, 0)
        grad_pre = (hidden * slope[:, at].astype(F32)).astype(BF)
        sums += contract(x[:, at], grad_pre, 1, 1)
    stack[0] = grad_out[...].astype(F32)
    stack[1] = jnp.zeros(stack.shape[1:], F32)
    stack[1, :features, :] = sums
    stack[1, features : features + 1, :] = grad_gain[...]
    count, matrices, size, _ = grads.shape
    for j in range(count):
        at = pl.ds(pl.multiple_of(perm[j] * size, size), size)
        for k in range(matrices):
            grads[j, k] = stack[k, at, :].astype(BF)


def order_mesh_kernel(perm, *refs):
    from_chunks(refs[-2:], refs[:-2], perm)


def order_grid_kernel(perm, *refs):
    grad_out, grad_embed, grad_gain, total = refs[-4:]
    from_chunks((grad_out, total), refs[:-4], perm)
    features = grad_embed.shape[0]
    grad_embed[...] = total[:features, :]
    grad_gain[...] = total[features : features + 1, :]


def role_steps():
    lat = [("lat", 2 << k) for k in range(lax.axis_size("lat").bit_length() - 2)]
    lon = [("lon", 1 << k) for k in range(lax.axis_size("lon").bit_length() - 1)]
    rest = lat[1:] + lon[1:]
    return ([lat[0], lon[0]] + rest, [lon[0], lat[0]] + rest)


def core_swapped(value):
    return lax.ppermute(value, "lat", [(i, i ^ 1) for i in range(lax.axis_size("lat"))])


def swapped(value, step):
    lats = lax.axis_size("lat")
    pairs = []
    for lon in range(lax.axis_size("lon")):
        for lat in range(lats):
            axis, bit = role_steps()[lat & 1][step]
            other = (lon ^ bit) * lats + lat if axis == "lon" else lon * lats + (lat ^ bit)
            pairs.append((lon * lats + lat, other))
    return lax.ppermute(value, ("lon", "lat"), pairs)


def chunk_order():
    core = lax.axis_index("lat") & 1
    sides = []
    for steps in role_steps():
        low = [((lax.axis_index(axis) & bit) != 0).astype(jnp.int32) for axis, bit in steps[:2]]
        sides.append(2 * low[0] + low[1])
    mine = jnp.where(core == 0, sides[0], sides[1])
    theirs = jnp.where(core == 0, sides[1], sides[0])
    return jnp.stack([4 * core + (mine ^ j) for j in range(4)] + [4 - 4 * core + (theirs ^ j) for j in range(4)])


def added(a, b):
    return (a.astype(F32) + b.astype(F32)).astype(BF)


def core_summed(grads):
    return added(grads[:4], core_swapped(grads[4:]))


def halved(kept):
    return added(kept[:2], swapped(kept[2:], 0))


def all_summed(kept):
    mine = added(kept[:1], swapped(kept[1:], 1))
    for step in range(2, len(role_steps()[0])):
        mine = added(mine, swapped(mine, step))
    second = swapped(mine, 1)
    return mine, second, swapped(jnp.concatenate([mine, second]), 0)


def from_both_cores(chunks):
    return (*chunks, *(core_swapped(chunk) for chunk in chunks))


def on_device(grid_in, mesh_lat, edge_w, edge_src, edge_dst, block_count, embed_w, message_w, up_w, out_w, gain, cot):
    rows, cols, features = grid_in.shape
    latent = message_w.shape[0]
    block = edge_w.shape[1]
    half = block // 2
    nodes = mesh_lat.shape[0]
    own = rows * cols
    side = rows * half
    points = own + 2 * side
    grid = jnp.transpose(grid_in, (2, 0, 1))

    def call(kernel, name, in_specs, out_shape, flops, bytes_accessed, limit, scratch_shapes=()):
        return pl.pallas_call(
            kernel,
            name=name,
            in_specs=in_specs,
            out_specs=[VMEM] * len(out_shape),
            out_shape=out_shape,
            scratch_shapes=list(scratch_shapes),
            compiler_params=pltpu.CompilerParams(vmem_limit_bytes=limit * MIB),
            cost_estimate=pl.CostEstimate(flops=flops, bytes_accessed=bytes_accessed, transcendentals=0),
        )

    to_west, to_east = call(
        pack_kernel, "pack", [HBM], [shape((features, side), BF)] * 2, 0, 3 * MIB, 60,
        [
            pltpu.VMEM((features, rows, cols), BF),
            pltpu.VMEM((cols // block, features * rows, block), F32),
            pltpu.SemaphoreType.DMA((-(-features // PIECE),)),
        ],
    )(grid)
    count = lax.axis_size("lon")
    x_west = lax.ppermute(to_east, "lon", [(i, (i + 1) % count) for i in range(count)])
    x_east = lax.ppermute(to_west, "lon", [((i + 1) % count, i) for i in range(count)])

    weights_all, x_own, embed_t, h_own, slope_own, grad_update = call(
        own_kernel, "own_points", [SMEM] * 3 + [VMEM] * 5,
        [
            shape((nodes, points), BF),
            shape((features, own), BF),
            shape((latent, features), BF),
            shape((nodes, latent), F32),
            shape((latent, own), BF),
            shape((nodes, latent), F32),
        ],
        4_000_000_000, 12 * MIB, 32,
        [pltpu.VMEM((points // block, nodes, block), F32), pltpu.VMEM((cols // block, features * rows, block), F32)],
    )(edge_src, edge_dst, block_count, grid, embed_w, edge_w, cot, out_w)

    h_sum, slope_west = call(
        lambda *refs: west_kernel(own, *refs), "west_points", [VMEM] * 4,
        [shape((nodes, latent), F32), shape((latent, side), BF)],
        600_000_000, 3 * MIB, 16,
    )(x_west, embed_t, weights_all, h_own)

    perm = chunk_order()
    grads_a, mesh_grad, gain_term, grad_aggregate, update, slope_east = call(
        mesh_kernel, "mesh_nodes", [SMEM] + [VMEM] * 10,
        [
            shape((8, 2, latent // 8, latent), BF),
            shape((nodes, latent), F32),
            shape((1, latent), F32),
            shape((nodes, latent), BF),
            shape((nodes, latent), BF),
            shape((latent, side), BF),
        ],
        2_000_000_000, 8 * MIB, 16, [pltpu.VMEM((2, latent, latent), BF)],
    )(perm, x_east, embed_t, weights_all, h_sum, message_w, up_w, gain.reshape(1, latent), mesh_lat, cot, grad_update)
    back, mesh_new, grad_out_term = call(
        tail_kernel, "mesh_tail", [VMEM] * 6,
        [shape((latent, nodes), BF), shape((nodes, latent), BF), shape((latent, latent), BF)],
        400_000_000, 3 * MIB, 16,
    )(grad_aggregate, update, message_w, out_w, mesh_lat, cot)

    kept_a, back = lax.optimization_barrier((core_summed(grads_a), back))
    padded = -(-(features + 1) // 128) * 128
    assert padded == latent
    (grads_b,) = call(
        grid_kernel, "grid_points", [SMEM] + [VMEM] * 10, [shape((8, 2, latent // 8, latent), BF)],
        2_400_000_000, 9 * MIB, 16, [pltpu.VMEM((2, latent, latent), F32)],
    )(perm, back, weights_all, slope_own, slope_west, slope_east, x_own, x_west, x_east, gain_term, grad_out_term)

    kept_a, grads_b = lax.optimization_barrier((halved(kept_a), grads_b))
    summed_a = all_summed(kept_a)
    summed_b = all_summed(halved(core_summed(grads_b)))
    square = shape((latent, latent), F32)
    grad_message, grad_up = call(
        order_mesh_kernel, "order_a", [SMEM] + [VMEM] * 6, [square, square], 0, 3 * MIB, 16
    )(perm, *from_both_cores(summed_a))
    last, grad_message, grad_up = lax.optimization_barrier((summed_b[2], grad_message, grad_up))
    grad_out, grad_embed, grad_gain = call(
        order_grid_kernel, "order_b", [SMEM] + [VMEM] * 6,
        [square, shape((features, latent), F32), shape((1, latent), F32)], 0, 3 * MIB, 16,
        [pltpu.VMEM((latent, latent), F32)],
    )(perm, *from_both_cores((*summed_b[:2], last)))
    return (mesh_new, mesh_grad, grad_embed, grad_message, grad_up, grad_out, grad_gain[0])


def solution(mesh):
    tiles = ("grp", "lon", "lat")
    return jax.shard_map(
        on_device,
        mesh=mesh,
        in_specs=(
            P(("grp", "lat"), "lon", None),
            P(tiles, None),
            P(tiles, None, None),
            P(tiles),
            P(tiles),
            P(tiles),
            P(),
            P(),
            P(),
            P(),
            P(),
            P(tiles, None),
        ),
        out_specs=(
            P(tiles, None),
            P(tiles, None),
            P("grp", None),
            P("grp", None),
            P("grp", None),
            P("grp", None),
            P("grp"),
        ),
        check_vma=False,
    )
```

```python
import jax
import jax.numpy as jnp
from jax import lax
from jax.experimental import pallas as pl
from jax.experimental.pallas import tpu as pltpu
from jax.sharding import PartitionSpec as P

epsilon = 1e-05
BF = jnp.bfloat16
F32 = jnp.float32
MIB = 1024 * 1024
PIECE = 128
SMEM = pl.BlockSpec(memory_space=pltpu.SMEM)
VMEM = pl.BlockSpec(memory_space=pltpu.VMEM)
HBM = pl.BlockSpec(memory_space=pltpu.HBM)
shape = jax.ShapeDtypeStruct


def contract(a, b, dim_a, dim_b):
    return lax.dot_general(a, b, (((dim_a,), (dim_b,)), ((), ())), preferred_element_type=F32)


def silu_pair(pre):
    sigma = jax.nn.sigmoid(pre)
    return pre * sigma, sigma * (1.0 + pre * (1.0 - sigma))


def pack_rows(wide, out, rows, first, size, from_high):
    block = wide.shape[1]
    half = block // 2
    lane = lax.broadcasted_iota(jnp.int32, (size, block), 1)
    for pair in range(rows // 2):
        even = wide[pl.ds(first * rows + 2 * pair, size, stride=rows), :]
        odd = wide[pl.ds(first * rows + 2 * pair + 1, size, stride=rows), :]
        if from_high:
            even = pltpu.roll(even, half, 1)
        else:
            odd = pltpu.roll(odd, half, 1)
        out[pl.ds(first, size), pair * block : (pair + 1) * block] = jnp.where(lane < half, even, odd).astype(BF)


def pack_east_kernel(grid, to_east, held, wide, sems):
    features, rows, cols = grid.shape
    block = wide.shape[1]
    pieces = []
    for n, first in enumerate(range(0, features, PIECE)):
        at = pl.ds(first, min(PIECE, features - first))
        source = grid.at[at, :, pl.ds(cols - block, block)]
        pieces.append((at, pltpu.make_async_copy(source, held.at[at], sems.at[n])))
    for _, copy in pieces:
        copy.start()
    for at, copy in pieces:
        copy.wait()
        wide[pl.ds(at.start * rows, at.size * rows), :] = held[at].astype(F32).reshape(at.size * rows, block)
        pack_rows(wide, to_east, rows, at.start, at.size, True)


def pack_west_kernel(grid, to_west, wide):
    features, rows, _ = grid.shape
    block = wide.shape[1]
    wide[...] = grid[:, :, :block].astype(F32).reshape(features * rows, block)
    pack_rows(wide, to_west, rows, 0, features, False)


def own_kernel(
    src, dst, count, grid, embed_w, edge_w, cot, out_w,
    weights_all, x_t, embed_t, h_own, slope, grad_update, acc, wide,
):
    features, rows, cols = grid.shape
    block = edge_w.shape[1]
    half = block // 2
    own_blocks = cols // block
    windows = 2 * own_blocks + 1
    west_base = rows * own_blocks
    east_base = west_base + rows // 2
    acc[...] = jnp.zeros(acc.shape, F32)
    lane = lax.broadcasted_iota(jnp.int32, (block, block), 1)

    def slot(b, carry):
        source = src[b]
        row = source // windows
        window = source - row * windows
        at = window // 2
        target = pl.ds(pl.multiple_of(dst[b] * block, block), block)
        weights = edge_w[b].astype(F32)

        @pl.when(window % 2 == 1)
        def _():
            acc[row * own_blocks + at, target, :] += weights

        @pl.when(window % 2 == 0)
        def _():
            turned = pltpu.roll(weights, half, 1)
            odd_row = row % 2 == 1
            first = jnp.where(at == 0, west_base + row // 2, row * own_blocks + at - 1)
            first_high = (at > 0) | odd_row
            second = jnp.where(at == own_blocks, east_base + row // 2, row * own_blocks + at)
            second_high = (at == own_blocks) & odd_row
            acc[first, target, :] += jnp.where(
                first_high, jnp.where(lane >= half, turned, 0.0), jnp.where(lane < half, weights, 0.0)
            )
            acc[second, target, :] += jnp.where(
                second_high, jnp.where(lane >= half, weights, 0.0), jnp.where(lane < half, turned, 0.0)
            )

        return carry

    lax.fori_loop(0, count[0], slot, 0)
    for k in range(acc.shape[0]):
        weights_all[:, k * block : (k + 1) * block] = acc[k].astype(BF)
    for k in range(own_blocks):
        wide[k] = grid[:, :, k * block : (k + 1) * block].astype(F32).reshape(features * rows, block)
    embed_t[...] = embed_w[...].T
    total = jnp.zeros(h_own.shape, F32)
    for r in range(rows):
        at = slice(r * cols, (r + 1) * cols)
        for k in range(own_blocks):
            x_t[:, r * cols + k * block : r * cols + (k + 1) * block] = wide[
                k, pl.ds(r, features, stride=rows), :
            ].astype(BF)
        hidden, hidden_slope = silu_pair(contract(embed_t[...], x_t[:, at], 1, 0))
        slope[:, at] = hidden_slope.astype(BF)
        total += contract(weights_all[:, at], hidden.astype(BF), 1, 1)
    h_own[...] = total
    grad_update[...] = contract(cot[...], out_w[...], 1, 1)


def halo_part(x, embed_t, weights, slope):
    hidden, hidden_slope = silu_pair(contract(embed_t[...], x[...], 1, 0))
    slope[...] = hidden_slope.astype(BF)
    return contract(weights, hidden.astype(BF), 1, 1)


def west_kernel(first, x, embed_t, weights_all, h_own, h_sum, slope):
    points = x.shape[1]
    h_sum[...] = h_own[...] + halo_part(x, embed_t, weights_all[:, first : first + points], slope)


def to_chunks(grads, stack, perm):
    count, parts, size, _ = grads.shape
    for j in range(count):
        at = pl.ds(pl.multiple_of(perm[j] * size, size), size)
        for k in range(parts):
            grads[j, k] = stack[k, at, :].astype(BF)


def from_chunks(outs, chunks, perm):
    j = 0
    for chunk in chunks:
        for n in range(chunk.shape[0]):
            size = chunk.shape[2]
            for k, (out, first) in enumerate(outs):
                out[pl.ds(pl.multiple_of(first + perm[j] * size, size), size), :] = chunk[n, k].astype(F32)
            j += 1


def mesh_kernel(
    perm, x, embed_t, weights_all, h_sum, message_w, up_w, gain, mesh_lat, cot, grad_update,
    grads, mesh_grad, grad_gain, grad_aggregate, update, slope, stack,
):
    points = x.shape[1]
    first = weights_all.shape[1] - points
    total = h_sum[...] + halo_part(x, embed_t, weights_all[:, first:], slope)
    gathered = total.astype(BF)
    summed = mesh_lat[...].astype(F32) + contract(gathered, message_w[...], 1, 0)
    rinv = lax.rsqrt(jnp.mean(summed * summed, axis=1, keepdims=True) + epsilon)
    qhat = summed * rinv
    gains = gain[...]
    normed = (qhat * gains).astype(BF)
    pre_up = contract(normed, up_w[...], 1, 0)
    silu_up, up_slope = silu_pair(pre_up)
    update[...] = silu_up.astype(BF)
    grad_pre_up = (grad_update[...] * up_slope).astype(BF)
    grad_normed = contract(grad_pre_up, up_w[...], 1, 1)
    grad_gain[...] = jnp.sum(grad_normed * qhat, axis=0, keepdims=True)
    grad_qhat = grad_normed * gains
    grad_q = rinv * (grad_qhat - qhat * jnp.mean(grad_qhat * qhat, axis=1, keepdims=True))
    grad_aggregate[...] = grad_q.astype(BF)
    mesh_grad[...] = cot[...].astype(F32) + grad_q
    rows = stack.shape[1]
    for k, grad in enumerate(
        (
            contract(gathered, grad_q.astype(BF), 0, 0),
            contract(normed, grad_pre_up, 0, 0),
            contract(update[:, :rows], cot[...], 0, 0),
        )
    ):
        for n in range(grad.shape[0] // rows):
            stack[2 * k + n] = grad[n * rows : (n + 1) * rows].astype(BF)
    to_chunks(grads, stack, perm)


def tail_kernel(grad_aggregate, update, message_w, out_w, mesh_lat, cot, back, mesh_new, grad_out):
    back[...] = contract(message_w[...], grad_aggregate[...], 1, 1).astype(BF)
    mesh_new[...] = (mesh_lat[...].astype(F32) + contract(update[...], out_w[...], 1, 0)).astype(BF)
    grad_out[...] = contract(update[:, grad_out.shape[0] :], cot[...], 0, 0)


def grid_kernel(
    perm, back, weights_all, slope_own, slope_west, slope_east, x_own, x_west, x_east, grad_gain, grad_out, grads, stack
):
    features = x_own.shape[0]
    tile = x_west.shape[1]
    pieces = []
    for x, slope in ((x_own, slope_own), (x_west, slope_west), (x_east, slope_east)):
        pieces += [(x, slope, k) for k in range(x.shape[1] // tile)]
    sums = jnp.zeros((features, stack.shape[2]), F32)
    for n, (x, slope, k) in enumerate(pieces):
        at = slice(k * tile, (k + 1) * tile)
        hidden = contract(back[...], weights_all[:, n * tile : (n + 1) * tile], 1, 0)
        grad_pre = (hidden * slope[:, at].astype(F32)).astype(BF)
        sums += contract(x[:, at], grad_pre, 1, 1)
    rows = stack.shape[1]
    stack[0] = grad_out[...]
    stack[1] = sums[:rows]
    stack[2] = jnp.zeros(stack.shape[1:], F32)
    stack[2, : features - rows, :] = sums[rows:]
    stack[2, features - rows : features - rows + 1, :] = grad_gain[...]
    to_chunks(grads, stack, perm)


def order_a_kernel(perm, *refs):
    chunks, (grad_message, grad_up, grad_out, half, sem) = refs[:6], refs[6:]
    rows = half.shape[0]
    from_chunks(((half, 0),), [chunk.at[:, 4:] for chunk in chunks], perm)
    copy = pltpu.make_async_copy(half, grad_out.at[pl.ds(0, rows)], sem)
    copy.start()
    outs = ((grad_message, 0), (grad_message, rows), (grad_up, 0), (grad_up, rows))
    from_chunks(outs, [chunk.at[:, :4] for chunk in chunks], perm)
    copy.wait()


def order_b_kernel(perm, *refs):
    chunks, (_, grad_out, grad_embed, grad_gain, half, total, sem) = refs[:6], refs[6:]
    rows = half.shape[0]
    from_chunks(((half, 0),), [chunk.at[:, :1] for chunk in chunks], perm)
    copy = pltpu.make_async_copy(half, grad_out.at[pl.ds(rows, rows)], sem)
    copy.start()
    from_chunks(((total, 0), (total, rows)), [chunk.at[:, 1:] for chunk in chunks], perm)
    features = grad_embed.shape[0]
    grad_embed[...] = total[:features, :]
    grad_gain[...] = total[features : features + 1, :]
    copy.wait()


def role_steps():
    lat = [("lat", 2 << k) for k in range(lax.axis_size("lat").bit_length() - 2)]
    lon = [("lon", 1 << k) for k in range(lax.axis_size("lon").bit_length() - 1)]
    rest = lat[1:] + lon[1:]
    return ([lat[0], lon[0]] + rest, [lon[0], lat[0]] + rest)


def core_swapped(value):
    return lax.ppermute(value, "lat", [(i, i ^ 1) for i in range(lax.axis_size("lat"))])


def swapped(value, step):
    lats = lax.axis_size("lat")
    pairs = []
    for lon in range(lax.axis_size("lon")):
        for lat in range(lats):
            axis, bit = role_steps()[lat & 1][step]
            other = (lon ^ bit) * lats + lat if axis == "lon" else lon * lats + (lat ^ bit)
            pairs.append((lon * lats + lat, other))
    return lax.ppermute(value, ("lon", "lat"), pairs)


def chunk_order():
    core = lax.axis_index("lat") & 1
    sides = []
    for steps in role_steps():
        low = [((lax.axis_index(axis) & bit) != 0).astype(jnp.int32) for axis, bit in steps[:2]]
        sides.append(2 * low[0] + low[1])
    mine = jnp.where(core == 0, sides[0], sides[1])
    theirs = jnp.where(core == 0, sides[1], sides[0])
    return jnp.stack([4 * core + (mine ^ j) for j in range(4)] + [4 - 4 * core + (theirs ^ j) for j in range(4)])


def added(a, b):
    return (a.astype(F32) + b.astype(F32)).astype(BF)


def core_summed(grads):
    return added(grads[:4], core_swapped(grads[4:]))


def halved(kept):
    return added(kept[:2], swapped(kept[2:], 0))


def all_summed(kept):
    mine = added(kept[:1], swapped(kept[1:], 1))
    for step in range(2, len(role_steps()[0])):
        mine = added(mine, swapped(mine, step))
    second = swapped(mine, 1)
    return mine, second, swapped(jnp.concatenate([mine, second]), 0)


def from_both_cores(chunks):
    return (*chunks, *(core_swapped(chunk) for chunk in chunks))


def on_device(grid_in, mesh_lat, edge_w, edge_src, edge_dst, block_count, embed_w, message_w, up_w, out_w, gain, cot):
    rows, cols, features = grid_in.shape
    latent = message_w.shape[0]
    block = edge_w.shape[1]
    half = block // 2
    nodes = mesh_lat.shape[0]
    own = rows * cols
    side = rows * half
    points = own + 2 * side
    grid = jnp.transpose(grid_in, (2, 0, 1))

    def call(kernel, name, in_specs, out_shape, flops, bytes_accessed, limit, scratch_shapes=(), out_specs=None, **more):
        return pl.pallas_call(
            kernel,
            name=name,
            in_specs=in_specs,
            out_specs=out_specs or [VMEM] * len(out_shape),
            out_shape=out_shape,
            scratch_shapes=list(scratch_shapes),
            compiler_params=pltpu.CompilerParams(vmem_limit_bytes=limit * MIB),
            cost_estimate=pl.CostEstimate(flops=flops, bytes_accessed=bytes_accessed, transcendentals=0),
            **more,
        )

    strip = shape((features, side), BF)
    wide = pltpu.VMEM((features * rows, block), F32)
    (to_east,) = call(
        pack_east_kernel, "pack_east", [HBM], [strip], 0, MIB, 60,
        [pltpu.VMEM((features, rows, block), BF), wide, pltpu.SemaphoreType.DMA((-(-features // PIECE),))],
    )(grid)
    count = lax.axis_size("lon")
    x_west = lax.ppermute(to_east, "lon", [(i, (i + 1) % count) for i in range(count)])
    to_east, later = lax.optimization_barrier((to_east, grid))
    (to_west,) = call(pack_west_kernel, "pack_west", [VMEM], [strip], 0, MIB, 20, [wide])(later)
    x_east = lax.ppermute(to_west, "lon", [((i + 1) % count, i) for i in range(count)])

    weights_all, x_own, embed_t, h_own, slope_own, grad_update = call(
        own_kernel, "own_points", [SMEM] * 3 + [VMEM] * 5,
        [
            shape((nodes, points), BF),
            shape((features, own), BF),
            shape((latent, features), BF),
            shape((nodes, latent), F32),
            shape((latent, own), BF),
            shape((nodes, latent), F32),
        ],
        4_000_000_000, 12 * MIB, 32,
        [pltpu.VMEM((points // block, nodes, block), F32), pltpu.VMEM((cols // block, features * rows, block), F32)],
    )(edge_src, edge_dst, block_count, grid, embed_w, edge_w, cot, out_w)

    h_sum, slope_west = call(
        lambda *refs: west_kernel(own, *refs), "west_points", [VMEM] * 4,
        [shape((nodes, latent), F32), shape((latent, side), BF)],
        600_000_000, 3 * MIB, 16,
    )(x_west, embed_t, weights_all, h_own)

    perm = chunk_order()
    grads_a, mesh_grad, gain_term, grad_aggregate, update, slope_east = call(
        mesh_kernel, "mesh_nodes", [SMEM] + [VMEM] * 10,
        [
            shape((8, 5, latent // 16, latent), BF),
            shape((nodes, latent), F32),
            shape((1, latent), F32),
            shape((nodes, latent), BF),
            shape((nodes, latent), BF),
            shape((latent, side), BF),
        ],
        2_000_000_000, 8 * MIB, 16, [pltpu.VMEM((5, latent // 2, latent), BF)],
    )(perm, x_east, embed_t, weights_all, h_sum, message_w, up_w, gain.reshape(1, latent), mesh_lat, cot, grad_update)
    back, mesh_new, grad_out_term = call(
        tail_kernel, "mesh_tail", [VMEM] * 6,
        [shape((latent, nodes), BF), shape((nodes, latent), BF), shape((latent // 2, latent), F32)],
        400_000_000, 3 * MIB, 16,
    )(grad_aggregate, update, message_w, out_w, mesh_lat, cot)

    kept_a, back = lax.optimization_barrier((core_summed(grads_a), back))
    padded = -(-(features + 1) // 128) * 128
    assert padded == latent
    (grads_b,) = call(
        grid_kernel, "grid_points", [SMEM] + [VMEM] * 10, [shape((8, 3, latent // 16, latent), BF)],
        2_400_000_000, 9 * MIB, 16, [pltpu.VMEM((3, latent // 2, latent), F32)],
    )(perm, back, weights_all, slope_own, slope_west, slope_east, x_own, x_west, x_east, gain_term, grad_out_term)

    kept_a, grads_b = lax.optimization_barrier((halved(kept_a), grads_b))
    summed_a = all_summed(kept_a)
    summed_b = all_summed(halved(core_summed(grads_b)))
    square = shape((latent, latent), F32)
    half_square = pltpu.VMEM((latent // 2, latent), F32)
    grad_message, grad_up, grad_out = call(
        order_a_kernel, "order_a", [SMEM] + [VMEM] * 6, [square, square, square], 0, 4 * MIB, 16,
        [half_square, pltpu.SemaphoreType.DMA], out_specs=[VMEM, VMEM, HBM],
    )(perm, *from_both_cores(summed_a))
    last, grad_message, grad_up, grad_out = lax.optimization_barrier((summed_b[2], grad_message, grad_up, grad_out))
    grad_out, grad_embed, grad_gain = call(
        order_b_kernel, "order_b", [SMEM] + [VMEM] * 6 + [HBM],
        [square, shape((features, latent), F32), shape((1, latent), F32)], 0, 3 * MIB, 16,
        [half_square, pltpu.VMEM((latent, latent), F32), pltpu.SemaphoreType.DMA],
        out_specs=[HBM, VMEM, VMEM], input_output_aliases={7: 0},
    )(perm, *from_both_cores((*summed_b[:2], last)), grad_out)
    return (mesh_new, mesh_grad, grad_embed, grad_message, grad_up, grad_out, grad_gain[0])


def solution(mesh):
    tiles = ("grp", "lon", "lat")
    return jax.shard_map(
        on_device,
        mesh=mesh,
        in_specs=(
            P(("grp", "lat"), "lon", None),
            P(tiles, None),
            P(tiles, None, None),
            P(tiles),
            P(tiles),
            P(tiles),
            P(),
            P(),
            P(),
            P(),
            P(),
            P(tiles, None),
        ),
        out_specs=(
            P(tiles, None),
            P(tiles, None),
            P("grp", None),
            P("grp", None),
            P("grp", None),
            P("grp", None),
            P("grp"),
        ),
        check_vma=False,
    )
```

```python
import jax
import jax.numpy as jnp
from jax import lax
from jax.experimental import pallas as pl
from jax.experimental.pallas import tpu as pltpu
from jax.sharding import PartitionSpec as P

epsilon = 1e-05
BF = jnp.bfloat16
F32 = jnp.float32
MIB = 1024 * 1024
SMEM = pl.BlockSpec(memory_space=pltpu.SMEM)
VMEM = pl.BlockSpec(memory_space=pltpu.VMEM)
HBM = pl.BlockSpec(memory_space=pltpu.HBM)
shape = jax.ShapeDtypeStruct


def contract(a, b, dim_a, dim_b):
    return lax.dot_general(a, b, (((dim_a,), (dim_b,)), ((), ())), preferred_element_type=F32)


def silu_pair(pre):
    sigma = jax.nn.sigmoid(pre)
    return pre * sigma, sigma * (1.0 + pre * (1.0 - sigma))


def pack_kernel(from_high, grid, out, wide):
    features, rows, cols = grid.shape
    block = wide.shape[1]
    half = block // 2
    start = cols - block if from_high else 0
    wide[...] = grid[:, :, start : start + block].astype(F32).reshape(features * rows, block)
    lane = lax.broadcasted_iota(jnp.int32, (features, block), 1)
    for pair in range(rows // 2):
        even = wide[pl.ds(2 * pair, features, stride=rows), :]
        odd = wide[pl.ds(2 * pair + 1, features, stride=rows), :]
        if from_high:
            even = pltpu.roll(even, half, 1)
        else:
            odd = pltpu.roll(odd, half, 1)
        out[:, pair * block : (pair + 1) * block] = jnp.where(lane < half, even, odd).astype(BF)


def own_kernel(
    src, dst, count, grid, embed_w, edge_w, cot, out_w,
    weights_all, x_t, embed_t, h_own, slope, grad_update, acc, wide,
):
    features, rows, cols = grid.shape
    block = edge_w.shape[1]
    half = block // 2
    own_blocks = cols // block
    windows = 2 * own_blocks + 1
    west_base = rows * own_blocks
    east_base = west_base + rows // 2
    acc[...] = jnp.zeros(acc.shape, F32)
    lane = lax.broadcasted_iota(jnp.int32, (block, block), 1)

    def slot(b, carry):
        source = src[b]
        row = source // windows
        window = source - row * windows
        at = window // 2
        target = pl.ds(pl.multiple_of(dst[b] * block, block), block)
        weights = edge_w[b].astype(F32)

        @pl.when(window % 2 == 1)
        def _():
            acc[row * own_blocks + at, target, :] += weights

        @pl.when(window % 2 == 0)
        def _():
            turned = pltpu.roll(weights, half, 1)
            odd_row = row % 2 == 1
            first = jnp.where(at == 0, west_base + row // 2, row * own_blocks + at - 1)
            first_high = (at > 0) | odd_row
            second = jnp.where(at == own_blocks, east_base + row // 2, row * own_blocks + at)
            second_high = (at == own_blocks) & odd_row
            acc[first, target, :] += jnp.where(
                first_high, jnp.where(lane >= half, turned, 0.0), jnp.where(lane < half, weights, 0.0)
            )
            acc[second, target, :] += jnp.where(
                second_high, jnp.where(lane >= half, weights, 0.0), jnp.where(lane < half, turned, 0.0)
            )

        return carry

    lax.fori_loop(0, count[0], slot, 0)
    for k in range(acc.shape[0]):
        weights_all[:, k * block : (k + 1) * block] = acc[k].astype(BF)
    for k in range(own_blocks):
        wide[k] = grid[:, :, k * block : (k + 1) * block].astype(F32).reshape(features * rows, block)
    embed_t[...] = embed_w[...].T
    total = jnp.zeros(h_own.shape, F32)
    for r in range(rows):
        at = slice(r * cols, (r + 1) * cols)
        for k in range(own_blocks):
            x_t[:, r * cols + k * block : r * cols + (k + 1) * block] = wide[
                k, pl.ds(r, features, stride=rows), :
            ].astype(BF)
        hidden, hidden_slope = silu_pair(contract(embed_t[...], x_t[:, at], 1, 0))
        slope[:, at] = hidden_slope.astype(BF)
        total += contract(weights_all[:, at], hidden.astype(BF), 1, 1)
    h_own[...] = total
    grad_update[...] = contract(cot[...], out_w[...], 1, 1)


def halo_part(x, embed_t, weights, slope):
    hidden, hidden_slope = silu_pair(contract(embed_t[...], x[...], 1, 0))
    slope[...] = hidden_slope.astype(BF)
    return contract(weights, hidden.astype(BF), 1, 1)


def west_kernel(first, x, embed_t, weights_all, h_own, h_sum, slope):
    points = x.shape[1]
    h_sum[...] = h_own[...] + halo_part(x, embed_t, weights_all[:, first : first + points], slope)


def to_chunks(grads, stack, perm):
    count, matrices, size, _ = grads.shape
    for j in range(count):
        at = pl.ds(pl.multiple_of(perm[j] * size, size), size)
        for k in range(matrices):
            grads[j, k] = stack[k, at, :]


def from_chunks(outs, chunks, perm):
    j = 0
    for chunk in chunks:
        for n in range(chunk.shape[0]):
            size = chunk.shape[2]
            at = pl.ds(pl.multiple_of(perm[j] * size, size), size)
            for k, out in enumerate(outs):
                out[at, :] = chunk[n, k].astype(F32)
            j += 1


def mesh_kernel(
    perm, x, embed_t, weights_all, h_sum, message_w, up_w, gain, mesh_lat, cot, grad_update,
    grads, mesh_grad, grad_gain, grad_aggregate, update, slope, stack,
):
    points = x.shape[1]
    first = weights_all.shape[1] - points
    total = h_sum[...] + halo_part(x, embed_t, weights_all[:, first:], slope)
    gathered = total.astype(BF)
    summed = mesh_lat[...].astype(F32) + contract(gathered, message_w[...], 1, 0)
    rinv = lax.rsqrt(jnp.mean(summed * summed, axis=1, keepdims=True) + epsilon)
    qhat = summed * rinv
    gains = gain[...]
    normed = (qhat * gains).astype(BF)
    pre_up = contract(normed, up_w[...], 1, 0)
    silu_up, up_slope = silu_pair(pre_up)
    update[...] = silu_up.astype(BF)
    grad_pre_up = (grad_update[...] * up_slope).astype(BF)
    grad_normed = contract(grad_pre_up, up_w[...], 1, 1)
    grad_gain[...] = jnp.sum(grad_normed * qhat, axis=0, keepdims=True)
    grad_qhat = grad_normed * gains
    grad_q = rinv * (grad_qhat - qhat * jnp.mean(grad_qhat * qhat, axis=1, keepdims=True))
    grad_aggregate[...] = grad_q.astype(BF)
    mesh_grad[...] = cot[...].astype(F32) + grad_q
    stack[0] = contract(gathered, grad_q.astype(BF), 0, 0).astype(BF)
    stack[1] = contract(normed, grad_pre_up, 0, 0).astype(BF)
    to_chunks(grads, stack, perm)


def tail_kernel(grad_aggregate, update, message_w, out_w, mesh_lat, cot, back, mesh_new, grad_out):
    back[...] = contract(message_w[...], grad_aggregate[...], 1, 1).astype(BF)
    mesh_new[...] = (mesh_lat[...].astype(F32) + contract(update[...], out_w[...], 1, 0)).astype(BF)
    grad_out[...] = contract(update[...], cot[...], 0, 0).astype(BF)


def grid_kernel(
    perm, back, weights_all, slope_own, slope_west, slope_east, x_own, x_west, x_east, grad_gain, grad_out, grads, stack
):
    features = x_own.shape[0]
    tile = x_west.shape[1]
    pieces = []
    for x, slope in ((x_own, slope_own), (x_west, slope_west), (x_east, slope_east)):
        pieces += [(x, slope, k) for k in range(x.shape[1] // tile)]
    sums = jnp.zeros((features, stack.shape[2]), F32)
    for n, (x, slope, k) in enumerate(pieces):
        at = slice(k * tile, (k + 1) * tile)
        hidden = contract(back[...], weights_all[:, n * tile : (n + 1) * tile], 1, 0)
        grad_pre = (hidden * slope[:, at].astype(F32)).astype(BF)
        sums += contract(x[:, at], grad_pre, 1, 1)
    stack[0] = grad_out[...].astype(F32)
    stack[1] = jnp.zeros(stack.shape[1:], F32)
    stack[1, :features, :] = sums
    stack[1, features : features + 1, :] = grad_gain[...]
    count, matrices, size, _ = grads.shape
    for j in range(count):
        at = pl.ds(pl.multiple_of(perm[j] * size, size), size)
        for k in range(matrices):
            grads[j, k] = stack[k, at, :].astype(BF)


def order_mesh_kernel(perm, *refs):
    from_chunks(refs[-2:], refs[:-2], perm)


def order_grid_kernel(perm, *refs):
    grad_out, grad_embed, grad_gain, held, total, sems = refs[-6:]
    copies = []
    chunks = [(chunk, n) for chunk in refs[:-6] for n in range(chunk.shape[0])]
    size = held.shape[1]
    for j, (chunk, n) in enumerate(chunks):
        held[j] = chunk[n, 0].astype(F32)
        at = pl.ds(pl.multiple_of(perm[j] * size, size), size)
        copies.append(pltpu.make_async_copy(held.at[j], grad_out.at[at], sems.at[j]))
        copies[-1].start()
    for j, (chunk, n) in enumerate(chunks):
        total[pl.ds(pl.multiple_of(perm[j] * size, size), size), :] = chunk[n, 1].astype(F32)
    features = grad_embed.shape[0]
    grad_embed[...] = total[:features, :]
    grad_gain[...] = total[features : features + 1, :]
    for copy in copies:
        copy.wait()


def role_steps():
    lat = [("lat", 2 << k) for k in range(lax.axis_size("lat").bit_length() - 2)]
    lon = [("lon", 1 << k) for k in range(lax.axis_size("lon").bit_length() - 1)]
    rest = lat[1:] + lon[2:]
    return ([lat[0], lon[1], lon[0]] + rest, [lon[0], lat[0], lon[1]] + rest)


def core_swapped(value):
    return lax.ppermute(value, "lat", [(i, i ^ 1) for i in range(lax.axis_size("lat"))])


def swapped(value, step):
    lats = lax.axis_size("lat")
    pairs = []
    for lon in range(lax.axis_size("lon")):
        for lat in range(lats):
            axis, bit = role_steps()[lat & 1][step]
            other = (lon ^ bit) * lats + lat if axis == "lon" else lon * lats + (lat ^ bit)
            pairs.append((lon * lats + lat, other))
    return lax.ppermute(value, ("lon", "lat"), pairs)


def chunk_order():
    core = lax.axis_index("lat") & 1
    sides = []
    for steps in role_steps():
        low = [((lax.axis_index(axis) & bit) != 0).astype(jnp.int32) for axis, bit in steps[:2]]
        sides.append(2 * low[0] + low[1])
    mine = jnp.where(core == 0, sides[0], sides[1])
    theirs = jnp.where(core == 0, sides[1], sides[0])
    return jnp.stack([4 * core + (mine ^ j) for j in range(4)] + [4 - 4 * core + (theirs ^ j) for j in range(4)])


def added(a, b):
    return (a.astype(F32) + b.astype(F32)).astype(BF)


def core_summed(grads):
    return added(grads[:4], core_swapped(grads[4:]))


def halved(kept):
    return added(kept[:2], swapped(kept[2:], 0))


def all_summed(kept):
    mine = added(kept[:1], swapped(kept[1:], 1))
    for step in range(2, len(role_steps()[0])):
        mine = added(mine, swapped(mine, step))
    second = swapped(mine, 1)
    return mine, second, swapped(jnp.concatenate([mine, second]), 0)


def from_both_cores(chunks):
    return (*chunks, *(core_swapped(chunk) for chunk in chunks))


def on_device(grid_in, mesh_lat, edge_w, edge_src, edge_dst, block_count, embed_w, message_w, up_w, out_w, gain, cot):
    rows, cols, features = grid_in.shape
    latent = message_w.shape[0]
    block = edge_w.shape[1]
    half = block // 2
    nodes = mesh_lat.shape[0]
    own = rows * cols
    side = rows * half
    points = own + 2 * side
    grid = jnp.transpose(grid_in, (2, 0, 1))

    def call(kernel, name, in_specs, out_shape, flops, bytes_accessed, limit, scratch_shapes=(), out_specs=None):
        return pl.pallas_call(
            kernel,
            name=name,
            in_specs=in_specs,
            out_specs=out_specs or [VMEM] * len(out_shape),
            out_shape=out_shape,
            scratch_shapes=list(scratch_shapes),
            compiler_params=pltpu.CompilerParams(vmem_limit_bytes=limit * MIB),
            cost_estimate=pl.CostEstimate(flops=flops, bytes_accessed=bytes_accessed, transcendentals=0),
        )

    strip = shape((features, side), BF)
    wide = pltpu.VMEM((features * rows, block), F32)
    count = lax.axis_size("lon")
    (to_east,) = call(lambda *refs: pack_kernel(True, *refs), "pack_east", [VMEM], [strip], 0, MIB, 20, [wide])(grid)
    x_west = lax.ppermute(to_east, "lon", [(i, (i + 1) % count) for i in range(count)])
    to_east, later = lax.optimization_barrier((to_east, grid))
    (to_west,) = call(lambda *refs: pack_kernel(False, *refs), "pack_west", [VMEM], [strip], 0, MIB, 20, [wide])(later)
    x_east = lax.ppermute(to_west, "lon", [((i + 1) % count, i) for i in range(count)])

    weights_all, x_own, embed_t, h_own, slope_own, grad_update = call(
        own_kernel, "own_points", [SMEM] * 3 + [VMEM] * 5,
        [
            shape((nodes, points), BF),
            shape((features, own), BF),
            shape((latent, features), BF),
            shape((nodes, latent), F32),
            shape((latent, own), BF),
            shape((nodes, latent), F32),
        ],
        4_000_000_000, 12 * MIB, 32,
        [pltpu.VMEM((points // block, nodes, block), F32), pltpu.VMEM((cols // block, features * rows, block), F32)],
    )(edge_src, edge_dst, block_count, grid, embed_w, edge_w, cot, out_w)

    h_sum, slope_west = call(
        lambda *refs: west_kernel(own, *refs), "west_points", [VMEM] * 4,
        [shape((nodes, latent), F32), shape((latent, side), BF)],
        600_000_000, 3 * MIB, 16,
    )(x_west, embed_t, weights_all, h_own)

    perm = chunk_order()
    grads_a, mesh_grad, gain_term, grad_aggregate, update, slope_east = call(
        mesh_kernel, "mesh_nodes", [SMEM] + [VMEM] * 10,
        [
            shape((8, 2, latent // 8, latent), BF),
            shape((nodes, latent), F32),
            shape((1, latent), F32),
            shape((nodes, latent), BF),
            shape((nodes, latent), BF),
            shape((latent, side), BF),
        ],
        2_000_000_000, 8 * MIB, 16, [pltpu.VMEM((2, latent, latent), BF)],
    )(perm, x_east, embed_t, weights_all, h_sum, message_w, up_w, gain.reshape(1, latent), mesh_lat, cot, grad_update)
    back, mesh_new, grad_out_term = call(
        tail_kernel, "mesh_tail", [VMEM] * 6,
        [shape((latent, nodes), BF), shape((nodes, latent), BF), shape((latent, latent), BF)],
        400_000_000, 3 * MIB, 16,
    )(grad_aggregate, update, message_w, out_w, mesh_lat, cot)

    kept_a, back = lax.optimization_barrier((core_summed(grads_a), back))
    padded = -(-(features + 1) // 128) * 128
    assert padded == latent
    (grads_b,) = call(
        grid_kernel, "grid_points", [SMEM] + [VMEM] * 10, [shape((8, 2, latent // 8, latent), BF)],
        2_400_000_000, 9 * MIB, 16, [pltpu.VMEM((2, latent, latent), F32)],
    )(perm, back, weights_all, slope_own, slope_west, slope_east, x_own, x_west, x_east, gain_term, grad_out_term)

    kept_a, grads_b = lax.optimization_barrier((halved(kept_a), grads_b))
    summed_a = all_summed(kept_a)
    summed_b = all_summed(halved(core_summed(grads_b)))
    square = shape((latent, latent), F32)
    grad_message, grad_up = call(
        order_mesh_kernel, "order_a", [SMEM] + [VMEM] * 6, [square, square], 0, 3 * MIB, 16
    )(perm, *from_both_cores(summed_a))
    last, grad_message, grad_up = lax.optimization_barrier((summed_b[2], grad_message, grad_up))
    grad_out, grad_embed, grad_gain = call(
        order_grid_kernel, "order_b", [SMEM] + [VMEM] * 6,
        [square, shape((features, latent), F32), shape((1, latent), F32)], 0, 3 * MIB, 16,
        [pltpu.VMEM((8, latent // 8, latent), F32), pltpu.VMEM((latent, latent), F32), pltpu.SemaphoreType.DMA((8,))],
        out_specs=[HBM, VMEM, VMEM],
    )(perm, *from_both_cores((*summed_b[:2], last)))
    return (mesh_new, mesh_grad, grad_embed, grad_message, grad_up, grad_out, grad_gain[0])


def solution(mesh):
    tiles = ("grp", "lon", "lat")
    return jax.shard_map(
        on_device,
        mesh=mesh,
        in_specs=(
            P(("grp", "lat"), "lon", None),
            P(tiles, None),
            P(tiles, None, None),
            P(tiles),
            P(tiles),
            P(tiles),
            P(),
            P(),
            P(),
            P(),
            P(),
            P(tiles, None),
        ),
        out_specs=(
            P(tiles, None),
            P(tiles, None),
            P("grp", None),
            P("grp", None),
            P("grp", None),
            P("grp", None),
            P("grp"),
        ),
        check_vma=False,
    )
```

```python
import jax
import jax.numpy as jnp
from jax import lax
from jax.experimental import pallas as pl
from jax.experimental.pallas import tpu as pltpu
from jax.sharding import PartitionSpec as P

epsilon = 1e-05
BF = jnp.bfloat16
F32 = jnp.float32
MIB = 1024 * 1024
SMEM = pl.BlockSpec(memory_space=pltpu.SMEM)
VMEM = pl.BlockSpec(memory_space=pltpu.VMEM)
shape = jax.ShapeDtypeStruct


def contract(a, b, dim_a, dim_b):
    return lax.dot_general(a, b, (((dim_a,), (dim_b,)), ((), ())), preferred_element_type=F32)


def silu_pair(pre):
    sigma = jax.nn.sigmoid(pre)
    return pre * sigma, sigma * (1.0 + pre * (1.0 - sigma))


def pack_kernel(from_high, grid, out, wide):
    features, rows, cols = grid.shape
    block = wide.shape[1]
    half = block // 2
    start = cols - block if from_high else 0
    wide[...] = grid[:, :, start : start + block].astype(F32).reshape(features * rows, block)
    lane = lax.broadcasted_iota(jnp.int32, (features, block), 1)
    for pair in range(rows // 2):
        even = wide[pl.ds(2 * pair, features, stride=rows), :]
        odd = wide[pl.ds(2 * pair + 1, features, stride=rows), :]
        if from_high:
            even = pltpu.roll(even, half, 1)
        else:
            odd = pltpu.roll(odd, half, 1)
        out[:, pair * block : (pair + 1) * block] = jnp.where(lane < half, even, odd).astype(BF)


def own_kernel(
    src, dst, count, grid, embed_w, edge_w, cot, out_w,
    weights_all, x_t, embed_t, h_own, slope, grad_update, acc, wide,
):
    features, rows, cols = grid.shape
    block = edge_w.shape[1]
    half = block // 2
    own_blocks = cols // block
    windows = 2 * own_blocks + 1
    west_base = rows * own_blocks
    east_base = west_base + rows // 2
    acc[...] = jnp.zeros(acc.shape, F32)
    lane = lax.broadcasted_iota(jnp.int32, (block, block), 1)

    def slot(b, carry):
        source = src[b]
        row = source // windows
        window = source - row * windows
        at = window // 2
        target = pl.ds(pl.multiple_of(dst[b] * block, block), block)
        weights = edge_w[b].astype(F32)

        @pl.when(window % 2 == 1)
        def _():
            acc[row * own_blocks + at, target, :] += weights

        @pl.when(window % 2 == 0)
        def _():
            turned = pltpu.roll(weights, half, 1)
            odd_row = row % 2 == 1
            first = jnp.where(at == 0, west_base + row // 2, row * own_blocks + at - 1)
            first_high = (at > 0) | odd_row
            second = jnp.where(at == own_blocks, east_base + row // 2, row * own_blocks + at)
            second_high = (at == own_blocks) & odd_row
            acc[first, target, :] += jnp.where(
                first_high, jnp.where(lane >= half, turned, 0.0), jnp.where(lane < half, weights, 0.0)
            )
            acc[second, target, :] += jnp.where(
                second_high, jnp.where(lane >= half, weights, 0.0), jnp.where(lane < half, turned, 0.0)
            )

        return carry

    lax.fori_loop(0, count[0], slot, 0)
    for k in range(acc.shape[0]):
        weights_all[:, k * block : (k + 1) * block] = acc[k].astype(BF)
    for k in range(own_blocks):
        wide[k] = grid[:, :, k * block : (k + 1) * block].astype(F32).reshape(features * rows, block)
    embed_t[...] = embed_w[...].T
    total = jnp.zeros(h_own.shape, F32)
    for r in range(rows):
        at = slice(r * cols, (r + 1) * cols)
        for k in range(own_blocks):
            x_t[:, r * cols + k * block : r * cols + (k + 1) * block] = wide[
                k, pl.ds(r, features, stride=rows), :
            ].astype(BF)
        hidden, hidden_slope = silu_pair(contract(embed_t[...], x_t[:, at], 1, 0))
        slope[:, at] = hidden_slope.astype(BF)
        total += contract(weights_all[:, at], hidden.astype(BF), 1, 1)
    h_own[...] = total
    grad_update[...] = contract(cot[...], out_w[...], 1, 1)


def halo_part(x, embed_t, weights, slope):
    hidden, hidden_slope = silu_pair(contract(embed_t[...], x[...], 1, 0))
    slope[...] = hidden_slope.astype(BF)
    return contract(weights, hidden.astype(BF), 1, 1)


def west_kernel(first, x, embed_t, weights_all, h_own, h_sum, slope):
    points = x.shape[1]
    h_sum[...] = h_own[...] + halo_part(x, embed_t, weights_all[:, first : first + points], slope)


def to_chunks(grads, stack, perm):
    count, matrices, size, _ = grads.shape
    for j in range(count):
        at = pl.ds(pl.multiple_of(perm[j] * size, size), size)
        for k in range(matrices):
            grads[j, k] = stack[k, at, :]


def from_chunks(outs, chunks, perm):
    j = 0
    for chunk in chunks:
        for n in range(chunk.shape[0]):
            size = chunk.shape[2]
            at = pl.ds(pl.multiple_of(perm[j] * size, size), size)
            for k, out in enumerate(outs):
                out[at, :] = chunk[n, k].astype(F32)
            j += 1


def mesh_kernel(
    perm, x, embed_t, weights_all, h_sum, message_w, up_w, gain, mesh_lat, cot, grad_update,
    grads, mesh_grad, grad_gain, grad_aggregate, update, slope, stack,
):
    points = x.shape[1]
    first = weights_all.shape[1] - points
    total = h_sum[...] + halo_part(x, embed_t, weights_all[:, first:], slope)
    gathered = total.astype(BF)
    summed = mesh_lat[...].astype(F32) + contract(gathered, message_w[...], 1, 0)
    rinv = lax.rsqrt(jnp.mean(summed * summed, axis=1, keepdims=True) + epsilon)
    qhat = summed * rinv
    gains = gain[...]
    normed = (qhat * gains).astype(BF)
    pre_up = contract(normed, up_w[...], 1, 0)
    silu_up, up_slope = silu_pair(pre_up)
    update[...] = silu_up.astype(BF)
    grad_pre_up = (grad_update[...] * up_slope).astype(BF)
    grad_normed = contract(grad_pre_up, up_w[...], 1, 1)
    grad_gain[...] = jnp.sum(grad_normed * qhat, axis=0, keepdims=True)
    grad_qhat = grad_normed * gains
    grad_q = rinv * (grad_qhat - qhat * jnp.mean(grad_qhat * qhat, axis=1, keepdims=True))
    grad_aggregate[...] = grad_q.astype(BF)
    mesh_grad[...] = cot[...].astype(F32) + grad_q
    stack[0] = contract(gathered, grad_q.astype(BF), 0, 0).astype(BF)
    stack[1] = contract(normed, grad_pre_up, 0, 0).astype(BF)
    to_chunks(grads, stack, perm)


def tail_kernel(grad_aggregate, update, message_w, out_w, mesh_lat, cot, back, mesh_new, grad_out):
    back[...] = contract(message_w[...], grad_aggregate[...], 1, 1).astype(BF)
    mesh_new[...] = (mesh_lat[...].astype(F32) + contract(update[...], out_w[...], 1, 0)).astype(BF)
    grad_out[...] = contract(update[...], cot[...], 0, 0).astype(BF)


def grid_kernel(
    perm, back, weights_all, slope_own, slope_west, slope_east, x_own, x_west, x_east, grad_gain, grad_out, grads, stack
):
    features = x_own.shape[0]
    tile = x_west.shape[1]
    pieces = []
    for x, slope in ((x_own, slope_own), (x_west, slope_west), (x_east, slope_east)):
        pieces += [(x, slope, k) for k in range(x.shape[1] // tile)]
    sums = jnp.zeros((features, stack.shape[2]), F32)
    for n, (x, slope, k) in enumerate(pieces):
        at = slice(k * tile, (k + 1) * tile)
        hidden = contract(back[...], weights_all[:, n * tile : (n + 1) * tile], 1, 0)
        grad_pre = (hidden * slope[:, at].astype(F32)).astype(BF)
        sums += contract(x[:, at], grad_pre, 1, 1)
    stack[0] = grad_out[...].astype(F32)
    stack[1] = jnp.zeros(stack.shape[1:], F32)
    stack[1, :features, :] = sums
    stack[1, features : features + 1, :] = grad_gain[...]
    count, matrices, size, _ = grads.shape
    for j in range(count):
        at = pl.ds(pl.multiple_of(perm[j] * size, size), size)
        for k in range(matrices):
            grads[j, k] = stack[k, at, :].astype(BF)


def order_mesh_kernel(perm, *refs):
    from_chunks(refs[-2:], refs[:-2], perm)


def order_grid_kernel(perm, *refs):
    grad_out, grad_embed, grad_gain, total = refs[-4:]
    from_chunks((grad_out, total), refs[:-4], perm)
    features = grad_embed.shape[0]
    grad_embed[...] = total[:features, :]
    grad_gain[...] = total[features : features + 1, :]


def role_steps():
    lat = [("lat", 2 << k) for k in range(lax.axis_size("lat").bit_length() - 2)]
    lon = [("lon", 1 << k) for k in range(lax.axis_size("lon").bit_length() - 1)]
    rest = lat[1:] + lon[1:]
    return ([lat[0], lon[0]] + rest, [lon[0], lat[0]] + rest)


def core_swapped(value):
    return lax.ppermute(value, "lat", [(i, i ^ 1) for i in range(lax.axis_size("lat"))])


def swapped(value, step):
    lats = lax.axis_size("lat")
    pairs = []
    for lon in range(lax.axis_size("lon")):
        for lat in range(lats):
            axis, bit = role_steps()[lat & 1][step]
            other = (lon ^ bit) * lats + lat if axis == "lon" else lon * lats + (lat ^ bit)
            pairs.append((lon * lats + lat, other))
    return lax.ppermute(value, ("lon", "lat"), pairs)


def chunk_order():
    core = lax.axis_index("lat") & 1
    sides = []
    for steps in role_steps():
        low = [((lax.axis_index(axis) & bit) != 0).astype(jnp.int32) for axis, bit in steps[:2]]
        sides.append(2 * low[0] + low[1])
    mine = jnp.where(core == 0, sides[0], sides[1])
    theirs = jnp.where(core == 0, sides[1], sides[0])
    return jnp.stack([4 * core + (mine ^ j) for j in range(4)] + [4 - 4 * core + (theirs ^ j) for j in range(4)])


def added(a, b):
    return (a.astype(F32) + b.astype(F32)).astype(BF)


def core_summed(grads):
    return added(grads[:4], core_swapped(grads[4:]))


def halved(kept):
    return added(kept[:2], swapped(kept[2:], 0))


def all_summed(kept):
    mine = added(kept[:1], swapped(kept[1:], 1))
    for step in range(2, len(role_steps()[0])):
        mine = added(mine, swapped(mine, step))
    second = swapped(mine, 1)
    return mine, second, swapped(jnp.concatenate([mine, second]), 0)


def from_both_cores(chunks):
    return (*chunks, *(core_swapped(chunk) for chunk in chunks))


def on_device(grid_in, mesh_lat, edge_w, edge_src, edge_dst, block_count, embed_w, message_w, up_w, out_w, gain, cot):
    rows, cols, features = grid_in.shape
    latent = message_w.shape[0]
    block = edge_w.shape[1]
    half = block // 2
    nodes = mesh_lat.shape[0]
    own = rows * cols
    side = rows * half
    points = own + 2 * side
    grid = jnp.transpose(grid_in, (2, 0, 1))

    def call(kernel, name, in_specs, out_shape, flops, bytes_accessed, limit, scratch_shapes=()):
        return pl.pallas_call(
            kernel,
            name=name,
            in_specs=in_specs,
            out_specs=[VMEM] * len(out_shape),
            out_shape=out_shape,
            scratch_shapes=list(scratch_shapes),
            compiler_params=pltpu.CompilerParams(vmem_limit_bytes=limit * MIB),
            cost_estimate=pl.CostEstimate(flops=flops, bytes_accessed=bytes_accessed, transcendentals=0),
        )

    strip = shape((features, side), BF)
    wide = pltpu.VMEM((features * rows, block), F32)
    count = lax.axis_size("lon")
    (to_east,) = call(lambda *refs: pack_kernel(True, *refs), "pack_east", [VMEM], [strip], 0, MIB, 8, [wide])(grid)
    x_west = lax.ppermute(to_east, "lon", [(i, (i + 1) % count) for i in range(count)])
    to_east, later = lax.optimization_barrier((to_east, grid))
    (to_west,) = call(lambda *refs: pack_kernel(False, *refs), "pack_west", [VMEM], [strip], 0, MIB, 8, [wide])(later)
    x_east = lax.ppermute(to_west, "lon", [((i + 1) % count, i) for i in range(count)])

    weights_all, x_own, embed_t, h_own, slope_own, grad_update = call(
        own_kernel, "own_points", [SMEM] * 3 + [VMEM] * 5,
        [
            shape((nodes, points), BF),
            shape((features, own), BF),
            shape((latent, features), BF),
            shape((nodes, latent), F32),
            shape((latent, own), BF),
            shape((nodes, latent), F32),
        ],
        4_000_000_000, 12 * MIB, 24,
        [pltpu.VMEM((points // block, nodes, block), F32), pltpu.VMEM((cols // block, features * rows, block), F32)],
    )(edge_src, edge_dst, block_count, grid, embed_w, edge_w, cot, out_w)

    h_sum, slope_west = call(
        lambda *refs: west_kernel(own, *refs), "west_points", [VMEM] * 4,
        [shape((nodes, latent), F32), shape((latent, side), BF)],
        600_000_000, 3 * MIB, 16,
    )(x_west, embed_t, weights_all, h_own)

    perm = chunk_order()
    grads_a, mesh_grad, gain_term, grad_aggregate, update, slope_east = call(
        mesh_kernel, "mesh_nodes", [SMEM] + [VMEM] * 10,
        [
            shape((8, 2, latent // 8, latent), BF),
            shape((nodes, latent), F32),
            shape((1, latent), F32),
            shape((nodes, latent), BF),
            shape((nodes, latent), BF),
            shape((latent, side), BF),
        ],
        2_000_000_000, 8 * MIB, 16, [pltpu.VMEM((2, latent, latent), BF)],
    )(perm, x_east, embed_t, weights_all, h_sum, message_w, up_w, gain.reshape(1, latent), mesh_lat, cot, grad_update)
    back, mesh_new, grad_out_term = call(
        tail_kernel, "mesh_tail", [VMEM] * 6,
        [shape((latent, nodes), BF), shape((nodes, latent), BF), shape((latent, latent), BF)],
        400_000_000, 3 * MIB, 16,
    )(grad_aggregate, update, message_w, out_w, mesh_lat, cot)

    kept_a, back = lax.optimization_barrier((core_summed(grads_a), back))
    padded = -(-(features + 1) // 128) * 128
    assert padded == latent
    (grads_b,) = call(
        grid_kernel, "grid_points", [SMEM] + [VMEM] * 10, [shape((8, 2, latent // 8, latent), BF)],
        2_400_000_000, 9 * MIB, 16, [pltpu.VMEM((2, latent, latent), F32)],
    )(perm, back, weights_all, slope_own, slope_west, slope_east, x_own, x_west, x_east, gain_term, grad_out_term)

    kept_a, grads_b = lax.optimization_barrier((halved(kept_a), grads_b))
    summed_a = all_summed(kept_a)
    summed_b = all_summed(halved(core_summed(grads_b)))
    square = shape((latent, latent), F32)
    grad_message, grad_up = call(
        order_mesh_kernel, "order_a", [SMEM] + [VMEM] * 6, [square, square], 0, 3 * MIB, 16
    )(perm, *from_both_cores(summed_a))
    last, grad_message, grad_up = lax.optimization_barrier((summed_b[2], grad_message, grad_up))
    grad_out, grad_embed, grad_gain = call(
        order_grid_kernel, "order_b", [SMEM] + [VMEM] * 6,
        [square, shape((features, latent), F32), shape((1, latent), F32)], 0, 3 * MIB, 16,
        [pltpu.VMEM((latent, latent), F32)],
    )(perm, *from_both_cores((*summed_b[:2], last)))
    return (mesh_new, mesh_grad, grad_embed, grad_message, grad_up, grad_out, grad_gain[0])


def solution(mesh):
    tiles = ("grp", "lon", "lat")
    return jax.shard_map(
        on_device,
        mesh=mesh,
        in_specs=(
            P(("grp", "lat"), "lon", None),
            P(tiles, None),
            P(tiles, None, None),
            P(tiles),
            P(tiles),
            P(tiles),
            P(),
            P(),
            P(),
            P(),
            P(),
            P(tiles, None),
        ),
        out_specs=(
            P(tiles, None),
            P(tiles, None),
            P("grp", None),
            P("grp", None),
            P("grp", None),
            P("grp", None),
            P("grp"),
        ),
        check_vma=False,
    )
```

```python
import jax
import jax.numpy as jnp
from jax import lax
from jax.experimental import pallas as pl
from jax.experimental.pallas import tpu as pltpu
from jax.sharding import PartitionSpec as P

epsilon = 1e-05
BF = jnp.bfloat16
F32 = jnp.float32
MIB = 1024 * 1024
SMEM = pl.BlockSpec(memory_space=pltpu.SMEM)
VMEM = pl.BlockSpec(memory_space=pltpu.VMEM)
shape = jax.ShapeDtypeStruct


def contract(a, b, dim_a, dim_b):
    return lax.dot_general(a, b, (((dim_a,), (dim_b,)), ((), ())), preferred_element_type=F32)


def silu_pair(pre):
    sigma = jax.nn.sigmoid(pre)
    return pre * sigma, sigma * (1.0 + pre * (1.0 - sigma))


def pack_kernel(from_high, grid, out, wide):
    features, rows, cols = grid.shape
    block = wide.shape[1]
    half = block // 2
    start = cols - block if from_high else 0
    wide[...] = grid[:, :, start : start + block].astype(F32).reshape(features * rows, block)
    lane = lax.broadcasted_iota(jnp.int32, (features, block), 1)
    for pair in range(rows // 2):
        even = wide[pl.ds(2 * pair, features, stride=rows), :]
        odd = wide[pl.ds(2 * pair + 1, features, stride=rows), :]
        if from_high:
            even = pltpu.roll(even, half, 1)
        else:
            odd = pltpu.roll(odd, half, 1)
        out[:, pair * block : (pair + 1) * block] = jnp.where(lane < half, even, odd).astype(BF)


def own_kernel(
    src, dst, count, grid, embed_w, edge_w, cot, out_w,
    weights_all, x_t, embed_t, h_own, slope, grad_update, acc, wide,
):
    features, rows, cols = grid.shape
    block = edge_w.shape[1]
    half = block // 2
    own_blocks = cols // block
    windows = 2 * own_blocks + 1
    west_base = rows * own_blocks
    east_base = west_base + rows // 2
    acc[...] = jnp.zeros(acc.shape, F32)
    lane = lax.broadcasted_iota(jnp.int32, (block, block), 1)

    def slot(b, carry):
        source = src[b]
        row = source // windows
        window = source - row * windows
        at = window // 2
        target = pl.ds(pl.multiple_of(dst[b] * block, block), block)
        weights = edge_w[b].astype(F32)

        @pl.when(window % 2 == 1)
        def _():
            acc[row * own_blocks + at, target, :] += weights

        @pl.when(window % 2 == 0)
        def _():
            turned = pltpu.roll(weights, half, 1)
            odd_row = row % 2 == 1
            first = jnp.where(at == 0, west_base + row // 2, row * own_blocks + at - 1)
            first_high = (at > 0) | odd_row
            second = jnp.where(at == own_blocks, east_base + row // 2, row * own_blocks + at)
            second_high = (at == own_blocks) & odd_row
            acc[first, target, :] += jnp.where(
                first_high, jnp.where(lane >= half, turned, 0.0), jnp.where(lane < half, weights, 0.0)
            )
            acc[second, target, :] += jnp.where(
                second_high, jnp.where(lane >= half, weights, 0.0), jnp.where(lane < half, turned, 0.0)
            )

        return carry

    lax.fori_loop(0, count[0], slot, 0)
    for k in range(acc.shape[0]):
        weights_all[:, k * block : (k + 1) * block] = acc[k].astype(BF)
    for k in range(own_blocks):
        wide[k] = grid[:, :, k * block : (k + 1) * block].astype(F32).reshape(features * rows, block)
    embed_t[...] = embed_w[...].T
    total = jnp.zeros(h_own.shape, F32)
    for r in range(rows):
        at = slice(r * cols, (r + 1) * cols)
        for k in range(own_blocks):
            x_t[:, r * cols + k * block : r * cols + (k + 1) * block] = wide[
                k, pl.ds(r, features, stride=rows), :
            ].astype(BF)
        hidden, hidden_slope = silu_pair(contract(embed_t[...], x_t[:, at], 1, 0))
        slope[:, at] = hidden_slope.astype(BF)
        total += contract(weights_all[:, at], hidden.astype(BF), 1, 1)
    h_own[...] = total
    grad_update[...] = contract(cot[...], out_w[...], 1, 1)


def halo_part(x, embed_t, weights, slope):
    hidden, hidden_slope = silu_pair(contract(embed_t[...], x[...], 1, 0))
    slope[...] = hidden_slope.astype(BF)
    return contract(weights, hidden.astype(BF), 1, 1)


def west_kernel(first, x, embed_t, weights_all, h_own, h_sum, slope):
    points = x.shape[1]
    h_sum[...] = h_own[...] + halo_part(x, embed_t, weights_all[:, first : first + points], slope)


def to_chunks(grads, stack, perm, start):
    count, matrices, size, _ = grads.shape
    for j in range(count):
        at = pl.ds(pl.multiple_of((perm[start + j] & (count - 1)) * size, size), size)
        for k in range(matrices):
            grads[j, k] = stack[k, at, :].astype(BF)


def from_chunks(outs, chunks, perm):
    j = 0
    for chunk in chunks:
        for n in range(chunk.shape[0]):
            size = chunk.shape[2]
            at = pl.ds(pl.multiple_of(perm[j] * size, size), size)
            for k, out in enumerate(outs):
                out[at, :] = chunk[n, k].astype(F32)
            j += 1


def rows_of_half(half, rows):
    return pl.ds(pl.multiple_of(half * rows, rows), rows)


def mesh_kernel(
    perm, x, embed_t, weights_all, h_sum, message_w, up_w, gain, mesh_lat, cot, grad_update,
    sent, mesh_grad, grad_gain, gathered, grad_aggregate, normed, grad_pre_up, update, slope, stack,
):
    points = x.shape[1]
    first = weights_all.shape[1] - points
    total = h_sum[...] + halo_part(x, embed_t, weights_all[:, first:], slope)
    gathered[...] = total.astype(BF)
    summed = mesh_lat[...].astype(F32) + contract(gathered[...], message_w[...], 1, 0)
    rinv = lax.rsqrt(jnp.mean(summed * summed, axis=1, keepdims=True) + epsilon)
    qhat = summed * rinv
    gains = gain[...]
    normed[...] = (qhat * gains).astype(BF)
    pre_up = contract(normed[...], up_w[...], 1, 0)
    silu_up, up_slope = silu_pair(pre_up)
    update[...] = silu_up.astype(BF)
    grad_pre_up[...] = (grad_update[...] * up_slope).astype(BF)
    grad_normed = contract(grad_pre_up[...], up_w[...], 1, 1)
    grad_gain[...] = jnp.sum(grad_normed * qhat, axis=0, keepdims=True)
    grad_qhat = grad_normed * gains
    grad_q = rinv * (grad_qhat - qhat * jnp.mean(grad_qhat * qhat, axis=1, keepdims=True))
    grad_aggregate[...] = grad_q.astype(BF)
    mesh_grad[...] = cot[...].astype(F32) + grad_q
    theirs = rows_of_half(1 - perm[0] // 4, stack.shape[1])
    stack[0] = contract(gathered[:, theirs], grad_aggregate[...], 0, 0).astype(BF)
    stack[1] = contract(normed[:, theirs], grad_pre_up[...], 0, 0).astype(BF)
    to_chunks(sent, stack, perm, 4)


def tail_kernel(
    perm, gathered, grad_aggregate, normed, grad_pre_up, update, message_w, out_w, mesh_lat, cot,
    kept, back, mesh_new, grad_out, stack,
):
    mine = rows_of_half(perm[0] // 4, stack.shape[1])
    stack[0] = contract(gathered[:, mine], grad_aggregate[...], 0, 0).astype(BF)
    stack[1] = contract(normed[:, mine], grad_pre_up[...], 0, 0).astype(BF)
    to_chunks(kept, stack, perm, 0)
    back[...] = contract(message_w[...], grad_aggregate[...], 1, 1).astype(BF)
    mesh_new[...] = (mesh_lat[...].astype(F32) + contract(update[...], out_w[...], 1, 0)).astype(BF)
    grad_out[...] = contract(update[...], cot[...], 0, 0).astype(BF)


def points_of(x_own, x_west, x_east):
    tile = x_west.shape[1]
    pieces = []
    for x in (x_own, x_west, x_east):
        pieces += [(x, slice(k * tile, (k + 1) * tile)) for k in range(x.shape[1] // tile)]
    return [(x, at, slice(n * tile, (n + 1) * tile)) for n, (x, at) in enumerate(pieces)]


def embed_rows(half, x_parts, grad_pre, grad_gain, out):
    rows = out.shape[0]
    features = x_parts[0].shape[0]
    for side in range(2):
        count = min(rows, features - side * rows)

        @pl.when(half == side)
        def _():
            sums = jnp.zeros((count, out.shape[1]), F32)
            for x, at, all_at in points_of(*x_parts):
                sums += contract(x[side * rows : side * rows + count, at], grad_pre[:, all_at], 1, 1)
            if count < rows:
                out[...] = jnp.zeros(out.shape, F32)
                out[count : count + 1, :] = grad_gain[...]
            out[:count, :] = sums


def grid_kernel(
    perm, back, weights_all, slope_own, slope_west, slope_east, x_own, x_west, x_east, grad_gain, grad_out,
    sent, grad_pre, stack,
):
    for slope, at, all_at in points_of(slope_own, slope_west, slope_east):
        hidden = contract(back[...], weights_all[:, all_at], 1, 0)
        grad_pre[:, all_at] = (hidden * slope[:, at].astype(F32)).astype(BF)
    half = 1 - perm[0] // 4
    stack[0] = grad_out[rows_of_half(half, stack.shape[1]), :].astype(F32)
    embed_rows(half, (x_own, x_west, x_east), grad_pre, grad_gain, stack.at[1])
    to_chunks(sent, stack, perm, 4)


def grid_kept_kernel(perm, grad_pre, x_own, x_west, x_east, grad_gain, grad_out, kept, stack):
    half = perm[0] // 4
    stack[0] = grad_out[rows_of_half(half, stack.shape[1]), :].astype(F32)
    embed_rows(half, (x_own, x_west, x_east), grad_pre, grad_gain, stack.at[1])
    to_chunks(kept, stack, perm, 0)


def order_mesh_kernel(perm, *refs):
    from_chunks(refs[-2:], refs[:-2], perm)


def order_grid_kernel(perm, *refs):
    grad_out, grad_embed, grad_gain, total = refs[-4:]
    from_chunks((grad_out, total), refs[:-4], perm)
    features = grad_embed.shape[0]
    grad_embed[...] = total[:features, :]
    grad_gain[...] = total[features : features + 1, :]


def role_steps():
    lat = [("lat", 2 << k) for k in range(lax.axis_size("lat").bit_length() - 2)]
    lon = [("lon", 1 << k) for k in range(lax.axis_size("lon").bit_length() - 1)]
    rest = lat[1:] + lon[1:]
    return ([lat[0], lon[0]] + rest, [lon[0], lat[0]] + rest)


def core_swapped(value):
    return lax.ppermute(value, "lat", [(i, i ^ 1) for i in range(lax.axis_size("lat"))])


def swapped(value, step):
    lats = lax.axis_size("lat")
    pairs = []
    for lon in range(lax.axis_size("lon")):
        for lat in range(lats):
            axis, bit = role_steps()[lat & 1][step]
            other = (lon ^ bit) * lats + lat if axis == "lon" else lon * lats + (lat ^ bit)
            pairs.append((lon * lats + lat, other))
    return lax.ppermute(value, ("lon", "lat"), pairs)


def chunk_order():
    core = lax.axis_index("lat") & 1
    sides = []
    for steps in role_steps():
        low = [((lax.axis_index(axis) & bit) != 0).astype(jnp.int32) for axis, bit in steps[:2]]
        sides.append(2 * low[0] + low[1])
    mine = jnp.where(core == 0, sides[0], sides[1])
    theirs = jnp.where(core == 0, sides[1], sides[0])
    return jnp.stack([4 * core + (mine ^ j) for j in range(4)] + [4 - 4 * core + (theirs ^ j) for j in range(4)])


def added(a, b):
    return (a.astype(F32) + b.astype(F32)).astype(BF)


def halved(kept):
    return added(kept[:2], swapped(kept[2:], 0))


def all_summed(kept):
    mine = added(kept[:1], swapped(kept[1:], 1))
    for step in range(2, len(role_steps()[0])):
        mine = added(mine, swapped(mine, step))
    second = swapped(mine, 1)
    return mine, second, swapped(jnp.concatenate([mine, second]), 0)


def from_both_cores(chunks):
    return (*chunks, *(core_swapped(chunk) for chunk in chunks))


def on_device(grid_in, mesh_lat, edge_w, edge_src, edge_dst, block_count, embed_w, message_w, up_w, out_w, gain, cot):
    rows, cols, features = grid_in.shape
    latent = message_w.shape[0]
    block = edge_w.shape[1]
    half = block // 2
    nodes = mesh_lat.shape[0]
    own = rows * cols
    side = rows * half
    points = own + 2 * side
    grid = jnp.transpose(grid_in, (2, 0, 1))

    def call(kernel, name, in_specs, out_shape, flops, bytes_accessed, limit, scratch_shapes=()):
        return pl.pallas_call(
            kernel,
            name=name,
            in_specs=in_specs,
            out_specs=[VMEM] * len(out_shape),
            out_shape=out_shape,
            scratch_shapes=list(scratch_shapes),
            compiler_params=pltpu.CompilerParams(vmem_limit_bytes=limit * MIB),
            cost_estimate=pl.CostEstimate(flops=flops, bytes_accessed=bytes_accessed, transcendentals=0),
        )

    strip = shape((features, side), BF)
    wide = pltpu.VMEM((features * rows, block), F32)
    count = lax.axis_size("lon")
    (to_east,) = call(lambda *refs: pack_kernel(True, *refs), "pack_east", [VMEM], [strip], 0, MIB, 8, [wide])(grid)
    x_west = lax.ppermute(to_east, "lon", [(i, (i + 1) % count) for i in range(count)])
    to_east, later = lax.optimization_barrier((to_east, grid))
    (to_west,) = call(lambda *refs: pack_kernel(False, *refs), "pack_west", [VMEM], [strip], 0, MIB, 60, [wide])(later)
    x_east = lax.ppermute(to_west, "lon", [((i + 1) % count, i) for i in range(count)])

    weights_all, x_own, embed_t, h_own, slope_own, grad_update = call(
        own_kernel, "own_points", [SMEM] * 3 + [VMEM] * 5,
        [
            shape((nodes, points), BF),
            shape((features, own), BF),
            shape((latent, features), BF),
            shape((nodes, latent), F32),
            shape((latent, own), BF),
            shape((nodes, latent), F32),
        ],
        4_000_000_000, 12 * MIB, 24,
        [pltpu.VMEM((points // block, nodes, block), F32), pltpu.VMEM((cols // block, features * rows, block), F32)],
    )(edge_src, edge_dst, block_count, grid, embed_w, edge_w, cot, out_w)

    h_sum, slope_west = call(
        lambda *refs: west_kernel(own, *refs), "west_points", [VMEM] * 4,
        [shape((nodes, latent), F32), shape((latent, side), BF)],
        600_000_000, 3 * MIB, 16,
    )(x_west, embed_t, weights_all, h_own)

    perm = chunk_order()
    half_chunks = shape((4, 2, latent // 8, latent), BF)
    node_rows = shape((nodes, latent), BF)
    (
        sent_a, mesh_grad, gain_term, gathered, grad_aggregate, normed, grad_pre_up, update, slope_east
    ) = call(
        mesh_kernel, "mesh_nodes", [SMEM] + [VMEM] * 10,
        [half_chunks, shape((nodes, latent), F32), shape((1, latent), F32)]
        + [node_rows] * 5
        + [shape((latent, side), BF)],
        2_000_000_000, 8 * MIB, 16, [pltpu.VMEM((2, latent // 2, latent), BF)],
    )(perm, x_east, embed_t, weights_all, h_sum, message_w, up_w, gain.reshape(1, latent), mesh_lat, cot, grad_update)
    got_a = core_swapped(sent_a)
    kept_a, back, mesh_new, grad_out_term = call(
        tail_kernel, "mesh_tail", [SMEM] + [VMEM] * 9,
        [half_chunks, shape((latent, nodes), BF), node_rows, shape((latent, latent), BF)],
        500_000_000, 3 * MIB, 16, [pltpu.VMEM((2, latent // 2, latent), BF)],
    )(perm, gathered, grad_aggregate, normed, grad_pre_up, update, message_w, out_w, mesh_lat, cot)

    kept_a, back = lax.optimization_barrier((added(kept_a, got_a), back))
    padded = -(-(features + 1) // 128) * 128
    assert padded == latent
    x_parts = (x_own, x_west, x_east)
    stack = pltpu.VMEM((2, latent // 2, latent), F32)
    sent_b, grad_pre = call(
        grid_kernel, "grid_points", [SMEM] + [VMEM] * 10, [half_chunks, shape((latent, points), BF)],
        1_600_000_000, 9 * MIB, 20, [stack],
    )(perm, back, weights_all, slope_own, slope_west, slope_east, *x_parts, gain_term, grad_out_term)
    got_b = core_swapped(sent_b)
    kept_a, grad_pre = lax.optimization_barrier((halved(kept_a), grad_pre))
    (kept_b,) = call(
        grid_kept_kernel, "grid_kept", [SMEM] + [VMEM] * 6, [half_chunks], 800_000_000, 6 * MIB, 16, [stack]
    )(perm, grad_pre, *x_parts, gain_term, grad_out_term)

    summed_a = all_summed(kept_a)
    summed_b = all_summed(halved(added(kept_b, got_b)))
    square = shape((latent, latent), F32)
    grad_message, grad_up = call(
        order_mesh_kernel, "order_a", [SMEM] + [VMEM] * 6, [square, square], 0, 3 * MIB, 16
    )(perm, *from_both_cores(summed_a))
    last, grad_message, grad_up = lax.optimization_barrier((summed_b[2], grad_message, grad_up))
    grad_out, grad_embed, grad_gain = call(
        order_grid_kernel, "order_b", [SMEM] + [VMEM] * 6,
        [square, shape((features, latent), F32), shape((1, latent), F32)], 0, 3 * MIB, 16,
        [pltpu.VMEM((latent, latent), F32)],
    )(perm, *from_both_cores((*summed_b[:2], last)))
    return (mesh_new, mesh_grad, grad_embed, grad_message, grad_up, grad_out, grad_gain[0])


def solution(mesh):
    tiles = ("grp", "lon", "lat")
    return jax.shard_map(
        on_device,
        mesh=mesh,
        in_specs=(
            P(("grp", "lat"), "lon", None),
            P(tiles, None),
            P(tiles, None, None),
            P(tiles),
            P(tiles),
            P(tiles),
            P(),
            P(),
            P(),
            P(),
            P(),
            P(tiles, None),
        ),
        out_specs=(
            P(tiles, None),
            P(tiles, None),
            P("grp", None),
            P("grp", None),
            P("grp", None),
            P("grp", None),
            P("grp"),
        ),
        check_vma=False,
    )
```

```python
import jax
import jax.numpy as jnp
from jax import lax
from jax.experimental import pallas as pl
from jax.experimental.pallas import tpu as pltpu
from jax.sharding import PartitionSpec as P

epsilon = 1e-05
BF = jnp.bfloat16
F32 = jnp.float32
MIB = 1024 * 1024
SMEM = pl.BlockSpec(memory_space=pltpu.SMEM)
VMEM = pl.BlockSpec(memory_space=pltpu.VMEM)
shape = jax.ShapeDtypeStruct


def contract(a, b, dim_a, dim_b):
    return lax.dot_general(a, b, (((dim_a,), (dim_b,)), ((), ())), preferred_element_type=F32)


def silu_pair(pre):
    sigma = jax.nn.sigmoid(pre)
    return pre * sigma, sigma * (1.0 + pre * (1.0 - sigma))


def pack_kernel(from_high, grid, out, wide):
    features, rows, cols = grid.shape
    block = wide.shape[1]
    half = block // 2
    start = cols - block if from_high else 0
    wide[...] = grid[:, :, start : start + block].astype(F32).reshape(features * rows, block)
    lane = lax.broadcasted_iota(jnp.int32, (features, block), 1)
    for pair in range(rows // 2):
        even = wide[pl.ds(2 * pair, features, stride=rows), :]
        odd = wide[pl.ds(2 * pair + 1, features, stride=rows), :]
        if from_high:
            even = pltpu.roll(even, half, 1)
        else:
            odd = pltpu.roll(odd, half, 1)
        out[:, pair * block : (pair + 1) * block] = jnp.where(lane < half, even, odd).astype(BF)


def weights_kernel(rows, own_blocks, src, dst, count, edge_w, cot, out_w, weights_all, grad_update, acc):
    block = edge_w.shape[1]
    half = block // 2
    windows = 2 * own_blocks + 1
    west_base = rows * own_blocks
    east_base = west_base + rows // 2
    acc[...] = jnp.zeros(acc.shape, F32)
    lane = lax.broadcasted_iota(jnp.int32, (block, block), 1)

    def slot(b, carry):
        source = src[b]
        row = source // windows
        window = source - row * windows
        at = window // 2
        target = pl.ds(pl.multiple_of(dst[b] * block, block), block)
        weights = edge_w[b].astype(F32)

        @pl.when(window % 2 == 1)
        def _():
            acc[row * own_blocks + at, target, :] += weights

        @pl.when(window % 2 == 0)
        def _():
            turned = pltpu.roll(weights, half, 1)
            odd_row = row % 2 == 1
            first = jnp.where(at == 0, west_base + row // 2, row * own_blocks + at - 1)
            first_high = (at > 0) | odd_row
            second = jnp.where(at == own_blocks, east_base + row // 2, row * own_blocks + at)
            second_high = (at == own_blocks) & odd_row
            acc[first, target, :] += jnp.where(
                first_high, jnp.where(lane >= half, turned, 0.0), jnp.where(lane < half, weights, 0.0)
            )
            acc[second, target, :] += jnp.where(
                second_high, jnp.where(lane >= half, weights, 0.0), jnp.where(lane < half, turned, 0.0)
            )

        return carry

    lax.fori_loop(0, count[0], slot, 0)
    for k in range(acc.shape[0]):
        weights_all[:, k * block : (k + 1) * block] = acc[k].astype(BF)
    grad_update[...] = contract(cot[...], out_w[...], 1, 1)


def rows_kernel(grid, embed_w, x_t, embed_t, wide):
    features, rows, cols = grid.shape
    block = wide.shape[2]
    for k in range(cols // block):
        wide[k] = grid[:, :, k * block : (k + 1) * block].astype(F32).reshape(features * rows, block)
        for r in range(rows):
            x_t[:, r * cols + k * block : r * cols + (k + 1) * block] = wide[
                k, pl.ds(r, features, stride=rows), :
            ].astype(BF)
    embed_t[...] = embed_w[...].T


def own_kernel(x_t, embed_t, weights_all, h_own, slope):
    points = x_t.shape[1]
    tile = points // 8
    total = jnp.zeros(h_own.shape, F32)
    for r in range(8):
        at = slice(r * tile, (r + 1) * tile)
        hidden, hidden_slope = silu_pair(contract(embed_t[...], x_t[:, at], 1, 0))
        slope[:, at] = hidden_slope.astype(BF)
        total += contract(weights_all[:, at], hidden.astype(BF), 1, 1)
    h_own[...] = total


def halo_part(x, embed_t, weights, slope):
    hidden, hidden_slope = silu_pair(contract(embed_t[...], x[...], 1, 0))
    slope[...] = hidden_slope.astype(BF)
    return contract(weights, hidden.astype(BF), 1, 1)


def west_kernel(first, x, embed_t, weights_all, h_own, h_sum, slope):
    points = x.shape[1]
    h_sum[...] = h_own[...] + halo_part(x, embed_t, weights_all[:, first : first + points], slope)


def to_chunks(grads, stack, perm, start):
    count, matrices, size, _ = grads.shape
    for j in range(count):
        at = pl.ds(pl.multiple_of((perm[start + j] & (count - 1)) * size, size), size)
        for k in range(matrices):
            grads[j, k] = stack[k, at, :].astype(BF)


def from_chunks(outs, chunks, perm):
    j = 0
    for chunk in chunks:
        for n in range(chunk.shape[0]):
            size = chunk.shape[2]
            at = pl.ds(pl.multiple_of(perm[j] * size, size), size)
            for k, out in enumerate(outs):
                out[at, :] = chunk[n, k].astype(F32)
            j += 1


def rows_of_half(half, rows):
    return pl.ds(pl.multiple_of(half * rows, rows), rows)


def mesh_kernel(
    perm, x, embed_t, weights_all, h_sum, message_w, up_w, gain, mesh_lat, cot, grad_update,
    sent, mesh_grad, grad_gain, gathered, grad_aggregate, normed, grad_pre_up, update, slope, stack,
):
    points = x.shape[1]
    first = weights_all.shape[1] - points
    total = h_sum[...] + halo_part(x, embed_t, weights_all[:, first:], slope)
    gathered[...] = total.astype(BF)
    summed = mesh_lat[...].astype(F32) + contract(gathered[...], message_w[...], 1, 0)
    rinv = lax.rsqrt(jnp.mean(summed * summed, axis=1, keepdims=True) + epsilon)
    qhat = summed * rinv
    gains = gain[...]
    normed[...] = (qhat * gains).astype(BF)
    pre_up = contract(normed[...], up_w[...], 1, 0)
    silu_up, up_slope = silu_pair(pre_up)
    update[...] = silu_up.astype(BF)
    grad_pre_up[...] = (grad_update[...] * up_slope).astype(BF)
    grad_normed = contract(grad_pre_up[...], up_w[...], 1, 1)
    grad_gain[...] = jnp.sum(grad_normed * qhat, axis=0, keepdims=True)
    grad_qhat = grad_normed * gains
    grad_q = rinv * (grad_qhat - qhat * jnp.mean(grad_qhat * qhat, axis=1, keepdims=True))
    grad_aggregate[...] = grad_q.astype(BF)
    mesh_grad[...] = cot[...].astype(F32) + grad_q
    theirs = rows_of_half(1 - perm[0] // 4, stack.shape[1])
    stack[0] = contract(gathered[:, theirs], grad_aggregate[...], 0, 0).astype(BF)
    stack[1] = contract(normed[:, theirs], grad_pre_up[...], 0, 0).astype(BF)
    to_chunks(sent, stack, perm, 4)


def tail_kernel(
    perm, gathered, grad_aggregate, normed, grad_pre_up, update, message_w, out_w, mesh_lat, cot,
    kept, back, mesh_new, grad_out, stack,
):
    mine = rows_of_half(perm[0] // 4, stack.shape[1])
    stack[0] = contract(gathered[:, mine], grad_aggregate[...], 0, 0).astype(BF)
    stack[1] = contract(normed[:, mine], grad_pre_up[...], 0, 0).astype(BF)
    to_chunks(kept, stack, perm, 0)
    back[...] = contract(message_w[...], grad_aggregate[...], 1, 1).astype(BF)
    mesh_new[...] = (mesh_lat[...].astype(F32) + contract(update[...], out_w[...], 1, 0)).astype(BF)
    grad_out[...] = contract(update[...], cot[...], 0, 0).astype(BF)


def points_of(x_own, x_west, x_east):
    tile = x_west.shape[1]
    pieces = []
    for x in (x_own, x_west, x_east):
        pieces += [(x, slice(k * tile, (k + 1) * tile)) for k in range(x.shape[1] // tile)]
    return [(x, at, slice(n * tile, (n + 1) * tile)) for n, (x, at) in enumerate(pieces)]


def embed_rows(half, x_parts, grad_pre, grad_gain, out):
    rows = out.shape[0]
    features = x_parts[0].shape[0]
    for side in range(2):
        count = min(rows, features - side * rows)

        @pl.when(half == side)
        def _():
            sums = jnp.zeros((count, out.shape[1]), F32)
            for x, at, all_at in points_of(*x_parts):
                sums += contract(x[side * rows : side * rows + count, at], grad_pre[:, all_at], 1, 1)
            if count < rows:
                out[...] = jnp.zeros(out.shape, F32)
                out[count : count + 1, :] = grad_gain[...]
            out[:count, :] = sums


def grid_kernel(
    perm, back, weights_all, slope_own, slope_west, slope_east, x_own, x_west, x_east, grad_gain, grad_out,
    sent, grad_pre, stack,
):
    for slope, at, all_at in points_of(slope_own, slope_west, slope_east):
        hidden = contract(back[...], weights_all[:, all_at], 1, 0)
        grad_pre[:, all_at] = (hidden * slope[:, at].astype(F32)).astype(BF)
    half = 1 - perm[0] // 4
    stack[0] = grad_out[rows_of_half(half, stack.shape[1]), :].astype(F32)
    embed_rows(half, (x_own, x_west, x_east), grad_pre, grad_gain, stack.at[1])
    to_chunks(sent, stack, perm, 4)


def grid_kept_kernel(perm, grad_pre, x_own, x_west, x_east, grad_gain, grad_out, kept, stack):
    half = perm[0] // 4
    stack[0] = grad_out[rows_of_half(half, stack.shape[1]), :].astype(F32)
    embed_rows(half, (x_own, x_west, x_east), grad_pre, grad_gain, stack.at[1])
    to_chunks(kept, stack, perm, 0)


def order_mesh_kernel(perm, *refs):
    from_chunks(refs[-2:], refs[:-2], perm)


def order_grid_kernel(half, behind, perm, *refs):
    chunks, others, (grad_out, grad_embed, grad_gain) = refs[:3], refs[3:-3], refs[-3:]
    j = 4 * half
    for chunk in chunks:
        for n in range(chunk.shape[0]):
            size = chunk.shape[2]
            at = pl.ds(pl.multiple_of((perm[j] & 3) * size, size), size)
            grad_out[at, :] = chunk[n, 0].astype(F32)
            grad_embed[at, :] = chunk[n, 1].astype(F32)
            j += 1
    row = others[0][...] if others else jnp.zeros(grad_gain.shape, F32)
    grad_gain[...] = jnp.where(perm[4 * half] >= 4, grad_embed[behind : behind + 1, :], row)


def role_steps():
    lat = [("lat", 2 << k) for k in range(lax.axis_size("lat").bit_length() - 2)]
    lon = [("lon", 1 << k) for k in range(lax.axis_size("lon").bit_length() - 1)]
    rest = lat[1:] + lon[1:]
    return ([lat[0], lon[0]] + rest, [lon[0], lat[0]] + rest)


def core_swapped(value):
    return lax.ppermute(value, "lat", [(i, i ^ 1) for i in range(lax.axis_size("lat"))])


def swapped(value, step):
    lats = lax.axis_size("lat")
    pairs = []
    for lon in range(lax.axis_size("lon")):
        for lat in range(lats):
            axis, bit = role_steps()[lat & 1][step]
            other = (lon ^ bit) * lats + lat if axis == "lon" else lon * lats + (lat ^ bit)
            pairs.append((lon * lats + lat, other))
    return lax.ppermute(value, ("lon", "lat"), pairs)


def chunk_order():
    core = lax.axis_index("lat") & 1
    sides = []
    for steps in role_steps():
        low = [((lax.axis_index(axis) & bit) != 0).astype(jnp.int32) for axis, bit in steps[:2]]
        sides.append(2 * low[0] + low[1])
    mine = jnp.where(core == 0, sides[0], sides[1])
    theirs = jnp.where(core == 0, sides[1], sides[0])
    return jnp.stack([4 * core + (mine ^ j) for j in range(4)] + [4 - 4 * core + (theirs ^ j) for j in range(4)])


def added(a, b):
    return (a.astype(F32) + b.astype(F32)).astype(BF)


def halved(kept):
    return added(kept[:2], swapped(kept[2:], 0))


def all_summed(kept):
    mine = added(kept[:1], swapped(kept[1:], 1))
    for step in range(2, len(role_steps()[0])):
        mine = added(mine, swapped(mine, step))
    second = swapped(mine, 1)
    return mine, second, swapped(jnp.concatenate([mine, second]), 0)


def from_both_cores(chunks):
    return (*chunks, *(core_swapped(chunk) for chunk in chunks))


def on_device(grid_in, mesh_lat, edge_w, edge_src, edge_dst, block_count, embed_w, message_w, up_w, out_w, gain, cot):
    rows, cols, features = grid_in.shape
    latent = message_w.shape[0]
    block = edge_w.shape[1]
    half = block // 2
    nodes = mesh_lat.shape[0]
    own = rows * cols
    side = rows * half
    points = own + 2 * side
    grid = jnp.transpose(grid_in, (2, 0, 1))

    def call(kernel, name, in_specs, out_shape, flops, bytes_accessed, limit, scratch_shapes=()):
        return pl.pallas_call(
            kernel,
            name=name,
            in_specs=in_specs,
            out_specs=[VMEM] * len(out_shape),
            out_shape=out_shape,
            scratch_shapes=list(scratch_shapes),
            compiler_params=pltpu.CompilerParams(vmem_limit_bytes=limit * MIB),
            cost_estimate=pl.CostEstimate(flops=flops, bytes_accessed=bytes_accessed, transcendentals=0),
        )

    strip = shape((features, side), BF)
    wide = pltpu.VMEM((features * rows, block), F32)
    count = lax.axis_size("lon")
    (to_east,) = call(lambda *refs: pack_kernel(True, *refs), "pack_east", [VMEM], [strip], 0, MIB, 8, [wide])(grid)
    x_west = lax.ppermute(to_east, "lon", [(i, (i + 1) % count) for i in range(count)])
    to_east, later = lax.optimization_barrier((to_east, grid))
    (to_west,) = call(lambda *refs: pack_kernel(False, *refs), "pack_west", [VMEM], [strip], 0, MIB, 8, [wide])(later)
    x_east = lax.ppermute(to_west, "lon", [((i + 1) % count, i) for i in range(count)])

    weights_all, grad_update = call(
        lambda *refs: weights_kernel(rows, cols // block, *refs), "slot_weights", [SMEM] * 3 + [VMEM] * 3,
        [shape((nodes, points), BF), shape((nodes, latent), F32)],
        200_000_000, 4 * MIB, 16, [pltpu.VMEM((points // block, nodes, block), F32)],
    )(edge_src, edge_dst, block_count, edge_w, cot, out_w)
    x_own, embed_t = call(
        rows_kernel, "own_rows", [VMEM] * 2, [shape((features, own), BF), shape((latent, features), BF)],
        1_000_000_000, 5 * MIB, 16, [pltpu.VMEM((cols // block, features * rows, block), F32)],
    )(later, embed_w)
    h_own, slope_own = call(
        own_kernel, "own_points", [VMEM] * 3, [shape((nodes, latent), F32), shape((latent, own), BF)],
        2_000_000_000, 7 * MIB, 16,
    )(x_own, embed_t, weights_all)

    h_sum, slope_west = call(
        lambda *refs: west_kernel(own, *refs), "west_points", [VMEM] * 4,
        [shape((nodes, latent), F32), shape((latent, side), BF)],
        600_000_000, 3 * MIB, 16,
    )(x_west, embed_t, weights_all, h_own)

    perm = chunk_order()
    half_chunks = shape((4, 2, latent // 8, latent), BF)
    node_rows = shape((nodes, latent), BF)
    (
        sent_a, mesh_grad, gain_term, gathered, grad_aggregate, normed, grad_pre_up, update, slope_east
    ) = call(
        mesh_kernel, "mesh_nodes", [SMEM] + [VMEM] * 10,
        [half_chunks, shape((nodes, latent), F32), shape((1, latent), F32)]
        + [node_rows] * 5
        + [shape((latent, side), BF)],
        2_000_000_000, 8 * MIB, 16, [pltpu.VMEM((2, latent // 2, latent), BF)],
    )(perm, x_east, embed_t, weights_all, h_sum, message_w, up_w, gain.reshape(1, latent), mesh_lat, cot, grad_update)
    got_a = core_swapped(sent_a)
    kept_a, back, mesh_new, grad_out_term = call(
        tail_kernel, "mesh_tail", [SMEM] + [VMEM] * 9,
        [half_chunks, shape((latent, nodes), BF), node_rows, shape((latent, latent), BF)],
        500_000_000, 3 * MIB, 16, [pltpu.VMEM((2, latent // 2, latent), BF)],
    )(perm, gathered, grad_aggregate, normed, grad_pre_up, update, message_w, out_w, mesh_lat, cot)

    kept_a, back = lax.optimization_barrier((added(kept_a, got_a), back))
    padded = -(-(features + 1) // 128) * 128
    assert padded == latent
    x_parts = (x_own, x_west, x_east)
    stack = pltpu.VMEM((2, latent // 2, latent), F32)
    sent_b, grad_pre = call(
        grid_kernel, "grid_points", [SMEM] + [VMEM] * 10, [half_chunks, shape((latent, points), BF)],
        1_600_000_000, 9 * MIB, 20, [stack],
    )(perm, back, weights_all, slope_own, slope_west, slope_east, *x_parts, gain_term, grad_out_term)
    got_b = core_swapped(sent_b)
    kept_a, grad_pre = lax.optimization_barrier((halved(kept_a), grad_pre))
    (kept_b,) = call(
        grid_kept_kernel, "grid_kept", [SMEM] + [VMEM] * 6, [half_chunks], 800_000_000, 6 * MIB, 16, [stack]
    )(perm, grad_pre, *x_parts, gain_term, grad_out_term)

    summed_a = all_summed(kept_a)
    summed_b = all_summed(halved(added(kept_b, got_b)))
    square = shape((latent, latent), F32)
    grad_message, grad_up = call(
        order_mesh_kernel, "order_a", [SMEM] + [VMEM] * 6, [square, square], 0, 3 * MIB, 16
    )(perm, *from_both_cores(summed_a))
    last, grad_message, grad_up = lax.optimization_barrier((summed_b[2], grad_message, grad_up))
    summed_b = (*summed_b[:2], last)
    rows_half = latent // 2
    behind = features - rows_half
    outs = [square, shape((features, latent), F32), shape((1, latent), F32)]

    def order_b(half, chunks, more, more_specs, aliases):
        block_of = pl.BlockSpec((rows_half, latent), lambda i, perm: (perm[4 * half] // 4, 0))
        return pl.pallas_call(
            lambda *refs: order_grid_kernel(half, behind, *refs),
            name="order_b",
            grid_spec=pltpu.PrefetchScalarGridSpec(
                num_scalar_prefetch=1,
                grid=(1,),
                in_specs=[VMEM] * 3 + more_specs,
                out_specs=[block_of, block_of, VMEM],
            ),
            out_shape=outs,
            input_output_aliases=aliases,
            compiler_params=pltpu.CompilerParams(vmem_limit_bytes=16 * MIB),
            cost_estimate=pl.CostEstimate(flops=0, bytes_accessed=2 * MIB, transcendentals=0),
        )(perm, *chunks, *more)

    from_other = [core_swapped(chunk) for chunk in summed_b]
    held = order_b(0, summed_b, (), [], {})
    grad_out, grad_embed, grad_gain = order_b(
        1, from_other, (held[2], held[0], held[1]), [VMEM] + [pl.BlockSpec(memory_space=pl.ANY)] * 2, {5: 0, 6: 1}
    )
    return (mesh_new, mesh_grad, grad_embed, grad_message, grad_up, grad_out, grad_gain[0])


def solution(mesh):
    tiles = ("grp", "lon", "lat")
    return jax.shard_map(
        on_device,
        mesh=mesh,
        in_specs=(
            P(("grp", "lat"), "lon", None),
            P(tiles, None),
            P(tiles, None, None),
            P(tiles),
            P(tiles),
            P(tiles),
            P(),
            P(),
            P(),
            P(),
            P(),
            P(tiles, None),
        ),
        out_specs=(
            P(tiles, None),
            P(tiles, None),
            P("grp", None),
            P("grp", None),
            P("grp", None),
            P("grp", None),
            P("grp"),
        ),
        check_vma=False,
    )
```

```python
import jax
import jax.numpy as jnp
from jax import lax
from jax.experimental import pallas as pl
from jax.experimental.pallas import tpu as pltpu
from jax.sharding import PartitionSpec as P

epsilon = 1e-05
BF = jnp.bfloat16
F32 = jnp.float32
MIB = 1024 * 1024
SMEM = pl.BlockSpec(memory_space=pltpu.SMEM)
VMEM = pl.BlockSpec(memory_space=pltpu.VMEM)
shape = jax.ShapeDtypeStruct


def contract(a, b, dim_a, dim_b):
    return lax.dot_general(a, b, (((dim_a,), (dim_b,)), ((), ())), preferred_element_type=F32)


def silu_pair(pre):
    sigma = jax.nn.sigmoid(pre)
    return pre * sigma, sigma * (1.0 + pre * (1.0 - sigma))


def pack_kernel(from_high, grid, out, wide):
    features, rows, cols = grid.shape
    block = wide.shape[1]
    half = block // 2
    start = cols - block if from_high else 0
    wide[...] = grid[:, :, start : start + block].astype(F32).reshape(features * rows, block)
    lane = lax.broadcasted_iota(jnp.int32, (features, block), 1)
    for pair in range(rows // 2):
        even = wide[pl.ds(2 * pair, features, stride=rows), :]
        odd = wide[pl.ds(2 * pair + 1, features, stride=rows), :]
        if from_high:
            even = pltpu.roll(even, half, 1)
        else:
            odd = pltpu.roll(odd, half, 1)
        out[:, pair * block : (pair + 1) * block] = jnp.where(lane < half, even, odd).astype(BF)


def weights_kernel(rows, own_blocks, src, dst, count, edge_w, cot, out_w, weights_all, grad_update, acc):
    block = edge_w.shape[1]
    half = block // 2
    windows = 2 * own_blocks + 1
    west_base = rows * own_blocks
    east_base = west_base + rows // 2
    acc[...] = jnp.zeros(acc.shape, F32)
    lane = lax.broadcasted_iota(jnp.int32, (block, block), 1)

    def slot(b, carry):
        source = src[b]
        row = source // windows
        window = source - row * windows
        at = window // 2
        target = pl.ds(pl.multiple_of(dst[b] * block, block), block)
        weights = edge_w[b].astype(F32)

        @pl.when(window % 2 == 1)
        def _():
            acc[row * own_blocks + at, target, :] += weights

        @pl.when(window % 2 == 0)
        def _():
            turned = pltpu.roll(weights, half, 1)
            odd_row = row % 2 == 1
            first = jnp.where(at == 0, west_base + row // 2, row * own_blocks + at - 1)
            first_high = (at > 0) | odd_row
            second = jnp.where(at == own_blocks, east_base + row // 2, row * own_blocks + at)
            second_high = (at == own_blocks) & odd_row
            acc[first, target, :] += jnp.where(
                first_high, jnp.where(lane >= half, turned, 0.0), jnp.where(lane < half, weights, 0.0)
            )
            acc[second, target, :] += jnp.where(
                second_high, jnp.where(lane >= half, weights, 0.0), jnp.where(lane < half, turned, 0.0)
            )

        return carry

    lax.fori_loop(0, count[0], slot, 0)
    for k in range(acc.shape[0]):
        weights_all[:, k * block : (k + 1) * block] = acc[k].astype(BF)
    grad_update[...] = contract(cot[...], out_w[...], 1, 1)


def rows_kernel(grid, embed_w, x_t, embed_t, wide):
    features, rows, cols = grid.shape
    block = wide.shape[2]
    for k in range(cols // block):
        wide[k] = grid[:, :, k * block : (k + 1) * block].astype(F32).reshape(features * rows, block)
        for r in range(rows):
            x_t[:, r * cols + k * block : r * cols + (k + 1) * block] = wide[
                k, pl.ds(r, features, stride=rows), :
            ].astype(BF)
    embed_t[...] = embed_w[...].T


def own_kernel(x_t, embed_t, weights_all, h_own, slope):
    points = x_t.shape[1]
    tile = points // 8
    total = jnp.zeros(h_own.shape, F32)
    for r in range(8):
        at = slice(r * tile, (r + 1) * tile)
        hidden, hidden_slope = silu_pair(contract(embed_t[...], x_t[:, at], 1, 0))
        slope[:, at] = hidden_slope.astype(BF)
        total += contract(weights_all[:, at], hidden.astype(BF), 1, 1)
    h_own[...] = total


def halo_part(x, embed_t, weights, slope):
    hidden, hidden_slope = silu_pair(contract(embed_t[...], x[...], 1, 0))
    slope[...] = hidden_slope.astype(BF)
    return contract(weights, hidden.astype(BF), 1, 1)


def west_kernel(first, x, embed_t, weights_all, h_own, h_sum, slope):
    points = x.shape[1]
    h_sum[...] = h_own[...] + halo_part(x, embed_t, weights_all[:, first : first + points], slope)


def to_chunks(grads, stack, perm, start):
    count, matrices, size, _ = grads.shape
    for j in range(count):
        at = pl.ds(pl.multiple_of((perm[start + j] & (count - 1)) * size, size), size)
        for k in range(matrices):
            grads[j, k] = stack[k, at, :].astype(BF)


def from_chunks(outs, chunks, perm):
    j = 0
    for chunk in chunks:
        for n in range(chunk.shape[0]):
            size = chunk.shape[2]
            at = pl.ds(pl.multiple_of(perm[j] * size, size), size)
            for k, out in enumerate(outs):
                out[at, :] = chunk[n, k].astype(F32)
            j += 1


def rows_of_half(half, rows):
    return pl.ds(pl.multiple_of(half * rows, rows), rows)


def mesh_kernel(
    x, embed_t, weights_all, h_sum, message_w, up_w, gain, mesh_lat, cot, grad_update,
    sent, mesh_grad, grad_gain, gathered, grad_aggregate, normed, grad_pre_up, update, slope, stack,
):
    perm = chunk_order()
    points = x.shape[1]
    first = weights_all.shape[1] - points
    total = h_sum[...] + halo_part(x, embed_t, weights_all[:, first:], slope)
    gathered[...] = total.astype(BF)
    summed = mesh_lat[...].astype(F32) + contract(gathered[...], message_w[...], 1, 0)
    rinv = lax.rsqrt(jnp.mean(summed * summed, axis=1, keepdims=True) + epsilon)
    qhat = summed * rinv
    gains = gain[...]
    normed[...] = (qhat * gains).astype(BF)
    pre_up = contract(normed[...], up_w[...], 1, 0)
    silu_up, up_slope = silu_pair(pre_up)
    update[...] = silu_up.astype(BF)
    grad_pre_up[...] = (grad_update[...] * up_slope).astype(BF)
    grad_normed = contract(grad_pre_up[...], up_w[...], 1, 1)
    grad_gain[...] = jnp.sum(grad_normed * qhat, axis=0, keepdims=True)
    grad_qhat = grad_normed * gains
    grad_q = rinv * (grad_qhat - qhat * jnp.mean(grad_qhat * qhat, axis=1, keepdims=True))
    grad_aggregate[...] = grad_q.astype(BF)
    mesh_grad[...] = cot[...].astype(F32) + grad_q
    theirs = rows_of_half(1 - perm[0] // 4, stack.shape[1])
    stack[0] = contract(gathered[:, theirs], grad_aggregate[...], 0, 0).astype(BF)
    stack[1] = contract(normed[:, theirs], grad_pre_up[...], 0, 0).astype(BF)
    to_chunks(sent, stack, perm, 4)


def tail_kernel(
    gathered, grad_aggregate, normed, grad_pre_up, update, message_w, out_w, mesh_lat, cot,
    kept, back, mesh_new, grad_out, stack,
):
    perm = chunk_order()
    mine = rows_of_half(perm[0] // 4, stack.shape[1])
    stack[0] = contract(gathered[:, mine], grad_aggregate[...], 0, 0).astype(BF)
    stack[1] = contract(normed[:, mine], grad_pre_up[...], 0, 0).astype(BF)
    to_chunks(kept, stack, perm, 0)
    back[...] = contract(message_w[...], grad_aggregate[...], 1, 1).astype(BF)
    mesh_new[...] = (mesh_lat[...].astype(F32) + contract(update[...], out_w[...], 1, 0)).astype(BF)
    grad_out[...] = contract(update[...], cot[...], 0, 0).astype(BF)


def points_of(x_own, x_west, x_east):
    tile = x_west.shape[1]
    pieces = []
    for x in (x_own, x_west, x_east):
        pieces += [(x, slice(k * tile, (k + 1) * tile)) for k in range(x.shape[1] // tile)]
    return [(x, at, slice(n * tile, (n + 1) * tile)) for n, (x, at) in enumerate(pieces)]


def embed_rows(half, x_parts, grad_pre, grad_gain, out):
    rows = out.shape[0]
    features = x_parts[0].shape[0]
    for side in range(2):
        count = min(rows, features - side * rows)

        @pl.when(half == side)
        def _():
            sums = jnp.zeros((count, out.shape[1]), F32)
            for x, at, all_at in points_of(*x_parts):
                sums += contract(x[side * rows : side * rows + count, at], grad_pre[:, all_at], 1, 1)
            if count < rows:
                out[...] = jnp.zeros(out.shape, F32)
                out[count : count + 1, :] = grad_gain[...]
            out[:count, :] = sums


def grid_kernel(
    back, weights_all, slope_own, slope_west, slope_east, x_own, x_west, x_east, grad_gain, grad_out,
    sent, grad_pre, stack,
):
    perm = chunk_order()
    for slope, at, all_at in points_of(slope_own, slope_west, slope_east):
        hidden = contract(back[...], weights_all[:, all_at], 1, 0)
        grad_pre[:, all_at] = (hidden * slope[:, at].astype(F32)).astype(BF)
    half = 1 - perm[0] // 4
    stack[0] = grad_out[rows_of_half(half, stack.shape[1]), :].astype(F32)
    embed_rows(half, (x_own, x_west, x_east), grad_pre, grad_gain, stack.at[1])
    to_chunks(sent, stack, perm, 4)


def grid_kept_kernel(grad_pre, x_own, x_west, x_east, grad_gain, sums):
    perm = chunk_order()
    embed_rows(perm[0] // 4, (x_own, x_west, x_east), grad_pre, grad_gain, sums)


def kept_chunks_kernel(grad_out, sums, kept):
    perm = chunk_order()
    count, _, size, _ = kept.shape
    for j in range(count):
        kept[j, 0] = grad_out[pl.ds(pl.multiple_of(perm[j] * size, size), size), :]
        kept[j, 1] = sums[pl.ds(pl.multiple_of((perm[j] & (count - 1)) * size, size), size), :].astype(BF)


def order_mesh_kernel(*refs):
    from_chunks(refs[-2:], refs[:-2], chunk_order())


def order_grid_kernel(half, behind, *refs):
    perm = chunk_order()
    chunks, others, (grad_out, grad_embed, grad_gain) = refs[:3], refs[3:-3], refs[-3:]
    j = 4 * half
    for chunk in chunks:
        for n in range(chunk.shape[0]):
            size = chunk.shape[2]
            at = pl.ds(pl.multiple_of((perm[j] & 3) * size, size), size)
            grad_out[at, :] = chunk[n, 0].astype(F32)
            grad_embed[at, :] = chunk[n, 1].astype(F32)
            j += 1
    row = others[0][...] if others else jnp.zeros(grad_gain.shape, F32)
    grad_gain[...] = jnp.where(perm[4 * half] >= 4, grad_embed[behind : behind + 1, :], row)


def role_steps():
    lat = [("lat", 2 << k) for k in range(lax.axis_size("lat").bit_length() - 2)]
    lon = [("lon", 1 << k) for k in range(lax.axis_size("lon").bit_length() - 1)]
    rest = lat[1:] + lon[1:]
    return ([lat[0], lon[0]] + rest, [lon[0], lat[0]] + rest)


def core_swapped(value):
    return lax.ppermute(value, "lat", [(i, i ^ 1) for i in range(lax.axis_size("lat"))])


def swapped(value, step):
    lats = lax.axis_size("lat")
    pairs = []
    for lon in range(lax.axis_size("lon")):
        for lat in range(lats):
            axis, bit = role_steps()[lat & 1][step]
            other = (lon ^ bit) * lats + lat if axis == "lon" else lon * lats + (lat ^ bit)
            pairs.append((lon * lats + lat, other))
    return lax.ppermute(value, ("lon", "lat"), pairs)


def chunk_order():
    core = lax.axis_index("lat") & 1
    sides = []
    for steps in role_steps():
        low = [((lax.axis_index(axis) & bit) != 0).astype(jnp.int32) for axis, bit in steps[:2]]
        sides.append(2 * low[0] + low[1])
    mine = jnp.where(core == 0, sides[0], sides[1])
    theirs = jnp.where(core == 0, sides[1], sides[0])
    return [4 * core + (mine ^ j) for j in range(4)] + [4 - 4 * core + (theirs ^ j) for j in range(4)]


def added(a, b):
    return (a.astype(F32) + b.astype(F32)).astype(BF)


def halved(kept):
    return added(kept[:2], swapped(kept[2:], 0))


def all_summed(kept):
    mine = added(kept[:1], swapped(kept[1:], 1))
    for step in range(2, len(role_steps()[0])):
        mine = added(mine, swapped(mine, step))
    second = swapped(mine, 1)
    return mine, second, swapped(jnp.concatenate([mine, second]), 0)


def from_both_cores(chunks):
    return (*chunks, *(core_swapped(chunk) for chunk in chunks))


def on_device(grid_in, mesh_lat, edge_w, edge_src, edge_dst, block_count, embed_w, message_w, up_w, out_w, gain, cot):
    rows, cols, features = grid_in.shape
    latent = message_w.shape[0]
    block = edge_w.shape[1]
    half = block // 2
    nodes = mesh_lat.shape[0]
    own = rows * cols
    side = rows * half
    points = own + 2 * side
    grid = jnp.transpose(grid_in, (2, 0, 1))

    def call(kernel, name, in_specs, out_shape, flops, bytes_accessed, limit, scratch_shapes=()):
        return pl.pallas_call(
            kernel,
            name=name,
            in_specs=in_specs,
            out_specs=[VMEM] * len(out_shape),
            out_shape=out_shape,
            scratch_shapes=list(scratch_shapes),
            compiler_params=pltpu.CompilerParams(vmem_limit_bytes=limit * MIB),
            cost_estimate=pl.CostEstimate(flops=flops, bytes_accessed=bytes_accessed, transcendentals=0),
        )

    strip = shape((features, side), BF)
    wide = pltpu.VMEM((features * rows, block), F32)
    count = lax.axis_size("lon")
    (to_east,) = call(lambda *refs: pack_kernel(True, *refs), "pack_east", [VMEM], [strip], 0, MIB, 8, [wide])(grid)
    x_west = lax.ppermute(to_east, "lon", [(i, (i + 1) % count) for i in range(count)])
    to_east, later = lax.optimization_barrier((to_east, grid))
    (to_west,) = call(lambda *refs: pack_kernel(False, *refs), "pack_west", [VMEM], [strip], 0, MIB, 8, [wide])(later)
    x_east = lax.ppermute(to_west, "lon", [((i + 1) % count, i) for i in range(count)])

    weights_all, grad_update = call(
        lambda *refs: weights_kernel(rows, cols // block, *refs), "slot_weights", [SMEM] * 3 + [VMEM] * 3,
        [shape((nodes, points), BF), shape((nodes, latent), F32)],
        200_000_000, 4 * MIB, 16, [pltpu.VMEM((points // block, nodes, block), F32)],
    )(edge_src, edge_dst, block_count, edge_w, cot, out_w)
    x_own, embed_t = call(
        rows_kernel, "own_rows", [VMEM] * 2, [shape((features, own), BF), shape((latent, features), BF)],
        1_000_000_000, 5 * MIB, 16, [pltpu.VMEM((cols // block, features * rows, block), F32)],
    )(later, embed_w)
    h_own, slope_own = call(
        own_kernel, "own_points", [VMEM] * 3, [shape((nodes, latent), F32), shape((latent, own), BF)],
        2_000_000_000, 7 * MIB, 16,
    )(x_own, embed_t, weights_all)

    h_sum, slope_west = call(
        lambda *refs: west_kernel(own, *refs), "west_points", [VMEM] * 4,
        [shape((nodes, latent), F32), shape((latent, side), BF)],
        600_000_000, 3 * MIB, 16,
    )(x_west, embed_t, weights_all, h_own)

    half_chunks = shape((4, 2, latent // 8, latent), BF)
    node_rows = shape((nodes, latent), BF)
    (
        sent_a, mesh_grad, gain_term, gathered, grad_aggregate, normed, grad_pre_up, update, slope_east
    ) = call(
        mesh_kernel, "mesh_nodes", [VMEM] * 10,
        [half_chunks, shape((nodes, latent), F32), shape((1, latent), F32)]
        + [node_rows] * 5
        + [shape((latent, side), BF)],
        2_000_000_000, 8 * MIB, 16, [pltpu.VMEM((2, latent // 2, latent), BF)],
    )(x_east, embed_t, weights_all, h_sum, message_w, up_w, gain.reshape(1, latent), mesh_lat, cot, grad_update)
    got_a = core_swapped(sent_a)
    kept_a, back, mesh_new, grad_out_term = call(
        tail_kernel, "mesh_tail", [VMEM] * 9,
        [half_chunks, shape((latent, nodes), BF), node_rows, shape((latent, latent), BF)],
        500_000_000, 3 * MIB, 16, [pltpu.VMEM((2, latent // 2, latent), BF)],
    )(gathered, grad_aggregate, normed, grad_pre_up, update, message_w, out_w, mesh_lat, cot)

    kept_a, back = lax.optimization_barrier((added(kept_a, got_a), back))
    padded = -(-(features + 1) // 128) * 128
    assert padded == latent
    x_parts = (x_own, x_west, x_east)
    stack = pltpu.VMEM((2, latent // 2, latent), F32)
    sent_b, grad_pre = call(
        grid_kernel, "grid_points", [VMEM] * 10, [half_chunks, shape((latent, points), BF)],
        1_600_000_000, 9 * MIB, 20, [stack],
    )(back, weights_all, slope_own, slope_west, slope_east, *x_parts, gain_term, grad_out_term)
    got_b = core_swapped(sent_b)
    (sums_b,) = call(
        grid_kept_kernel, "grid_kept", [VMEM] * 5, [shape((latent // 2, latent), F32)], 800_000_000, 6 * MIB, 16
    )(grad_pre, *x_parts, gain_term)
    kept_a, sums_b = lax.optimization_barrier((halved(kept_a), sums_b))
    (kept_b,) = call(
        kept_chunks_kernel, "kept_chunks", [VMEM] * 2, [half_chunks], 8_000_000_000, MIB, 16
    )(grad_out_term, sums_b)

    summed_a = all_summed(kept_a)
    summed_b = all_summed(halved(added(kept_b, got_b)))
    square = shape((latent, latent), F32)
    grad_message, grad_up = call(
        order_mesh_kernel, "order_a", [VMEM] * 6, [square, square], 0, 3 * MIB, 16
    )(*from_both_cores(summed_a))
    last, grad_message, grad_up = lax.optimization_barrier((summed_b[2], grad_message, grad_up))
    summed_b = (*summed_b[:2], last)
    rows_half = latent // 2
    behind = features - rows_half
    outs = [square, shape((features, latent), F32), shape((1, latent), F32)]

    def order_b(half, chunks, more, more_specs, aliases):
        block_of = pl.BlockSpec((rows_half, latent), lambda i: ((lax.axis_index("lat") & 1) ^ half, 0))
        return pl.pallas_call(
            lambda *refs: order_grid_kernel(half, behind, *refs),
            name="order_b",
            grid=(1,),
            in_specs=[VMEM] * 3 + more_specs,
            out_specs=[block_of, block_of, VMEM],
            out_shape=outs,
            input_output_aliases=aliases,
            compiler_params=pltpu.CompilerParams(vmem_limit_bytes=16 * MIB),
            cost_estimate=pl.CostEstimate(flops=0, bytes_accessed=2 * MIB, transcendentals=0),
        )(*chunks, *more)

    from_other = [core_swapped(chunk) for chunk in summed_b]
    held = order_b(0, summed_b, (), [], {})
    grad_out, grad_embed, grad_gain = order_b(
        1, from_other, (held[2], held[0], held[1]), [VMEM] + [pl.BlockSpec(memory_space=pl.ANY)] * 2, {4: 0, 5: 1}
    )
    return (mesh_new, mesh_grad, grad_embed, grad_message, grad_up, grad_out, grad_gain[0])


def solution(mesh):
    tiles = ("grp", "lon", "lat")
    return jax.shard_map(
        on_device,
        mesh=mesh,
        in_specs=(
            P(("grp", "lat"), "lon", None),
            P(tiles, None),
            P(tiles, None, None),
            P(tiles),
            P(tiles),
            P(tiles),
            P(),
            P(),
            P(),
            P(),
            P(),
            P(tiles, None),
        ),
        out_specs=(
            P(tiles, None),
            P(tiles, None),
            P("grp", None),
            P("grp", None),
            P("grp", None),
            P("grp", None),
            P("grp"),
        ),
        check_vma=False,
    )
```

```python
import jax
import jax.numpy as jnp
from jax import lax
from jax.experimental import pallas as pl
from jax.experimental.pallas import tpu as pltpu
from jax.sharding import PartitionSpec as P

epsilon = 1e-05
BF = jnp.bfloat16
F32 = jnp.float32
MIB = 1024 * 1024
SMEM = pl.BlockSpec(memory_space=pltpu.SMEM)
VMEM = pl.BlockSpec(memory_space=pltpu.VMEM)
shape = jax.ShapeDtypeStruct


def contract(a, b, dim_a, dim_b):
    return lax.dot_general(a, b, (((dim_a,), (dim_b,)), ((), ())), preferred_element_type=F32)


def silu_pair(pre):
    sigma = jax.nn.sigmoid(pre)
    return pre * sigma, sigma * (1.0 + pre * (1.0 - sigma))


def pack_kernel(from_high, grid, out, wide):
    features, rows, cols = grid.shape
    block = wide.shape[1]
    half = block // 2
    start = cols - block if from_high else 0
    wide[...] = grid[:, :, start : start + block].astype(F32).reshape(features * rows, block)
    lane = lax.broadcasted_iota(jnp.int32, (features, block), 1)
    for pair in range(rows // 2):
        even = wide[pl.ds(2 * pair, features, stride=rows), :]
        odd = wide[pl.ds(2 * pair + 1, features, stride=rows), :]
        if from_high:
            even = pltpu.roll(even, half, 1)
        else:
            odd = pltpu.roll(odd, half, 1)
        out[:, pair * block : (pair + 1) * block] = jnp.where(lane < half, even, odd).astype(BF)


def weights_kernel(rows, own_blocks, src, dst, count, edge_w, cot, out_w, weights_all, grad_update, acc):
    block = edge_w.shape[1]
    half = block // 2
    windows = 2 * own_blocks + 1
    west_base = rows * own_blocks
    east_base = west_base + rows // 2
    acc[...] = jnp.zeros(acc.shape, F32)
    lane = lax.broadcasted_iota(jnp.int32, (block, block), 1)

    def slot(b, carry):
        source = src[b]
        row = source // windows
        window = source - row * windows
        at = window // 2
        target = pl.ds(pl.multiple_of(dst[b] * block, block), block)
        weights = edge_w[b].astype(F32)

        @pl.when(window % 2 == 1)
        def _():
            acc[row * own_blocks + at, target, :] += weights

        @pl.when(window % 2 == 0)
        def _():
            turned = pltpu.roll(weights, half, 1)
            odd_row = row % 2 == 1
            first = jnp.where(at == 0, west_base + row // 2, row * own_blocks + at - 1)
            first_high = (at > 0) | odd_row
            second = jnp.where(at == own_blocks, east_base + row // 2, row * own_blocks + at)
            second_high = (at == own_blocks) & odd_row
            acc[first, target, :] += jnp.where(
                first_high, jnp.where(lane >= half, turned, 0.0), jnp.where(lane < half, weights, 0.0)
            )
            acc[second, target, :] += jnp.where(
                second_high, jnp.where(lane >= half, weights, 0.0), jnp.where(lane < half, turned, 0.0)
            )

        return carry

    lax.fori_loop(0, count[0], slot, 0)
    for k in range(acc.shape[0]):
        weights_all[:, k * block : (k + 1) * block] = acc[k].astype(BF)
    grad_update[...] = contract(cot[...], out_w[...], 1, 1)


def rows_kernel(grid, embed_w, x_t, embed_t, wide):
    features, rows, cols = grid.shape
    block = wide.shape[2]
    for k in range(cols // block):
        wide[k] = grid[:, :, k * block : (k + 1) * block].astype(F32).reshape(features * rows, block)
        for r in range(rows):
            x_t[:, r * cols + k * block : r * cols + (k + 1) * block] = wide[
                k, pl.ds(r, features, stride=rows), :
            ].astype(BF)
    embed_t[...] = embed_w[...].T


def own_kernel(x_t, embed_t, weights_all, h_own, slope):
    points = x_t.shape[1]
    tile = points // 8
    total = jnp.zeros(h_own.shape, F32)
    for r in range(8):
        at = slice(r * tile, (r + 1) * tile)
        hidden, hidden_slope = silu_pair(contract(embed_t[...], x_t[:, at], 1, 0))
        slope[:, at] = hidden_slope.astype(BF)
        total += contract(weights_all[:, at], hidden.astype(BF), 1, 1)
    h_own[...] = total


def halo_part(x, embed_t, weights, slope):
    hidden, hidden_slope = silu_pair(contract(embed_t[...], x[...], 1, 0))
    slope[...] = hidden_slope.astype(BF)
    return contract(weights, hidden.astype(BF), 1, 1)


def west_kernel(first, x, embed_t, weights_all, h_own, h_sum, slope):
    points = x.shape[1]
    h_sum[...] = h_own[...] + halo_part(x, embed_t, weights_all[:, first : first + points], slope)


def to_chunks(grads, stack, perm, start):
    count, matrices, size, _ = grads.shape
    for j in range(count):
        at = pl.ds(pl.multiple_of((perm[start + j] & (count - 1)) * size, size), size)
        for k in range(matrices):
            grads[j, k] = stack[k, at, :].astype(BF)


def from_chunks(outs, chunks, perm):
    j = 0
    for chunk in chunks:
        for n in range(chunk.shape[0]):
            size = chunk.shape[2]
            at = pl.ds(pl.multiple_of(perm[j] * size, size), size)
            for k, out in enumerate(outs):
                out[at, :] = chunk[n, k].astype(F32)
            j += 1


def rows_of_half(half, rows):
    return pl.ds(pl.multiple_of(half * rows, rows), rows)


def mesh_kernel(
    x, embed_t, weights_all, h_sum, message_w, up_w, gain, mesh_lat, cot, grad_update,
    sent, mesh_grad, grad_gain, gathered, grad_aggregate, normed, grad_pre_up, update, slope, stack,
):
    perm = chunk_order()
    points = x.shape[1]
    first = weights_all.shape[1] - points
    total = h_sum[...] + halo_part(x, embed_t, weights_all[:, first:], slope)
    gathered[...] = total.astype(BF)
    summed = mesh_lat[...].astype(F32) + contract(gathered[...], message_w[...], 1, 0)
    rinv = lax.rsqrt(jnp.mean(summed * summed, axis=1, keepdims=True) + epsilon)
    qhat = summed * rinv
    gains = gain[...]
    normed[...] = (qhat * gains).astype(BF)
    pre_up = contract(normed[...], up_w[...], 1, 0)
    silu_up, up_slope = silu_pair(pre_up)
    update[...] = silu_up.astype(BF)
    grad_pre_up[...] = (grad_update[...] * up_slope).astype(BF)
    grad_normed = contract(grad_pre_up[...], up_w[...], 1, 1)
    grad_gain[...] = jnp.sum(grad_normed * qhat, axis=0, keepdims=True)
    grad_qhat = grad_normed * gains
    grad_q = rinv * (grad_qhat - qhat * jnp.mean(grad_qhat * qhat, axis=1, keepdims=True))
    grad_aggregate[...] = grad_q.astype(BF)
    mesh_grad[...] = cot[...].astype(F32) + grad_q
    theirs = rows_of_half(1 - perm[0] // 4, stack.shape[1])
    stack[0] = contract(gathered[:, theirs], grad_aggregate[...], 0, 0).astype(BF)
    stack[1] = contract(normed[:, theirs], grad_pre_up[...], 0, 0).astype(BF)
    to_chunks(sent, stack, perm, 4)


def tail_kernel(
    gathered, grad_aggregate, normed, grad_pre_up, update, message_w, out_w, mesh_lat, cot,
    kept, back, mesh_new, grad_out, stack,
):
    perm = chunk_order()
    mine = rows_of_half(perm[0] // 4, stack.shape[1])
    stack[0] = contract(gathered[:, mine], grad_aggregate[...], 0, 0).astype(BF)
    stack[1] = contract(normed[:, mine], grad_pre_up[...], 0, 0).astype(BF)
    to_chunks(kept, stack, perm, 0)
    back[...] = contract(message_w[...], grad_aggregate[...], 1, 1).astype(BF)
    mesh_new[...] = (mesh_lat[...].astype(F32) + contract(update[...], out_w[...], 1, 0)).astype(BF)
    grad_out[...] = contract(update[...], cot[...], 0, 0).astype(BF)


def points_of(x_own, x_west, x_east):
    tile = x_west.shape[1]
    pieces = []
    for x in (x_own, x_west, x_east):
        pieces += [(x, slice(k * tile, (k + 1) * tile)) for k in range(x.shape[1] // tile)]
    return [(x, at, slice(n * tile, (n + 1) * tile)) for n, (x, at) in enumerate(pieces)]


def embed_rows(half, x_parts, grad_pre, grad_gain, out):
    rows = out.shape[0]
    features = x_parts[0].shape[0]
    for side in range(2):
        count = min(rows, features - side * rows)

        @pl.when(half == side)
        def _():
            sums = jnp.zeros((count, out.shape[1]), F32)
            for x, at, all_at in points_of(*x_parts):
                sums += contract(x[side * rows : side * rows + count, at], grad_pre[:, all_at], 1, 1)
            if count < rows:
                out[...] = jnp.zeros(out.shape, F32)
                out[count : count + 1, :] = grad_gain[...]
            out[:count, :] = sums


def grid_kernel(
    back, weights_all, slope_own, slope_west, slope_east, x_own, x_west, x_east, grad_gain, grad_out,
    sent, grad_pre, stack,
):
    perm = chunk_order()
    for slope, at, all_at in points_of(slope_own, slope_west, slope_east):
        hidden = contract(back[...], weights_all[:, all_at], 1, 0)
        grad_pre[:, all_at] = (hidden * slope[:, at].astype(F32)).astype(BF)
    half = 1 - perm[0] // 4
    stack[0] = grad_out[rows_of_half(half, stack.shape[1]), :].astype(F32)
    embed_rows(half, (x_own, x_west, x_east), grad_pre, grad_gain, stack.at[1])
    to_chunks(sent, stack, perm, 4)


def grid_kept_kernel(grad_pre, x_own, x_west, x_east, grad_gain, sums):
    perm = chunk_order()
    embed_rows(perm[0] // 4, (x_own, x_west, x_east), grad_pre, grad_gain, sums)


def kept_chunks_kernel(grad_out, sums, kept):
    perm = chunk_order()
    count, _, size, _ = kept.shape
    for j in range(count):
        kept[j, 0] = grad_out[pl.ds(pl.multiple_of(perm[j] * size, size), size), :]
        kept[j, 1] = sums[pl.ds(pl.multiple_of((perm[j] & (count - 1)) * size, size), size), :].astype(BF)


def order_mesh_kernel(*refs):
    from_chunks(refs[-2:], refs[:-2], chunk_order())


def order_grid_kernel(half, behind, *refs):
    perm = chunk_order()
    chunks, others, (grad_out, grad_embed, grad_gain) = refs[:3], refs[3:-3], refs[-3:]
    j = 4 * half
    for chunk in chunks:
        for n in range(chunk.shape[0]):
            size = chunk.shape[2]
            at = pl.ds(pl.multiple_of((perm[j] & 3) * size, size), size)
            grad_out[at, :] = chunk[n, 0].astype(F32)
            grad_embed[at, :] = chunk[n, 1].astype(F32)
            j += 1
    row = others[0][...] if others else jnp.zeros(grad_gain.shape, F32)
    grad_gain[...] = jnp.where(perm[4 * half] >= 4, grad_embed[behind : behind + 1, :], row)


def role_steps():
    lat = [("lat", 2 << k) for k in range(lax.axis_size("lat").bit_length() - 2)]
    lon = [("lon", 1 << k) for k in range(lax.axis_size("lon").bit_length() - 1)]
    rest = lat[1:] + lon[1:]
    return ([lat[0], lon[0]] + rest, [lon[0], lat[0]] + rest)


def core_swapped(value):
    return lax.ppermute(value, "lat", [(i, i ^ 1) for i in range(lax.axis_size("lat"))])


def swapped(value, step):
    lats = lax.axis_size("lat")
    pairs = []
    for lon in range(lax.axis_size("lon")):
        for lat in range(lats):
            axis, bit = role_steps()[lat & 1][step]
            other = (lon ^ bit) * lats + lat if axis == "lon" else lon * lats + (lat ^ bit)
            pairs.append((lon * lats + lat, other))
    return lax.ppermute(value, ("lon", "lat"), pairs)


def chunk_order():
    core = lax.axis_index("lat") & 1
    sides = []
    for steps in role_steps():
        low = [((lax.axis_index(axis) & bit) != 0).astype(jnp.int32) for axis, bit in steps[:2]]
        sides.append(2 * low[0] + low[1])
    mine = jnp.where(core == 0, sides[0], sides[1])
    theirs = jnp.where(core == 0, sides[1], sides[0])
    return [4 * core + (mine ^ j) for j in range(4)] + [4 - 4 * core + (theirs ^ j) for j in range(4)]


def added(a, b):
    return (a.astype(F32) + b.astype(F32)).astype(BF)


def halved(kept):
    return added(kept[:2], swapped(kept[2:], 0))


def quartered(kept):
    return added(kept[:1], swapped(kept[1:], 1))


def exchanged(mine):
    for step in range(2, len(role_steps()[0])):
        mine = added(mine, swapped(mine, step))
    return mine


def gathered_back(mine, second):
    return mine, second, swapped(jnp.concatenate([mine, second]), 0)


def from_both_cores(chunks):
    return (*chunks, *(core_swapped(chunk) for chunk in chunks))


def on_device(grid_in, mesh_lat, edge_w, edge_src, edge_dst, block_count, embed_w, message_w, up_w, out_w, gain, cot):
    rows, cols, features = grid_in.shape
    latent = message_w.shape[0]
    block = edge_w.shape[1]
    half = block // 2
    nodes = mesh_lat.shape[0]
    own = rows * cols
    side = rows * half
    points = own + 2 * side
    grid = jnp.transpose(grid_in, (2, 0, 1))

    def call(kernel, name, in_specs, out_shape, flops, bytes_accessed, limit, scratch_shapes=()):
        return pl.pallas_call(
            kernel,
            name=name,
            in_specs=in_specs,
            out_specs=[VMEM] * len(out_shape),
            out_shape=out_shape,
            scratch_shapes=list(scratch_shapes),
            compiler_params=pltpu.CompilerParams(vmem_limit_bytes=limit * MIB),
            cost_estimate=pl.CostEstimate(flops=flops, bytes_accessed=bytes_accessed, transcendentals=0),
        )

    strip = shape((features, side), BF)
    wide = pltpu.VMEM((features * rows, block), F32)
    count = lax.axis_size("lon")
    (to_east,) = call(lambda *refs: pack_kernel(True, *refs), "pack_east", [VMEM], [strip], 0, MIB, 8, [wide])(grid)
    x_west = lax.ppermute(to_east, "lon", [(i, (i + 1) % count) for i in range(count)])
    to_east, later = lax.optimization_barrier((to_east, grid))
    (to_west,) = call(lambda *refs: pack_kernel(False, *refs), "pack_west", [VMEM], [strip], 0, MIB, 8, [wide])(later)
    x_east = lax.ppermute(to_west, "lon", [((i + 1) % count, i) for i in range(count)])

    weights_all, grad_update = call(
        lambda *refs: weights_kernel(rows, cols // block, *refs), "slot_weights", [SMEM] * 3 + [VMEM] * 3,
        [shape((nodes, points), BF), shape((nodes, latent), F32)],
        200_000_000, 4 * MIB, 16, [pltpu.VMEM((points // block, nodes, block), F32)],
    )(edge_src, edge_dst, block_count, edge_w, cot, out_w)
    x_own, embed_t = call(
        rows_kernel, "own_rows", [VMEM] * 2, [shape((features, own), BF), shape((latent, features), BF)],
        1_000_000_000, 5 * MIB, 16, [pltpu.VMEM((cols // block, features * rows, block), F32)],
    )(later, embed_w)
    h_own, slope_own = call(
        own_kernel, "own_points", [VMEM] * 3, [shape((nodes, latent), F32), shape((latent, own), BF)],
        2_000_000_000, 7 * MIB, 16,
    )(x_own, embed_t, weights_all)

    h_sum, slope_west = call(
        lambda *refs: west_kernel(own, *refs), "west_points", [VMEM] * 4,
        [shape((nodes, latent), F32), shape((latent, side), BF)],
        600_000_000, 3 * MIB, 16,
    )(x_west, embed_t, weights_all, h_own)

    half_chunks = shape((4, 2, latent // 8, latent), BF)
    node_rows = shape((nodes, latent), BF)
    (
        sent_a, mesh_grad, gain_term, gathered, grad_aggregate, normed, grad_pre_up, update, slope_east
    ) = call(
        mesh_kernel, "mesh_nodes", [VMEM] * 10,
        [half_chunks, shape((nodes, latent), F32), shape((1, latent), F32)]
        + [node_rows] * 5
        + [shape((latent, side), BF)],
        2_000_000_000, 8 * MIB, 16, [pltpu.VMEM((2, latent // 2, latent), BF)],
    )(x_east, embed_t, weights_all, h_sum, message_w, up_w, gain.reshape(1, latent), mesh_lat, cot, grad_update)
    got_a = core_swapped(sent_a)
    kept_a, back, mesh_new, grad_out_term = call(
        tail_kernel, "mesh_tail", [VMEM] * 9,
        [half_chunks, shape((latent, nodes), BF), node_rows, shape((latent, latent), BF)],
        500_000_000, 3 * MIB, 16, [pltpu.VMEM((2, latent // 2, latent), BF)],
    )(gathered, grad_aggregate, normed, grad_pre_up, update, message_w, out_w, mesh_lat, cot)

    kept_a, back = lax.optimization_barrier((added(kept_a, got_a), back))
    padded = -(-(features + 1) // 128) * 128
    assert padded == latent
    x_parts = (x_own, x_west, x_east)
    stack = pltpu.VMEM((2, latent // 2, latent), F32)
    sent_b, grad_pre = call(
        grid_kernel, "grid_points", [VMEM] * 10, [half_chunks, shape((latent, points), BF)],
        1_600_000_000, 9 * MIB, 20, [stack],
    )(back, weights_all, slope_own, slope_west, slope_east, *x_parts, gain_term, grad_out_term)
    got_b = core_swapped(sent_b)
    (sums_b,) = call(
        grid_kept_kernel, "grid_kept", [VMEM] * 5, [shape((latent // 2, latent), F32)], 800_000_000, 6 * MIB, 16
    )(grad_pre, *x_parts, gain_term)
    kept_a, sums_b = lax.optimization_barrier((halved(kept_a), sums_b))
    (kept_b,) = call(
        kept_chunks_kernel, "kept_chunks", [VMEM] * 2, [half_chunks], 8_000_000_000, MIB, 16
    )(grad_out_term, sums_b)

    mine_a = exchanged(quartered(kept_a))
    mine_b = quartered(halved(added(kept_b, got_b)))
    mine_a, _ = lax.optimization_barrier((mine_a, mine_b))
    second_a = swapped(mine_a, 1)
    mine_b = exchanged(mine_b)
    second_a, _ = lax.optimization_barrier((second_a, mine_b))
    summed_a = gathered_back(mine_a, second_a)
    summed_b = gathered_back(mine_b, swapped(mine_b, 1))
    square = shape((latent, latent), F32)
    grad_message, grad_up = call(
        order_mesh_kernel, "order_a", [VMEM] * 6, [square, square], 0, 3 * MIB, 16
    )(*from_both_cores(summed_a))
    last, grad_message, grad_up = lax.optimization_barrier((summed_b[2], grad_message, grad_up))
    summed_b = (*summed_b[:2], last)
    rows_half = latent // 2
    behind = features - rows_half
    outs = [square, shape((features, latent), F32), shape((1, latent), F32)]

    def order_b(half, chunks, more, more_specs, aliases):
        block_of = pl.BlockSpec((rows_half, latent), lambda i: ((lax.axis_index("lat") & 1) ^ half, 0))
        return pl.pallas_call(
            lambda *refs: order_grid_kernel(half, behind, *refs),
            name="order_b",
            grid=(1,),
            in_specs=[VMEM] * 3 + more_specs,
            out_specs=[block_of, block_of, VMEM],
            out_shape=outs,
            input_output_aliases=aliases,
            compiler_params=pltpu.CompilerParams(vmem_limit_bytes=16 * MIB),
            cost_estimate=pl.CostEstimate(flops=0, bytes_accessed=2 * MIB, transcendentals=0),
        )(*chunks, *more)

    from_other = [core_swapped(chunk) for chunk in summed_b]
    held = order_b(0, summed_b, (), [], {})
    grad_out, grad_embed, grad_gain = order_b(
        1, from_other, (held[2], held[0], held[1]), [VMEM] + [pl.BlockSpec(memory_space=pl.ANY)] * 2, {4: 0, 5: 1}
    )
    return (mesh_new, mesh_grad, grad_embed, grad_message, grad_up, grad_out, grad_gain[0])


def solution(mesh):
    tiles = ("grp", "lon", "lat")
    return jax.shard_map(
        on_device,
        mesh=mesh,
        in_specs=(
            P(("grp", "lat"), "lon", None),
            P(tiles, None),
            P(tiles, None, None),
            P(tiles),
            P(tiles),
            P(tiles),
            P(),
            P(),
            P(),
            P(),
            P(),
            P(tiles, None),
        ),
        out_specs=(
            P(tiles, None),
            P(tiles, None),
            P("grp", None),
            P("grp", None),
            P("grp", None),
            P("grp", None),
            P("grp"),
        ),
        check_vma=False,
    )
```

```python
import jax
import jax.numpy as jnp
from jax import lax
from jax.experimental import pallas as pl
from jax.experimental.pallas import tpu as pltpu
from jax.sharding import PartitionSpec as P

epsilon = 1e-05
BF = jnp.bfloat16
F32 = jnp.float32
MIB = 1024 * 1024
SMEM = pl.BlockSpec(memory_space=pltpu.SMEM)
VMEM = pl.BlockSpec(memory_space=pltpu.VMEM)
shape = jax.ShapeDtypeStruct


def contract(a, b, dim_a, dim_b):
    return lax.dot_general(a, b, (((dim_a,), (dim_b,)), ((), ())), preferred_element_type=F32)


def silu_pair(pre):
    sigma = jax.nn.sigmoid(pre)
    return pre * sigma, sigma * (1.0 + pre * (1.0 - sigma))


def pack_kernel(from_high, grid, out, wide):
    features, rows, cols = grid.shape
    block = wide.shape[1]
    half = block // 2
    start = cols - block if from_high else 0
    wide[...] = grid[:, :, start : start + block].astype(F32).reshape(features * rows, block)
    lane = lax.broadcasted_iota(jnp.int32, (features, block), 1)
    for pair in range(rows // 2):
        even = wide[pl.ds(2 * pair, features, stride=rows), :]
        odd = wide[pl.ds(2 * pair + 1, features, stride=rows), :]
        if from_high:
            even = pltpu.roll(even, half, 1)
        else:
            odd = pltpu.roll(odd, half, 1)
        out[:, pair * block : (pair + 1) * block] = jnp.where(lane < half, even, odd).astype(BF)


def weights_kernel(rows, own_blocks, src, dst, count, edge_w, cot, out_w, weights_all, grad_update, acc):
    block = edge_w.shape[1]
    half = block // 2
    windows = 2 * own_blocks + 1
    west_base = rows * own_blocks
    east_base = west_base + rows // 2
    acc[...] = jnp.zeros(acc.shape, F32)
    lane = lax.broadcasted_iota(jnp.int32, (block, block), 1)

    def slot(b, carry):
        source = src[b]
        row = source // windows
        window = source - row * windows
        at = window // 2
        target = pl.ds(pl.multiple_of(dst[b] * block, block), block)
        weights = edge_w[b].astype(F32)

        @pl.when(window % 2 == 1)
        def _():
            acc[row * own_blocks + at, target, :] += weights

        @pl.when(window % 2 == 0)
        def _():
            turned = pltpu.roll(weights, half, 1)
            odd_row = row % 2 == 1
            first = jnp.where(at == 0, west_base + row // 2, row * own_blocks + at - 1)
            first_high = (at > 0) | odd_row
            second = jnp.where(at == own_blocks, east_base + row // 2, row * own_blocks + at)
            second_high = (at == own_blocks) & odd_row
            acc[first, target, :] += jnp.where(
                first_high, jnp.where(lane >= half, turned, 0.0), jnp.where(lane < half, weights, 0.0)
            )
            acc[second, target, :] += jnp.where(
                second_high, jnp.where(lane >= half, weights, 0.0), jnp.where(lane < half, turned, 0.0)
            )

        return carry

    lax.fori_loop(0, count[0], slot, 0)
    for k in range(acc.shape[0]):
        weights_all[:, k * block : (k + 1) * block] = acc[k].astype(BF)
    grad_update[...] = contract(cot[...], out_w[...], 1, 1)


def rows_kernel(grid, embed_w, x_t, embed_t, wide):
    features, rows, cols = grid.shape
    block = wide.shape[2]
    for k in range(cols // block):
        wide[k] = grid[:, :, k * block : (k + 1) * block].astype(F32).reshape(features * rows, block)
        for r in range(rows):
            x_t[:, r * cols + k * block : r * cols + (k + 1) * block] = wide[
                k, pl.ds(r, features, stride=rows), :
            ].astype(BF)
    embed_t[...] = embed_w[...].T


def own_kernel(x_t, embed_t, weights_all, h_own, slope):
    points = x_t.shape[1]
    tile = points // 8
    total = jnp.zeros(h_own.shape, F32)
    for r in range(8):
        at = slice(r * tile, (r + 1) * tile)
        hidden, hidden_slope = silu_pair(contract(embed_t[...], x_t[:, at], 1, 0))
        slope[:, at] = hidden_slope.astype(BF)
        total += contract(weights_all[:, at], hidden.astype(BF), 1, 1)
    h_own[...] = total


def halo_part(x, embed_t, weights, slope):
    hidden, hidden_slope = silu_pair(contract(embed_t[...], x[...], 1, 0))
    slope[...] = hidden_slope.astype(BF)
    return contract(weights, hidden.astype(BF), 1, 1)


def west_kernel(first, x, embed_t, weights_all, h_own, h_sum, slope):
    points = x.shape[1]
    h_sum[...] = h_own[...] + halo_part(x, embed_t, weights_all[:, first : first + points], slope)


def to_chunks(grads, stack, perm, start):
    count, matrices, size, _ = grads.shape
    for j in range(count):
        at = pl.ds(pl.multiple_of((perm[start + j] & 3) * size, size), size)
        for k in range(matrices):
            grads[j, k] = stack[k, at, :].astype(BF)


def from_chunks(outs, chunks, perm):
    j = 0
    for chunk in chunks:
        for n in range(chunk.shape[0]):
            size = chunk.shape[2]
            at = pl.ds(pl.multiple_of(perm[j] * size, size), size)
            for k, out in enumerate(outs):
                out[at, :] = chunk[n, k].astype(F32)
            j += 1


def rows_of_half(half, rows):
    return pl.ds(pl.multiple_of(half * rows, rows), rows)


def mesh_kernel(
    x, embed_t, weights_all, h_sum, message_w, up_w, gain, mesh_lat, cot, grad_update,
    sent_high, sent_low, mesh_grad, grad_gain, gathered, grad_aggregate, normed, grad_pre_up, update, slope, stack,
):
    perm = chunk_order()
    points = x.shape[1]
    first = weights_all.shape[1] - points
    total = h_sum[...] + halo_part(x, embed_t, weights_all[:, first:], slope)
    gathered[...] = total.astype(BF)
    summed = mesh_lat[...].astype(F32) + contract(gathered[...], message_w[...], 1, 0)
    rinv = lax.rsqrt(jnp.mean(summed * summed, axis=1, keepdims=True) + epsilon)
    qhat = summed * rinv
    gains = gain[...]
    normed[...] = (qhat * gains).astype(BF)
    pre_up = contract(normed[...], up_w[...], 1, 0)
    silu_up, up_slope = silu_pair(pre_up)
    update[...] = silu_up.astype(BF)
    grad_pre_up[...] = (grad_update[...] * up_slope).astype(BF)
    grad_normed = contract(grad_pre_up[...], up_w[...], 1, 1)
    grad_gain[...] = jnp.sum(grad_normed * qhat, axis=0, keepdims=True)
    grad_qhat = grad_normed * gains
    grad_q = rinv * (grad_qhat - qhat * jnp.mean(grad_qhat * qhat, axis=1, keepdims=True))
    grad_aggregate[...] = grad_q.astype(BF)
    mesh_grad[...] = cot[...].astype(F32) + grad_q
    theirs = rows_of_half(1 - perm[0] // 4, stack.shape[1])
    stack[0] = contract(gathered[:, theirs], grad_aggregate[...], 0, 0).astype(BF)
    stack[1] = contract(normed[:, theirs], grad_pre_up[...], 0, 0).astype(BF)
    to_chunks(sent_high, stack, perm, 6)
    to_chunks(sent_low, stack, perm, 4)


def tail_kernel(gathered, grad_aggregate, normed, grad_pre_up, message_w, kept_high, kept_low, back, stack):
    perm = chunk_order()
    mine = rows_of_half(perm[0] // 4, stack.shape[1])
    stack[0] = contract(gathered[:, mine], grad_aggregate[...], 0, 0).astype(BF)
    stack[1] = contract(normed[:, mine], grad_pre_up[...], 0, 0).astype(BF)
    to_chunks(kept_high, stack, perm, 2)
    to_chunks(kept_low, stack, perm, 0)
    back[...] = contract(message_w[...], grad_aggregate[...], 1, 1).astype(BF)


def points_of(x_own, x_west, x_east):
    tile = x_west.shape[1]
    pieces = []
    for x in (x_own, x_west, x_east):
        pieces += [(x, slice(k * tile, (k + 1) * tile)) for k in range(x.shape[1] // tile)]
    return [(x, at, slice(n * tile, (n + 1) * tile)) for n, (x, at) in enumerate(pieces)]


def embed_rows(half, x_parts, grad_pre, grad_gain, out):
    rows = out.shape[0]
    features = x_parts[0].shape[0]
    for side in range(2):
        count = min(rows, features - side * rows)

        @pl.when(half == side)
        def _():
            sums = jnp.zeros((count, out.shape[1]), F32)
            for x, at, all_at in points_of(*x_parts):
                sums += contract(x[side * rows : side * rows + count, at], grad_pre[:, all_at], 1, 1)
            if count < rows:
                out[...] = jnp.zeros(out.shape, F32)
                out[count : count + 1, :] = grad_gain[...]
            out[:count, :] = sums


def grid_kernel(
    back, weights_all, slope_own, slope_west, slope_east, x_own, x_west, x_east, grad_gain, update, out_w, mesh_lat, cot,
    sent_high, sent_low, grad_pre, grad_out, mesh_new, stack,
):
    perm = chunk_order()
    for slope, at, all_at in points_of(slope_own, slope_west, slope_east):
        hidden = contract(back[...], weights_all[:, all_at], 1, 0)
        grad_pre[:, all_at] = (hidden * slope[:, at].astype(F32)).astype(BF)
    grad_out[...] = contract(update[...], cot[...], 0, 0).astype(BF)
    half = 1 - perm[0] // 4
    stack[0] = grad_out[rows_of_half(half, stack.shape[1]), :].astype(F32)
    embed_rows(half, (x_own, x_west, x_east), grad_pre, grad_gain, stack.at[1])
    to_chunks(sent_high, stack, perm, 6)
    to_chunks(sent_low, stack, perm, 4)
    mesh_new[...] = (mesh_lat[...].astype(F32) + contract(update[...], out_w[...], 1, 0)).astype(BF)


def grid_kept_kernel(grad_pre, x_own, x_west, x_east, grad_gain, sums):
    perm = chunk_order()
    embed_rows(perm[0] // 4, (x_own, x_west, x_east), grad_pre, grad_gain, sums)


def kept_chunks_kernel(grad_out, sums, kept_high, kept_low):
    perm = chunk_order()
    for kept, start in ((kept_high, 2), (kept_low, 0)):
        count, _, size, _ = kept.shape
        for j in range(count):
            chunk = perm[start + j]
            kept[j, 0] = grad_out[pl.ds(pl.multiple_of(chunk * size, size), size), :]
            kept[j, 1] = sums[pl.ds(pl.multiple_of((chunk & 3) * size, size), size), :].astype(BF)


def order_mesh_kernel(*refs):
    from_chunks(refs[-2:], refs[:-2], chunk_order())


def order_grid_kernel(half, behind, *refs):
    perm = chunk_order()
    chunks, others, (grad_out, grad_embed, grad_gain) = refs[:3], refs[3:-3], refs[-3:]
    j = 4 * half
    for chunk in chunks:
        for n in range(chunk.shape[0]):
            size = chunk.shape[2]
            at = pl.ds(pl.multiple_of((perm[j] & 3) * size, size), size)
            grad_out[at, :] = chunk[n, 0].astype(F32)
            grad_embed[at, :] = chunk[n, 1].astype(F32)
            j += 1
    row = others[0][...] if others else jnp.zeros(grad_gain.shape, F32)
    grad_gain[...] = jnp.where(perm[4 * half] >= 4, grad_embed[behind : behind + 1, :], row)


def role_steps():
    lat = [("lat", 2 << k) for k in range(lax.axis_size("lat").bit_length() - 2)]
    lon = [("lon", 1 << k) for k in range(lax.axis_size("lon").bit_length() - 1)]
    rest = lat[1:] + lon[1:]
    return ([lat[0], lon[0]] + rest, [lon[0], lat[0]] + rest)


def core_swapped(value):
    return lax.ppermute(value, "lat", [(i, i ^ 1) for i in range(lax.axis_size("lat"))])


def swapped(value, step):
    lats = lax.axis_size("lat")
    pairs = []
    for lon in range(lax.axis_size("lon")):
        for lat in range(lats):
            axis, bit = role_steps()[lat & 1][step]
            other = (lon ^ bit) * lats + lat if axis == "lon" else lon * lats + (lat ^ bit)
            pairs.append((lon * lats + lat, other))
    return lax.ppermute(value, ("lon", "lat"), pairs)


def chunk_order():
    core = lax.axis_index("lat") & 1
    sides = []
    for steps in role_steps():
        low = [((lax.axis_index(axis) & bit) != 0).astype(jnp.int32) for axis, bit in steps[:2]]
        sides.append(2 * low[0] + low[1])
    mine = jnp.where(core == 0, sides[0], sides[1])
    theirs = jnp.where(core == 0, sides[1], sides[0])
    return [4 * core + (mine ^ j) for j in range(4)] + [4 - 4 * core + (theirs ^ j) for j in range(4)]


def added(a, b):
    return (a.astype(F32) + b.astype(F32)).astype(BF)


def halved(high, low):
    return added(low, swapped(high, 0))


def all_summed(kept):
    mine = added(kept[:1], swapped(kept[1:], 1))
    for step in range(2, len(role_steps()[0])):
        mine = added(mine, swapped(mine, step))
    second = swapped(mine, 1)
    return mine, second, swapped(jnp.concatenate([mine, second]), 0)


def from_both_cores(chunks):
    return (*chunks, *(core_swapped(chunk) for chunk in chunks))


def on_device(grid_in, mesh_lat, edge_w, edge_src, edge_dst, block_count, embed_w, message_w, up_w, out_w, gain, cot):
    rows, cols, features = grid_in.shape
    latent = message_w.shape[0]
    block = edge_w.shape[1]
    half = block // 2
    nodes = mesh_lat.shape[0]
    own = rows * cols
    side = rows * half
    points = own + 2 * side
    grid = jnp.transpose(grid_in, (2, 0, 1))

    def call(kernel, name, in_specs, out_shape, flops, bytes_accessed, limit, scratch_shapes=()):
        return pl.pallas_call(
            kernel,
            name=name,
            in_specs=in_specs,
            out_specs=[VMEM] * len(out_shape),
            out_shape=out_shape,
            scratch_shapes=list(scratch_shapes),
            compiler_params=pltpu.CompilerParams(vmem_limit_bytes=limit * MIB),
            cost_estimate=pl.CostEstimate(flops=flops, bytes_accessed=bytes_accessed, transcendentals=0),
        )

    strip = shape((features, side), BF)
    wide = pltpu.VMEM((features * rows, block), F32)
    count = lax.axis_size("lon")
    (to_east,) = call(lambda *refs: pack_kernel(True, *refs), "pack_east", [VMEM], [strip], 0, MIB, 8, [wide])(grid)
    x_west = lax.ppermute(to_east, "lon", [(i, (i + 1) % count) for i in range(count)])
    to_east, later = lax.optimization_barrier((to_east, grid))
    (to_west,) = call(lambda *refs: pack_kernel(False, *refs), "pack_west", [VMEM], [strip], 0, MIB, 8, [wide])(later)
    x_east = lax.ppermute(to_west, "lon", [((i + 1) % count, i) for i in range(count)])

    weights_all, grad_update = call(
        lambda *refs: weights_kernel(rows, cols // block, *refs), "slot_weights", [SMEM] * 3 + [VMEM] * 3,
        [shape((nodes, points), BF), shape((nodes, latent), F32)],
        200_000_000, 4 * MIB, 16, [pltpu.VMEM((points // block, nodes, block), F32)],
    )(edge_src, edge_dst, block_count, edge_w, cot, out_w)
    x_own, embed_t = call(
        rows_kernel, "own_rows", [VMEM] * 2, [shape((features, own), BF), shape((latent, features), BF)],
        1_000_000_000, 5 * MIB, 16, [pltpu.VMEM((cols // block, features * rows, block), F32)],
    )(later, embed_w)
    h_own, slope_own = call(
        own_kernel, "own_points", [VMEM] * 3, [shape((nodes, latent), F32), shape((latent, own), BF)],
        2_000_000_000, 7 * MIB, 16,
    )(x_own, embed_t, weights_all)

    h_sum, slope_west = call(
        lambda *refs: west_kernel(own, *refs), "west_points", [VMEM] * 4,
        [shape((nodes, latent), F32), shape((latent, side), BF)],
        600_000_000, 3 * MIB, 16,
    )(x_west, embed_t, weights_all, h_own)

    quarter = shape((2, 2, latent // 8, latent), BF)
    node_rows = shape((nodes, latent), BF)
    (
        sent_high, sent_low, mesh_grad, gain_term, gathered, grad_aggregate, normed, grad_pre_up, update, slope_east
    ) = call(
        mesh_kernel, "mesh_nodes", [VMEM] * 10,
        [quarter, quarter, shape((nodes, latent), F32), shape((1, latent), F32)]
        + [node_rows] * 5
        + [shape((latent, side), BF)],
        2_000_000_000, 8 * MIB, 16, [pltpu.VMEM((2, latent // 2, latent), BF)],
    )(x_east, embed_t, weights_all, h_sum, message_w, up_w, gain.reshape(1, latent), mesh_lat, cot, grad_update)
    got_high, got_low = core_swapped(sent_high), core_swapped(sent_low)
    kept_high, kept_low, back = call(
        tail_kernel, "mesh_tail", [VMEM] * 5, [quarter, quarter, shape((latent, nodes), BF)],
        500_000_000, 3 * MIB, 16, [pltpu.VMEM((2, latent // 2, latent), BF)],
    )(gathered, grad_aggregate, normed, grad_pre_up, message_w)

    high_a, back = lax.optimization_barrier((added(kept_high, got_high), back))
    low_a = added(kept_low, got_low)
    padded = -(-(features + 1) // 128) * 128
    assert padded == latent
    x_parts = (x_own, x_west, x_east)
    sent_high, sent_low, grad_pre, grad_out_term, mesh_new = call(
        grid_kernel, "grid_points", [VMEM] * 13,
        [quarter, quarter, shape((latent, points), BF), shape((latent, latent), BF), node_rows],
        1_600_000_000, 9 * MIB, 20, [pltpu.VMEM((2, latent // 2, latent), F32)],
    )(
        back, weights_all, slope_own, slope_west, slope_east, *x_parts, gain_term, update, out_w, mesh_lat, cot
    )
    got_high, got_low = core_swapped(sent_high), core_swapped(sent_low)
    (sums_b,) = call(
        grid_kept_kernel, "grid_kept", [VMEM] * 5, [shape((latent // 2, latent), F32)], 800_000_000, 6 * MIB, 16
    )(grad_pre, *x_parts, gain_term)
    kept_a, sums_b = lax.optimization_barrier((halved(high_a, low_a), sums_b))
    kept_high, kept_low = call(
        kept_chunks_kernel, "kept_chunks", [VMEM] * 2, [quarter, quarter], 8_000_000_000, MIB, 16
    )(grad_out_term, sums_b)

    summed_a = all_summed(kept_a)
    summed_b = all_summed(halved(added(kept_high, got_high), added(kept_low, got_low)))
    square = shape((latent, latent), F32)
    grad_message, grad_up = call(
        order_mesh_kernel, "order_a", [VMEM] * 6, [square, square], 0, 3 * MIB, 16
    )(*from_both_cores(summed_a))
    last, grad_message, grad_up = lax.optimization_barrier((summed_b[2], grad_message, grad_up))
    summed_b = (*summed_b[:2], last)
    rows_half = latent // 2
    behind = features - rows_half
    outs = [square, shape((features, latent), F32), shape((1, latent), F32)]

    def order_b(half, chunks, more, more_specs, aliases):
        block_of = pl.BlockSpec((rows_half, latent), lambda i: ((lax.axis_index("lat") & 1) ^ half, 0))
        return pl.pallas_call(
            lambda *refs: order_grid_kernel(half, behind, *refs),
            name="order_b",
            grid=(1,),
            in_specs=[VMEM] * 3 + more_specs,
            out_specs=[block_of, block_of, VMEM],
            out_shape=outs,
            input_output_aliases=aliases,
            compiler_params=pltpu.CompilerParams(vmem_limit_bytes=16 * MIB),
            cost_estimate=pl.CostEstimate(flops=0, bytes_accessed=2 * MIB, transcendentals=0),
        )(*chunks, *more)

    from_other = [core_swapped(chunk) for chunk in summed_b]
    held = order_b(0, summed_b, (), [], {})
    grad_out, grad_embed, grad_gain = order_b(
        1, from_other, (held[2], held[0], held[1]), [VMEM] + [pl.BlockSpec(memory_space=pl.ANY)] * 2, {4: 0, 5: 1}
    )
    return (mesh_new, mesh_grad, grad_embed, grad_message, grad_up, grad_out, grad_gain[0])


def solution(mesh):
    tiles = ("grp", "lon", "lat")
    return jax.shard_map(
        on_device,
        mesh=mesh,
        in_specs=(
            P(("grp", "lat"), "lon", None),
            P(tiles, None),
            P(tiles, None, None),
            P(tiles),
            P(tiles),
            P(tiles),
            P(),
            P(),
            P(),
            P(),
            P(),
            P(tiles, None),
        ),
        out_specs=(
            P(tiles, None),
            P(tiles, None),
            P("grp", None),
            P("grp", None),
            P("grp", None),
            P("grp", None),
            P("grp"),
        ),
        check_vma=False,
    )
```

```python
import jax
import jax.numpy as jnp
from jax import lax
from jax.experimental import pallas as pl
from jax.experimental.pallas import tpu as pltpu
from jax.sharding import PartitionSpec as P

epsilon = 1e-05
BF = jnp.bfloat16
F32 = jnp.float32
MIB = 1024 * 1024
SMEM = pl.BlockSpec(memory_space=pltpu.SMEM)
VMEM = pl.BlockSpec(memory_space=pltpu.VMEM)
shape = jax.ShapeDtypeStruct


def contract(a, b, dim_a, dim_b):
    return lax.dot_general(a, b, (((dim_a,), (dim_b,)), ((), ())), preferred_element_type=F32)


def silu_pair(pre):
    sigma = jax.nn.sigmoid(pre)
    return pre * sigma, sigma * (1.0 + pre * (1.0 - sigma))


def pack_kernel(from_high, grid, out, wide):
    features, rows, cols = grid.shape
    block = wide.shape[1]
    half = block // 2
    start = cols - block if from_high else 0
    wide[...] = grid[:, :, start : start + block].astype(F32).reshape(features * rows, block)
    lane = lax.broadcasted_iota(jnp.int32, (features, block), 1)
    for pair in range(rows // 2):
        even = wide[pl.ds(2 * pair, features, stride=rows), :]
        odd = wide[pl.ds(2 * pair + 1, features, stride=rows), :]
        if from_high:
            even = pltpu.roll(even, half, 1)
        else:
            odd = pltpu.roll(odd, half, 1)
        out[:, pair * block : (pair + 1) * block] = jnp.where(lane < half, even, odd).astype(BF)


def weights_kernel(rows, own_blocks, src, dst, count, edge_w, cot, out_w, weights_all, grad_update, acc):
    block = edge_w.shape[1]
    half = block // 2
    windows = 2 * own_blocks + 1
    west_base = rows * own_blocks
    east_base = west_base + rows // 2
    acc[...] = jnp.zeros(acc.shape, F32)
    lane = lax.broadcasted_iota(jnp.int32, (block, block), 1)

    def slot(b, carry):
        source = src[b]
        row = source // windows
        window = source - row * windows
        at = window // 2
        target = pl.ds(pl.multiple_of(dst[b] * block, block), block)
        weights = edge_w[b].astype(F32)

        @pl.when(window % 2 == 1)
        def _():
            acc[row * own_blocks + at, target, :] += weights

        @pl.when(window % 2 == 0)
        def _():
            turned = pltpu.roll(weights, half, 1)
            odd_row = row % 2 == 1
            first = jnp.where(at == 0, west_base + row // 2, row * own_blocks + at - 1)
            first_high = (at > 0) | odd_row
            second = jnp.where(at == own_blocks, east_base + row // 2, row * own_blocks + at)
            second_high = (at == own_blocks) & odd_row
            acc[first, target, :] += jnp.where(
                first_high, jnp.where(lane >= half, turned, 0.0), jnp.where(lane < half, weights, 0.0)
            )
            acc[second, target, :] += jnp.where(
                second_high, jnp.where(lane >= half, weights, 0.0), jnp.where(lane < half, turned, 0.0)
            )

        return carry

    lax.fori_loop(0, count[0], slot, 0)
    for k in range(acc.shape[0]):
        weights_all[:, k * block : (k + 1) * block] = acc[k].astype(BF)
    grad_update[...] = contract(cot[...], out_w[...], 1, 1)


def rows_kernel(grid, embed_w, x_t, embed_t, wide):
    features, rows, cols = grid.shape
    block = wide.shape[2]
    for k in range(cols // block):
        wide[k] = grid[:, :, k * block : (k + 1) * block].astype(F32).reshape(features * rows, block)
        for r in range(rows):
            x_t[:, r * cols + k * block : r * cols + (k + 1) * block] = wide[
                k, pl.ds(r, features, stride=rows), :
            ].astype(BF)
    embed_t[...] = embed_w[...].T


def own_kernel(x_t, embed_t, weights_all, h_own, slope):
    points = x_t.shape[1]
    tile = points // 8
    total = jnp.zeros(h_own.shape, F32)
    for r in range(8):
        at = slice(r * tile, (r + 1) * tile)
        hidden, hidden_slope = silu_pair(contract(embed_t[...], x_t[:, at], 1, 0))
        slope[:, at] = hidden_slope.astype(BF)
        total += contract(weights_all[:, at], hidden.astype(BF), 1, 1)
    h_own[...] = total


def halo_part(x, embed_t, weights, slope):
    hidden, hidden_slope = silu_pair(contract(embed_t[...], x[...], 1, 0))
    slope[...] = hidden_slope.astype(BF)
    return contract(weights, hidden.astype(BF), 1, 1)


def west_kernel(first, x, embed_t, weights_all, h_own, h_sum, slope):
    points = x.shape[1]
    h_sum[...] = h_own[...] + halo_part(x, embed_t, weights_all[:, first : first + points], slope)


def to_chunks(grads, stack, perm, start):
    count, matrices, size, _ = grads.shape
    for j in range(count):
        at = pl.ds(pl.multiple_of((perm[start + j] & 3) * size, size), size)
        for k in range(matrices):
            grads[j, k] = stack[k, at, :].astype(BF)


def from_chunks(outs, chunks, perm):
    j = 0
    for chunk in chunks:
        for n in range(chunk.shape[0]):
            size = chunk.shape[2]
            at = pl.ds(pl.multiple_of(perm[j] * size, size), size)
            for k, out in enumerate(outs):
                out[at, :] = chunk[n, k].astype(F32)
            j += 1


def rows_of_half(half, rows):
    return pl.ds(pl.multiple_of(half * rows, rows), rows)


def mesh_kernel(
    x, embed_t, weights_all, h_sum, message_w, up_w, gain, mesh_lat, grad_update,
    sent_high, sent_low, grad_mesh, grad_gain, gathered, grad_aggregate, normed, grad_pre_up, update, slope, stack,
):
    perm = chunk_order()
    points = x.shape[1]
    first = weights_all.shape[1] - points
    total = h_sum[...] + halo_part(x, embed_t, weights_all[:, first:], slope)
    gathered[...] = total.astype(BF)
    summed = mesh_lat[...].astype(F32) + contract(gathered[...], message_w[...], 1, 0)
    rinv = lax.rsqrt(jnp.mean(summed * summed, axis=1, keepdims=True) + epsilon)
    qhat = summed * rinv
    gains = gain[...]
    normed[...] = (qhat * gains).astype(BF)
    pre_up = contract(normed[...], up_w[...], 1, 0)
    silu_up, up_slope = silu_pair(pre_up)
    update[...] = silu_up.astype(BF)
    grad_pre_up[...] = (grad_update[...] * up_slope).astype(BF)
    grad_normed = contract(grad_pre_up[...], up_w[...], 1, 1)
    grad_gain[...] = jnp.sum(grad_normed * qhat, axis=0, keepdims=True)
    grad_qhat = grad_normed * gains
    grad_q = rinv * (grad_qhat - qhat * jnp.mean(grad_qhat * qhat, axis=1, keepdims=True))
    grad_aggregate[...] = grad_q.astype(BF)
    grad_mesh[...] = grad_q
    theirs = rows_of_half(1 - perm[0] // 4, stack.shape[1])
    stack[0] = contract(gathered[:, theirs], grad_aggregate[...], 0, 0).astype(BF)
    stack[1] = contract(normed[:, theirs], grad_pre_up[...], 0, 0).astype(BF)
    to_chunks(sent_high, stack, perm, 6)
    to_chunks(sent_low, stack, perm, 4)


def tail_kernel(gathered, grad_aggregate, normed, grad_pre_up, message_w, kept_high, kept_low, back, stack):
    perm = chunk_order()
    mine = rows_of_half(perm[0] // 4, stack.shape[1])
    stack[0] = contract(gathered[:, mine], grad_aggregate[...], 0, 0).astype(BF)
    stack[1] = contract(normed[:, mine], grad_pre_up[...], 0, 0).astype(BF)
    to_chunks(kept_high, stack, perm, 2)
    to_chunks(kept_low, stack, perm, 0)
    back[...] = contract(message_w[...], grad_aggregate[...], 1, 1).astype(BF)


def points_of(x_own, x_west, x_east):
    tile = x_west.shape[1]
    pieces = []
    for x in (x_own, x_west, x_east):
        pieces += [(x, slice(k * tile, (k + 1) * tile)) for k in range(x.shape[1] // tile)]
    return [(x, at, slice(n * tile, (n + 1) * tile)) for n, (x, at) in enumerate(pieces)]


def embed_rows(half, x_parts, grad_pre, grad_gain, out):
    rows = out.shape[0]
    features = x_parts[0].shape[0]
    for side in range(2):
        count = min(rows, features - side * rows)

        @pl.when(half == side)
        def _():
            sums = jnp.zeros((count, out.shape[1]), F32)
            for x, at, all_at in points_of(*x_parts):
                sums += contract(x[side * rows : side * rows + count, at], grad_pre[:, all_at], 1, 1)
            if count < rows:
                out[...] = jnp.zeros(out.shape, F32)
                out[count : count + 1, :] = grad_gain[...]
            out[:count, :] = sums


def grid_kernel(
    back, weights_all, slope_own, slope_west, slope_east, x_own, x_west, x_east, grad_gain, update, cot,
    sent_high, sent_low, grad_pre, grad_out, stack,
):
    perm = chunk_order()
    for slope, at, all_at in points_of(slope_own, slope_west, slope_east):
        hidden = contract(back[...], weights_all[:, all_at], 1, 0)
        grad_pre[:, all_at] = (hidden * slope[:, at].astype(F32)).astype(BF)
    grad_out[...] = contract(update[...], cot[...], 0, 0).astype(BF)
    half = 1 - perm[0] // 4
    stack[0] = grad_out[rows_of_half(half, stack.shape[1]), :].astype(F32)
    embed_rows(half, (x_own, x_west, x_east), grad_pre, grad_gain, stack.at[1])
    to_chunks(sent_high, stack, perm, 6)
    to_chunks(sent_low, stack, perm, 4)


def nodes_kernel(update, out_w, mesh_lat, cot, grad_mesh, mesh_new, mesh_grad):
    mesh_new[...] = (mesh_lat[...].astype(F32) + contract(update[...], out_w[...], 1, 0)).astype(BF)
    mesh_grad[...] = cot[...].astype(F32) + grad_mesh[...]


def grid_kept_kernel(grad_pre, x_own, x_west, x_east, grad_gain, sums):
    perm = chunk_order()
    embed_rows(perm[0] // 4, (x_own, x_west, x_east), grad_pre, grad_gain, sums)


def kept_chunks_kernel(grad_out, sums, kept_high, kept_low):
    perm = chunk_order()
    for kept, start in ((kept_high, 2), (kept_low, 0)):
        count, _, size, _ = kept.shape
        for j in range(count):
            chunk = perm[start + j]
            kept[j, 0] = grad_out[pl.ds(pl.multiple_of(chunk * size, size), size), :]
            kept[j, 1] = sums[pl.ds(pl.multiple_of((chunk & 3) * size, size), size), :].astype(BF)


def order_mesh_kernel(*refs):
    from_chunks(refs[-2:], refs[:-2], chunk_order())


def order_grid_kernel(half, behind, *refs):
    perm = chunk_order()
    chunks, others, (grad_out, grad_embed, grad_gain) = refs[:3], refs[3:-3], refs[-3:]
    j = 4 * half
    for chunk in chunks:
        for n in range(chunk.shape[0]):
            size = chunk.shape[2]
            at = pl.ds(pl.multiple_of((perm[j] & 3) * size, size), size)
            grad_out[at, :] = chunk[n, 0].astype(F32)
            grad_embed[at, :] = chunk[n, 1].astype(F32)
            j += 1
    row = others[0][...] if others else jnp.zeros(grad_gain.shape, F32)
    grad_gain[...] = jnp.where(perm[4 * half] >= 4, grad_embed[behind : behind + 1, :], row)


def role_steps():
    lat = [("lat", 2 << k) for k in range(lax.axis_size("lat").bit_length() - 2)]
    lon = [("lon", 1 << k) for k in range(lax.axis_size("lon").bit_length() - 1)]
    rest = lat[1:] + lon[1:]
    return ([lat[0], lon[0]] + rest, [lon[0], lat[0]] + rest)


def core_swapped(value):
    return lax.ppermute(value, "lat", [(i, i ^ 1) for i in range(lax.axis_size("lat"))])


def swapped(value, step):
    lats = lax.axis_size("lat")
    pairs = []
    for lon in range(lax.axis_size("lon")):
        for lat in range(lats):
            axis, bit = role_steps()[lat & 1][step]
            other = (lon ^ bit) * lats + lat if axis == "lon" else lon * lats + (lat ^ bit)
            pairs.append((lon * lats + lat, other))
    return lax.ppermute(value, ("lon", "lat"), pairs)


def chunk_order():
    core = lax.axis_index("lat") & 1
    sides = []
    for steps in role_steps():
        low = [((lax.axis_index(axis) & bit) != 0).astype(jnp.int32) for axis, bit in steps[:2]]
        sides.append(2 * low[0] + low[1])
    mine = jnp.where(core == 0, sides[0], sides[1])
    theirs = jnp.where(core == 0, sides[1], sides[0])
    return [4 * core + (mine ^ j) for j in range(4)] + [4 - 4 * core + (theirs ^ j) for j in range(4)]


def added(a, b):
    return (a.astype(F32) + b.astype(F32)).astype(BF)


def halved(high, low):
    return added(low, swapped(high, 0))


def all_summed(kept):
    mine = added(kept[:1], swapped(kept[1:], 1))
    for step in range(2, len(role_steps()[0])):
        mine = added(mine, swapped(mine, step))
    second = swapped(mine, 1)
    return mine, second, swapped(jnp.concatenate([mine, second]), 0)


def from_both_cores(chunks):
    return (*chunks, *(core_swapped(chunk) for chunk in chunks))


def on_device(grid_in, mesh_lat, edge_w, edge_src, edge_dst, block_count, embed_w, message_w, up_w, out_w, gain, cot):
    rows, cols, features = grid_in.shape
    latent = message_w.shape[0]
    block = edge_w.shape[1]
    half = block // 2
    nodes = mesh_lat.shape[0]
    own = rows * cols
    side = rows * half
    points = own + 2 * side
    grid = jnp.transpose(grid_in, (2, 0, 1))

    def call(kernel, name, in_specs, out_shape, flops, bytes_accessed, limit, scratch_shapes=()):
        return pl.pallas_call(
            kernel,
            name=name,
            in_specs=in_specs,
            out_specs=[VMEM] * len(out_shape),
            out_shape=out_shape,
            scratch_shapes=list(scratch_shapes),
            compiler_params=pltpu.CompilerParams(vmem_limit_bytes=limit * MIB),
            cost_estimate=pl.CostEstimate(flops=flops, bytes_accessed=bytes_accessed, transcendentals=0),
        )

    strip = shape((features, side), BF)
    wide = pltpu.VMEM((features * rows, block), F32)
    count = lax.axis_size("lon")
    (to_east,) = call(lambda *refs: pack_kernel(True, *refs), "pack_east", [VMEM], [strip], 0, MIB, 8, [wide])(grid)
    x_west = lax.ppermute(to_east, "lon", [(i, (i + 1) % count) for i in range(count)])
    to_east, later = lax.optimization_barrier((to_east, grid))
    (to_west,) = call(lambda *refs: pack_kernel(False, *refs), "pack_west", [VMEM], [strip], 0, MIB, 8, [wide])(later)
    x_east = lax.ppermute(to_west, "lon", [((i + 1) % count, i) for i in range(count)])

    weights_all, grad_update = call(
        lambda *refs: weights_kernel(rows, cols // block, *refs), "slot_weights", [SMEM] * 3 + [VMEM] * 3,
        [shape((nodes, points), BF), shape((nodes, latent), F32)],
        200_000_000, 4 * MIB, 16, [pltpu.VMEM((points // block, nodes, block), F32)],
    )(edge_src, edge_dst, block_count, edge_w, cot, out_w)
    x_own, embed_t = call(
        rows_kernel, "own_rows", [VMEM] * 2, [shape((features, own), BF), shape((latent, features), BF)],
        1_000_000_000, 5 * MIB, 16, [pltpu.VMEM((cols // block, features * rows, block), F32)],
    )(later, embed_w)
    h_own, slope_own = call(
        own_kernel, "own_points", [VMEM] * 3, [shape((nodes, latent), F32), shape((latent, own), BF)],
        2_000_000_000, 7 * MIB, 16,
    )(x_own, embed_t, weights_all)

    h_sum, slope_west = call(
        lambda *refs: west_kernel(own, *refs), "west_points", [VMEM] * 4,
        [shape((nodes, latent), F32), shape((latent, side), BF)],
        600_000_000, 3 * MIB, 16,
    )(x_west, embed_t, weights_all, h_own)

    quarter = shape((2, 2, latent // 8, latent), BF)
    node_rows = shape((nodes, latent), BF)
    (
        sent_high, sent_low, grad_mesh, gain_term, gathered, grad_aggregate, normed, grad_pre_up, update, slope_east
    ) = call(
        mesh_kernel, "mesh_nodes", [VMEM] * 9,
        [quarter, quarter, shape((nodes, latent), F32), shape((1, latent), F32)]
        + [node_rows] * 5
        + [shape((latent, side), BF)],
        2_000_000_000, 8 * MIB, 16, [pltpu.VMEM((2, latent // 2, latent), BF)],
    )(x_east, embed_t, weights_all, h_sum, message_w, up_w, gain.reshape(1, latent), mesh_lat, grad_update)
    got_high, got_low = core_swapped(sent_high), core_swapped(sent_low)
    kept_high, kept_low, back = call(
        tail_kernel, "mesh_tail", [VMEM] * 5, [quarter, quarter, shape((latent, nodes), BF)],
        500_000_000, 3 * MIB, 16, [pltpu.VMEM((2, latent // 2, latent), BF)],
    )(gathered, grad_aggregate, normed, grad_pre_up, message_w)

    high_a, back = lax.optimization_barrier((added(kept_high, got_high), back))
    low_a = added(kept_low, got_low)
    padded = -(-(features + 1) // 128) * 128
    assert padded == latent
    x_parts = (x_own, x_west, x_east)
    sent_high, sent_low, grad_pre, grad_out_term = call(
        grid_kernel, "grid_points", [VMEM] * 11,
        [quarter, quarter, shape((latent, points), BF), shape((latent, latent), BF)],
        1_600_000_000, 9 * MIB, 20, [pltpu.VMEM((2, latent // 2, latent), F32)],
    )(
        back, weights_all, slope_own, slope_west, slope_east, *x_parts, gain_term, update, cot
    )
    got_high, got_low = core_swapped(sent_high), core_swapped(sent_low)
    (sums_b,) = call(
        grid_kept_kernel, "grid_kept", [VMEM] * 5, [shape((latent // 2, latent), F32)], 800_000_000, 6 * MIB, 16
    )(grad_pre, *x_parts, gain_term)
    kept_a, sums_b = lax.optimization_barrier((halved(high_a, low_a), sums_b))
    kept_high, kept_low = call(
        kept_chunks_kernel, "kept_chunks", [VMEM] * 2, [quarter, quarter], 8_000_000_000, MIB, 16
    )(grad_out_term, sums_b)

    high_b, low_b = added(kept_high, got_high), added(kept_low, got_low)
    _, update, grad_mesh = lax.optimization_barrier((high_b, update, grad_mesh))
    mesh_new, mesh_grad = call(
        nodes_kernel, "mesh_outputs", [VMEM] * 5, [node_rows, shape((nodes, latent), F32)], 200_000_000, 3 * MIB, 16
    )(update, out_w, mesh_lat, cot, grad_mesh)
    summed_a = all_summed(kept_a)
    kept_b, mesh_new, mesh_grad = lax.optimization_barrier((halved(high_b, low_b), mesh_new, mesh_grad))
    summed_b = all_summed(kept_b)
    square = shape((latent, latent), F32)
    grad_message, grad_up = call(
        order_mesh_kernel, "order_a", [VMEM] * 6, [square, square], 0, 3 * MIB, 16
    )(*from_both_cores(summed_a))
    last, grad_message, grad_up = lax.optimization_barrier((summed_b[2], grad_message, grad_up))
    summed_b = (*summed_b[:2], last)
    rows_half = latent // 2
    behind = features - rows_half
    outs = [square, shape((features, latent), F32), shape((1, latent), F32)]

    def order_b(half, chunks, more, more_specs, aliases):
        block_of = pl.BlockSpec((rows_half, latent), lambda i: ((lax.axis_index("lat") & 1) ^ half, 0))
        return pl.pallas_call(
            lambda *refs: order_grid_kernel(half, behind, *refs),
            name="order_b",
            grid=(1,),
            in_specs=[VMEM] * 3 + more_specs,
            out_specs=[block_of, block_of, VMEM],
            out_shape=outs,
            input_output_aliases=aliases,
            compiler_params=pltpu.CompilerParams(vmem_limit_bytes=16 * MIB),
            cost_estimate=pl.CostEstimate(flops=0, bytes_accessed=2 * MIB, transcendentals=0),
        )(*chunks, *more)

    from_other = [core_swapped(chunk) for chunk in summed_b]
    held = order_b(0, summed_b, (), [], {})
    grad_out, grad_embed, grad_gain = order_b(
        1, from_other, (held[2], held[0], held[1]), [VMEM] + [pl.BlockSpec(memory_space=pl.ANY)] * 2, {4: 0, 5: 1}
    )
    return (mesh_new, mesh_grad, grad_embed, grad_message, grad_up, grad_out, grad_gain[0])


def solution(mesh):
    tiles = ("grp", "lon", "lat")
    return jax.shard_map(
        on_device,
        mesh=mesh,
        in_specs=(
            P(("grp", "lat"), "lon", None),
            P(tiles, None),
            P(tiles, None, None),
            P(tiles),
            P(tiles),
            P(tiles),
            P(),
            P(),
            P(),
            P(),
            P(),
            P(tiles, None),
        ),
        out_specs=(
            P(tiles, None),
            P(tiles, None),
            P("grp", None),
            P("grp", None),
            P("grp", None),
            P("grp", None),
            P("grp"),
        ),
        check_vma=False,
    )
```

```python
import jax
import jax.numpy as jnp
from jax import lax
from jax.experimental import pallas as pl
from jax.experimental.pallas import tpu as pltpu
from jax.sharding import PartitionSpec as P

epsilon = 1e-05
BF = jnp.bfloat16
F32 = jnp.float32
MIB = 1024 * 1024
SMEM = pl.BlockSpec(memory_space=pltpu.SMEM)
VMEM = pl.BlockSpec(memory_space=pltpu.VMEM)
shape = jax.ShapeDtypeStruct


def contract(a, b, dim_a, dim_b):
    return lax.dot_general(a, b, (((dim_a,), (dim_b,)), ((), ())), preferred_element_type=F32)


def silu_pair(pre):
    sigma = jax.nn.sigmoid(pre)
    return pre * sigma, sigma * (1.0 + pre * (1.0 - sigma))


def pack_kernel(from_high, grid, out, wide):
    features, rows, cols = grid.shape
    block = wide.shape[1]
    half = block // 2
    start = cols - block if from_high else 0
    wide[...] = grid[:, :, start : start + block].astype(F32).reshape(features * rows, block)
    lane = lax.broadcasted_iota(jnp.int32, (features, block), 1)
    for pair in range(rows // 2):
        even = wide[pl.ds(2 * pair, features, stride=rows), :]
        odd = wide[pl.ds(2 * pair + 1, features, stride=rows), :]
        if from_high:
            even = pltpu.roll(even, half, 1)
        else:
            odd = pltpu.roll(odd, half, 1)
        out[:, pair * block : (pair + 1) * block] = jnp.where(lane < half, even, odd).astype(BF)


def weights_kernel(rows, own_blocks, src, dst, count, edge_w, cot, out_w, weights_all, grad_update, acc):
    block = edge_w.shape[1]
    half = block // 2
    windows = 2 * own_blocks + 1
    west_base = rows * own_blocks
    east_base = west_base + rows // 2
    acc[...] = jnp.zeros(acc.shape, F32)
    lane = lax.broadcasted_iota(jnp.int32, (block, block), 1)

    def slot(b, carry):
        source = src[b]
        row = source // windows
        window = source - row * windows
        at = window // 2
        target = pl.ds(pl.multiple_of(dst[b] * block, block), block)
        weights = edge_w[b].astype(F32)

        @pl.when(window % 2 == 1)
        def _():
            acc[row * own_blocks + at, target, :] += weights

        @pl.when(window % 2 == 0)
        def _():
            turned = pltpu.roll(weights, half, 1)
            odd_row = row % 2 == 1
            first = jnp.where(at == 0, west_base + row // 2, row * own_blocks + at - 1)
            first_high = (at > 0) | odd_row
            second = jnp.where(at == own_blocks, east_base + row // 2, row * own_blocks + at)
            second_high = (at == own_blocks) & odd_row
            acc[first, target, :] += jnp.where(
                first_high, jnp.where(lane >= half, turned, 0.0), jnp.where(lane < half, weights, 0.0)
            )
            acc[second, target, :] += jnp.where(
                second_high, jnp.where(lane >= half, weights, 0.0), jnp.where(lane < half, turned, 0.0)
            )

        return carry

    lax.fori_loop(0, count[0], slot, 0)
    for k in range(acc.shape[0]):
        weights_all[:, k * block : (k + 1) * block] = acc[k].astype(BF)
    grad_update[...] = contract(cot[...], out_w[...], 1, 1)


def rows_kernel(grid, embed_w, x_t, embed_t, wide):
    features, rows, cols = grid.shape
    block = wide.shape[2]
    for k in range(cols // block):
        wide[k] = grid[:, :, k * block : (k + 1) * block].astype(F32).reshape(features * rows, block)
        for r in range(rows):
            x_t[:, r * cols + k * block : r * cols + (k + 1) * block] = wide[
                k, pl.ds(r, features, stride=rows), :
            ].astype(BF)
    embed_t[...] = embed_w[...].T


def own_kernel(x_t, embed_t, weights_all, h_own, slope):
    points = x_t.shape[1]
    tile = points // 8
    total = jnp.zeros(h_own.shape, F32)
    for r in range(8):
        at = slice(r * tile, (r + 1) * tile)
        hidden, hidden_slope = silu_pair(contract(embed_t[...], x_t[:, at], 1, 0))
        slope[:, at] = hidden_slope.astype(BF)
        total += contract(weights_all[:, at], hidden.astype(BF), 1, 1)
    h_own[...] = total


def halo_part(x, embed_t, weights, slope):
    hidden, hidden_slope = silu_pair(contract(embed_t[...], x[...], 1, 0))
    slope[...] = hidden_slope.astype(BF)
    return contract(weights, hidden.astype(BF), 1, 1)


def west_kernel(first, x, embed_t, weights_all, h_own, h_sum, slope):
    points = x.shape[1]
    h_sum[...] = h_own[...] + halo_part(x, embed_t, weights_all[:, first : first + points], slope)


def to_chunks(grads, stack, perm, start):
    count, matrices, size, _ = grads.shape
    for j in range(count):
        at = pl.ds(pl.multiple_of((perm[start + j] & 3) * size, size), size)
        for k in range(matrices):
            grads[j, k] = stack[k, at, :].astype(BF)


def from_chunks(outs, chunks, perm):
    j = 0
    for chunk in chunks:
        for n in range(chunk.shape[0]):
            size = chunk.shape[2]
            at = pl.ds(pl.multiple_of(perm[j] * size, size), size)
            for k, out in enumerate(outs):
                out[at, :] = chunk[n, k].astype(F32)
            j += 1


def rows_of_half(half, rows):
    return pl.ds(pl.multiple_of(half * rows, rows), rows)


def mesh_kernel(
    x, embed_t, weights_all, h_sum, message_w, up_w, gain, mesh_lat, grad_update,
    sent_high, sent_low, grad_mesh, grad_gain, gathered, grad_aggregate, normed, grad_pre_up, update, slope, stack,
):
    perm = chunk_order()
    points = x.shape[1]
    first = weights_all.shape[1] - points
    total = h_sum[...] + halo_part(x, embed_t, weights_all[:, first:], slope)
    gathered[...] = total.astype(BF)
    summed = mesh_lat[...].astype(F32) + contract(gathered[...], message_w[...], 1, 0)
    rinv = lax.rsqrt(jnp.mean(summed * summed, axis=1, keepdims=True) + epsilon)
    qhat = summed * rinv
    gains = gain[...]
    normed[...] = (qhat * gains).astype(BF)
    pre_up = contract(normed[...], up_w[...], 1, 0)
    silu_up, up_slope = silu_pair(pre_up)
    update[...] = silu_up.astype(BF)
    grad_pre_up[...] = (grad_update[...] * up_slope).astype(BF)
    grad_normed = contract(grad_pre_up[...], up_w[...], 1, 1)
    grad_gain[...] = jnp.sum(grad_normed * qhat, axis=0, keepdims=True)
    grad_qhat = grad_normed * gains
    grad_q = rinv * (grad_qhat - qhat * jnp.mean(grad_qhat * qhat, axis=1, keepdims=True))
    grad_aggregate[...] = grad_q.astype(BF)
    grad_mesh[...] = grad_q
    theirs = rows_of_half(1 - perm[0] // 4, stack.shape[1])
    stack[0] = contract(gathered[:, theirs], grad_aggregate[...], 0, 0).astype(BF)
    stack[1] = contract(normed[:, theirs], grad_pre_up[...], 0, 0).astype(BF)
    to_chunks(sent_high, stack, perm, 6)
    to_chunks(sent_low, stack, perm, 4)


def tail_kernel(gathered, grad_aggregate, normed, grad_pre_up, message_w, kept_high, kept_low, back, stack):
    perm = chunk_order()
    mine = rows_of_half(perm[0] // 4, stack.shape[1])
    stack[0] = contract(gathered[:, mine], grad_aggregate[...], 0, 0).astype(BF)
    stack[1] = contract(normed[:, mine], grad_pre_up[...], 0, 0).astype(BF)
    to_chunks(kept_high, stack, perm, 2)
    to_chunks(kept_low, stack, perm, 0)
    back[...] = contract(message_w[...], grad_aggregate[...], 1, 1).astype(BF)


def points_of(x_own, x_west, x_east):
    tile = x_west.shape[1]
    pieces = []
    for x in (x_own, x_west, x_east):
        pieces += [(x, slice(k * tile, (k + 1) * tile)) for k in range(x.shape[1] // tile)]
    return [(x, at, slice(n * tile, (n + 1) * tile)) for n, (x, at) in enumerate(pieces)]


def embed_rows(half, x_parts, grad_pre, grad_gain, out):
    rows = out.shape[0]
    features = x_parts[0].shape[0]
    for side in range(2):
        count = min(rows, features - side * rows)

        @pl.when(half == side)
        def _():
            sums = jnp.zeros((count, out.shape[1]), F32)
            for x, at, all_at in points_of(*x_parts):
                sums += contract(x[side * rows : side * rows + count, at], grad_pre[:, all_at], 1, 1)
            if count < rows:
                out[...] = jnp.zeros(out.shape, F32)
                out[count : count + 1, :] = grad_gain[...]
            out[:count, :] = sums


def grid_kernel(
    back, weights_all, slope_own, slope_west, slope_east, x_own, x_west, x_east, grad_gain, update, cot,
    sent_high, sent_low, grad_pre, grad_out, stack,
):
    perm = chunk_order()
    for slope, at, all_at in points_of(slope_own, slope_west, slope_east):
        hidden = contract(back[...], weights_all[:, all_at], 1, 0)
        grad_pre[:, all_at] = (hidden * slope[:, at].astype(F32)).astype(BF)
    grad_out[...] = contract(update[...], cot[...], 0, 0).astype(BF)
    half = 1 - perm[0] // 4
    stack[0] = grad_out[rows_of_half(half, stack.shape[1]), :].astype(F32)
    embed_rows(half, (x_own, x_west, x_east), grad_pre, grad_gain, stack.at[1])
    to_chunks(sent_high, stack, perm, 6)
    to_chunks(sent_low, stack, perm, 4)


def nodes_kernel(update, out_w, mesh_lat, cot, grad_mesh, mesh_new, mesh_grad):
    mesh_new[...] = (mesh_lat[...].astype(F32) + contract(update[...], out_w[...], 1, 0)).astype(BF)
    mesh_grad[...] = cot[...].astype(F32) + grad_mesh[...]


def grid_kept_kernel(grad_pre, x_own, x_west, x_east, grad_gain, sums):
    perm = chunk_order()
    embed_rows(perm[0] // 4, (x_own, x_west, x_east), grad_pre, grad_gain, sums)


def kept_chunks_kernel(grad_out, sums, kept_high, kept_low):
    perm = chunk_order()
    for kept, start in ((kept_high, 2), (kept_low, 0)):
        count, _, size, _ = kept.shape
        for j in range(count):
            chunk = perm[start + j]
            kept[j, 0] = grad_out[pl.ds(pl.multiple_of(chunk * size, size), size), :]
            kept[j, 1] = sums[pl.ds(pl.multiple_of((chunk & 3) * size, size), size), :].astype(BF)


def order_mesh_kernel(*refs):
    from_chunks(refs[-2:], refs[:-2], chunk_order())


def order_grid_kernel(half, behind, *refs):
    perm = chunk_order()
    chunks, others, (grad_out, grad_embed, grad_gain) = refs[:3], refs[3:-3], refs[-3:]
    j = 4 * half
    for chunk in chunks:
        for n in range(chunk.shape[0]):
            size = chunk.shape[2]
            at = pl.ds(pl.multiple_of((perm[j] & 3) * size, size), size)
            grad_out[at, :] = chunk[n, 0].astype(F32)
            grad_embed[at, :] = chunk[n, 1].astype(F32)
            j += 1
    row = others[0][...] if others else jnp.zeros(grad_gain.shape, F32)
    grad_gain[...] = jnp.where(perm[4 * half] >= 4, grad_embed[behind : behind + 1, :], row)


def role_steps():
    lat = [("lat", 2 << k) for k in range(lax.axis_size("lat").bit_length() - 2)]
    lon = [("lon", 1 << k) for k in range(lax.axis_size("lon").bit_length() - 1)]
    rest = lat[1:] + lon[1:]
    return ([lat[0], lon[0]] + rest, [lon[0], lat[0]] + rest)


def core_swapped(value):
    return lax.ppermute(value, "lat", [(i, i ^ 1) for i in range(lax.axis_size("lat"))])


def swapped(value, step):
    lats = lax.axis_size("lat")
    pairs = []
    for lon in range(lax.axis_size("lon")):
        for lat in range(lats):
            axis, bit = role_steps()[lat & 1][step]
            other = (lon ^ bit) * lats + lat if axis == "lon" else lon * lats + (lat ^ bit)
            pairs.append((lon * lats + lat, other))
    return lax.ppermute(value, ("lon", "lat"), pairs)


def chunk_order():
    core = lax.axis_index("lat") & 1
    sides = []
    for steps in role_steps():
        low = [((lax.axis_index(axis) & bit) != 0).astype(jnp.int32) for axis, bit in steps[:2]]
        sides.append(2 * low[0] + low[1])
    mine = jnp.where(core == 0, sides[0], sides[1])
    theirs = jnp.where(core == 0, sides[1], sides[0])
    return [4 * core + (mine ^ j) for j in range(4)] + [4 - 4 * core + (theirs ^ j) for j in range(4)]


def added(a, b):
    return (a.astype(F32) + b.astype(F32)).astype(BF)


def halved(high, low):
    return added(low, swapped(high, 0))


def all_summed(kept):
    mine = added(kept[:1], swapped(kept[1:], 1))
    for step in range(2, len(role_steps()[0])):
        mine = added(mine, swapped(mine, step))
    second = swapped(mine, 1)
    return mine, second, swapped(jnp.concatenate([mine, second]), 0)


def from_both_cores(chunks):
    return (*chunks, *(core_swapped(chunk) for chunk in chunks))


def on_device(grid_in, mesh_lat, edge_w, edge_src, edge_dst, block_count, embed_w, message_w, up_w, out_w, gain, cot):
    rows, cols, features = grid_in.shape
    latent = message_w.shape[0]
    block = edge_w.shape[1]
    half = block // 2
    nodes = mesh_lat.shape[0]
    own = rows * cols
    side = rows * half
    points = own + 2 * side
    grid = jnp.transpose(grid_in, (2, 0, 1))

    def call(kernel, name, in_specs, out_shape, flops, bytes_accessed, limit, scratch_shapes=()):
        return pl.pallas_call(
            kernel,
            name=name,
            in_specs=in_specs,
            out_specs=[VMEM] * len(out_shape),
            out_shape=out_shape,
            scratch_shapes=list(scratch_shapes),
            compiler_params=pltpu.CompilerParams(vmem_limit_bytes=limit * MIB),
            cost_estimate=pl.CostEstimate(flops=flops, bytes_accessed=bytes_accessed, transcendentals=0),
        )

    strip = shape((features, side), BF)
    wide = pltpu.VMEM((features * rows, block), F32)
    count = lax.axis_size("lon")
    (to_east,) = call(lambda *refs: pack_kernel(True, *refs), "pack_east", [VMEM], [strip], 0, MIB, 8, [wide])(
        grid[:, :, cols - block :]
    )
    x_west = lax.ppermute(to_east, "lon", [(i, (i + 1) % count) for i in range(count)])
    to_east, later = lax.optimization_barrier((to_east, grid))
    (to_west,) = call(lambda *refs: pack_kernel(False, *refs), "pack_west", [VMEM], [strip], 0, MIB, 8, [wide])(later)
    x_east = lax.ppermute(to_west, "lon", [((i + 1) % count, i) for i in range(count)])

    weights_all, grad_update = call(
        lambda *refs: weights_kernel(rows, cols // block, *refs), "slot_weights", [SMEM] * 3 + [VMEM] * 3,
        [shape((nodes, points), BF), shape((nodes, latent), F32)],
        200_000_000, 4 * MIB, 16, [pltpu.VMEM((points // block, nodes, block), F32)],
    )(edge_src, edge_dst, block_count, edge_w, cot, out_w)
    x_own, embed_t = call(
        rows_kernel, "own_rows", [VMEM] * 2, [shape((features, own), BF), shape((latent, features), BF)],
        1_000_000_000, 5 * MIB, 16, [pltpu.VMEM((cols // block, features * rows, block), F32)],
    )(later, embed_w)
    h_own, slope_own = call(
        own_kernel, "own_points", [VMEM] * 3, [shape((nodes, latent), F32), shape((latent, own), BF)],
        2_000_000_000, 7 * MIB, 16,
    )(x_own, embed_t, weights_all)

    h_sum, slope_west = call(
        lambda *refs: west_kernel(own, *refs), "west_points", [VMEM] * 4,
        [shape((nodes, latent), F32), shape((latent, side), BF)],
        600_000_000, 3 * MIB, 16,
    )(x_west, embed_t, weights_all, h_own)

    quarter = shape((2, 2, latent // 8, latent), BF)
    node_rows = shape((nodes, latent), BF)
    (
        sent_high, sent_low, grad_mesh, gain_term, gathered, grad_aggregate, normed, grad_pre_up, update, slope_east
    ) = call(
        mesh_kernel, "mesh_nodes", [VMEM] * 9,
        [quarter, quarter, shape((nodes, latent), F32), shape((1, latent), F32)]
        + [node_rows] * 5
        + [shape((latent, side), BF)],
        2_000_000_000, 8 * MIB, 16, [pltpu.VMEM((2, latent // 2, latent), BF)],
    )(x_east, embed_t, weights_all, h_sum, message_w, up_w, gain.reshape(1, latent), mesh_lat, grad_update)
    got_high = core_swapped(sent_high)
    kept_high, kept_low, back = call(
        tail_kernel, "mesh_tail", [VMEM] * 5, [quarter, quarter, shape((latent, nodes), BF)],
        500_000_000, 3 * MIB, 16, [pltpu.VMEM((2, latent // 2, latent), BF)],
    )(gathered, grad_aggregate, normed, grad_pre_up, message_w)

    high_a, back, sent_low = lax.optimization_barrier((added(kept_high, got_high), back, sent_low))
    low_a = added(kept_low, core_swapped(sent_low))
    padded = -(-(features + 1) // 128) * 128
    assert padded == latent
    x_parts = (x_own, x_west, x_east)
    sent_high, sent_low, grad_pre, grad_out_term = call(
        grid_kernel, "grid_points", [VMEM] * 11,
        [quarter, quarter, shape((latent, points), BF), shape((latent, latent), BF)],
        1_600_000_000, 9 * MIB, 20, [pltpu.VMEM((2, latent // 2, latent), F32)],
    )(
        back, weights_all, slope_own, slope_west, slope_east, *x_parts, gain_term, update, cot
    )
    got_high, got_low = core_swapped(sent_high), core_swapped(sent_low)
    (sums_b,) = call(
        grid_kept_kernel, "grid_kept", [VMEM] * 5, [shape((latent // 2, latent), F32)], 800_000_000, 6 * MIB, 16
    )(grad_pre, *x_parts, gain_term)
    kept_a, sums_b = lax.optimization_barrier((halved(high_a, low_a), sums_b))
    kept_high, kept_low = call(
        kept_chunks_kernel, "kept_chunks", [VMEM] * 2, [quarter, quarter], 8_000_000_000, MIB, 16
    )(grad_out_term, sums_b)

    high_b, low_b = added(kept_high, got_high), added(kept_low, got_low)
    _, update, grad_mesh = lax.optimization_barrier((high_b, update, grad_mesh))
    mesh_new, mesh_grad = call(
        nodes_kernel, "mesh_outputs", [VMEM] * 5, [node_rows, shape((nodes, latent), F32)], 200_000_000, 3 * MIB, 16
    )(update, out_w, mesh_lat, cot, grad_mesh)
    summed_a = all_summed(kept_a)
    kept_b, mesh_new, mesh_grad = lax.optimization_barrier((halved(high_b, low_b), mesh_new, mesh_grad))
    summed_b = all_summed(kept_b)
    square = shape((latent, latent), F32)
    grad_message, grad_up = call(
        order_mesh_kernel, "order_a", [VMEM] * 6, [square, square], 0, 3 * MIB, 16
    )(*from_both_cores(summed_a))
    last, grad_message, grad_up = lax.optimization_barrier((summed_b[2], grad_message, grad_up))
    summed_b = (*summed_b[:2], last)
    rows_half = latent // 2
    behind = features - rows_half
    outs = [square, shape((features, latent), F32), shape((1, latent), F32)]

    def order_b(half, chunks, more, more_specs, aliases):
        block_of = pl.BlockSpec((rows_half, latent), lambda i: ((lax.axis_index("lat") & 1) ^ half, 0))
        return pl.pallas_call(
            lambda *refs: order_grid_kernel(half, behind, *refs),
            name="order_b",
            grid=(1,),
            in_specs=[VMEM] * 3 + more_specs,
            out_specs=[block_of, block_of, VMEM],
            out_shape=outs,
            input_output_aliases=aliases,
            compiler_params=pltpu.CompilerParams(vmem_limit_bytes=16 * MIB),
            cost_estimate=pl.CostEstimate(flops=0, bytes_accessed=2 * MIB, transcendentals=0),
        )(*chunks, *more)

    from_other = [core_swapped(chunk) for chunk in summed_b]
    held = order_b(0, summed_b, (), [], {})
    grad_out, grad_embed, grad_gain = order_b(
        1, from_other, (held[2], held[0], held[1]), [VMEM] + [pl.BlockSpec(memory_space=pl.ANY)] * 2, {4: 0, 5: 1}
    )
    return (mesh_new, mesh_grad, grad_embed, grad_message, grad_up, grad_out, grad_gain[0])


def solution(mesh):
    tiles = ("grp", "lon", "lat")
    return jax.shard_map(
        on_device,
        mesh=mesh,
        in_specs=(
            P(("grp", "lat"), "lon", None),
            P(tiles, None),
            P(tiles, None, None),
            P(tiles),
            P(tiles),
            P(tiles),
            P(),
            P(),
            P(),
            P(),
            P(),
            P(tiles, None),
        ),
        out_specs=(
            P(tiles, None),
            P(tiles, None),
            P("grp", None),
            P("grp", None),
            P("grp", None),
            P("grp", None),
            P("grp"),
        ),
        check_vma=False,
    )
```

```python
import jax
import jax.numpy as jnp
from jax import lax
from jax.experimental import pallas as pl
from jax.experimental.pallas import tpu as pltpu
from jax.sharding import PartitionSpec as P

epsilon = 1e-05
BF = jnp.bfloat16
F32 = jnp.float32
MIB = 1024 * 1024
SMEM = pl.BlockSpec(memory_space=pltpu.SMEM)
VMEM = pl.BlockSpec(memory_space=pltpu.VMEM)
shape = jax.ShapeDtypeStruct


def contract(a, b, dim_a, dim_b):
    return lax.dot_general(a, b, (((dim_a,), (dim_b,)), ((), ())), preferred_element_type=F32)


def silu_pair(pre):
    sigma = jax.nn.sigmoid(pre)
    return pre * sigma, sigma * (1.0 + pre * (1.0 - sigma))


def pack_kernel(from_high, grid, out, wide):
    features, rows, cols = grid.shape
    block = wide.shape[1]
    half = block // 2
    start = cols - block if from_high else 0
    wide[...] = grid[:, :, start : start + block].astype(F32).reshape(features * rows, block)
    lane = lax.broadcasted_iota(jnp.int32, (features, block), 1)
    for pair in range(rows // 2):
        even = wide[pl.ds(2 * pair, features, stride=rows), :]
        odd = wide[pl.ds(2 * pair + 1, features, stride=rows), :]
        if from_high:
            even = pltpu.roll(even, half, 1)
        else:
            odd = pltpu.roll(odd, half, 1)
        out[:, pair * block : (pair + 1) * block] = jnp.where(lane < half, even, odd).astype(BF)


def weights_kernel(rows, own_blocks, src, dst, count, edge_w, cot, out_w, weights_all, grad_update, acc):
    block = edge_w.shape[1]
    half = block // 2
    windows = 2 * own_blocks + 1
    west_base = rows * own_blocks
    east_base = west_base + rows // 2
    acc[...] = jnp.zeros(acc.shape, F32)
    lane = lax.broadcasted_iota(jnp.int32, (block, block), 1)

    def slot(b, carry):
        source = src[b]
        row = source // windows
        window = source - row * windows
        at = window // 2
        target = pl.ds(pl.multiple_of(dst[b] * block, block), block)
        weights = edge_w[b].astype(F32)

        @pl.when(window % 2 == 1)
        def _():
            acc[row * own_blocks + at, target, :] += weights

        @pl.when(window % 2 == 0)
        def _():
            turned = pltpu.roll(weights, half, 1)
            odd_row = row % 2 == 1
            first = jnp.where(at == 0, west_base + row // 2, row * own_blocks + at - 1)
            first_high = (at > 0) | odd_row
            second = jnp.where(at == own_blocks, east_base + row // 2, row * own_blocks + at)
            second_high = (at == own_blocks) & odd_row
            acc[first, target, :] += jnp.where(
                first_high, jnp.where(lane >= half, turned, 0.0), jnp.where(lane < half, weights, 0.0)
            )
            acc[second, target, :] += jnp.where(
                second_high, jnp.where(lane >= half, weights, 0.0), jnp.where(lane < half, turned, 0.0)
            )

        return carry

    lax.fori_loop(0, count[0], slot, 0)
    for k in range(acc.shape[0]):
        weights_all[:, k * block : (k + 1) * block] = acc[k].astype(BF)
    grad_update[...] = contract(cot[...], out_w[...], 1, 1)


def rows_kernel(grid, embed_w, x_t, embed_t, wide):
    features, rows, cols = grid.shape
    block = wide.shape[2]
    for k in range(cols // block):
        wide[k] = grid[:, :, k * block : (k + 1) * block].astype(F32).reshape(features * rows, block)
        for r in range(rows):
            x_t[:, r * cols + k * block : r * cols + (k + 1) * block] = wide[
                k, pl.ds(r, features, stride=rows), :
            ].astype(BF)
    embed_t[...] = embed_w[...].T


def own_kernel(x_t, embed_t, weights_all, h_own, slope):
    points = x_t.shape[1]
    tile = points // 8
    total = jnp.zeros(h_own.shape, F32)
    for r in range(8):
        at = slice(r * tile, (r + 1) * tile)
        hidden, hidden_slope = silu_pair(contract(embed_t[...], x_t[:, at], 1, 0))
        slope[:, at] = hidden_slope.astype(BF)
        total += contract(weights_all[:, at], hidden.astype(BF), 1, 1)
    h_own[...] = total


def halo_part(x, embed_t, weights, slope):
    hidden, hidden_slope = silu_pair(contract(embed_t[...], x[...], 1, 0))
    slope[...] = hidden_slope.astype(BF)
    return contract(weights, hidden.astype(BF), 1, 1)


def west_kernel(first, x, embed_t, weights_all, h_own, h_sum, slope):
    points = x.shape[1]
    h_sum[...] = h_own[...] + halo_part(x, embed_t, weights_all[:, first : first + points], slope)


def to_chunks(grads, stack, perm, start):
    count, matrices, size, _ = grads.shape
    for j in range(count):
        at = pl.ds(pl.multiple_of((perm[start + j] & 3) * size, size), size)
        for k in range(matrices):
            grads[j, k] = stack[k, at, :].astype(BF)


def from_chunks(outs, chunks, perm):
    j = 0
    for chunk in chunks:
        for n in range(chunk.shape[0]):
            size = chunk.shape[2]
            at = pl.ds(pl.multiple_of(perm[j] * size, size), size)
            for k, out in enumerate(outs):
                out[at, :] = chunk[n, k].astype(F32)
            j += 1


def rows_of_half(half, rows):
    return pl.ds(pl.multiple_of(half * rows, rows), rows)


def mesh_kernel(
    x, embed_t, weights_all, h_sum, message_w, up_w, gain, mesh_lat, grad_update,
    sent_high, sent_low, grad_mesh, grad_gain, gathered, grad_aggregate, normed, grad_pre_up, update, slope, stack,
):
    perm = chunk_order()
    points = x.shape[1]
    first = weights_all.shape[1] - points
    total = h_sum[...] + halo_part(x, embed_t, weights_all[:, first:], slope)
    gathered[...] = total.astype(BF)
    summed = mesh_lat[...].astype(F32) + contract(gathered[...], message_w[...], 1, 0)
    rinv = lax.rsqrt(jnp.mean(summed * summed, axis=1, keepdims=True) + epsilon)
    qhat = summed * rinv
    gains = gain[...]
    normed[...] = (qhat * gains).astype(BF)
    pre_up = contract(normed[...], up_w[...], 1, 0)
    silu_up, up_slope = silu_pair(pre_up)
    update[...] = silu_up.astype(BF)
    grad_pre_up[...] = (grad_update[...] * up_slope).astype(BF)
    grad_normed = contract(grad_pre_up[...], up_w[...], 1, 1)
    grad_gain[...] = jnp.sum(grad_normed * qhat, axis=0, keepdims=True)
    grad_qhat = grad_normed * gains
    grad_q = rinv * (grad_qhat - qhat * jnp.mean(grad_qhat * qhat, axis=1, keepdims=True))
    grad_aggregate[...] = grad_q.astype(BF)
    grad_mesh[...] = grad_q
    theirs = rows_of_half(1 - perm[0] // 4, stack.shape[1])
    stack[0] = contract(gathered[:, theirs], grad_aggregate[...], 0, 0).astype(BF)
    stack[1] = contract(normed[:, theirs], grad_pre_up[...], 0, 0).astype(BF)
    to_chunks(sent_high, stack, perm, 6)
    to_chunks(sent_low, stack, perm, 4)


def tail_kernel(gathered, grad_aggregate, normed, grad_pre_up, message_w, kept_high, kept_low, back, stack):
    perm = chunk_order()
    mine = rows_of_half(perm[0] // 4, stack.shape[1])
    stack[0] = contract(gathered[:, mine], grad_aggregate[...], 0, 0).astype(BF)
    stack[1] = contract(normed[:, mine], grad_pre_up[...], 0, 0).astype(BF)
    to_chunks(kept_high, stack, perm, 2)
    to_chunks(kept_low, stack, perm, 0)
    back[...] = contract(message_w[...], grad_aggregate[...], 1, 1).astype(BF)


def points_of(x_own, x_west, x_east):
    tile = x_west.shape[1]
    pieces = []
    for x in (x_own, x_west, x_east):
        pieces += [(x, slice(k * tile, (k + 1) * tile)) for k in range(x.shape[1] // tile)]
    return [(x, at, slice(n * tile, (n + 1) * tile)) for n, (x, at) in enumerate(pieces)]


def embed_rows(half, x_parts, grad_pre, grad_gain, out):
    rows = out.shape[0]
    features = x_parts[0].shape[0]
    for side in range(2):
        count = min(rows, features - side * rows)

        @pl.when(half == side)
        def _():
            sums = jnp.zeros((count, out.shape[1]), F32)
            for x, at, all_at in points_of(*x_parts):
                sums += contract(x[side * rows : side * rows + count, at], grad_pre[:, all_at], 1, 1)
            if count < rows:
                out[...] = jnp.zeros(out.shape, F32)
                out[count : count + 1, :] = grad_gain[...]
            out[:count, :] = sums


def grid_kernel(
    back, weights_all, slope_own, slope_west, slope_east, x_own, x_west, x_east, grad_gain, update, cot,
    sent_high, sent_low, grad_pre, grad_out, stack,
):
    perm = chunk_order()
    for slope, at, all_at in points_of(slope_own, slope_west, slope_east):
        hidden = contract(back[...], weights_all[:, all_at], 1, 0)
        grad_pre[:, all_at] = (hidden * slope[:, at].astype(F32)).astype(BF)
    grad_out[...] = contract(update[...], cot[...], 0, 0).astype(BF)
    half = 1 - perm[0] // 4
    stack[0] = grad_out[rows_of_half(half, stack.shape[1]), :].astype(F32)
    embed_rows(half, (x_own, x_west, x_east), grad_pre, grad_gain, stack.at[1])
    to_chunks(sent_high, stack, perm, 6)
    to_chunks(sent_low, stack, perm, 4)


def nodes_kernel(update, out_w, mesh_lat, cot, grad_mesh, mesh_new, mesh_grad):
    mesh_new[...] = (mesh_lat[...].astype(F32) + contract(update[...], out_w[...], 1, 0)).astype(BF)
    mesh_grad[...] = cot[...].astype(F32) + grad_mesh[...]


def grid_kept_kernel(grad_pre, x_own, x_west, x_east, grad_gain, sums):
    perm = chunk_order()
    embed_rows(perm[0] // 4, (x_own, x_west, x_east), grad_pre, grad_gain, sums)


def kept_chunks_kernel(grad_out, sums, kept_high, kept_low):
    perm = chunk_order()
    for kept, start in ((kept_high, 2), (kept_low, 0)):
        count, _, size, _ = kept.shape
        for j in range(count):
            chunk = perm[start + j]
            kept[j, 0] = grad_out[pl.ds(pl.multiple_of(chunk * size, size), size), :]
            kept[j, 1] = sums[pl.ds(pl.multiple_of((chunk & 3) * size, size), size), :].astype(BF)


def order_mesh_kernel(*refs):
    from_chunks(refs[-2:], refs[:-2], chunk_order())


def order_grid_kernel(half, behind, *refs):
    perm = chunk_order()
    chunks, others, (grad_out, grad_embed, grad_gain) = refs[:3], refs[3:-3], refs[-3:]
    j = 4 * half
    for chunk in chunks:
        for n in range(chunk.shape[0]):
            size = chunk.shape[2]
            at = pl.ds(pl.multiple_of((perm[j] & 3) * size, size), size)
            grad_out[at, :] = chunk[n, 0].astype(F32)
            grad_embed[at, :] = chunk[n, 1].astype(F32)
            j += 1
    row = others[0][...] if others else jnp.zeros(grad_gain.shape, F32)
    grad_gain[...] = jnp.where(perm[4 * half] >= 4, grad_embed[behind : behind + 1, :], row)


def role_steps():
    lat = [("lat", 2 << k) for k in range(lax.axis_size("lat").bit_length() - 2)]
    lon = [("lon", 1 << k) for k in range(lax.axis_size("lon").bit_length() - 1)]
    rest = lat[1:] + lon[1:]
    return ([lat[0], lon[0]] + rest, [lon[0], lat[0]] + rest)


def core_swapped(value):
    return lax.ppermute(value, "lat", [(i, i ^ 1) for i in range(lax.axis_size("lat"))])


def swapped(value, step):
    lats = lax.axis_size("lat")
    pairs = []
    for lon in range(lax.axis_size("lon")):
        for lat in range(lats):
            axis, bit = role_steps()[lat & 1][step]
            other = (lon ^ bit) * lats + lat if axis == "lon" else lon * lats + (lat ^ bit)
            pairs.append((lon * lats + lat, other))
    return lax.ppermute(value, ("lon", "lat"), pairs)


def chunk_order():
    core = lax.axis_index("lat") & 1
    sides = []
    for steps in role_steps():
        low = [((lax.axis_index(axis) & bit) != 0).astype(jnp.int32) for axis, bit in steps[:2]]
        sides.append(2 * low[0] + low[1])
    mine = jnp.where(core == 0, sides[0], sides[1])
    theirs = jnp.where(core == 0, sides[1], sides[0])
    return [4 * core + (mine ^ j) for j in range(4)] + [4 - 4 * core + (theirs ^ j) for j in range(4)]


def added(a, b):
    return (a.astype(F32) + b.astype(F32)).astype(BF)


def halved(high, low):
    return added(low, swapped(high, 0))


def all_summed(kept):
    mine = added(kept[:1], swapped(kept[1:], 1))
    for step in range(2, len(role_steps()[0])):
        mine = added(mine, swapped(mine, step))
    second = swapped(mine, 1)
    return mine, second, swapped(jnp.concatenate([mine, second]), 0)


def from_both_cores(chunks):
    return (*chunks, *(core_swapped(chunk) for chunk in chunks))


def on_device(grid_in, mesh_lat, edge_w, edge_src, edge_dst, block_count, embed_w, message_w, up_w, out_w, gain, cot):
    rows, cols, features = grid_in.shape
    latent = message_w.shape[0]
    block = edge_w.shape[1]
    half = block // 2
    nodes = mesh_lat.shape[0]
    own = rows * cols
    side = rows * half
    points = own + 2 * side
    grid = jnp.transpose(grid_in, (2, 0, 1))

    def call(kernel, name, in_specs, out_shape, flops, bytes_accessed, limit, scratch_shapes=()):
        return pl.pallas_call(
            kernel,
            name=name,
            in_specs=in_specs,
            out_specs=[VMEM] * len(out_shape),
            out_shape=out_shape,
            scratch_shapes=list(scratch_shapes),
            compiler_params=pltpu.CompilerParams(vmem_limit_bytes=limit * MIB),
            cost_estimate=pl.CostEstimate(flops=flops, bytes_accessed=bytes_accessed, transcendentals=0),
        )

    strip = shape((features, side), BF)
    wide = pltpu.VMEM((features * rows, block), F32)
    count = lax.axis_size("lon")
    (to_east,) = call(lambda *refs: pack_kernel(True, *refs), "pack_east", [VMEM], [strip], 0, MIB, 8, [wide])(
        grid[:, :, cols - block :]
    )
    x_west = lax.ppermute(to_east, "lon", [(i, (i + 1) % count) for i in range(count)])
    to_east, later = lax.optimization_barrier((to_east, grid))
    (to_west,) = call(lambda *refs: pack_kernel(False, *refs), "pack_west", [VMEM], [strip], 0, MIB, 8, [wide])(later)
    x_east = lax.ppermute(to_west, "lon", [((i + 1) % count, i) for i in range(count)])

    weights_all, grad_update = call(
        lambda *refs: weights_kernel(rows, cols // block, *refs), "slot_weights", [SMEM] * 3 + [VMEM] * 3,
        [shape((nodes, points), BF), shape((nodes, latent), F32)],
        200_000_000, 4 * MIB, 16, [pltpu.VMEM((points // block, nodes, block), F32)],
    )(edge_src, edge_dst, block_count, edge_w, cot, out_w)
    x_own, embed_t = call(
        rows_kernel, "own_rows", [VMEM] * 2, [shape((features, own), BF), shape((latent, features), BF)],
        1_000_000_000, 5 * MIB, 16, [pltpu.VMEM((cols // block, features * rows, block), F32)],
    )(later, embed_w)
    h_own, slope_own = call(
        own_kernel, "own_points", [VMEM] * 3, [shape((nodes, latent), F32), shape((latent, own), BF)],
        2_000_000_000, 7 * MIB, 16,
    )(x_own, embed_t, weights_all)

    h_sum, slope_west = call(
        lambda *refs: west_kernel(own, *refs), "west_points", [VMEM] * 4,
        [shape((nodes, latent), F32), shape((latent, side), BF)],
        600_000_000, 3 * MIB, 16,
    )(x_west, embed_t, weights_all, h_own)

    quarter = shape((2, 2, latent // 8, latent), BF)
    node_rows = shape((nodes, latent), BF)
    (
        sent_high, sent_low, grad_mesh, gain_term, gathered, grad_aggregate, normed, grad_pre_up, update, slope_east
    ) = call(
        mesh_kernel, "mesh_nodes", [VMEM] * 9,
        [quarter, quarter, shape((nodes, latent), F32), shape((1, latent), F32)]
        + [node_rows] * 5
        + [shape((latent, side), BF)],
        2_000_000_000, 8 * MIB, 16, [pltpu.VMEM((2, latent // 2, latent), BF)],
    )(x_east, embed_t, weights_all, h_sum, message_w, up_w, gain.reshape(1, latent), mesh_lat, grad_update)
    got_high = core_swapped(sent_high)
    kept_high, kept_low, back = call(
        tail_kernel, "mesh_tail", [VMEM] * 5, [quarter, quarter, shape((latent, nodes), BF)],
        500_000_000, 3 * MIB, 16, [pltpu.VMEM((2, latent // 2, latent), BF)],
    )(gathered, grad_aggregate, normed, grad_pre_up, message_w)

    high_a, back, sent_low = lax.optimization_barrier((added(kept_high, got_high), back, sent_low))
    low_a = added(kept_low, core_swapped(sent_low))
    padded = -(-(features + 1) // 128) * 128
    assert padded == latent
    x_parts = (x_own, x_west, x_east)
    sent_high, sent_low, grad_pre, grad_out_term = call(
        grid_kernel, "grid_points", [VMEM] * 11,
        [quarter, quarter, shape((latent, points), BF), shape((latent, latent), BF)],
        1_600_000_000, 9 * MIB, 20, [pltpu.VMEM((2, latent // 2, latent), F32)],
    )(
        back, weights_all, slope_own, slope_west, slope_east, *x_parts, gain_term, update, cot
    )
    got_high, got_low = core_swapped(sent_high), core_swapped(sent_low)
    (sums_b,) = call(
        grid_kept_kernel, "grid_kept", [VMEM] * 5, [shape((latent // 2, latent), F32)], 800_000_000, 6 * MIB, 16
    )(grad_pre, *x_parts, gain_term)
    kept_a, sums_b = lax.optimization_barrier((halved(high_a, low_a), sums_b))
    kept_high, kept_low = call(
        kept_chunks_kernel, "kept_chunks", [VMEM] * 2, [quarter, quarter], 8_000_000_000, MIB, 16
    )(grad_out_term, sums_b)

    high_b, low_b = added(kept_high, got_high), added(kept_low, got_low)
    _, update, grad_mesh = lax.optimization_barrier((high_b, update, grad_mesh))
    mesh_new, mesh_grad = call(
        nodes_kernel, "mesh_outputs", [VMEM] * 5, [node_rows, shape((nodes, latent), F32)], 200_000_000, 3 * MIB, 16
    )(update, out_w, mesh_lat, cot, grad_mesh)
    summed_a = all_summed(kept_a)
    kept_b, mesh_new, mesh_grad = lax.optimization_barrier((halved(high_b, low_b), mesh_new, mesh_grad))
    summed_b = all_summed(kept_b)
    chunks_a, early_b = lax.optimization_barrier(
        (from_both_cores(summed_a), tuple(core_swapped(chunk) for chunk in summed_b[:2]))
    )
    square = shape((latent, latent), F32)
    grad_message, grad_up = call(
        order_mesh_kernel, "order_a", [VMEM] * 6, [square, square], 0, 3 * MIB, 16
    )(*chunks_a)
    last, grad_message, grad_up = lax.optimization_barrier((summed_b[2], grad_message, grad_up))
    summed_b = (*summed_b[:2], last)
    rows_half = latent // 2
    behind = features - rows_half
    outs = [square, shape((features, latent), F32), shape((1, latent), F32)]

    def order_b(half, chunks, more, more_specs, aliases):
        block_of = pl.BlockSpec((rows_half, latent), lambda i: ((lax.axis_index("lat") & 1) ^ half, 0))
        return pl.pallas_call(
            lambda *refs: order_grid_kernel(half, behind, *refs),
            name="order_b",
            grid=(1,),
            in_specs=[VMEM] * 3 + more_specs,
            out_specs=[block_of, block_of, VMEM],
            out_shape=outs,
            input_output_aliases=aliases,
            compiler_params=pltpu.CompilerParams(vmem_limit_bytes=16 * MIB),
            cost_estimate=pl.CostEstimate(flops=0, bytes_accessed=2 * MIB, transcendentals=0),
        )(*chunks, *more)

    from_other = (*early_b, core_swapped(last))
    held = order_b(0, summed_b, (), [], {})
    grad_out, grad_embed, grad_gain = order_b(
        1, from_other, (held[2], held[0], held[1]), [VMEM] + [pl.BlockSpec(memory_space=pl.ANY)] * 2, {4: 0, 5: 1}
    )
    return (mesh_new, mesh_grad, grad_embed, grad_message, grad_up, grad_out, grad_gain[0])


def solution(mesh):
    tiles = ("grp", "lon", "lat")
    return jax.shard_map(
        on_device,
        mesh=mesh,
        in_specs=(
            P(("grp", "lat"), "lon", None),
            P(tiles, None),
            P(tiles, None, None),
            P(tiles),
            P(tiles),
            P(tiles),
            P(),
            P(),
            P(),
            P(),
            P(),
            P(tiles, None),
        ),
        out_specs=(
            P(tiles, None),
            P(tiles, None),
            P("grp", None),
            P("grp", None),
            P("grp", None),
            P("grp", None),
            P("grp"),
        ),
        check_vma=False,
    )
```

```python
import jax
import jax.numpy as jnp
from jax import lax
from jax.experimental import pallas as pl
from jax.experimental.pallas import tpu as pltpu
from jax.sharding import PartitionSpec as P

epsilon = 1e-05
BF = jnp.bfloat16
F32 = jnp.float32
MIB = 1024 * 1024
SMEM = pl.BlockSpec(memory_space=pltpu.SMEM)
VMEM = pl.BlockSpec(memory_space=pltpu.VMEM)
shape = jax.ShapeDtypeStruct


def contract(a, b, dim_a, dim_b):
    return lax.dot_general(a, b, (((dim_a,), (dim_b,)), ((), ())), preferred_element_type=F32)


def silu_pair(pre):
    sigma = 0.5 * jnp.tanh(0.5 * pre) + 0.5
    silu = pre * sigma
    return silu, sigma + silu * (1.0 - sigma)


def pack_kernel(from_high, grid, out, wide):
    features, rows, cols = grid.shape
    block = wide.shape[1]
    half = block // 2
    start = cols - block if from_high else 0
    wide[...] = grid[:, :, start : start + block].astype(F32).reshape(features * rows, block)
    lane = lax.broadcasted_iota(jnp.int32, (features, block), 1)
    for pair in range(rows // 2):
        even = wide[pl.ds(2 * pair, features, stride=rows), :]
        odd = wide[pl.ds(2 * pair + 1, features, stride=rows), :]
        if from_high:
            even = pltpu.roll(even, half, 1)
        else:
            odd = pltpu.roll(odd, half, 1)
        out[:, pair * block : (pair + 1) * block] = jnp.where(lane < half, even, odd).astype(BF)


def weights_kernel(rows, own_blocks, src, dst, count, edge_w, cot, out_w, weights_all, grad_update, acc):
    block = edge_w.shape[1]
    half = block // 2
    windows = 2 * own_blocks + 1
    west_base = rows * own_blocks
    east_base = west_base + rows // 2
    acc[...] = jnp.zeros(acc.shape, F32)
    lane = lax.broadcasted_iota(jnp.int32, (block, block), 1)

    def slot(b, carry):
        source = src[b]
        row = source // windows
        window = source - row * windows
        at = window // 2
        target = pl.ds(pl.multiple_of(dst[b] * block, block), block)
        weights = edge_w[b].astype(F32)

        @pl.when(window % 2 == 1)
        def _():
            acc[row * own_blocks + at, target, :] += weights

        @pl.when(window % 2 == 0)
        def _():
            turned = pltpu.roll(weights, half, 1)
            odd_row = row % 2 == 1
            first = jnp.where(at == 0, west_base + row // 2, row * own_blocks + at - 1)
            first_high = (at > 0) | odd_row
            second = jnp.where(at == own_blocks, east_base + row // 2, row * own_blocks + at)
            second_high = (at == own_blocks) & odd_row
            acc[first, target, :] += jnp.where(
                first_high, jnp.where(lane >= half, turned, 0.0), jnp.where(lane < half, weights, 0.0)
            )
            acc[second, target, :] += jnp.where(
                second_high, jnp.where(lane >= half, weights, 0.0), jnp.where(lane < half, turned, 0.0)
            )

        return carry

    lax.fori_loop(0, count[0], slot, 0)
    for k in range(acc.shape[0]):
        weights_all[:, k * block : (k + 1) * block] = acc[k].astype(BF)
    grad_update[...] = contract(cot[...], out_w[...], 1, 1)


def rows_kernel(grid, embed_w, x_t, embed_t, wide):
    features, rows, cols = grid.shape
    block = wide.shape[2]
    for k in range(cols // block):
        wide[k] = grid[:, :, k * block : (k + 1) * block].astype(F32).reshape(features * rows, block)
        for r in range(rows):
            x_t[:, r * cols + k * block : r * cols + (k + 1) * block] = wide[
                k, pl.ds(r, features, stride=rows), :
            ].astype(BF)
    embed_t[...] = embed_w[...].T


def own_kernel(x_t, embed_t, weights_all, h_own, slope):
    points = x_t.shape[1]
    tile = points // 8
    total = jnp.zeros(h_own.shape, F32)
    for r in range(8):
        at = slice(r * tile, (r + 1) * tile)
        hidden, hidden_slope = silu_pair(contract(embed_t[...], x_t[:, at], 1, 0))
        slope[:, at] = hidden_slope.astype(BF)
        total += contract(weights_all[:, at], hidden.astype(BF), 1, 1)
    h_own[...] = total


def halo_part(x, embed_t, weights, slope):
    hidden, hidden_slope = silu_pair(contract(embed_t[...], x[...], 1, 0))
    slope[...] = hidden_slope.astype(BF)
    return contract(weights, hidden.astype(BF), 1, 1)


def west_kernel(first, x, embed_t, weights_all, h_own, h_sum, slope):
    points = x.shape[1]
    h_sum[...] = h_own[...] + halo_part(x, embed_t, weights_all[:, first : first + points], slope)


def to_chunks(grads, stack, perm, start):
    count, matrices, size, _ = grads.shape
    for j in range(count):
        at = pl.ds(pl.multiple_of((perm[start + j] & 3) * size, size), size)
        for k in range(matrices):
            grads[j, k] = stack[k, at, :].astype(BF)


def from_chunks(outs, chunks, perm):
    j = 0
    for chunk in chunks:
        for n in range(chunk.shape[0]):
            size = chunk.shape[2]
            at = pl.ds(pl.multiple_of(perm[j] * size, size), size)
            for k, out in enumerate(outs):
                out[at, :] = chunk[n, k].astype(F32)
            j += 1


def rows_of_half(half, rows):
    return pl.ds(pl.multiple_of(half * rows, rows), rows)


def mesh_kernel(
    x, embed_t, weights_all, h_sum, message_w, up_w, gain, mesh_lat, grad_update,
    sent_high, sent_low, grad_mesh, grad_gain, gathered, grad_aggregate, normed, grad_pre_up, update, slope, stack,
):
    perm = chunk_order()
    points = x.shape[1]
    first = weights_all.shape[1] - points
    total = h_sum[...] + halo_part(x, embed_t, weights_all[:, first:], slope)
    gathered[...] = total.astype(BF)
    summed = mesh_lat[...].astype(F32) + contract(gathered[...], message_w[...], 1, 0)
    rinv = lax.rsqrt(jnp.mean(summed * summed, axis=1, keepdims=True) + epsilon)
    qhat = summed * rinv
    gains = gain[...]
    normed[...] = (qhat * gains).astype(BF)
    pre_up = contract(normed[...], up_w[...], 1, 0)
    silu_up, up_slope = silu_pair(pre_up)
    update[...] = silu_up.astype(BF)
    grad_pre_up[...] = (grad_update[...] * up_slope).astype(BF)
    grad_normed = contract(grad_pre_up[...], up_w[...], 1, 1)
    grad_gain[...] = jnp.sum(grad_normed * qhat, axis=0, keepdims=True)
    grad_qhat = grad_normed * gains
    grad_q = rinv * (grad_qhat - qhat * jnp.mean(grad_qhat * qhat, axis=1, keepdims=True))
    grad_aggregate[...] = grad_q.astype(BF)
    grad_mesh[...] = grad_q
    theirs = rows_of_half(1 - perm[0] // 4, stack.shape[1])
    stack[0] = contract(gathered[:, theirs], grad_aggregate[...], 0, 0).astype(BF)
    stack[1] = contract(normed[:, theirs], grad_pre_up[...], 0, 0).astype(BF)
    to_chunks(sent_high, stack, perm, 6)
    to_chunks(sent_low, stack, perm, 4)


def tail_kernel(gathered, grad_aggregate, normed, grad_pre_up, message_w, kept_high, kept_low, back, stack):
    perm = chunk_order()
    mine = rows_of_half(perm[0] // 4, stack.shape[1])
    stack[0] = contract(gathered[:, mine], grad_aggregate[...], 0, 0).astype(BF)
    stack[1] = contract(normed[:, mine], grad_pre_up[...], 0, 0).astype(BF)
    to_chunks(kept_high, stack, perm, 2)
    to_chunks(kept_low, stack, perm, 0)
    back[...] = contract(message_w[...], grad_aggregate[...], 1, 1).astype(BF)


def points_of(x_own, x_west, x_east):
    tile = x_west.shape[1]
    pieces = []
    for x in (x_own, x_west, x_east):
        pieces += [(x, slice(k * tile, (k + 1) * tile)) for k in range(x.shape[1] // tile)]
    return [(x, at, slice(n * tile, (n + 1) * tile)) for n, (x, at) in enumerate(pieces)]


def embed_rows(half, x_parts, grad_pre, grad_gain, out):
    rows = out.shape[0]
    features = x_parts[0].shape[0]
    for side in range(2):
        count = min(rows, features - side * rows)

        @pl.when(half == side)
        def _():
            sums = jnp.zeros((count, out.shape[1]), F32)
            for x, at, all_at in points_of(*x_parts):
                sums += contract(x[side * rows : side * rows + count, at], grad_pre[:, all_at], 1, 1)
            if count < rows:
                out[...] = jnp.zeros(out.shape, F32)
                out[count : count + 1, :] = grad_gain[...]
            out[:count, :] = sums


def grid_kernel(
    back, weights_all, slope_own, slope_west, slope_east, x_own, x_west, x_east, grad_gain, update, cot,
    sent_high, sent_low, grad_pre, grad_out, stack,
):
    perm = chunk_order()
    for slope, at, all_at in points_of(slope_own, slope_west, slope_east):
        hidden = contract(back[...], weights_all[:, all_at], 1, 0)
        grad_pre[:, all_at] = (hidden * slope[:, at].astype(F32)).astype(BF)
    grad_out[...] = contract(update[...], cot[...], 0, 0).astype(BF)
    half = 1 - perm[0] // 4
    stack[0] = grad_out[rows_of_half(half, stack.shape[1]), :].astype(F32)
    embed_rows(half, (x_own, x_west, x_east), grad_pre, grad_gain, stack.at[1])
    to_chunks(sent_high, stack, perm, 6)
    to_chunks(sent_low, stack, perm, 4)


def nodes_kernel(update, out_w, mesh_lat, cot, grad_mesh, mesh_new, mesh_grad):
    mesh_new[...] = (mesh_lat[...].astype(F32) + contract(update[...], out_w[...], 1, 0)).astype(BF)
    mesh_grad[...] = cot[...].astype(F32) + grad_mesh[...]


def grid_kept_kernel(grad_pre, x_own, x_west, x_east, grad_gain, sums):
    perm = chunk_order()
    embed_rows(perm[0] // 4, (x_own, x_west, x_east), grad_pre, grad_gain, sums)


def kept_chunks_kernel(grad_out, sums, kept_high, kept_low):
    perm = chunk_order()
    for kept, start in ((kept_high, 2), (kept_low, 0)):
        count, _, size, _ = kept.shape
        for j in range(count):
            chunk = perm[start + j]
            kept[j, 0] = grad_out[pl.ds(pl.multiple_of(chunk * size, size), size), :]
            kept[j, 1] = sums[pl.ds(pl.multiple_of((chunk & 3) * size, size), size), :].astype(BF)


def order_mesh_kernel(*refs):
    from_chunks(refs[-2:], refs[:-2], chunk_order())


def order_grid_kernel(half, behind, *refs):
    perm = chunk_order()
    chunks, others, (grad_out, grad_embed, grad_gain) = refs[:3], refs[3:-3], refs[-3:]
    j = 4 * half
    for chunk in chunks:
        for n in range(chunk.shape[0]):
            size = chunk.shape[2]
            at = pl.ds(pl.multiple_of((perm[j] & 3) * size, size), size)
            grad_out[at, :] = chunk[n, 0].astype(F32)
            grad_embed[at, :] = chunk[n, 1].astype(F32)
            j += 1
    row = others[0][...] if others else jnp.zeros(grad_gain.shape, F32)
    grad_gain[...] = jnp.where(perm[4 * half] >= 4, grad_embed[behind : behind + 1, :], row)


def role_steps():
    lat = [("lat", 2 << k) for k in range(lax.axis_size("lat").bit_length() - 2)]
    lon = [("lon", 1 << k) for k in range(lax.axis_size("lon").bit_length() - 1)]
    rest = lat[1:] + lon[1:]
    return ([lat[0], lon[0]] + rest, [lon[0], lat[0]] + rest)


def core_swapped(value):
    return lax.ppermute(value, "lat", [(i, i ^ 1) for i in range(lax.axis_size("lat"))])


def swapped(value, step):
    lats = lax.axis_size("lat")
    pairs = []
    for lon in range(lax.axis_size("lon")):
        for lat in range(lats):
            axis, bit = role_steps()[lat & 1][step]
            other = (lon ^ bit) * lats + lat if axis == "lon" else lon * lats + (lat ^ bit)
            pairs.append((lon * lats + lat, other))
    return lax.ppermute(value, ("lon", "lat"), pairs)


def chunk_order():
    core = lax.axis_index("lat") & 1
    sides = []
    for steps in role_steps():
        low = [((lax.axis_index(axis) & bit) != 0).astype(jnp.int32) for axis, bit in steps[:2]]
        sides.append(2 * low[0] + low[1])
    mine = jnp.where(core == 0, sides[0], sides[1])
    theirs = jnp.where(core == 0, sides[1], sides[0])
    return [4 * core + (mine ^ j) for j in range(4)] + [4 - 4 * core + (theirs ^ j) for j in range(4)]


def added(a, b):
    return (a.astype(F32) + b.astype(F32)).astype(BF)


def halved(high, low):
    return added(low, swapped(high, 0))


def all_summed(kept):
    mine = added(kept[:1], swapped(kept[1:], 1))
    for step in range(2, len(role_steps()[0])):
        mine = added(mine, swapped(mine, step))
    second = swapped(mine, 1)
    return mine, second, swapped(jnp.concatenate([mine, second]), 0)


def from_both_cores(chunks):
    return (*chunks, *(core_swapped(chunk) for chunk in chunks))


def on_device(grid_in, mesh_lat, edge_w, edge_src, edge_dst, block_count, embed_w, message_w, up_w, out_w, gain, cot):
    rows, cols, features = grid_in.shape
    latent = message_w.shape[0]
    block = edge_w.shape[1]
    half = block // 2
    nodes = mesh_lat.shape[0]
    own = rows * cols
    side = rows * half
    points = own + 2 * side
    grid = jnp.transpose(grid_in, (2, 0, 1))

    def call(kernel, name, in_specs, out_shape, flops, bytes_accessed, limit, scratch_shapes=()):
        return pl.pallas_call(
            kernel,
            name=name,
            in_specs=in_specs,
            out_specs=[VMEM] * len(out_shape),
            out_shape=out_shape,
            scratch_shapes=list(scratch_shapes),
            compiler_params=pltpu.CompilerParams(vmem_limit_bytes=limit * MIB),
            cost_estimate=pl.CostEstimate(flops=flops, bytes_accessed=bytes_accessed, transcendentals=0),
        )

    strip = shape((features, side), BF)
    wide = pltpu.VMEM((features * rows, block), F32)
    count = lax.axis_size("lon")
    (to_east,) = call(lambda *refs: pack_kernel(True, *refs), "pack_east", [VMEM], [strip], 0, MIB, 8, [wide])(
        grid[:, :, cols - block :]
    )
    x_west = lax.ppermute(to_east, "lon", [(i, (i + 1) % count) for i in range(count)])
    to_east, later = lax.optimization_barrier((to_east, grid))
    (to_west,) = call(lambda *refs: pack_kernel(False, *refs), "pack_west", [VMEM], [strip], 0, MIB, 8, [wide])(later)
    x_east = lax.ppermute(to_west, "lon", [((i + 1) % count, i) for i in range(count)])

    weights_all, grad_update = call(
        lambda *refs: weights_kernel(rows, cols // block, *refs), "slot_weights", [SMEM] * 3 + [VMEM] * 3,
        [shape((nodes, points), BF), shape((nodes, latent), F32)],
        200_000_000, 4 * MIB, 16, [pltpu.VMEM((points // block, nodes, block), F32)],
    )(edge_src, edge_dst, block_count, edge_w, cot, out_w)
    x_own, embed_t = call(
        rows_kernel, "own_rows", [VMEM] * 2, [shape((features, own), BF), shape((latent, features), BF)],
        1_000_000_000, 5 * MIB, 16, [pltpu.VMEM((cols // block, features * rows, block), F32)],
    )(later, embed_w)
    h_own, slope_own = call(
        own_kernel, "own_points", [VMEM] * 3, [shape((nodes, latent), F32), shape((latent, own), BF)],
        2_000_000_000, 7 * MIB, 16,
    )(x_own, embed_t, weights_all)

    h_sum, slope_west = call(
        lambda *refs: west_kernel(own, *refs), "west_points", [VMEM] * 4,
        [shape((nodes, latent), F32), shape((latent, side), BF)],
        600_000_000, 3 * MIB, 16,
    )(x_west, embed_t, weights_all, h_own)

    quarter = shape((2, 2, latent // 8, latent), BF)
    node_rows = shape((nodes, latent), BF)
    (
        sent_high, sent_low, grad_mesh, gain_term, gathered, grad_aggregate, normed, grad_pre_up, update, slope_east
    ) = call(
        mesh_kernel, "mesh_nodes", [VMEM] * 9,
        [quarter, quarter, shape((nodes, latent), F32), shape((1, latent), F32)]
        + [node_rows] * 5
        + [shape((latent, side), BF)],
        2_000_000_000, 8 * MIB, 16, [pltpu.VMEM((2, latent // 2, latent), BF)],
    )(x_east, embed_t, weights_all, h_sum, message_w, up_w, gain.reshape(1, latent), mesh_lat, grad_update)
    got_high = core_swapped(sent_high)
    kept_high, kept_low, back = call(
        tail_kernel, "mesh_tail", [VMEM] * 5, [quarter, quarter, shape((latent, nodes), BF)],
        500_000_000, 3 * MIB, 16, [pltpu.VMEM((2, latent // 2, latent), BF)],
    )(gathered, grad_aggregate, normed, grad_pre_up, message_w)

    high_a, back, sent_low = lax.optimization_barrier((added(kept_high, got_high), back, sent_low))
    low_a = added(kept_low, core_swapped(sent_low))
    padded = -(-(features + 1) // 128) * 128
    assert padded == latent
    x_parts = (x_own, x_west, x_east)
    sent_high, sent_low, grad_pre, grad_out_term = call(
        grid_kernel, "grid_points", [VMEM] * 11,
        [quarter, quarter, shape((latent, points), BF), shape((latent, latent), BF)],
        1_600_000_000, 9 * MIB, 20, [pltpu.VMEM((2, latent // 2, latent), F32)],
    )(
        back, weights_all, slope_own, slope_west, slope_east, *x_parts, gain_term, update, cot
    )
    got_high, got_low = core_swapped(sent_high), core_swapped(sent_low)
    (sums_b,) = call(
        grid_kept_kernel, "grid_kept", [VMEM] * 5, [shape((latent // 2, latent), F32)], 800_000_000, 6 * MIB, 16
    )(grad_pre, *x_parts, gain_term)
    kept_a, sums_b = lax.optimization_barrier((halved(high_a, low_a), sums_b))
    kept_high, kept_low = call(
        kept_chunks_kernel, "kept_chunks", [VMEM] * 2, [quarter, quarter], 8_000_000_000, MIB, 16
    )(grad_out_term, sums_b)

    high_b, low_b = added(kept_high, got_high), added(kept_low, got_low)
    _, update, grad_mesh = lax.optimization_barrier((high_b, update, grad_mesh))
    mesh_new, mesh_grad = call(
        nodes_kernel, "mesh_outputs", [VMEM] * 5, [node_rows, shape((nodes, latent), F32)], 200_000_000, 3 * MIB, 16
    )(update, out_w, mesh_lat, cot, grad_mesh)
    summed_a = all_summed(kept_a)
    kept_b, mesh_new, mesh_grad = lax.optimization_barrier((halved(high_b, low_b), mesh_new, mesh_grad))
    summed_b = all_summed(kept_b)
    chunks_a, early_b = lax.optimization_barrier(
        (from_both_cores(summed_a), tuple(core_swapped(chunk) for chunk in summed_b[:2]))
    )
    square = shape((latent, latent), F32)
    grad_message, grad_up = call(
        order_mesh_kernel, "order_a", [VMEM] * 6, [square, square], 0, 3 * MIB, 16
    )(*chunks_a)
    last, grad_message, grad_up = lax.optimization_barrier((summed_b[2], grad_message, grad_up))
    summed_b = (*summed_b[:2], last)
    rows_half = latent // 2
    behind = features - rows_half
    outs = [square, shape((features, latent), F32), shape((1, latent), F32)]

    def order_b(half, chunks, more, more_specs, aliases):
        block_of = pl.BlockSpec((rows_half, latent), lambda i: ((lax.axis_index("lat") & 1) ^ half, 0))
        return pl.pallas_call(
            lambda *refs: order_grid_kernel(half, behind, *refs),
            name="order_b",
            grid=(1,),
            in_specs=[VMEM] * 3 + more_specs,
            out_specs=[block_of, block_of, VMEM],
            out_shape=outs,
            input_output_aliases=aliases,
            compiler_params=pltpu.CompilerParams(vmem_limit_bytes=16 * MIB),
            cost_estimate=pl.CostEstimate(flops=0, bytes_accessed=2 * MIB, transcendentals=0),
        )(*chunks, *more)

    from_other = (*early_b, core_swapped(last))
    held = order_b(0, summed_b, (), [], {})
    grad_out, grad_embed, grad_gain = order_b(
        1, from_other, (held[2], held[0], held[1]), [VMEM] + [pl.BlockSpec(memory_space=pl.ANY)] * 2, {4: 0, 5: 1}
    )
    return (mesh_new, mesh_grad, grad_embed, grad_message, grad_up, grad_out, grad_gain[0])


def solution(mesh):
    tiles = ("grp", "lon", "lat")
    return jax.shard_map(
        on_device,
        mesh=mesh,
        in_specs=(
            P(("grp", "lat"), "lon", None),
            P(tiles, None),
            P(tiles, None, None),
            P(tiles),
            P(tiles),
            P(tiles),
            P(),
            P(),
            P(),
            P(),
            P(),
            P(tiles, None),
        ),
        out_specs=(
            P(tiles, None),
            P(tiles, None),
            P("grp", None),
            P("grp", None),
            P("grp", None),
            P("grp", None),
            P("grp"),
        ),
        check_vma=False,
    )
```

```python
import jax
import jax.numpy as jnp
from jax import lax
from jax.experimental import pallas as pl
from jax.experimental.pallas import tpu as pltpu
from jax.sharding import PartitionSpec as P

epsilon = 1e-05
BF = jnp.bfloat16
F32 = jnp.float32
MIB = 1024 * 1024
SMEM = pl.BlockSpec(memory_space=pltpu.SMEM)
VMEM = pl.BlockSpec(memory_space=pltpu.VMEM)
shape = jax.ShapeDtypeStruct


def contract(a, b, dim_a, dim_b):
    return lax.dot_general(a, b, (((dim_a,), (dim_b,)), ((), ())), preferred_element_type=F32)


def silu_pair(pre):
    sigma = jax.nn.sigmoid(pre)
    return pre * sigma, sigma * (1.0 + pre * (1.0 - sigma))


def pack_kernel(from_high, grid, out, wide):
    features, rows, cols = grid.shape
    block = wide.shape[1]
    half = block // 2
    start = cols - block if from_high else 0
    wide[...] = grid[:, :, start : start + block].astype(F32).reshape(features * rows, block)
    lane = lax.broadcasted_iota(jnp.int32, (features, block), 1)
    for pair in range(rows // 2):
        even = wide[pl.ds(2 * pair, features, stride=rows), :]
        odd = wide[pl.ds(2 * pair + 1, features, stride=rows), :]
        if from_high:
            even = pltpu.roll(even, half, 1)
        else:
            odd = pltpu.roll(odd, half, 1)
        out[:, pair * block : (pair + 1) * block] = jnp.where(lane < half, even, odd).astype(BF)


def weights_kernel(rows, own_blocks, src, dst, count, edge_w, cot, out_w, weights_all, grad_update, acc):
    block = edge_w.shape[1]
    half = block // 2
    windows = 2 * own_blocks + 1
    west_base = rows * own_blocks
    east_base = west_base + rows // 2
    acc[...] = jnp.zeros(acc.shape, F32)
    lane = lax.broadcasted_iota(jnp.int32, (block, block), 1)

    def slot(b, carry):
        source = src[b]
        row = source // windows
        window = source - row * windows
        at = window // 2
        target = pl.ds(pl.multiple_of(dst[b] * block, block), block)
        weights = edge_w[b].astype(F32)

        @pl.when(window % 2 == 1)
        def _():
            acc[row * own_blocks + at, target, :] += weights

        @pl.when(window % 2 == 0)
        def _():
            turned = pltpu.roll(weights, half, 1)
            odd_row = row % 2 == 1
            first = jnp.where(at == 0, west_base + row // 2, row * own_blocks + at - 1)
            first_high = (at > 0) | odd_row
            second = jnp.where(at == own_blocks, east_base + row // 2, row * own_blocks + at)
            second_high = (at == own_blocks) & odd_row
            acc[first, target, :] += jnp.where(
                first_high, jnp.where(lane >= half, turned, 0.0), jnp.where(lane < half, weights, 0.0)
            )
            acc[second, target, :] += jnp.where(
                second_high, jnp.where(lane >= half, weights, 0.0), jnp.where(lane < half, turned, 0.0)
            )

        return carry

    lax.fori_loop(0, count[0], slot, 0)
    for k in range(acc.shape[0]):
        weights_all[:, k * block : (k + 1) * block] = acc[k].astype(BF)
    grad_update[...] = contract(cot[...], out_w[...], 1, 1)


def rows_kernel(grid, embed_w, x_t, embed_t, wide):
    features, rows, cols = grid.shape
    block = wide.shape[2]
    for k in range(cols // block):
        wide[k] = grid[:, :, k * block : (k + 1) * block].astype(F32).reshape(features * rows, block)
        for r in range(rows):
            x_t[:, r * cols + k * block : r * cols + (k + 1) * block] = wide[
                k, pl.ds(r, features, stride=rows), :
            ].astype(BF)
    embed_t[...] = embed_w[...].T


def own_kernel(x_t, embed_t, weights_all, h_own, slope):
    points = x_t.shape[1]
    tile = points // 8
    total = jnp.zeros(h_own.shape, F32)
    for r in range(8):
        at = slice(r * tile, (r + 1) * tile)
        hidden, hidden_slope = silu_pair(contract(embed_t[...], x_t[:, at], 1, 0))
        slope[:, at] = hidden_slope.astype(BF)
        total += contract(weights_all[:, at], hidden.astype(BF), 1, 1)
    h_own[...] = total


def halo_part(x, embed_t, weights, slope):
    hidden, hidden_slope = silu_pair(contract(embed_t[...], x[...], 1, 0))
    slope[...] = hidden_slope.astype(BF)
    return contract(weights, hidden.astype(BF), 1, 1)


def to_chunks(grads, stack, perm, start):
    count, matrices, size, _ = grads.shape
    for j in range(count):
        at = pl.ds(pl.multiple_of((perm[start + j] & 3) * size, size), size)
        for k in range(matrices):
            grads[j, k] = stack[k, at, :].astype(BF)


def from_chunks(outs, chunks, perm):
    j = 0
    for chunk in chunks:
        for n in range(chunk.shape[0]):
            size = chunk.shape[2]
            at = pl.ds(pl.multiple_of(perm[j] * size, size), size)
            for k, out in enumerate(outs):
                out[at, :] = chunk[n, k].astype(F32)
            j += 1


def rows_of_half(half, rows):
    return pl.ds(pl.multiple_of(half * rows, rows), rows)


def mesh_kernel(
    x_west, x_east, embed_t, weights_all, h_own, message_w, up_w, gain, mesh_lat, grad_update,
    sent_high, sent_low, grad_mesh, grad_gain, gathered, grad_aggregate, normed, grad_pre_up, update, slope_west, slope_east,
    stack,
):
    perm = chunk_order()
    side = x_west.shape[1]
    first = weights_all.shape[1] - 2 * side
    total = h_own[...] + halo_part(x_west, embed_t, weights_all[:, first : first + side], slope_west)
    total += halo_part(x_east, embed_t, weights_all[:, first + side :], slope_east)
    gathered[...] = total.astype(BF)
    summed = mesh_lat[...].astype(F32) + contract(gathered[...], message_w[...], 1, 0)
    rinv = lax.rsqrt(jnp.mean(summed * summed, axis=1, keepdims=True) + epsilon)
    qhat = summed * rinv
    gains = gain[...]
    normed[...] = (qhat * gains).astype(BF)
    pre_up = contract(normed[...], up_w[...], 1, 0)
    silu_up, up_slope = silu_pair(pre_up)
    update[...] = silu_up.astype(BF)
    grad_pre_up[...] = (grad_update[...] * up_slope).astype(BF)
    grad_normed = contract(grad_pre_up[...], up_w[...], 1, 1)
    grad_gain[...] = jnp.sum(grad_normed * qhat, axis=0, keepdims=True)
    grad_qhat = grad_normed * gains
    grad_q = rinv * (grad_qhat - qhat * jnp.mean(grad_qhat * qhat, axis=1, keepdims=True))
    grad_aggregate[...] = grad_q.astype(BF)
    grad_mesh[...] = grad_q
    theirs = rows_of_half(1 - perm[0] // 4, stack.shape[1])
    stack[0] = contract(gathered[:, theirs], grad_aggregate[...], 0, 0).astype(BF)
    stack[1] = contract(normed[:, theirs], grad_pre_up[...], 0, 0).astype(BF)
    to_chunks(sent_high, stack, perm, 6)
    to_chunks(sent_low, stack, perm, 4)


def tail_kernel(gathered, grad_aggregate, normed, grad_pre_up, message_w, kept_high, kept_low, back, stack):
    perm = chunk_order()
    mine = rows_of_half(perm[0] // 4, stack.shape[1])
    stack[0] = contract(gathered[:, mine], grad_aggregate[...], 0, 0).astype(BF)
    stack[1] = contract(normed[:, mine], grad_pre_up[...], 0, 0).astype(BF)
    to_chunks(kept_high, stack, perm, 2)
    to_chunks(kept_low, stack, perm, 0)
    back[...] = contract(message_w[...], grad_aggregate[...], 1, 1).astype(BF)


def points_of(x_own, x_west, x_east):
    tile = x_west.shape[1]
    pieces = []
    for x in (x_own, x_west, x_east):
        pieces += [(x, slice(k * tile, (k + 1) * tile)) for k in range(x.shape[1] // tile)]
    return [(x, at, slice(n * tile, (n + 1) * tile)) for n, (x, at) in enumerate(pieces)]


def embed_rows(half, x_parts, grad_pre, grad_gain, out):
    rows = out.shape[0]
    features = x_parts[0].shape[0]
    for side in range(2):
        count = min(rows, features - side * rows)

        @pl.when(half == side)
        def _():
            sums = jnp.zeros((count, out.shape[1]), F32)
            for x, at, all_at in points_of(*x_parts):
                sums += contract(x[side * rows : side * rows + count, at], grad_pre[:, all_at], 1, 1)
            if count < rows:
                out[...] = jnp.zeros(out.shape, F32)
                out[count : count + 1, :] = grad_gain[...]
            out[:count, :] = sums


def grid_kernel(
    back, weights_all, slope_own, slope_west, slope_east, x_own, x_west, x_east, grad_gain, update, cot,
    sent_high, sent_low, grad_pre, grad_out, stack,
):
    perm = chunk_order()
    for slope, at, all_at in points_of(slope_own, slope_west, slope_east):
        hidden = contract(back[...], weights_all[:, all_at], 1, 0)
        grad_pre[:, all_at] = (hidden * slope[:, at].astype(F32)).astype(BF)
    grad_out[...] = contract(update[...], cot[...], 0, 0).astype(BF)
    half = 1 - perm[0] // 4
    stack[0] = grad_out[rows_of_half(half, stack.shape[1]), :].astype(F32)
    embed_rows(half, (x_own, x_west, x_east), grad_pre, grad_gain, stack.at[1])
    to_chunks(sent_high, stack, perm, 6)
    to_chunks(sent_low, stack, perm, 4)


def nodes_kernel(update, out_w, mesh_lat, cot, grad_mesh, mesh_new, mesh_grad):
    mesh_new[...] = (mesh_lat[...].astype(F32) + contract(update[...], out_w[...], 1, 0)).astype(BF)
    mesh_grad[...] = cot[...].astype(F32) + grad_mesh[...]


def grid_kept_kernel(grad_pre, x_own, x_west, x_east, grad_gain, sums):
    perm = chunk_order()
    embed_rows(perm[0] // 4, (x_own, x_west, x_east), grad_pre, grad_gain, sums)


def kept_chunks_kernel(grad_out, sums, kept_high, kept_low):
    perm = chunk_order()
    for kept, start in ((kept_high, 2), (kept_low, 0)):
        count, _, size, _ = kept.shape
        for j in range(count):
            chunk = perm[start + j]
            kept[j, 0] = grad_out[pl.ds(pl.multiple_of(chunk * size, size), size), :]
            kept[j, 1] = sums[pl.ds(pl.multiple_of((chunk & 3) * size, size), size), :].astype(BF)


def order_mesh_kernel(*refs):
    from_chunks(refs[-2:], refs[:-2], chunk_order())


def order_grid_kernel(half, behind, *refs):
    perm = chunk_order()
    chunks, others, (grad_out, grad_embed, grad_gain) = refs[:3], refs[3:-3], refs[-3:]
    j = 4 * half
    for chunk in chunks:
        for n in range(chunk.shape[0]):
            size = chunk.shape[2]
            at = pl.ds(pl.multiple_of((perm[j] & 3) * size, size), size)
            grad_out[at, :] = chunk[n, 0].astype(F32)
            grad_embed[at, :] = chunk[n, 1].astype(F32)
            j += 1
    row = others[0][...] if others else jnp.zeros(grad_gain.shape, F32)
    grad_gain[...] = jnp.where(perm[4 * half] >= 4, grad_embed[behind : behind + 1, :], row)


def role_steps():
    lat = [("lat", 2 << k) for k in range(lax.axis_size("lat").bit_length() - 2)]
    lon = [("lon", 1 << k) for k in range(lax.axis_size("lon").bit_length() - 1)]
    rest = lat[1:] + lon[1:]
    return ([lat[0], lon[0]] + rest, [lon[0], lat[0]] + rest)


def core_swapped(value):
    return lax.ppermute(value, "lat", [(i, i ^ 1) for i in range(lax.axis_size("lat"))])


def swapped(value, step):
    lats = lax.axis_size("lat")
    pairs = []
    for lon in range(lax.axis_size("lon")):
        for lat in range(lats):
            axis, bit = role_steps()[lat & 1][step]
            other = (lon ^ bit) * lats + lat if axis == "lon" else lon * lats + (lat ^ bit)
            pairs.append((lon * lats + lat, other))
    return lax.ppermute(value, ("lon", "lat"), pairs)


def chunk_order():
    core = lax.axis_index("lat") & 1
    sides = []
    for steps in role_steps():
        low = [((lax.axis_index(axis) & bit) != 0).astype(jnp.int32) for axis, bit in steps[:2]]
        sides.append(2 * low[0] + low[1])
    mine = jnp.where(core == 0, sides[0], sides[1])
    theirs = jnp.where(core == 0, sides[1], sides[0])
    return [4 * core + (mine ^ j) for j in range(4)] + [4 - 4 * core + (theirs ^ j) for j in range(4)]


def added(a, b):
    return (a.astype(F32) + b.astype(F32)).astype(BF)


def halved(high, low):
    return added(low, swapped(high, 0))


def all_summed(kept):
    mine = added(kept[:1], swapped(kept[1:], 1))
    for step in range(2, len(role_steps()[0])):
        mine = added(mine, swapped(mine, step))
    second = swapped(mine, 1)
    return mine, second, swapped(jnp.concatenate([mine, second]), 0)


def from_both_cores(chunks):
    return (*chunks, *(core_swapped(chunk) for chunk in chunks))


def on_device(grid_in, mesh_lat, edge_w, edge_src, edge_dst, block_count, embed_w, message_w, up_w, out_w, gain, cot):
    rows, cols, features = grid_in.shape
    latent = message_w.shape[0]
    block = edge_w.shape[1]
    half = block // 2
    nodes = mesh_lat.shape[0]
    own = rows * cols
    side = rows * half
    points = own + 2 * side
    grid = jnp.transpose(grid_in, (2, 0, 1))

    def call(kernel, name, in_specs, out_shape, flops, bytes_accessed, limit, scratch_shapes=()):
        return pl.pallas_call(
            kernel,
            name=name,
            in_specs=in_specs,
            out_specs=[VMEM] * len(out_shape),
            out_shape=out_shape,
            scratch_shapes=list(scratch_shapes),
            compiler_params=pltpu.CompilerParams(vmem_limit_bytes=limit * MIB),
            cost_estimate=pl.CostEstimate(flops=flops, bytes_accessed=bytes_accessed, transcendentals=0),
        )

    strip = shape((features, side), BF)
    wide = pltpu.VMEM((features * rows, block), F32)
    count = lax.axis_size("lon")
    (to_east,) = call(lambda *refs: pack_kernel(True, *refs), "pack_east", [VMEM], [strip], 0, MIB, 8, [wide])(
        grid[:, :, cols - block :]
    )
    x_west = lax.ppermute(to_east, "lon", [(i, (i + 1) % count) for i in range(count)])
    to_east, later = lax.optimization_barrier((to_east, grid))
    (to_west,) = call(lambda *refs: pack_kernel(False, *refs), "pack_west", [VMEM], [strip], 0, MIB, 8, [wide])(later)
    x_east = lax.ppermute(to_west, "lon", [((i + 1) % count, i) for i in range(count)])

    weights_all, grad_update = call(
        lambda *refs: weights_kernel(rows, cols // block, *refs), "slot_weights", [SMEM] * 3 + [VMEM] * 3,
        [shape((nodes, points), BF), shape((nodes, latent), F32)],
        200_000_000, 4 * MIB, 16, [pltpu.VMEM((points // block, nodes, block), F32)],
    )(edge_src, edge_dst, block_count, edge_w, cot, out_w)
    x_own, embed_t = call(
        rows_kernel, "own_rows", [VMEM] * 2, [shape((features, own), BF), shape((latent, features), BF)],
        1_000_000_000, 5 * MIB, 16, [pltpu.VMEM((cols // block, features * rows, block), F32)],
    )(later, embed_w)
    h_own, slope_own = call(
        own_kernel, "own_points", [VMEM] * 3, [shape((nodes, latent), F32), shape((latent, own), BF)],
        2_000_000_000, 7 * MIB, 16,
    )(x_own, embed_t, weights_all)

    quarter = shape((2, 2, latent // 8, latent), BF)
    node_rows = shape((nodes, latent), BF)
    (
        sent_high, sent_low, grad_mesh, gain_term, gathered, grad_aggregate, normed, grad_pre_up, update, slope_west,
        slope_east,
    ) = call(
        mesh_kernel, "mesh_nodes", [VMEM] * 10,
        [quarter, quarter, shape((nodes, latent), F32), shape((1, latent), F32)]
        + [node_rows] * 5
        + [shape((latent, side), BF)] * 2,
        2_000_000_000, 8 * MIB, 16, [pltpu.VMEM((2, latent // 2, latent), BF)],
    )(x_west, x_east, embed_t, weights_all, h_own, message_w, up_w, gain.reshape(1, latent), mesh_lat, grad_update)
    got_high = core_swapped(sent_high)
    kept_high, kept_low, back = call(
        tail_kernel, "mesh_tail", [VMEM] * 5, [quarter, quarter, shape((latent, nodes), BF)],
        500_000_000, 3 * MIB, 16, [pltpu.VMEM((2, latent // 2, latent), BF)],
    )(gathered, grad_aggregate, normed, grad_pre_up, message_w)

    high_a, back, sent_low = lax.optimization_barrier((added(kept_high, got_high), back, sent_low))
    low_a = added(kept_low, core_swapped(sent_low))
    padded = -(-(features + 1) // 128) * 128
    assert padded == latent
    x_parts = (x_own, x_west, x_east)
    sent_high, sent_low, grad_pre, grad_out_term = call(
        grid_kernel, "grid_points", [VMEM] * 11,
        [quarter, quarter, shape((latent, points), BF), shape((latent, latent), BF)],
        1_600_000_000, 9 * MIB, 20, [pltpu.VMEM((2, latent // 2, latent), F32)],
    )(
        back, weights_all, slope_own, slope_west, slope_east, *x_parts, gain_term, update, cot
    )
    got_high, got_low = core_swapped(sent_high), core_swapped(sent_low)
    (sums_b,) = call(
        grid_kept_kernel, "grid_kept", [VMEM] * 5, [shape((latent // 2, latent), F32)], 800_000_000, 6 * MIB, 16
    )(grad_pre, *x_parts, gain_term)
    kept_a, sums_b = lax.optimization_barrier((halved(high_a, low_a), sums_b))
    kept_high, kept_low = call(
        kept_chunks_kernel, "kept_chunks", [VMEM] * 2, [quarter, quarter], 8_000_000_000, MIB, 16
    )(grad_out_term, sums_b)

    high_b, low_b = added(kept_high, got_high), added(kept_low, got_low)
    _, update, grad_mesh = lax.optimization_barrier((high_b, update, grad_mesh))
    mesh_new, mesh_grad = call(
        nodes_kernel, "mesh_outputs", [VMEM] * 5, [node_rows, shape((nodes, latent), F32)], 200_000_000, 3 * MIB, 16
    )(update, out_w, mesh_lat, cot, grad_mesh)
    summed_a = all_summed(kept_a)
    kept_b, mesh_new, mesh_grad = lax.optimization_barrier((halved(high_b, low_b), mesh_new, mesh_grad))
    summed_b = all_summed(kept_b)
    chunks_a, early_b = lax.optimization_barrier(
        (from_both_cores(summed_a), tuple(core_swapped(chunk) for chunk in summed_b[:2]))
    )
    square = shape((latent, latent), F32)
    grad_message, grad_up = call(
        order_mesh_kernel, "order_a", [VMEM] * 6, [square, square], 0, 3 * MIB, 16
    )(*chunks_a)
    last, grad_message, grad_up = lax.optimization_barrier((summed_b[2], grad_message, grad_up))
    summed_b = (*summed_b[:2], last)
    rows_half = latent // 2
    behind = features - rows_half
    outs = [square, shape((features, latent), F32), shape((1, latent), F32)]

    def order_b(half, chunks, more, more_specs, aliases):
        block_of = pl.BlockSpec((rows_half, latent), lambda i: ((lax.axis_index("lat") & 1) ^ half, 0))
        return pl.pallas_call(
            lambda *refs: order_grid_kernel(half, behind, *refs),
            name="order_b",
            grid=(1,),
            in_specs=[VMEM] * 3 + more_specs,
            out_specs=[block_of, block_of, VMEM],
            out_shape=outs,
            input_output_aliases=aliases,
            compiler_params=pltpu.CompilerParams(vmem_limit_bytes=16 * MIB),
            cost_estimate=pl.CostEstimate(flops=0, bytes_accessed=2 * MIB, transcendentals=0),
        )(*chunks, *more)

    from_other = (*early_b, core_swapped(last))
    held = order_b(0, summed_b, (), [], {})
    grad_out, grad_embed, grad_gain = order_b(
        1, from_other, (held[2], held[0], held[1]), [VMEM] + [pl.BlockSpec(memory_space=pl.ANY)] * 2, {4: 0, 5: 1}
    )
    return (mesh_new, mesh_grad, grad_embed, grad_message, grad_up, grad_out, grad_gain[0])


def solution(mesh):
    tiles = ("grp", "lon", "lat")
    return jax.shard_map(
        on_device,
        mesh=mesh,
        in_specs=(
            P(("grp", "lat"), "lon", None),
            P(tiles, None),
            P(tiles, None, None),
            P(tiles),
            P(tiles),
            P(tiles),
            P(),
            P(),
            P(),
            P(),
            P(),
            P(tiles, None),
        ),
        out_specs=(
            P(tiles, None),
            P(tiles, None),
            P("grp", None),
            P("grp", None),
            P("grp", None),
            P("grp", None),
            P("grp"),
        ),
        check_vma=False,
    )
```

```python
import jax
import jax.numpy as jnp
from jax import lax
from jax.experimental import pallas as pl
from jax.experimental.pallas import tpu as pltpu
from jax.sharding import PartitionSpec as P

epsilon = 1e-05
BF = jnp.bfloat16
F32 = jnp.float32
MIB = 1024 * 1024
SMEM = pl.BlockSpec(memory_space=pltpu.SMEM)
VMEM = pl.BlockSpec(memory_space=pltpu.VMEM)
shape = jax.ShapeDtypeStruct


def contract(a, b, dim_a, dim_b):
    return lax.dot_general(a, b, (((dim_a,), (dim_b,)), ((), ())), preferred_element_type=F32)


def silu_pair(pre):
    sigma = jax.nn.sigmoid(pre)
    return pre * sigma, sigma * (1.0 + pre * (1.0 - sigma))


def pack_side(from_high, grid, out, wide):
    features, rows, cols = grid.shape
    block = wide.shape[1]
    half = block // 2
    start = cols - block if from_high else 0
    wide[...] = grid[:, :, start : start + block].astype(F32).reshape(features * rows, block)
    lane = lax.broadcasted_iota(jnp.int32, (features, block), 1)
    for pair in range(rows // 2):
        even = wide[pl.ds(2 * pair, features, stride=rows), :]
        odd = wide[pl.ds(2 * pair + 1, features, stride=rows), :]
        if from_high:
            even = pltpu.roll(even, half, 1)
        else:
            odd = pltpu.roll(odd, half, 1)
        out[:, pair * block : (pair + 1) * block] = jnp.where(lane < half, even, odd).astype(BF)


def pack_kernel(second, grid, out, wide):
    odd_tile = lax.axis_index("lon") & 1
    high = odd_tile if second else 1 - odd_tile
    for side in range(2):

        @pl.when(high == side)
        def _():
            pack_side(side == 1, grid, out, wide)


def weights_kernel(rows, own_blocks, src, dst, count, edge_w, cot, out_w, weights_all, grad_update, acc):
    block = edge_w.shape[1]
    half = block // 2
    windows = 2 * own_blocks + 1
    odd_tile = lax.axis_index("lon") & 1
    west_base = rows * own_blocks + (1 - odd_tile) * (rows // 2)
    east_base = rows * own_blocks + odd_tile * (rows // 2)
    acc[...] = jnp.zeros(acc.shape, F32)
    lane = lax.broadcasted_iota(jnp.int32, (block, block), 1)

    def slot(b, carry):
        source = src[b]
        row = source // windows
        window = source - row * windows
        at = window // 2
        target = pl.ds(pl.multiple_of(dst[b] * block, block), block)
        weights = edge_w[b].astype(F32)

        @pl.when(window % 2 == 1)
        def _():
            acc[row * own_blocks + at, target, :] += weights

        @pl.when(window % 2 == 0)
        def _():
            turned = pltpu.roll(weights, half, 1)
            odd_row = row % 2 == 1
            first = jnp.where(at == 0, west_base + row // 2, row * own_blocks + at - 1)
            first_high = (at > 0) | odd_row
            second = jnp.where(at == own_blocks, east_base + row // 2, row * own_blocks + at)
            second_high = (at == own_blocks) & odd_row
            acc[first, target, :] += jnp.where(
                first_high, jnp.where(lane >= half, turned, 0.0), jnp.where(lane < half, weights, 0.0)
            )
            acc[second, target, :] += jnp.where(
                second_high, jnp.where(lane >= half, weights, 0.0), jnp.where(lane < half, turned, 0.0)
            )

        return carry

    lax.fori_loop(0, count[0], slot, 0)
    for k in range(acc.shape[0]):
        weights_all[:, k * block : (k + 1) * block] = acc[k].astype(BF)
    grad_update[...] = contract(cot[...], out_w[...], 1, 1)


def rows_kernel(grid, embed_w, x_t, embed_t, wide):
    features, rows, cols = grid.shape
    block = wide.shape[2]
    for k in range(cols // block):
        wide[k] = grid[:, :, k * block : (k + 1) * block].astype(F32).reshape(features * rows, block)
        for r in range(rows):
            x_t[:, r * cols + k * block : r * cols + (k + 1) * block] = wide[
                k, pl.ds(r, features, stride=rows), :
            ].astype(BF)
    embed_t[...] = embed_w[...].T


def own_kernel(x_t, embed_t, weights_all, h_own, slope):
    points = x_t.shape[1]
    tile = points // 8
    total = jnp.zeros(h_own.shape, F32)
    for r in range(8):
        at = slice(r * tile, (r + 1) * tile)
        hidden, hidden_slope = silu_pair(contract(embed_t[...], x_t[:, at], 1, 0))
        slope[:, at] = hidden_slope.astype(BF)
        total += contract(weights_all[:, at], hidden.astype(BF), 1, 1)
    h_own[...] = total


def halo_part(x, embed_t, weights, slope):
    hidden, hidden_slope = silu_pair(contract(embed_t[...], x[...], 1, 0))
    slope[...] = hidden_slope.astype(BF)
    return contract(weights, hidden.astype(BF), 1, 1)


def first_kernel(first, x, embed_t, weights_all, h_own, h_sum, slope):
    points = x.shape[1]
    h_sum[...] = h_own[...] + halo_part(x, embed_t, weights_all[:, first : first + points], slope)


def to_chunks(grads, stack, perm, start):
    count, matrices, size, _ = grads.shape
    for j in range(count):
        at = pl.ds(pl.multiple_of((perm[start + j] & 3) * size, size), size)
        for k in range(matrices):
            grads[j, k] = stack[k, at, :].astype(BF)


def from_chunks(outs, chunks, perm):
    j = 0
    for chunk in chunks:
        for n in range(chunk.shape[0]):
            size = chunk.shape[2]
            at = pl.ds(pl.multiple_of(perm[j] * size, size), size)
            for k, out in enumerate(outs):
                out[at, :] = chunk[n, k].astype(F32)
            j += 1


def rows_of_half(half, rows):
    return pl.ds(pl.multiple_of(half * rows, rows), rows)


def mesh_kernel(
    x, embed_t, weights_all, h_sum, message_w, up_w, gain, mesh_lat, grad_update,
    sent_high, sent_low, grad_mesh, grad_gain, gathered, grad_aggregate, normed, grad_pre_up, update, slope, stack,
):
    perm = chunk_order()
    points = x.shape[1]
    first = weights_all.shape[1] - points
    total = h_sum[...] + halo_part(x, embed_t, weights_all[:, first:], slope)
    gathered[...] = total.astype(BF)
    summed = mesh_lat[...].astype(F32) + contract(gathered[...], message_w[...], 1, 0)
    rinv = lax.rsqrt(jnp.mean(summed * summed, axis=1, keepdims=True) + epsilon)
    qhat = summed * rinv
    gains = gain[...]
    normed[...] = (qhat * gains).astype(BF)
    pre_up = contract(normed[...], up_w[...], 1, 0)
    silu_up, up_slope = silu_pair(pre_up)
    update[...] = silu_up.astype(BF)
    grad_pre_up[...] = (grad_update[...] * up_slope).astype(BF)
    grad_normed = contract(grad_pre_up[...], up_w[...], 1, 1)
    grad_gain[...] = jnp.sum(grad_normed * qhat, axis=0, keepdims=True)
    grad_qhat = grad_normed * gains
    grad_q = rinv * (grad_qhat - qhat * jnp.mean(grad_qhat * qhat, axis=1, keepdims=True))
    grad_aggregate[...] = grad_q.astype(BF)
    grad_mesh[...] = grad_q
    theirs = rows_of_half(1 - perm[0] // 4, stack.shape[1])
    stack[0] = contract(gathered[:, theirs], grad_aggregate[...], 0, 0).astype(BF)
    stack[1] = contract(normed[:, theirs], grad_pre_up[...], 0, 0).astype(BF)
    to_chunks(sent_high, stack, perm, 6)
    to_chunks(sent_low, stack, perm, 4)


def tail_kernel(gathered, grad_aggregate, normed, grad_pre_up, message_w, kept_high, kept_low, back, stack):
    perm = chunk_order()
    mine = rows_of_half(perm[0] // 4, stack.shape[1])
    stack[0] = contract(gathered[:, mine], grad_aggregate[...], 0, 0).astype(BF)
    stack[1] = contract(normed[:, mine], grad_pre_up[...], 0, 0).astype(BF)
    to_chunks(kept_high, stack, perm, 2)
    to_chunks(kept_low, stack, perm, 0)
    back[...] = contract(message_w[...], grad_aggregate[...], 1, 1).astype(BF)


def points_of(x_own, x_first, x_second):
    tile = x_first.shape[1]
    pieces = []
    for x in (x_own, x_first, x_second):
        pieces += [(x, slice(k * tile, (k + 1) * tile)) for k in range(x.shape[1] // tile)]
    return [(x, at, slice(n * tile, (n + 1) * tile)) for n, (x, at) in enumerate(pieces)]


def embed_rows(half, x_parts, grad_pre, grad_gain, out):
    rows = out.shape[0]
    features = x_parts[0].shape[0]
    for side in range(2):
        count = min(rows, features - side * rows)

        @pl.when(half == side)
        def _():
            sums = jnp.zeros((count, out.shape[1]), F32)
            for x, at, all_at in points_of(*x_parts):
                sums += contract(x[side * rows : side * rows + count, at], grad_pre[:, all_at], 1, 1)
            if count < rows:
                out[...] = jnp.zeros(out.shape, F32)
                out[count : count + 1, :] = grad_gain[...]
            out[:count, :] = sums


def grid_kernel(
    back, weights_all, slope_own, slope_first, slope_second, x_own, x_first, x_second, grad_gain, update, cot,
    sent_high, sent_low, grad_pre, grad_out, stack,
):
    perm = chunk_order()
    for slope, at, all_at in points_of(slope_own, slope_first, slope_second):
        hidden = contract(back[...], weights_all[:, all_at], 1, 0)
        grad_pre[:, all_at] = (hidden * slope[:, at].astype(F32)).astype(BF)
    grad_out[...] = contract(update[...], cot[...], 0, 0).astype(BF)
    half = 1 - perm[0] // 4
    stack[0] = grad_out[rows_of_half(half, stack.shape[1]), :].astype(F32)
    embed_rows(half, (x_own, x_first, x_second), grad_pre, grad_gain, stack.at[1])
    to_chunks(sent_high, stack, perm, 6)
    to_chunks(sent_low, stack, perm, 4)


def nodes_kernel(update, out_w, mesh_lat, cot, grad_mesh, mesh_new, mesh_grad):
    mesh_new[...] = (mesh_lat[...].astype(F32) + contract(update[...], out_w[...], 1, 0)).astype(BF)
    mesh_grad[...] = cot[...].astype(F32) + grad_mesh[...]


def grid_kept_kernel(grad_pre, x_own, x_first, x_second, grad_gain, sums):
    perm = chunk_order()
    embed_rows(perm[0] // 4, (x_own, x_first, x_second), grad_pre, grad_gain, sums)


def kept_chunks_kernel(grad_out, sums, kept_high, kept_low):
    perm = chunk_order()
    for kept, start in ((kept_high, 2), (kept_low, 0)):
        count, _, size, _ = kept.shape
        for j in range(count):
            chunk = perm[start + j]
            kept[j, 0] = grad_out[pl.ds(pl.multiple_of(chunk * size, size), size), :]
            kept[j, 1] = sums[pl.ds(pl.multiple_of((chunk & 3) * size, size), size), :].astype(BF)


def order_mesh_kernel(*refs):
    from_chunks(refs[-2:], refs[:-2], chunk_order())


def order_grid_kernel(half, behind, *refs):
    perm = chunk_order()
    chunks, others, (grad_out, grad_embed, grad_gain) = refs[:3], refs[3:-3], refs[-3:]
    j = 4 * half
    for chunk in chunks:
        for n in range(chunk.shape[0]):
            size = chunk.shape[2]
            at = pl.ds(pl.multiple_of((perm[j] & 3) * size, size), size)
            grad_out[at, :] = chunk[n, 0].astype(F32)
            grad_embed[at, :] = chunk[n, 1].astype(F32)
            j += 1
    row = others[0][...] if others else jnp.zeros(grad_gain.shape, F32)
    grad_gain[...] = jnp.where(perm[4 * half] >= 4, grad_embed[behind : behind + 1, :], row)


def role_steps():
    lat = [("lat", 2 << k) for k in range(lax.axis_size("lat").bit_length() - 2)]
    lon = [("lon", 1 << k) for k in range(lax.axis_size("lon").bit_length() - 1)]
    rest = lat[1:] + lon[1:]
    return ([lat[0], lon[0]] + rest, [lon[0], lat[0]] + rest)


def core_swapped(value):
    return lax.ppermute(value, "lat", [(i, i ^ 1) for i in range(lax.axis_size("lat"))])


def swapped(value, step):
    lats = lax.axis_size("lat")
    pairs = []
    for lon in range(lax.axis_size("lon")):
        for lat in range(lats):
            axis, bit = role_steps()[lat & 1][step]
            other = (lon ^ bit) * lats + lat if axis == "lon" else lon * lats + (lat ^ bit)
            pairs.append((lon * lats + lat, other))
    return lax.ppermute(value, ("lon", "lat"), pairs)


def chunk_order():
    core = lax.axis_index("lat") & 1
    sides = []
    for steps in role_steps():
        low = [((lax.axis_index(axis) & bit) != 0).astype(jnp.int32) for axis, bit in steps[:2]]
        sides.append(2 * low[0] + low[1])
    mine = jnp.where(core == 0, sides[0], sides[1])
    theirs = jnp.where(core == 0, sides[1], sides[0])
    return [4 * core + (mine ^ j) for j in range(4)] + [4 - 4 * core + (theirs ^ j) for j in range(4)]


def added(a, b):
    return (a.astype(F32) + b.astype(F32)).astype(BF)


def halved(high, low):
    return added(low, swapped(high, 0))


def all_summed(kept):
    mine = added(kept[:1], swapped(kept[1:], 1))
    for step in range(2, len(role_steps()[0])):
        mine = added(mine, swapped(mine, step))
    second = swapped(mine, 1)
    return mine, second, swapped(jnp.concatenate([mine, second]), 0)


def from_both_cores(chunks):
    return (*chunks, *(core_swapped(chunk) for chunk in chunks))


def on_device(grid_in, mesh_lat, edge_w, edge_src, edge_dst, block_count, embed_w, message_w, up_w, out_w, gain, cot):
    rows, cols, features = grid_in.shape
    latent = message_w.shape[0]
    block = edge_w.shape[1]
    half = block // 2
    nodes = mesh_lat.shape[0]
    own = rows * cols
    side = rows * half
    points = own + 2 * side
    grid = jnp.transpose(grid_in, (2, 0, 1))

    def call(kernel, name, in_specs, out_shape, flops, bytes_accessed, limit, scratch_shapes=()):
        return pl.pallas_call(
            kernel,
            name=name,
            in_specs=in_specs,
            out_specs=[VMEM] * len(out_shape),
            out_shape=out_shape,
            scratch_shapes=list(scratch_shapes),
            compiler_params=pltpu.CompilerParams(vmem_limit_bytes=limit * MIB),
            cost_estimate=pl.CostEstimate(flops=flops, bytes_accessed=bytes_accessed, transcendentals=0),
        )

    strip_shape = shape((features, side), BF)
    wide = pltpu.VMEM((features * rows, block), F32)
    count = lax.axis_size("lon")
    (strip,) = call(
        lambda *refs: pack_kernel(False, *refs), "pack_first", [VMEM], [strip_shape], 0, MIB, 8, [wide]
    )(grid)
    x_first = lax.ppermute(strip, "lon", [(i, i ^ 1) for i in range(count)])
    strip, later = lax.optimization_barrier((strip, grid))
    (strip,) = call(
        lambda *refs: pack_kernel(True, *refs), "pack_second", [VMEM], [strip_shape], 0, MIB, 8, [wide]
    )(later)
    x_second = lax.ppermute(strip, "lon", [(i, (i + 1 if i % 2 else i - 1) % count) for i in range(count)])

    weights_all, grad_update = call(
        lambda *refs: weights_kernel(rows, cols // block, *refs), "slot_weights", [SMEM] * 3 + [VMEM] * 3,
        [shape((nodes, points), BF), shape((nodes, latent), F32)],
        200_000_000, 4 * MIB, 16, [pltpu.VMEM((points // block, nodes, block), F32)],
    )(edge_src, edge_dst, block_count, edge_w, cot, out_w)
    x_own, embed_t = call(
        rows_kernel, "own_rows", [VMEM] * 2, [shape((features, own), BF), shape((latent, features), BF)],
        1_000_000_000, 5 * MIB, 16, [pltpu.VMEM((cols // block, features * rows, block), F32)],
    )(later, embed_w)
    h_own, slope_own = call(
        own_kernel, "own_points", [VMEM] * 3, [shape((nodes, latent), F32), shape((latent, own), BF)],
        2_000_000_000, 7 * MIB, 16,
    )(x_own, embed_t, weights_all)

    h_sum, slope_first = call(
        lambda *refs: first_kernel(own, *refs), "first_points", [VMEM] * 4,
        [shape((nodes, latent), F32), shape((latent, side), BF)],
        600_000_000, 3 * MIB, 16,
    )(x_first, embed_t, weights_all, h_own)

    quarter = shape((2, 2, latent // 8, latent), BF)
    node_rows = shape((nodes, latent), BF)
    (
        sent_high, sent_low, grad_mesh, gain_term, gathered, grad_aggregate, normed, grad_pre_up, update, slope_second
    ) = call(
        mesh_kernel, "mesh_nodes", [VMEM] * 9,
        [quarter, quarter, shape((nodes, latent), F32), shape((1, latent), F32)]
        + [node_rows] * 5
        + [shape((latent, side), BF)],
        2_000_000_000, 8 * MIB, 16, [pltpu.VMEM((2, latent // 2, latent), BF)],
    )(x_second, embed_t, weights_all, h_sum, message_w, up_w, gain.reshape(1, latent), mesh_lat, grad_update)
    got_high = core_swapped(sent_high)
    kept_high, kept_low, back = call(
        tail_kernel, "mesh_tail", [VMEM] * 5, [quarter, quarter, shape((latent, nodes), BF)],
        500_000_000, 3 * MIB, 16, [pltpu.VMEM((2, latent // 2, latent), BF)],
    )(gathered, grad_aggregate, normed, grad_pre_up, message_w)

    high_a, back, sent_low = lax.optimization_barrier((added(kept_high, got_high), back, sent_low))
    low_a = added(kept_low, core_swapped(sent_low))
    padded = -(-(features + 1) // 128) * 128
    assert padded == latent
    x_parts = (x_own, x_first, x_second)
    sent_high, sent_low, grad_pre, grad_out_term = call(
        grid_kernel, "grid_points", [VMEM] * 11,
        [quarter, quarter, shape((latent, points), BF), shape((latent, latent), BF)],
        1_600_000_000, 9 * MIB, 20, [pltpu.VMEM((2, latent // 2, latent), F32)],
    )(
        back, weights_all, slope_own, slope_first, slope_second, *x_parts, gain_term, update, cot
    )
    got_high, got_low = core_swapped(sent_high), core_swapped(sent_low)
    (sums_b,) = call(
        grid_kept_kernel, "grid_kept", [VMEM] * 5, [shape((latent // 2, latent), F32)], 800_000_000, 6 * MIB, 16
    )(grad_pre, *x_parts, gain_term)
    kept_a, sums_b = lax.optimization_barrier((halved(high_a, low_a), sums_b))
    kept_high, kept_low = call(
        kept_chunks_kernel, "kept_chunks", [VMEM] * 2, [quarter, quarter], 8_000_000_000, MIB, 16
    )(grad_out_term, sums_b)

    high_b, low_b = added(kept_high, got_high), added(kept_low, got_low)
    _, update, grad_mesh = lax.optimization_barrier((high_b, update, grad_mesh))
    mesh_new, mesh_grad = call(
        nodes_kernel, "mesh_outputs", [VMEM] * 5, [node_rows, shape((nodes, latent), F32)], 200_000_000, 3 * MIB, 16
    )(update, out_w, mesh_lat, cot, grad_mesh)
    summed_a = all_summed(kept_a)
    kept_b, mesh_new, mesh_grad = lax.optimization_barrier((halved(high_b, low_b), mesh_new, mesh_grad))
    summed_b = all_summed(kept_b)
    chunks_a, early_b = lax.optimization_barrier(
        (from_both_cores(summed_a), tuple(core_swapped(chunk) for chunk in summed_b[:2]))
    )
    square = shape((latent, latent), F32)
    grad_message, grad_up = call(
        order_mesh_kernel, "order_a", [VMEM] * 6, [square, square], 0, 3 * MIB, 16
    )(*chunks_a)
    last, grad_message, grad_up = lax.optimization_barrier((summed_b[2], grad_message, grad_up))
    summed_b = (*summed_b[:2], last)
    rows_half = latent // 2
    behind = features - rows_half
    outs = [square, shape((features, latent), F32), shape((1, latent), F32)]

    def order_b(half, chunks, more, more_specs, aliases):
        block_of = pl.BlockSpec((rows_half, latent), lambda i: ((lax.axis_index("lat") & 1) ^ half, 0))
        return pl.pallas_call(
            lambda *refs: order_grid_kernel(half, behind, *refs),
            name="order_b",
            grid=(1,),
            in_specs=[VMEM] * 3 + more_specs,
            out_specs=[block_of, block_of, VMEM],
            out_shape=outs,
            input_output_aliases=aliases,
            compiler_params=pltpu.CompilerParams(vmem_limit_bytes=16 * MIB),
            cost_estimate=pl.CostEstimate(flops=0, bytes_accessed=2 * MIB, transcendentals=0),
        )(*chunks, *more)

    from_other = (*early_b, core_swapped(last))
    held = order_b(0, summed_b, (), [], {})
    grad_out, grad_embed, grad_gain = order_b(
        1, from_other, (held[2], held[0], held[1]), [VMEM] + [pl.BlockSpec(memory_space=pl.ANY)] * 2, {4: 0, 5: 1}
    )
    return (mesh_new, mesh_grad, grad_embed, grad_message, grad_up, grad_out, grad_gain[0])


def solution(mesh):
    tiles = ("grp", "lon", "lat")
    return jax.shard_map(
        on_device,
        mesh=mesh,
        in_specs=(
            P(("grp", "lat"), "lon", None),
            P(tiles, None),
            P(tiles, None, None),
            P(tiles),
            P(tiles),
            P(tiles),
            P(),
            P(),
            P(),
            P(),
            P(),
            P(tiles, None),
        ),
        out_specs=(
            P(tiles, None),
            P(tiles, None),
            P("grp", None),
            P("grp", None),
            P("grp", None),
            P("grp", None),
            P("grp"),
        ),
        check_vma=False,
    )
```

```python
import jax
import jax.numpy as jnp
from jax import lax
from jax.experimental import pallas as pl
from jax.experimental.pallas import tpu as pltpu
from jax.sharding import PartitionSpec as P

epsilon = 1e-05
BF = jnp.bfloat16
F32 = jnp.float32
MIB = 1024 * 1024
SMEM = pl.BlockSpec(memory_space=pltpu.SMEM)
VMEM = pl.BlockSpec(memory_space=pltpu.VMEM)
shape = jax.ShapeDtypeStruct


def contract(a, b, dim_a, dim_b):
    return lax.dot_general(a, b, (((dim_a,), (dim_b,)), ((), ())), preferred_element_type=F32)


def silu_pair(pre):
    sigma = jax.nn.sigmoid(pre)
    return pre * sigma, sigma * (1.0 + pre * (1.0 - sigma))


def pack_side(from_high, grid, out, wide):
    features, rows, cols = grid.shape
    block = wide.shape[1]
    half = block // 2
    start = cols - block if from_high else 0
    wide[...] = grid[:, :, start : start + block].astype(F32).reshape(features * rows, block)
    lane = lax.broadcasted_iota(jnp.int32, (features, block), 1)
    for pair in range(rows // 2):
        even = wide[pl.ds(2 * pair, features, stride=rows), :]
        odd = wide[pl.ds(2 * pair + 1, features, stride=rows), :]
        if from_high:
            even = pltpu.roll(even, half, 1)
        else:
            odd = pltpu.roll(odd, half, 1)
        out[:, pair * block : (pair + 1) * block] = jnp.where(lane < half, even, odd).astype(BF)


def pack_kernel(second, grid, out, wide):
    odd_tile = lax.axis_index("lon") & 1
    high = 1 - odd_tile if second else odd_tile
    for side in range(2):

        @pl.when(high == side)
        def _():
            pack_side(side == 1, grid, out, wide)


def weights_kernel(rows, own_blocks, src, dst, count, edge_w, cot, out_w, weights_all, grad_update, acc):
    block = edge_w.shape[1]
    half = block // 2
    windows = 2 * own_blocks + 1
    odd_tile = lax.axis_index("lon") & 1
    west_base = rows * own_blocks + odd_tile * (rows // 2)
    east_base = rows * own_blocks + (1 - odd_tile) * (rows // 2)
    acc[...] = jnp.zeros(acc.shape, F32)
    lane = lax.broadcasted_iota(jnp.int32, (block, block), 1)

    def slot(b, carry):
        source = src[b]
        row = source // windows
        window = source - row * windows
        at = window // 2
        target = pl.ds(pl.multiple_of(dst[b] * block, block), block)
        weights = edge_w[b].astype(F32)

        @pl.when(window % 2 == 1)
        def _():
            acc[row * own_blocks + at, target, :] += weights

        @pl.when(window % 2 == 0)
        def _():
            turned = pltpu.roll(weights, half, 1)
            odd_row = row % 2 == 1
            first = jnp.where(at == 0, west_base + row // 2, row * own_blocks + at - 1)
            first_high = (at > 0) | odd_row
            second = jnp.where(at == own_blocks, east_base + row // 2, row * own_blocks + at)
            second_high = (at == own_blocks) & odd_row
            acc[first, target, :] += jnp.where(
                first_high, jnp.where(lane >= half, turned, 0.0), jnp.where(lane < half, weights, 0.0)
            )
            acc[second, target, :] += jnp.where(
                second_high, jnp.where(lane >= half, weights, 0.0), jnp.where(lane < half, turned, 0.0)
            )

        return carry

    lax.fori_loop(0, count[0], slot, 0)
    for k in range(acc.shape[0]):
        weights_all[:, k * block : (k + 1) * block] = acc[k].astype(BF)
    grad_update[...] = contract(cot[...], out_w[...], 1, 1)


def rows_kernel(grid, embed_w, x_t, embed_t, wide):
    features, rows, cols = grid.shape
    block = wide.shape[2]
    for k in range(cols // block):
        wide[k] = grid[:, :, k * block : (k + 1) * block].astype(F32).reshape(features * rows, block)
        for r in range(rows):
            x_t[:, r * cols + k * block : r * cols + (k + 1) * block] = wide[
                k, pl.ds(r, features, stride=rows), :
            ].astype(BF)
    embed_t[...] = embed_w[...].T


def own_kernel(x_t, embed_t, weights_all, h_own, slope):
    points = x_t.shape[1]
    tile = points // 8
    total = jnp.zeros(h_own.shape, F32)
    for r in range(8):
        at = slice(r * tile, (r + 1) * tile)
        hidden, hidden_slope = silu_pair(contract(embed_t[...], x_t[:, at], 1, 0))
        slope[:, at] = hidden_slope.astype(BF)
        total += contract(weights_all[:, at], hidden.astype(BF), 1, 1)
    h_own[...] = total


def halo_part(x, embed_t, weights, slope):
    hidden, hidden_slope = silu_pair(contract(embed_t[...], x[...], 1, 0))
    slope[...] = hidden_slope.astype(BF)
    return contract(weights, hidden.astype(BF), 1, 1)


def first_kernel(first, x, embed_t, weights_all, h_own, h_sum, slope):
    points = x.shape[1]
    h_sum[...] = h_own[...] + halo_part(x, embed_t, weights_all[:, first : first + points], slope)


def to_chunks(grads, stack, perm, start):
    count, matrices, size, _ = grads.shape
    for j in range(count):
        at = pl.ds(pl.multiple_of((perm[start + j] & 3) * size, size), size)
        for k in range(matrices):
            grads[j, k] = stack[k, at, :].astype(BF)


def from_chunks(outs, chunks, perm):
    j = 0
    for chunk in chunks:
        for n in range(chunk.shape[0]):
            size = chunk.shape[2]
            at = pl.ds(pl.multiple_of(perm[j] * size, size), size)
            for k, out in enumerate(outs):
                out[at, :] = chunk[n, k].astype(F32)
            j += 1


def rows_of_half(half, rows):
    return pl.ds(pl.multiple_of(half * rows, rows), rows)


def mesh_kernel(
    x, embed_t, weights_all, h_sum, message_w, up_w, gain, mesh_lat, grad_update,
    sent_high, sent_low, grad_mesh, grad_gain, gathered, grad_aggregate, normed, grad_pre_up, update, slope, stack,
):
    perm = chunk_order()
    points = x.shape[1]
    first = weights_all.shape[1] - points
    total = h_sum[...] + halo_part(x, embed_t, weights_all[:, first:], slope)
    gathered[...] = total.astype(BF)
    summed = mesh_lat[...].astype(F32) + contract(gathered[...], message_w[...], 1, 0)
    rinv = lax.rsqrt(jnp.mean(summed * summed, axis=1, keepdims=True) + epsilon)
    qhat = summed * rinv
    gains = gain[...]
    normed[...] = (qhat * gains).astype(BF)
    pre_up = contract(normed[...], up_w[...], 1, 0)
    silu_up, up_slope = silu_pair(pre_up)
    update[...] = silu_up.astype(BF)
    grad_pre_up[...] = (grad_update[...] * up_slope).astype(BF)
    grad_normed = contract(grad_pre_up[...], up_w[...], 1, 1)
    grad_gain[...] = jnp.sum(grad_normed * qhat, axis=0, keepdims=True)
    grad_qhat = grad_normed * gains
    grad_q = rinv * (grad_qhat - qhat * jnp.mean(grad_qhat * qhat, axis=1, keepdims=True))
    grad_aggregate[...] = grad_q.astype(BF)
    grad_mesh[...] = grad_q
    theirs = rows_of_half(1 - perm[0] // 4, stack.shape[1])
    stack[0] = contract(gathered[:, theirs], grad_aggregate[...], 0, 0).astype(BF)
    stack[1] = contract(normed[:, theirs], grad_pre_up[...], 0, 0).astype(BF)
    to_chunks(sent_high, stack, perm, 6)
    to_chunks(sent_low, stack, perm, 4)


def tail_kernel(gathered, grad_aggregate, normed, grad_pre_up, message_w, kept_high, kept_low, back, stack):
    perm = chunk_order()
    mine = rows_of_half(perm[0] // 4, stack.shape[1])
    stack[0] = contract(gathered[:, mine], grad_aggregate[...], 0, 0).astype(BF)
    stack[1] = contract(normed[:, mine], grad_pre_up[...], 0, 0).astype(BF)
    to_chunks(kept_high, stack, perm, 2)
    to_chunks(kept_low, stack, perm, 0)
    back[...] = contract(message_w[...], grad_aggregate[...], 1, 1).astype(BF)


def points_of(x_own, x_first, x_second):
    tile = x_first.shape[1]
    pieces = []
    for x in (x_own, x_first, x_second):
        pieces += [(x, slice(k * tile, (k + 1) * tile)) for k in range(x.shape[1] // tile)]
    return [(x, at, slice(n * tile, (n + 1) * tile)) for n, (x, at) in enumerate(pieces)]


def embed_rows(half, x_parts, grad_pre, grad_gain, out):
    rows = out.shape[0]
    features = x_parts[0].shape[0]
    for side in range(2):
        count = min(rows, features - side * rows)

        @pl.when(half == side)
        def _():
            sums = jnp.zeros((count, out.shape[1]), F32)
            for x, at, all_at in points_of(*x_parts):
                sums += contract(x[side * rows : side * rows + count, at], grad_pre[:, all_at], 1, 1)
            if count < rows:
                out[...] = jnp.zeros(out.shape, F32)
                out[count : count + 1, :] = grad_gain[...]
            out[:count, :] = sums


def grid_kernel(
    back, weights_all, slope_own, slope_first, slope_second, x_own, x_first, x_second, grad_gain, update, cot,
    sent_high, sent_low, grad_pre, grad_out, stack,
):
    perm = chunk_order()
    for slope, at, all_at in points_of(slope_own, slope_first, slope_second):
        hidden = contract(back[...], weights_all[:, all_at], 1, 0)
        grad_pre[:, all_at] = (hidden * slope[:, at].astype(F32)).astype(BF)
    grad_out[...] = contract(update[...], cot[...], 0, 0).astype(BF)
    half = 1 - perm[0] // 4
    stack[0] = grad_out[rows_of_half(half, stack.shape[1]), :].astype(F32)
    embed_rows(half, (x_own, x_first, x_second), grad_pre, grad_gain, stack.at[1])
    to_chunks(sent_high, stack, perm, 6)
    to_chunks(sent_low, stack, perm, 4)


def nodes_kernel(update, out_w, mesh_lat, cot, grad_mesh, mesh_new, mesh_grad):
    mesh_new[...] = (mesh_lat[...].astype(F32) + contract(update[...], out_w[...], 1, 0)).astype(BF)
    mesh_grad[...] = cot[...].astype(F32) + grad_mesh[...]


def grid_kept_kernel(grad_pre, x_own, x_first, x_second, grad_gain, sums):
    perm = chunk_order()
    embed_rows(perm[0] // 4, (x_own, x_first, x_second), grad_pre, grad_gain, sums)


def kept_chunks_kernel(grad_out, sums, kept_high, kept_low):
    perm = chunk_order()
    for kept, start in ((kept_high, 2), (kept_low, 0)):
        count, _, size, _ = kept.shape
        for j in range(count):
            chunk = perm[start + j]
            kept[j, 0] = grad_out[pl.ds(pl.multiple_of(chunk * size, size), size), :]
            kept[j, 1] = sums[pl.ds(pl.multiple_of((chunk & 3) * size, size), size), :].astype(BF)


def order_mesh_kernel(*refs):
    from_chunks(refs[-2:], refs[:-2], chunk_order())


def order_grid_kernel(half, behind, *refs):
    perm = chunk_order()
    chunks, others, (grad_out, grad_embed, grad_gain) = refs[:3], refs[3:-3], refs[-3:]
    j = 4 * half
    for chunk in chunks:
        for n in range(chunk.shape[0]):
            size = chunk.shape[2]
            at = pl.ds(pl.multiple_of((perm[j] & 3) * size, size), size)
            grad_out[at, :] = chunk[n, 0].astype(F32)
            grad_embed[at, :] = chunk[n, 1].astype(F32)
            j += 1
    row = others[0][...] if others else jnp.zeros(grad_gain.shape, F32)
    grad_gain[...] = jnp.where(perm[4 * half] >= 4, grad_embed[behind : behind + 1, :], row)


def role_steps():
    lat = [("lat", 2 << k) for k in range(lax.axis_size("lat").bit_length() - 2)]
    lon = [("lon", 1 << k) for k in range(lax.axis_size("lon").bit_length() - 1)]
    rest = lat[1:] + lon[1:]
    return ([lat[0], lon[0]] + rest, [lon[0], lat[0]] + rest)


def core_swapped(value):
    return lax.ppermute(value, "lat", [(i, i ^ 1) for i in range(lax.axis_size("lat"))])


def swapped(value, step):
    lats = lax.axis_size("lat")
    pairs = []
    for lon in range(lax.axis_size("lon")):
        for lat in range(lats):
            axis, bit = role_steps()[lat & 1][step]
            other = (lon ^ bit) * lats + lat if axis == "lon" else lon * lats + (lat ^ bit)
            pairs.append((lon * lats + lat, other))
    return lax.ppermute(value, ("lon", "lat"), pairs)


def chunk_order():
    core = lax.axis_index("lat") & 1
    sides = []
    for steps in role_steps():
        low = [((lax.axis_index(axis) & bit) != 0).astype(jnp.int32) for axis, bit in steps[:2]]
        sides.append(2 * low[0] + low[1])
    mine = jnp.where(core == 0, sides[0], sides[1])
    theirs = jnp.where(core == 0, sides[1], sides[0])
    return [4 * core + (mine ^ j) for j in range(4)] + [4 - 4 * core + (theirs ^ j) for j in range(4)]


def added(a, b):
    return (a.astype(F32) + b.astype(F32)).astype(BF)


def halved(high, low):
    return added(low, swapped(high, 0))


def all_summed(kept):
    mine = added(kept[:1], swapped(kept[1:], 1))
    for step in range(2, len(role_steps()[0])):
        mine = added(mine, swapped(mine, step))
    second = swapped(mine, 1)
    return mine, second, swapped(jnp.concatenate([mine, second]), 0)


def from_both_cores(chunks):
    return (*chunks, *(core_swapped(chunk) for chunk in chunks))


def on_device(grid_in, mesh_lat, edge_w, edge_src, edge_dst, block_count, embed_w, message_w, up_w, out_w, gain, cot):
    rows, cols, features = grid_in.shape
    latent = message_w.shape[0]
    block = edge_w.shape[1]
    half = block // 2
    nodes = mesh_lat.shape[0]
    own = rows * cols
    side = rows * half
    points = own + 2 * side
    grid = jnp.transpose(grid_in, (2, 0, 1))

    def call(kernel, name, in_specs, out_shape, flops, bytes_accessed, limit, scratch_shapes=()):
        return pl.pallas_call(
            kernel,
            name=name,
            in_specs=in_specs,
            out_specs=[VMEM] * len(out_shape),
            out_shape=out_shape,
            scratch_shapes=list(scratch_shapes),
            compiler_params=pltpu.CompilerParams(vmem_limit_bytes=limit * MIB),
            cost_estimate=pl.CostEstimate(flops=flops, bytes_accessed=bytes_accessed, transcendentals=0),
        )

    strip_shape = shape((features, side), BF)
    wide = pltpu.VMEM((features * rows, block), F32)
    count = lax.axis_size("lon")
    (strip,) = call(
        lambda *refs: pack_kernel(False, *refs), "pack_first", [VMEM], [strip_shape], 0, MIB, 8, [wide]
    )(grid)
    x_first = lax.ppermute(strip, "lon", [(i, (i + 1 if i % 2 else i - 1) % count) for i in range(count)])
    strip, later = lax.optimization_barrier((strip, grid))
    (strip,) = call(
        lambda *refs: pack_kernel(True, *refs), "pack_second", [VMEM], [strip_shape], 0, MIB, 8, [wide]
    )(later)
    x_second = lax.ppermute(strip, "lon", [(i, i ^ 1) for i in range(count)])

    weights_all, grad_update = call(
        lambda *refs: weights_kernel(rows, cols // block, *refs), "slot_weights", [SMEM] * 3 + [VMEM] * 3,
        [shape((nodes, points), BF), shape((nodes, latent), F32)],
        200_000_000, 4 * MIB, 16, [pltpu.VMEM((points // block, nodes, block), F32)],
    )(edge_src, edge_dst, block_count, edge_w, cot, out_w)
    x_own, embed_t = call(
        rows_kernel, "own_rows", [VMEM] * 2, [shape((features, own), BF), shape((latent, features), BF)],
        1_000_000_000, 5 * MIB, 16, [pltpu.VMEM((cols // block, features * rows, block), F32)],
    )(later, embed_w)
    h_own, slope_own = call(
        own_kernel, "own_points", [VMEM] * 3, [shape((nodes, latent), F32), shape((latent, own), BF)],
        2_000_000_000, 7 * MIB, 16,
    )(x_own, embed_t, weights_all)

    h_sum, slope_first = call(
        lambda *refs: first_kernel(own, *refs), "first_points", [VMEM] * 4,
        [shape((nodes, latent), F32), shape((latent, side), BF)],
        600_000_000, 3 * MIB, 16,
    )(x_first, embed_t, weights_all, h_own)

    quarter = shape((2, 2, latent // 8, latent), BF)
    node_rows = shape((nodes, latent), BF)
    (
        sent_high, sent_low, grad_mesh, gain_term, gathered, grad_aggregate, normed, grad_pre_up, update, slope_second
    ) = call(
        mesh_kernel, "mesh_nodes", [VMEM] * 9,
        [quarter, quarter, shape((nodes, latent), F32), shape((1, latent), F32)]
        + [node_rows] * 5
        + [shape((latent, side), BF)],
        2_000_000_000, 8 * MIB, 16, [pltpu.VMEM((2, latent // 2, latent), BF)],
    )(x_second, embed_t, weights_all, h_sum, message_w, up_w, gain.reshape(1, latent), mesh_lat, grad_update)
    got_high = core_swapped(sent_high)
    kept_high, kept_low, back = call(
        tail_kernel, "mesh_tail", [VMEM] * 5, [quarter, quarter, shape((latent, nodes), BF)],
        500_000_000, 3 * MIB, 16, [pltpu.VMEM((2, latent // 2, latent), BF)],
    )(gathered, grad_aggregate, normed, grad_pre_up, message_w)

    high_a, back, sent_low = lax.optimization_barrier((added(kept_high, got_high), back, sent_low))
    low_a = added(kept_low, core_swapped(sent_low))
    padded = -(-(features + 1) // 128) * 128
    assert padded == latent
    x_parts = (x_own, x_first, x_second)
    sent_high, sent_low, grad_pre, grad_out_term = call(
        grid_kernel, "grid_points", [VMEM] * 11,
        [quarter, quarter, shape((latent, points), BF), shape((latent, latent), BF)],
        1_600_000_000, 9 * MIB, 20, [pltpu.VMEM((2, latent // 2, latent), F32)],
    )(
        back, weights_all, slope_own, slope_first, slope_second, *x_parts, gain_term, update, cot
    )
    got_high, got_low = core_swapped(sent_high), core_swapped(sent_low)
    (sums_b,) = call(
        grid_kept_kernel, "grid_kept", [VMEM] * 5, [shape((latent // 2, latent), F32)], 800_000_000, 6 * MIB, 16
    )(grad_pre, *x_parts, gain_term)
    kept_a, sums_b = lax.optimization_barrier((halved(high_a, low_a), sums_b))
    kept_high, kept_low = call(
        kept_chunks_kernel, "kept_chunks", [VMEM] * 2, [quarter, quarter], 8_000_000_000, MIB, 16
    )(grad_out_term, sums_b)

    high_b, low_b = added(kept_high, got_high), added(kept_low, got_low)
    _, update, grad_mesh = lax.optimization_barrier((high_b, update, grad_mesh))
    mesh_new, mesh_grad = call(
        nodes_kernel, "mesh_outputs", [VMEM] * 5, [node_rows, shape((nodes, latent), F32)], 200_000_000, 3 * MIB, 16
    )(update, out_w, mesh_lat, cot, grad_mesh)
    summed_a = all_summed(kept_a)
    kept_b, mesh_new, mesh_grad = lax.optimization_barrier((halved(high_b, low_b), mesh_new, mesh_grad))
    summed_b = all_summed(kept_b)
    chunks_a, early_b = lax.optimization_barrier(
        (from_both_cores(summed_a), tuple(core_swapped(chunk) for chunk in summed_b[:2]))
    )
    square = shape((latent, latent), F32)
    grad_message, grad_up = call(
        order_mesh_kernel, "order_a", [VMEM] * 6, [square, square], 0, 3 * MIB, 16
    )(*chunks_a)
    last, grad_message, grad_up = lax.optimization_barrier((summed_b[2], grad_message, grad_up))
    summed_b = (*summed_b[:2], last)
    rows_half = latent // 2
    behind = features - rows_half
    outs = [square, shape((features, latent), F32), shape((1, latent), F32)]

    def order_b(half, chunks, more, more_specs, aliases):
        block_of = pl.BlockSpec((rows_half, latent), lambda i: ((lax.axis_index("lat") & 1) ^ half, 0))
        return pl.pallas_call(
            lambda *refs: order_grid_kernel(half, behind, *refs),
            name="order_b",
            grid=(1,),
            in_specs=[VMEM] * 3 + more_specs,
            out_specs=[block_of, block_of, VMEM],
            out_shape=outs,
            input_output_aliases=aliases,
            compiler_params=pltpu.CompilerParams(vmem_limit_bytes=16 * MIB),
            cost_estimate=pl.CostEstimate(flops=0, bytes_accessed=2 * MIB, transcendentals=0),
        )(*chunks, *more)

    from_other = (*early_b, core_swapped(last))
    held = order_b(0, summed_b, (), [], {})
    grad_out, grad_embed, grad_gain = order_b(
        1, from_other, (held[2], held[0], held[1]), [VMEM] + [pl.BlockSpec(memory_space=pl.ANY)] * 2, {4: 0, 5: 1}
    )
    return (mesh_new, mesh_grad, grad_embed, grad_message, grad_up, grad_out, grad_gain[0])


def solution(mesh):
    tiles = ("grp", "lon", "lat")
    return jax.shard_map(
        on_device,
        mesh=mesh,
        in_specs=(
            P(("grp", "lat"), "lon", None),
            P(tiles, None),
            P(tiles, None, None),
            P(tiles),
            P(tiles),
            P(tiles),
            P(),
            P(),
            P(),
            P(),
            P(),
            P(tiles, None),
        ),
        out_specs=(
            P(tiles, None),
            P(tiles, None),
            P("grp", None),
            P("grp", None),
            P("grp", None),
            P("grp", None),
            P("grp"),
        ),
        check_vma=False,
    )
```

```python
import jax
import jax.numpy as jnp
from jax import lax
from jax.experimental import pallas as pl
from jax.experimental.pallas import tpu as pltpu
from jax.sharding import PartitionSpec as P

epsilon = 1e-05
BF = jnp.bfloat16
F32 = jnp.float32
MIB = 1024 * 1024
SMEM = pl.BlockSpec(memory_space=pltpu.SMEM)
VMEM = pl.BlockSpec(memory_space=pltpu.VMEM)
shape = jax.ShapeDtypeStruct


def contract(a, b, dim_a, dim_b):
    return lax.dot_general(a, b, (((dim_a,), (dim_b,)), ((), ())), preferred_element_type=F32)


def silu_pair(pre):
    sigma = jax.nn.sigmoid(pre)
    return pre * sigma, sigma * (1.0 + pre * (1.0 - sigma))


def pack_kernel(from_high, grid, out, wide):
    features, rows, cols = grid.shape
    block = wide.shape[1]
    half = block // 2
    start = cols - block if from_high else 0
    wide[...] = grid[:, :, start : start + block].astype(F32).reshape(features * rows, block)
    lane = lax.broadcasted_iota(jnp.int32, (features, block), 1)
    for pair in range(rows // 2):
        even = wide[pl.ds(2 * pair, features, stride=rows), :]
        odd = wide[pl.ds(2 * pair + 1, features, stride=rows), :]
        if from_high:
            even = pltpu.roll(even, half, 1)
        else:
            odd = pltpu.roll(odd, half, 1)
        out[:, pair * block : (pair + 1) * block] = jnp.where(lane < half, even, odd).astype(BF)


def weights_kernel(rows, own_blocks, src, dst, count, edge_w, cot, out_w, weights_all, grad_update, acc):
    block = edge_w.shape[1]
    half = block // 2
    windows = 2 * own_blocks + 1
    west_base = rows * own_blocks
    east_base = west_base + rows // 2
    acc[...] = jnp.zeros(acc.shape, F32)
    lane = lax.broadcasted_iota(jnp.int32, (block, block), 1)

    def slot(b, carry):
        source = src[b]
        row = source // windows
        window = source - row * windows
        at = window // 2
        target = pl.ds(pl.multiple_of(dst[b] * block, block), block)
        weights = edge_w[b].astype(F32)

        @pl.when(window % 2 == 1)
        def _():
            acc[row * own_blocks + at, target, :] += weights

        @pl.when(window % 2 == 0)
        def _():
            turned = pltpu.roll(weights, half, 1)
            odd_row = row % 2 == 1
            first = jnp.where(at == 0, west_base + row // 2, row * own_blocks + at - 1)
            first_high = (at > 0) | odd_row
            second = jnp.where(at == own_blocks, east_base + row // 2, row * own_blocks + at)
            second_high = (at == own_blocks) & odd_row
            acc[first, target, :] += jnp.where(
                first_high, jnp.where(lane >= half, turned, 0.0), jnp.where(lane < half, weights, 0.0)
            )
            acc[second, target, :] += jnp.where(
                second_high, jnp.where(lane >= half, weights, 0.0), jnp.where(lane < half, turned, 0.0)
            )

        return carry

    lax.fori_loop(0, count[0], slot, 0)
    for k in range(acc.shape[0]):
        weights_all[:, k * block : (k + 1) * block] = acc[k].astype(BF)
    grad_update[...] = contract(cot[...], out_w[...], 1, 1)


def rows_kernel(grid, embed_w, x_t, embed_t, wide):
    features, rows, cols = grid.shape
    block = wide.shape[2]
    for k in range(cols // block):
        wide[k] = grid[:, :, k * block : (k + 1) * block].astype(F32).reshape(features * rows, block)
        for r in range(rows):
            x_t[:, r * cols + k * block : r * cols + (k + 1) * block] = wide[
                k, pl.ds(r, features, stride=rows), :
            ].astype(BF)
    embed_t[...] = embed_w[...].T


def own_kernel(x_t, embed_t, weights_all, h_own, slope):
    points = x_t.shape[1]
    tile = points // 8
    total = jnp.zeros(h_own.shape, F32)
    for r in range(8):
        at = slice(r * tile, (r + 1) * tile)
        hidden, hidden_slope = silu_pair(contract(embed_t[...], x_t[:, at], 1, 0))
        slope[:, at] = hidden_slope.astype(BF)
        total += contract(weights_all[:, at], hidden.astype(BF), 1, 1)
    h_own[...] = total


def halo_part(x, embed_t, weights, slope):
    hidden, hidden_slope = silu_pair(contract(embed_t[...], x[...], 1, 0))
    slope[...] = hidden_slope.astype(BF)
    return contract(weights, hidden.astype(BF), 1, 1)


def west_kernel(first, x, embed_t, weights_all, h_own, h_sum, slope):
    points = x.shape[1]
    h_sum[...] = h_own[...] + halo_part(x, embed_t, weights_all[:, first : first + points], slope)


def to_chunks(grads, stack, perm, start):
    count, matrices, size, _ = grads.shape
    for j in range(count):
        at = pl.ds(pl.multiple_of((perm[start + j] & 3) * size, size), size)
        for k in range(matrices):
            grads[j, k] = stack[k, at, :].astype(BF)


def from_chunks(outs, chunks, perm):
    j = 0
    for chunk in chunks:
        for n in range(chunk.shape[0]):
            size = chunk.shape[2]
            at = pl.ds(pl.multiple_of(perm[j] * size, size), size)
            for k, out in enumerate(outs):
                out[at, :] = chunk[n, k].astype(F32)
            j += 1


def rows_of_half(half, rows):
    return pl.ds(pl.multiple_of(half * rows, rows), rows)


def mesh_kernel(
    x, embed_t, weights_all, h_sum, message_w, up_w, gain, mesh_lat, grad_update,
    sent_high, sent_low, grad_mesh, grad_gain, gathered, grad_aggregate, normed, grad_pre_up, update, slope, stack,
):
    perm = chunk_order()
    points = x.shape[1]
    first = weights_all.shape[1] - points
    total = h_sum[...] + halo_part(x, embed_t, weights_all[:, first:], slope)
    gathered[...] = total.astype(BF)
    summed = mesh_lat[...].astype(F32) + contract(gathered[...], message_w[...], 1, 0)
    rinv = lax.rsqrt(jnp.mean(summed * summed, axis=1, keepdims=True) + epsilon)
    qhat = summed * rinv
    gains = gain[...]
    normed[...] = (qhat * gains).astype(BF)
    pre_up = contract(normed[...], up_w[...], 1, 0)
    silu_up, up_slope = silu_pair(pre_up)
    update[...] = silu_up.astype(BF)
    grad_pre_up[...] = (grad_update[...] * up_slope).astype(BF)
    grad_normed = contract(grad_pre_up[...], up_w[...], 1, 1)
    grad_gain[...] = jnp.sum(grad_normed * qhat, axis=0, keepdims=True)
    grad_qhat = grad_normed * gains
    grad_q = rinv * (grad_qhat - qhat * jnp.mean(grad_qhat * qhat, axis=1, keepdims=True))
    grad_aggregate[...] = grad_q.astype(BF)
    grad_mesh[...] = grad_q
    theirs = rows_of_half(1 - perm[0] // 4, stack.shape[1])
    stack[0] = contract(gathered[:, theirs], grad_aggregate[...], 0, 0).astype(BF)
    stack[1] = contract(normed[:, theirs], grad_pre_up[...], 0, 0).astype(BF)
    to_chunks(sent_high, stack, perm, 6)
    to_chunks(sent_low, stack, perm, 4)


def tail_kernel(gathered, grad_aggregate, normed, grad_pre_up, message_w, kept_high, kept_low, back, stack):
    perm = chunk_order()
    mine = rows_of_half(perm[0] // 4, stack.shape[1])
    stack[0] = contract(gathered[:, mine], grad_aggregate[...], 0, 0).astype(BF)
    stack[1] = contract(normed[:, mine], grad_pre_up[...], 0, 0).astype(BF)
    to_chunks(kept_high, stack, perm, 2)
    to_chunks(kept_low, stack, perm, 0)
    back[...] = contract(message_w[...], grad_aggregate[...], 1, 1).astype(BF)


def points_of(x_own, x_west, x_east):
    tile = x_west.shape[1]
    pieces = []
    for x in (x_own, x_west, x_east):
        pieces += [(x, slice(k * tile, (k + 1) * tile)) for k in range(x.shape[1] // tile)]
    return [(x, at, slice(n * tile, (n + 1) * tile)) for n, (x, at) in enumerate(pieces)]


def embed_rows(half, x_parts, grad_pre, grad_gain, out):
    rows = out.shape[0]
    features = x_parts[0].shape[0]
    for side in range(2):
        count = min(rows, features - side * rows)

        @pl.when(half == side)
        def _():
            sums = jnp.zeros((count, out.shape[1]), F32)
            for x, at, all_at in points_of(*x_parts):
                sums += contract(x[side * rows : side * rows + count, at], grad_pre[:, all_at], 1, 1)
            if count < rows:
                out[...] = jnp.zeros(out.shape, F32)
                out[count : count + 1, :] = grad_gain[...]
            out[:count, :] = sums


def grid_kernel(
    back, weights_all, slope_own, slope_west, slope_east, x_own, x_west, x_east, grad_gain, update, cot,
    sent_high, sent_low, grad_pre, grad_out, stack,
):
    perm = chunk_order()
    for slope, at, all_at in points_of(slope_own, slope_west, slope_east):
        hidden = contract(back[...], weights_all[:, all_at], 1, 0)
        grad_pre[:, all_at] = (hidden * slope[:, at].astype(F32)).astype(BF)
    grad_out[...] = contract(update[...], cot[...], 0, 0).astype(BF)
    half = 1 - perm[0] // 4
    stack[0] = grad_out[rows_of_half(half, stack.shape[1]), :].astype(F32)
    embed_rows(half, (x_own, x_west, x_east), grad_pre, grad_gain, stack.at[1])
    to_chunks(sent_high, stack, perm, 6)
    to_chunks(sent_low, stack, perm, 4)


def nodes_kernel(update, out_w, mesh_lat, cot, grad_mesh, mesh_new, mesh_grad):
    mesh_new[...] = (mesh_lat[...].astype(F32) + contract(update[...], out_w[...], 1, 0)).astype(BF)
    mesh_grad[...] = cot[...].astype(F32) + grad_mesh[...]


def grid_kept_kernel(grad_pre, x_own, x_west, x_east, grad_gain, sums):
    perm = chunk_order()
    embed_rows(perm[0] // 4, (x_own, x_west, x_east), grad_pre, grad_gain, sums)


def kept_chunks_kernel(grad_out, sums, kept_high, kept_low):
    perm = chunk_order()
    for kept, start in ((kept_high, 2), (kept_low, 0)):
        count, _, size, _ = kept.shape
        for j in range(count):
            chunk = perm[start + j]
            kept[j, 0] = grad_out[pl.ds(pl.multiple_of(chunk * size, size), size), :]
            kept[j, 1] = sums[pl.ds(pl.multiple_of((chunk & 3) * size, size), size), :].astype(BF)


def order_mesh_kernel(*refs):
    from_chunks(refs[-2:], refs[:-2], chunk_order())


def order_grid_kernel(half, behind, *refs):
    perm = chunk_order()
    chunks, others, (grad_out, grad_embed, grad_gain) = refs[:3], refs[3:-3], refs[-3:]
    j = 4 * half
    for chunk in chunks:
        for n in range(chunk.shape[0]):
            size = chunk.shape[2]
            at = pl.ds(pl.multiple_of((perm[j] & 3) * size, size), size)
            grad_out[at, :] = chunk[n, 0].astype(F32)
            grad_embed[at, :] = chunk[n, 1].astype(F32)
            j += 1
    row = others[0][...] if others else jnp.zeros(grad_gain.shape, F32)
    grad_gain[...] = jnp.where(perm[4 * half] >= 4, grad_embed[behind : behind + 1, :], row)


def role_steps():
    lat = [("lat", 2 << k) for k in range(lax.axis_size("lat").bit_length() - 2)]
    lon = [("lon", 1 << k) for k in range(lax.axis_size("lon").bit_length() - 1)]
    rest = lat[1:] + lon[2:]
    return (lat[:1] + lon[:2] + rest, lon[:2] + lat[:1] + rest)


def core_swapped(value):
    return lax.ppermute(value, "lat", [(i, i ^ 1) for i in range(lax.axis_size("lat"))])


def swapped(value, step):
    lats = lax.axis_size("lat")
    pairs = []
    for lon in range(lax.axis_size("lon")):
        for lat in range(lats):
            axis, bit = role_steps()[lat & 1][step]
            other = (lon ^ bit) * lats + lat if axis == "lon" else lon * lats + (lat ^ bit)
            pairs.append((lon * lats + lat, other))
    return lax.ppermute(value, ("lon", "lat"), pairs)


def chunk_order():
    core = lax.axis_index("lat") & 1
    sides = []
    for steps in role_steps():
        low = [((lax.axis_index(axis) & bit) != 0).astype(jnp.int32) for axis, bit in steps[:2]]
        sides.append(2 * low[0] + low[1])
    mine = jnp.where(core == 0, sides[0], sides[1])
    theirs = jnp.where(core == 0, sides[1], sides[0])
    return [4 * core + (mine ^ j) for j in range(4)] + [4 - 4 * core + (theirs ^ j) for j in range(4)]


def added(a, b):
    return (a.astype(F32) + b.astype(F32)).astype(BF)


def halved(high, low):
    return added(low, swapped(high, 0))


def all_summed(kept):
    mine = added(kept[:1], swapped(kept[1:], 1))
    for step in range(2, len(role_steps()[0])):
        mine = added(mine, swapped(mine, step))
    second = swapped(mine, 1)
    return mine, second, swapped(jnp.concatenate([mine, second]), 0)


def from_both_cores(chunks):
    return (*chunks, *(core_swapped(chunk) for chunk in chunks))


def on_device(grid_in, mesh_lat, edge_w, edge_src, edge_dst, block_count, embed_w, message_w, up_w, out_w, gain, cot):
    rows, cols, features = grid_in.shape
    latent = message_w.shape[0]
    block = edge_w.shape[1]
    half = block // 2
    nodes = mesh_lat.shape[0]
    own = rows * cols
    side = rows * half
    points = own + 2 * side
    grid = jnp.transpose(grid_in, (2, 0, 1))

    def call(kernel, name, in_specs, out_shape, flops, bytes_accessed, limit, scratch_shapes=()):
        return pl.pallas_call(
            kernel,
            name=name,
            in_specs=in_specs,
            out_specs=[VMEM] * len(out_shape),
            out_shape=out_shape,
            scratch_shapes=list(scratch_shapes),
            compiler_params=pltpu.CompilerParams(vmem_limit_bytes=limit * MIB),
            cost_estimate=pl.CostEstimate(flops=flops, bytes_accessed=bytes_accessed, transcendentals=0),
        )

    strip = shape((features, side), BF)
    wide = pltpu.VMEM((features * rows, block), F32)
    count = lax.axis_size("lon")
    (to_east,) = call(lambda *refs: pack_kernel(True, *refs), "pack_east", [VMEM], [strip], 0, MIB, 8, [wide])(
        grid[:, :, cols - block :]
    )
    x_west = lax.ppermute(to_east, "lon", [(i, (i + 1) % count) for i in range(count)])
    to_east, later = lax.optimization_barrier((to_east, grid))
    (to_west,) = call(lambda *refs: pack_kernel(False, *refs), "pack_west", [VMEM], [strip], 0, MIB, 8, [wide])(later)
    x_east = lax.ppermute(to_west, "lon", [((i + 1) % count, i) for i in range(count)])

    weights_all, grad_update = call(
        lambda *refs: weights_kernel(rows, cols // block, *refs), "slot_weights", [SMEM] * 3 + [VMEM] * 3,
        [shape((nodes, points), BF), shape((nodes, latent), F32)],
        200_000_000, 4 * MIB, 16, [pltpu.VMEM((points // block, nodes, block), F32)],
    )(edge_src, edge_dst, block_count, edge_w, cot, out_w)
    x_own, embed_t = call(
        rows_kernel, "own_rows", [VMEM] * 2, [shape((features, own), BF), shape((latent, features), BF)],
        1_000_000_000, 5 * MIB, 16, [pltpu.VMEM((cols // block, features * rows, block), F32)],
    )(later, embed_w)
    h_own, slope_own = call(
        own_kernel, "own_points", [VMEM] * 3, [shape((nodes, latent), F32), shape((latent, own), BF)],
        2_000_000_000, 7 * MIB, 16,
    )(x_own, embed_t, weights_all)

    h_sum, slope_west = call(
        lambda *refs: west_kernel(own, *refs), "west_points", [VMEM] * 4,
        [shape((nodes, latent), F32), shape((latent, side), BF)],
        600_000_000, 3 * MIB, 16,
    )(x_west, embed_t, weights_all, h_own)

    quarter = shape((2, 2, latent // 8, latent), BF)
    node_rows = shape((nodes, latent), BF)
    (
        sent_high, sent_low, grad_mesh, gain_term, gathered, grad_aggregate, normed, grad_pre_up, update, slope_east
    ) = call(
        mesh_kernel, "mesh_nodes", [VMEM] * 9,
        [quarter, quarter, shape((nodes, latent), F32), shape((1, latent), F32)]
        + [node_rows] * 5
        + [shape((latent, side), BF)],
        2_000_000_000, 8 * MIB, 16, [pltpu.VMEM((2, latent // 2, latent), BF)],
    )(x_east, embed_t, weights_all, h_sum, message_w, up_w, gain.reshape(1, latent), mesh_lat, grad_update)
    got_high = core_swapped(sent_high)
    kept_high, kept_low, back = call(
        tail_kernel, "mesh_tail", [VMEM] * 5, [quarter, quarter, shape((latent, nodes), BF)],
        500_000_000, 3 * MIB, 16, [pltpu.VMEM((2, latent // 2, latent), BF)],
    )(gathered, grad_aggregate, normed, grad_pre_up, message_w)

    high_a, back, sent_low = lax.optimization_barrier((added(kept_high, got_high), back, sent_low))
    low_a = added(kept_low, core_swapped(sent_low))
    padded = -(-(features + 1) // 128) * 128
    assert padded == latent
    x_parts = (x_own, x_west, x_east)
    sent_high, sent_low, grad_pre, grad_out_term = call(
        grid_kernel, "grid_points", [VMEM] * 11,
        [quarter, quarter, shape((latent, points), BF), shape((latent, latent), BF)],
        1_600_000_000, 9 * MIB, 20, [pltpu.VMEM((2, latent // 2, latent), F32)],
    )(
        back, weights_all, slope_own, slope_west, slope_east, *x_parts, gain_term, update, cot
    )
    got_high, got_low = core_swapped(sent_high), core_swapped(sent_low)
    (sums_b,) = call(
        grid_kept_kernel, "grid_kept", [VMEM] * 5, [shape((latent // 2, latent), F32)], 800_000_000, 6 * MIB, 16
    )(grad_pre, *x_parts, gain_term)
    kept_a, sums_b = lax.optimization_barrier((halved(high_a, low_a), sums_b))
    kept_high, kept_low = call(
        kept_chunks_kernel, "kept_chunks", [VMEM] * 2, [quarter, quarter], 8_000_000_000, MIB, 16
    )(grad_out_term, sums_b)

    high_b, low_b = added(kept_high, got_high), added(kept_low, got_low)
    _, update, grad_mesh = lax.optimization_barrier((high_b, update, grad_mesh))
    mesh_new, mesh_grad = call(
        nodes_kernel, "mesh_outputs", [VMEM] * 5, [node_rows, shape((nodes, latent), F32)], 200_000_000, 3 * MIB, 16
    )(update, out_w, mesh_lat, cot, grad_mesh)
    summed_a = all_summed(kept_a)
    kept_b, mesh_new, mesh_grad = lax.optimization_barrier((halved(high_b, low_b), mesh_new, mesh_grad))
    summed_b = all_summed(kept_b)
    chunks_a, early_b = lax.optimization_barrier(
        (from_both_cores(summed_a), tuple(core_swapped(chunk) for chunk in summed_b[:2]))
    )
    square = shape((latent, latent), F32)
    grad_message, grad_up = call(
        order_mesh_kernel, "order_a", [VMEM] * 6, [square, square], 0, 3 * MIB, 16
    )(*chunks_a)
    last, grad_message, grad_up = lax.optimization_barrier((summed_b[2], grad_message, grad_up))
    summed_b = (*summed_b[:2], last)
    rows_half = latent // 2
    behind = features - rows_half
    outs = [square, shape((features, latent), F32), shape((1, latent), F32)]

    def order_b(half, chunks, more, more_specs, aliases):
        block_of = pl.BlockSpec((rows_half, latent), lambda i: ((lax.axis_index("lat") & 1) ^ half, 0))
        return pl.pallas_call(
            lambda *refs: order_grid_kernel(half, behind, *refs),
            name="order_b",
            grid=(1,),
            in_specs=[VMEM] * 3 + more_specs,
            out_specs=[block_of, block_of, VMEM],
            out_shape=outs,
            input_output_aliases=aliases,
            compiler_params=pltpu.CompilerParams(vmem_limit_bytes=16 * MIB),
            cost_estimate=pl.CostEstimate(flops=0, bytes_accessed=2 * MIB, transcendentals=0),
        )(*chunks, *more)

    from_other = (*early_b, core_swapped(last))
    held = order_b(0, summed_b, (), [], {})
    grad_out, grad_embed, grad_gain = order_b(
        1, from_other, (held[2], held[0], held[1]), [VMEM] + [pl.BlockSpec(memory_space=pl.ANY)] * 2, {4: 0, 5: 1}
    )
    return (mesh_new, mesh_grad, grad_embed, grad_message, grad_up, grad_out, grad_gain[0])


def solution(mesh):
    tiles = ("grp", "lon", "lat")
    return jax.shard_map(
        on_device,
        mesh=mesh,
        in_specs=(
            P(("grp", "lat"), "lon", None),
            P(tiles, None),
            P(tiles, None, None),
            P(tiles),
            P(tiles),
            P(tiles),
            P(),
            P(),
            P(),
            P(),
            P(),
            P(tiles, None),
        ),
        out_specs=(
            P(tiles, None),
            P(tiles, None),
            P("grp", None),
            P("grp", None),
            P("grp", None),
            P("grp", None),
            P("grp"),
        ),
        check_vma=False,
    )
```
